32 devices in a mesh: rep: 16 (over z, y, x), sp: 2 (over core).
Axes of the slice: x: 2, y: 2, z: 4, core: 2. Of those that a mesh axis runs over, the one named last changes fastest.
Arguments:
- level_four: bfloat16 [16, 96, 96, 256], P('rep', 'sp'), may hold values from -25 to 25
- level_six: bfloat16 [16, 24, 24, 256], P('rep', 'sp'), may hold values from -25 to 25
- conv_weight: bfloat16 [9, 256, 256], replicated, may hold values from -0.125 to 0.125
- bn_gain: float32 [2, 256], replicated, may hold values from 0.1 to 1.9
- bn_shift: float32 [2, 256], replicated, may hold values from -3 to 3
- cotan_four: bfloat16 [16, 96, 96, 256], P('rep', 'sp'), may hold values from -6 to 6
- cotan_six: bfloat16 [16, 24, 24, 256], P('rep', 'sp'), may hold values from -6 to 6
Outputs:
- grad_four: bfloat16 [16, 96, 96, 256], P('rep', 'sp')
- grad_six: bfloat16 [16, 24, 24, 256], P('rep', 'sp')
- grad_weight: float32 [9, 256, 256], P(None, 'sp')
- grad_gain: float32 [2, 256], replicated
- grad_shift: float32 [2, 256], replicated
The draws below stay inside these ranges and needn't reach their ends.
All inputs are finite; a program needn't handle non-finite values.
Results may differ from the reference program's by a relative error of at most 0.0052.
Values may be sent and summed in bfloat16 or wider, within the bound.
No kernel may reach another device: no remote copies, remote signals or barrier semaphores. Data moves between devices by JAX's collectives and lax.ppermute only.
A program may use at most 128 MiB of HBM per device.

```python
import math
import jax
import jax.numpy as jnp
from jax import lax

C = 256
H4 = 96
W4 = 96
H6 = 24
W6 = 24
GROUP = 16
IMG_DEV = 1
BATCH = 16
N_REP = 16


def feature_map(key, heights, widths):
    base_key, chan_key = jax.random.split(key)
    base = jnp.clip(jax.random.normal(base_key, (BATCH, heights, widths, C), jnp.float32), -4.0, 4.0)
    channel = jnp.exp(jax.random.uniform(chan_key, (C,), jnp.float32, -0.7, 0.7))
    image = (jnp.arange(BATCH) % (IMG_DEV * GROUP)).astype(jnp.float32)
    height = jnp.arange(heights).astype(jnp.float32)
    position = (image[:, None] * heights + height[None, :]) / (IMG_DEV * GROUP * heights - 1)
    rise = jnp.exp(math.log(3.0) * position)
    return base * rise[:, :, None, None] * channel


def draw_level_four(key, part):
    key = jax.random.fold_in(key, 11)
    return feature_map(key, H4, W4).astype(jnp.bfloat16)


def draw_level_six(key, part):
    key = jax.random.fold_in(key, 23)
    return feature_map(key, H6, W6).astype(jnp.bfloat16)


def raised(entries, key, source, target, shards_of, factor):
    owner, partner = [(jnp.arange(entries.shape[axis_at]) // (entries.shape[axis_at] // shards_of)).reshape([-1 if axis == axis_at else 1 for axis in range(entries.ndim)]) for axis_at in (source, target)]
    chosen = jax.random.permutation(key, shards_of)[partner]
    strong = (owner == chosen) | (owner == (partner + shards_of // 2) % shards_of)
    return jnp.where(strong, factor * entries, entries)


def level_of(rng, dims, pieces, smallest, high):
    factor_of, own = 1.0, jax.random.fold_in(rng, 6)
    for axis_at, blocks in pieces:
        steps = jnp.exp(jax.random.uniform(jax.random.fold_in(own, axis_at), (blocks,), jnp.float32, smallest / len(pieces), high / len(pieces)))
        factor_of = factor_of * jnp.repeat(steps, dims[axis_at] // blocks).reshape([-1 if axis == axis_at else 1 for axis in range(len(dims))])
    return factor_of


def scatter_about(own_key, shape, deviation, reach, pieces=(), held_as=jnp.bfloat16):
    drawn = jax.random.normal(own_key, shape, jnp.float32) * deviation
    if len(pieces) > 0:
        drawn = level_of(own_key, shape, pieces, -0.22, 0.18) * drawn
    return jnp.clip(drawn, min=-reach, max=reach).astype(held_as)


def noise_with(stream_key, shape, scale, bound, shards, heavy, dtype=jnp.bfloat16):
    values = scale * jax.random.normal(stream_key, shape, jnp.float32)
    if shards:
        values = values * level_of(stream_key, shape, shards, -0.22, 0.18)
    return jnp.clip(raised(values, jax.random.fold_in(stream_key, 3), *heavy), -bound, bound).astype(dtype)


def setup_inputs(seed: int = 0) -> dict:
    splits = jax.random.split(jax.random.key(seed), 8)
    return {
        "level_four": draw_level_four(jax.random.fold_in(splits[7], 71), 0),
        "level_six": draw_level_six(jax.random.fold_in(splits[7], 71), 0),
        "conv_weight": scatter_about(splits[2], (9, C, C), (9 * C) ** -0.5, 0.125),
        "bn_gain": jnp.clip(1.0 + 0.18 * jax.random.normal(splits[3], (2, C), jnp.float32), 0.1, 1.9),
        "bn_shift": scatter_about(splits[4], (2, C), 0.5, 3.0, (), jnp.float32),
        "cotan_four": noise_with(splits[5], (BATCH, H4, W4, C), 1.0, 6.0, ((0, 16), (1, 2)), (0, 3, 16, 2.0)),
        "cotan_six": noise_with(splits[6], (BATCH, H6, W6, C), 1.0, 6.0, ((0, 16), (1, 2)), (0, 3, 16, 2.0)),
    }


EPSILON = 1e-05

def taps_forward(padded, conv_weight, rows, cols):
    result = jnp.zeros(padded.shape[:1] + (rows, cols, conv_weight.shape[2]), jnp.float32)
    for row_tap in range(3):
        for col_tap in range(3):
            result = result + jnp.einsum('nhwc,cd->nhwd', padded[:, row_tap:row_tap + rows, col_tap:col_tap + cols].astype(jnp.float32), conv_weight[3 * row_tap + col_tap].astype(jnp.float32))
    return result

def taps_backward(padded, conv_weight, rows, cols):
    result = jnp.zeros(padded.shape[:1] + (rows, cols, conv_weight.shape[1]), jnp.float32)
    for row_tap in range(3):
        for col_tap in range(3):
            result = result + jnp.einsum('nhwd,cd->nhwc', padded[:, 2 - row_tap:2 - row_tap + rows, 2 - col_tap:2 - col_tap + cols].astype(jnp.float32), conv_weight[3 * row_tap + col_tap].astype(jnp.float32))
    return result

def taps_weight(padded, gradient, rows, cols):
    terms = []
    for row_tap in range(3):
        for col_tap in range(3):
            terms.append(jnp.einsum('nhwc,nhwd->cd', padded[:, row_tap:row_tap + rows, col_tap:col_tap + cols].astype(jnp.float32), gradient.astype(jnp.float32)))
    return jnp.stack(terms)

def level_group(features, cotan, conv_weight, gain, shift):
    rows, cols = (features.shape[1], features.shape[2])
    count = features.shape[0] * rows * cols
    padded = jnp.pad(features, ((0, 0), (1, 1), (1, 1), (0, 0)))
    conv = lax.optimization_barrier(taps_forward(padded, conv_weight, rows, cols).astype(jnp.bfloat16)).astype(jnp.float32)
    mean = lax.optimization_barrier(jnp.sum(conv, (0, 1, 2))) / count
    spread = lax.optimization_barrier(jnp.sum(conv * conv, (0, 1, 2))) / count - mean * mean
    rstd = lax.rsqrt(spread + EPSILON)
    scaled = (conv - mean) * rstd
    normed = scaled * gain + shift
    sigm = jax.nn.sigmoid(normed)
    dnorm = cotan.astype(jnp.float32) * sigm * (1.0 + normed * (1.0 - sigm))
    first = lax.optimization_barrier(jnp.sum(dnorm, (0, 1, 2)))
    second = lax.optimization_barrier(jnp.sum(dnorm * scaled, (0, 1, 2)))
    dconv = (gain * rstd * (dnorm - first / count - scaled * second / count)).astype(jnp.bfloat16)
    dpadded = jnp.pad(dconv, ((0, 0), (1, 1), (1, 1), (0, 0)))
    grad_in = taps_backward(dpadded, conv_weight, rows, cols).astype(jnp.bfloat16)
    weight_part = taps_weight(padded, dconv, rows, cols)
    return (grad_in, weight_part, first, second)

def run_level(features, cotan, conv_weight, gain, shift):
    groups = N_REP // GROUP
    per_group = IMG_DEV * GROUP
    shaped = features.reshape((groups, per_group) + features.shape[1:])
    cotans = cotan.reshape((groups, per_group) + cotan.shape[1:])
    grad_in, weight_part, first, second = lax.map(lambda pair: level_group(pair[0], pair[1], conv_weight, gain, shift), (shaped, cotans))
    return (grad_in.reshape(features.shape), lax.optimization_barrier(jnp.sum(weight_part, 0)), lax.optimization_barrier(jnp.sum(first, 0)), lax.optimization_barrier(jnp.sum(second, 0)))

def reference(level_four, level_six, conv_weight, bn_gain, bn_shift, cotan_four, cotan_six):
    grad_four, weight_four, first_four, second_four = run_level(level_four, cotan_four, conv_weight, bn_gain[0], bn_shift[0])
    grad_six, weight_six, first_six, second_six = run_level(level_six, cotan_six, conv_weight, bn_gain[1], bn_shift[1])
    grad_weight = weight_four + weight_six
    grad_gain = jnp.stack([second_four, second_six])
    grad_shift = jnp.stack([first_four, first_six])
    return (grad_four, grad_six, grad_weight, grad_gain, grad_shift)
```

```python
import jax
import jax.numpy as jnp
from jax import lax
from jax.sharding import PartitionSpec as P

GROUP = 16
RADIX = 4


EPSILON = 1e-05


def padded_2(cells, sides, width):
    for axis, dim in sides:
        count = lax.axis_size(axis)
        ends = count - 1
        head = lax.slice_in_dim(cells, 0, width, axis=dim)
        tail = lax.slice_in_dim(cells, cells.shape[dim] - width, cells.shape[dim], axis=dim)
        cells = jnp.concatenate(
            [
                lax.ppermute(tail, axis, [(i, (i + 1) % count) for i in range(ends)]),
                cells,
                lax.ppermute(head, axis, [((i + 1) % count, i) for i in range(ends)]),
            ],
            axis=dim,
        )
    return cells


def taps_forward(framed, conv_weight, rows, cols):
    padded = jnp.pad(framed, ((0, 0), (0, 0), (1, 1), (0, 0)))
    result = None
    for row_tap in range(3):
        for col_tap in range(3):
            term = jnp.einsum(
                "nhwc,cd->nhwd",
                padded[:, row_tap : row_tap + rows, col_tap : col_tap + cols],
                conv_weight[3 * row_tap + col_tap],
                preferred_element_type=jnp.float32,
            )
            result = term if result is None else result + term
    return result


def taps_backward(framed, conv_weight, rows, cols):
    padded = jnp.pad(framed, ((0, 0), (0, 0), (1, 1), (0, 0)))
    result = None
    for row_tap in range(3):
        for col_tap in range(3):
            term = jnp.einsum(
                "nhwd,cd->nhwc",
                padded[:, 2 - row_tap : 2 - row_tap + rows, 2 - col_tap : 2 - col_tap + cols],
                conv_weight[3 * row_tap + col_tap],
                preferred_element_type=jnp.float32,
            )
            result = term if result is None else result + term
    return result


def taps_weight(framed, gradient, rows, cols):
    padded = jnp.pad(framed, ((0, 0), (0, 0), (1, 1), (0, 0)))
    terms = []
    for row_tap in range(3):
        for col_tap in range(3):
            terms.append(
                jnp.einsum(
                    "nhwc,nhwd->cd",
                    padded[:, row_tap : row_tap + rows, col_tap : col_tap + cols],
                    gradient,
                    preferred_element_type=jnp.float32,
                )
            )
    return jnp.stack(terms)


def digit_groups(count, stride):
    members = []
    for base in range(count):
        if base // stride % RADIX == 0:
            members.append([base + stride * digit for digit in range(RADIX)])
    return members


def exchange(pieces, stride):
    groups = digit_groups(lax.axis_size("rep"), stride)
    return lax.all_to_all(pieces, "rep", 0, 0, axis_index_groups=groups, tiled=True)


def moment_sum(moments):
    count = lax.axis_size("rep")
    if count == GROUP:
        total = lax.psum(moments, ("rep", "sp"))
        return (total, total)
    groups = [list(range(base, base + GROUP)) for base in range(0, count, GROUP)]
    total = lax.psum(lax.psum(moments, "sp"), "rep", axis_index_groups=groups)
    return (total, lax.psum(total, "rep") / GROUP)


def slope_sum(slopes):
    count = lax.axis_size("rep")
    if count == GROUP:
        copies = jnp.broadcast_to(slopes[None], (count * lax.axis_size("sp"),) + slopes.shape)
        total = jnp.sum(lax.all_to_all(copies, ("rep", "sp"), 0, 0, tiled=True), 0)
        return (total, total)
    return moment_sum(slopes)


def weight_sum(terms):
    count, sp_count = (lax.axis_size("rep"), lax.axis_size("sp"))
    share = terms.shape[1] // sp_count
    own = lax.axis_index("sp")
    total = lax.dynamic_slice_in_dim(terms, own * share, share, 1)
    for step in range(1, sp_count):
        sent = lax.dynamic_slice_in_dim(terms, (own ^ step) * share, share, 1)
        total = total + lax.ppermute(
            sent.astype(jnp.bfloat16), "sp", [(i, i ^ step) for i in range(sp_count)]
        ).astype(jnp.float32)
    shape = total.shape
    strides = []
    stride = 1
    while stride < count:
        strides.append(stride)
        stride = stride * RADIX
    total = total.reshape(-1, shape[-1])
    halved = strides[:2]
    for stride in halved:
        pieces = total.reshape(RADIX, -1, shape[-1]).astype(jnp.bfloat16)
        total = jnp.sum(exchange(pieces, stride).astype(jnp.float32), 0)
    for stride in strides[2:]:
        pieces = jnp.broadcast_to(total.astype(jnp.bfloat16)[None], (RADIX,) + total.shape)
        total = jnp.sum(exchange(pieces, stride).astype(jnp.float32), 0)
    total = total.astype(jnp.bfloat16)
    for stride in halved[::-1]:
        pieces = jnp.broadcast_to(total[None], (RADIX,) + total.shape)
        total = exchange(pieces, stride).reshape(-1, shape[-1])
    return total.reshape(shape).astype(jnp.float32)


def scale_level(conv, first, second, count):
    mean = first / count
    spread = second / count - mean * mean
    rstd = lax.rsqrt(spread + EPSILON)
    return ((conv - mean) * rstd, rstd)


def slope_level(scaled, cotan, gain, shift):
    normed = scaled * gain + shift
    sigm = jax.nn.sigmoid(normed)
    return cotan.astype(jnp.float32) * sigm * (1.0 + normed * (1.0 - sigm))


def local(level_four, level_six, conv_weight, bn_gain, bn_shift, cotan_four, cotan_six):
    sp_count = lax.axis_size("sp")
    images = level_four.shape[0]
    rows_four, cols_four = (level_four.shape[1], level_four.shape[2])
    rows_six, cols_six = (level_six.shape[1], level_six.shape[2])
    framed_four = padded_2(level_four, (("sp", 1),), 1)
    framed_six = padded_2(level_six, (("sp", 1),), 1)
    conv_four = lax.optimization_barrier(
        taps_forward(framed_four, conv_weight, rows_four, cols_four).astype(jnp.bfloat16)
    ).astype(jnp.float32)
    conv_six = lax.optimization_barrier(
        taps_forward(framed_six, conv_weight, rows_six, cols_six).astype(jnp.bfloat16)
    ).astype(jnp.float32)
    count_four = float(images * GROUP * rows_four * sp_count * cols_four)
    count_six = float(images * GROUP * rows_six * sp_count * cols_six)
    moments = jnp.stack(
        [
            jnp.sum(conv_four, (0, 1, 2)),
            jnp.sum(conv_four * conv_four, (0, 1, 2)),
            jnp.sum(conv_six, (0, 1, 2)),
            jnp.sum(conv_six * conv_six, (0, 1, 2)),
        ]
    )
    group_moments, unused = moment_sum(moments)
    scaled_four, rstd_four = scale_level(conv_four, group_moments[0], group_moments[1], count_four)
    scaled_six, rstd_six = scale_level(conv_six, group_moments[2], group_moments[3], count_six)
    slope_four = slope_level(scaled_four, cotan_four, bn_gain[0], bn_shift[0])
    slope_six = slope_level(scaled_six, cotan_six, bn_gain[1], bn_shift[1])
    slopes = jnp.stack(
        [
            jnp.sum(slope_four, (0, 1, 2)),
            jnp.sum(slope_four * scaled_four, (0, 1, 2)),
            jnp.sum(slope_six, (0, 1, 2)),
            jnp.sum(slope_six * scaled_six, (0, 1, 2)),
        ]
    )
    group_slopes, all_slopes = slope_sum(slopes)
    dconv_four = (
        bn_gain[0]
        * rstd_four
        * (slope_four - group_slopes[0] / count_four - scaled_four * group_slopes[1] / count_four)
    ).astype(jnp.bfloat16)
    dconv_six = (
        bn_gain[1]
        * rstd_six
        * (slope_six - group_slopes[2] / count_six - scaled_six * group_slopes[3] / count_six)
    ).astype(jnp.bfloat16)
    dframed_four = padded_2(dconv_four, (("sp", 1),), 1)
    dframed_six = padded_2(dconv_six, (("sp", 1),), 1)
    grad_four = taps_backward(dframed_four, conv_weight, rows_four, cols_four).astype(jnp.bfloat16)
    grad_six = taps_backward(dframed_six, conv_weight, rows_six, cols_six).astype(jnp.bfloat16)
    weight_terms = taps_weight(framed_four, dconv_four, rows_four, cols_four) + taps_weight(
        framed_six, dconv_six, rows_six, cols_six
    )
    grad_weight = weight_sum(weight_terms)
    grad_gain = jnp.stack([all_slopes[1], all_slopes[3]])
    grad_shift = jnp.stack([all_slopes[0], all_slopes[2]])
    return (grad_four, grad_six, grad_weight, grad_gain, grad_shift)


def solution(mesh):
    placed = (
        P("rep", "sp", None, None),
        P("rep", "sp", None, None),
        P(),
        P(),
        P(),
        P("rep", "sp", None, None),
        P("rep", "sp", None, None),
    )
    return jax.shard_map(
        local,
        mesh=mesh,
        in_specs=placed,
        out_specs=(
            P("rep", "sp", None, None),
            P("rep", "sp", None, None),
            P(None, "sp", None),
            P(),
            P(),
        ),
        check_vma=False,
    )
```

```python
import functools

import jax
import jax.numpy as jnp
from jax import lax
from jax.experimental import pallas as pl
from jax.experimental.pallas import tpu as pltpu
from jax.sharding import PartitionSpec as P

GROUP = 16
RADIX = 4
EPSILON = 1e-05
F32 = jnp.float32
BF16 = jnp.bfloat16
VMEM_LIMIT = 40 * 1024 * 1024


def chunk_of(rows, most):
    return max(size for size in range(1, most + 1) if rows % size == 0)


def pitch_of(cols):
    return -(-cols // 16) * 16


def widen(cells, pitch):
    cells = cells.astype(F32)
    extra = pitch - cells.shape[0]
    if extra:
        cells = jnp.concatenate([cells, jnp.zeros((extra, cells.shape[1]), F32)], 0)
    return cells


def shifted(cells, cols):
    pitch = cells.shape[0]
    col = lax.broadcasted_iota(jnp.int32, cells.shape, 0)
    left = jnp.where(col == 0, 0.0, pltpu.roll(cells, 1, 0))
    right = jnp.where(col >= cols - 1, 0.0, pltpu.roll(cells, pitch - 1, 0))
    return left, right


def put_three(three, row, parts):
    chan = parts[0].shape[1]
    for place, part in enumerate(parts):
        three[row, :, place * chan : (place + 1) * chan] = part.astype(BF16)


def frame_row(three, row, cells, cols):
    cells = widen(cells, three.shape[1])
    left, right = shifted(cells, cols)
    put_three(three, row, (left, cells, right))


def level_coefs(moments, gain, shift, count):
    mean = moments[0:1] / count
    spread = moments[1:2] / count - mean * mean
    return mean, lax.rsqrt(spread + EPSILON), gain, shift


def slope_of(conv, cotan, coefs):
    mean, rstd, gain, shift = coefs
    scaled = (conv.astype(F32) - mean) * rstd
    normed = scaled * gain + shift
    sigm = 0.5 + 0.5 * jnp.tanh(0.5 * normed)
    return scaled, cotan.astype(F32) * sigm * (1.0 + normed * (1.0 - sigm))


def masked(cells, cols):
    if cells.shape[0] == cols:
        return cells
    col = lax.broadcasted_iota(jnp.int32, cells.shape, 0)
    return jnp.where(col < cols, cells, 0.0)


def forward_level(x_ref, top, bottom, valid, w_ref, conv_ref, three, cols, most):
    rows, chan = x_ref.shape[0], x_ref.shape[2]
    pitch = three.shape[1]
    for edge in range(2):
        frame_row(three, edge, top(edge) * valid[0], cols)
        frame_row(three, rows + 2 + edge, bottom(edge) * valid[1], cols)

    def fill(row, unused):
        frame_row(three, row + 2, x_ref[row], cols)
        return unused

    lax.fori_loop(0, rows, fill, 0)

    def taps(start, size):
        total = None
        for tap in range(3):
            lhs = three[pl.ds(start + tap, size)].reshape(size * pitch, 3 * chan)
            rhs = w_ref[3 * tap : 3 * tap + 3].reshape(3 * chan, chan)
            term = jnp.dot(lhs, rhs, preferred_element_type=F32)
            total = term if total is None else total + term
        return total.astype(BF16)

    for edge in (0, rows + 1):
        conv_ref[edge] = taps(edge, 1)

    size = chunk_of(rows, most)

    def step(index, sums):
        start = index * size + 1
        conv = taps(start, size)
        conv_ref[pl.ds(start, size)] = conv.reshape(size, pitch, chan)
        conv = conv.astype(F32)
        if pitch != cols:
            col = lax.broadcasted_iota(jnp.int32, conv.shape, 0) % pitch
            conv = jnp.where(col < cols, conv, 0.0)
        conv = conv.reshape(-1, 8, chan)
        return sums[0] + jnp.sum(conv, 0), sums[1] + jnp.sum(conv * conv, 0)

    zero = jnp.zeros((8, chan), F32)
    first, second = lax.fori_loop(0, rows // size, step, (zero, zero))
    return jnp.sum(first, 0, keepdims=True), jnp.sum(second, 0, keepdims=True)


def forward_kernel(
    valid_ref, four_ref, six_ref, above_ref, below_ref, w_ref,
    conv_four_ref, conv_six_ref, moments_ref, three_four, three_six,
):
    cols_four, cols_six = four_ref.shape[1], six_ref.shape[1]
    valid = (valid_ref[0].astype(F32), valid_ref[1].astype(F32))
    base = 3 * cols_four

    def reader(ref, start, cols):
        return lambda edge: ref[start + edge * cols : start + (edge + 1) * cols].astype(F32)

    sums = forward_level(
        four_ref, reader(above_ref, 0, cols_four), reader(below_ref, 0, cols_four), valid, w_ref,
        conv_four_ref, three_four, cols_four, 16,
    )
    sums += forward_level(
        six_ref, reader(above_ref, base, cols_six), reader(below_ref, base, cols_six), valid, w_ref,
        conv_six_ref, three_six, cols_six, 16,
    )
    moments_ref[...] = jnp.concatenate(sums, 0)


def slope_level(conv_ref, cotan_ref, coefs):
    rows, cols, chan = cotan_ref.shape

    def step(row, sums):
        conv = conv_ref[row + 1][:cols]
        scaled, slope = slope_of(conv, cotan_ref[row], coefs)
        first = jnp.sum(slope.reshape(-1, 8, chan), 0)
        second = jnp.sum((slope * scaled).reshape(-1, 8, chan), 0)
        return sums[0] + first, sums[1] + second

    zero = jnp.zeros((8, chan), F32)
    first, second = lax.fori_loop(0, rows, step, (zero, zero))
    return jnp.sum(first, 0, keepdims=True), jnp.sum(second, 0, keepdims=True)


def slope_kernel(
    counts, conv_four_ref, conv_six_ref, cotan_four_ref, cotan_six_ref, moments_ref, gain_ref, shift_ref, slopes_ref
):
    sums = ()
    for level, (conv_ref, cotan_ref) in enumerate(
        ((conv_four_ref, cotan_four_ref), (conv_six_ref, cotan_six_ref))
    ):
        pair = moments_ref[2 * level : 2 * level + 2]
        here = slice(level, level + 1)
        coefs = level_coefs(pair, gain_ref[here], shift_ref[here], counts[level])
        sums += slope_level(conv_ref, cotan_ref, coefs)
    slopes_ref[...] = jnp.concatenate(sums, 0)


def backward_level(x_ref, conv_ref, cotan_ref, above, below, valid, coefs, slopes, count, dconv_ref, three, total, most):
    rows, cols, chan = x_ref.shape
    pitch = three.shape[1]
    mean, rstd, gain, shift = coefs
    lead = gain * rstd
    first, second = slopes[0:1] / count, slopes[1:2] / count

    def put(row, cotan):
        conv = conv_ref[row]
        scaled, slope = slope_of(conv, widen(cotan, pitch), coefs)
        dconv = masked(lead * (slope - first - scaled * second), cols)
        return dconv

    def store(row, dconv):
        dconv = dconv.astype(BF16).astype(F32)
        dconv_ref[row] = dconv.astype(BF16)
        left, right = shifted(dconv, cols)
        put_three(three, row, (right, dconv, left))

    def step(row, unused):
        store(row + 1, put(row + 1, cotan_ref[row]))
        return unused

    lax.fori_loop(0, rows, step, 0)
    store(0, put(0, above) * valid[0])
    store(rows + 1, put(rows + 1, below) * valid[1])

    size = chunk_of(rows, most)

    def chunk(index, unused):
        start = index * size
        cells = x_ref[pl.ds(start, size)].astype(F32)
        if pitch != cols:
            cells = jnp.concatenate([cells, jnp.zeros((size, pitch - cols, chan), F32)], 1)
        lhs = cells.astype(BF16).reshape(size * pitch, chan)
        for tap in range(3):
            rhs = three[pl.ds(start + 2 - tap, size)].reshape(size * pitch, 3 * chan)
            total[tap] += lax.dot_general(lhs, rhs, (((0,), (0,)), ((), ())), preferred_element_type=F32)
        return unused

    lax.fori_loop(0, rows // size, chunk, 0)


def backward_kernel(
    counts, place_ref, four_ref, six_ref, conv_four_ref, conv_six_ref, cotan_four_ref, cotan_six_ref,
    above_ref, below_ref, moments_ref, slopes_ref, gain_ref, shift_ref,
    dconv_four_ref, dconv_six_ref, own_ref, sent_ref, three_four, three_six, total,
):
    valid = (place_ref[0].astype(F32), place_ref[1].astype(F32))
    total[...] = jnp.zeros_like(total)
    cols_four, cols_six = four_ref.shape[1], six_ref.shape[1]
    starts = (2 * cols_four, 3 * cols_four + 2 * cols_six)
    for level, (x_ref, conv_ref, cotan_ref, dconv_ref, three) in enumerate(
        (
            (four_ref, conv_four_ref, cotan_four_ref, dconv_four_ref, three_four),
            (six_ref, conv_six_ref, cotan_six_ref, dconv_six_ref, three_six),
        )
    ):
        cols = x_ref.shape[1]
        here = slice(level, level + 1)
        pair = slice(2 * level, 2 * level + 2)
        coefs = level_coefs(moments_ref[pair], gain_ref[here], shift_ref[here], counts[level])
        edge = slice(starts[level], starts[level] + cols)
        backward_level(
            x_ref, conv_ref, cotan_ref, above_ref[edge], below_ref[edge], valid, coefs, slopes_ref[pair],
            counts[level], dconv_ref, three, total, 16,
        )
    chan = own_ref.shape[2]
    share = own_ref.shape[1]
    others = sent_ref.shape[0]
    for step in range(others + 1):
        begin = pl.multiple_of((place_ref[2] ^ step) * share, share)
        for tap in range(9):
            lanes = slice(tap % 3 * chan, (tap % 3 + 1) * chan)
            part = total[tap // 3, pl.ds(begin, share), lanes]
            if step == 0:
                own_ref[tap] = part
            else:
                sent_ref[step - 1, tap] = part.astype(BF16)


def input_level(dconv_ref, w_ref, grad_ref, three, most):
    rows, cols, chan = grad_ref.shape
    pitch = three.shape[1]

    def fill(row, unused):
        cells = dconv_ref[row].astype(F32)
        left, right = shifted(cells, cols)
        put_three(three, row, (right, cells, left))
        return unused

    lax.fori_loop(0, rows + 2, fill, 0)
    size = chunk_of(rows, most)

    def step(index, unused):
        start = index * size
        total = None
        for tap in range(3):
            lhs = three[pl.ds(start + 2 - tap, size)].reshape(size * pitch, 3 * chan)
            term = jnp.dot(lhs, w_ref[tap], preferred_element_type=F32)
            total = term if total is None else total + term
        total = total.reshape(size, pitch, chan)
        grad_ref[pl.ds(start, size)] = total[:, :cols].astype(BF16)
        return unused

    lax.fori_loop(0, rows // size, step, 0)


def input_kernel(dconv_four_ref, dconv_six_ref, w_ref, grad_four_ref, grad_six_ref, three_four, three_six):
    input_level(dconv_four_ref, w_ref, grad_four_ref, three_four, 16)
    input_level(dconv_six_ref, w_ref, grad_six_ref, three_six, 16)


def swap(array, axis, stride):
    count = lax.axis_size(axis)
    return lax.ppermute(array, axis, [(i, i ^ stride) for i in range(count)])


def edge_rows(cells, cotan, last):
    rows, cols, chan = cells.shape
    inner = cells[rows - 2 :] if last else cells[:2]
    outer = cotan[rows - 1 :] if last else cotan[:1]
    return [inner.reshape(2 * cols, chan), outer.reshape(cols, chan)]


def edges(four, six, cotan_four, cotan_six):
    count = lax.axis_size("sp")
    heads = jnp.concatenate(edge_rows(four, cotan_four, False) + edge_rows(six, cotan_six, False), 0)
    tails = jnp.concatenate(edge_rows(four, cotan_four, True) + edge_rows(six, cotan_six, True), 0)
    if count == 2:
        met = swap(jnp.where(lax.axis_index("sp") == 0, tails, heads), "sp", 1)
        return met, met
    above = lax.ppermute(tails, "sp", [(i, (i + 1) % count) for i in range(count)])
    below = lax.ppermute(heads, "sp", [((i + 1) % count, i) for i in range(count)])
    return above, below


def group_sum(sums):
    for axis, count in (("sp", lax.axis_size("sp")), ("rep", GROUP)):
        stride = 1
        while stride < count:
            sums = sums + swap(sums, axis, stride)
            stride = 2 * stride
    return sums


def every_group(sums):
    stride = GROUP
    while stride < lax.axis_size("rep"):
        sums = sums + swap(sums, "rep", stride)
        stride = 2 * stride
    return sums


def digit_order(parts, digit):
    odd = digit % 2 == 1
    high = digit >= 2
    even = [jnp.where(odd, parts[k ^ 1], parts[k]) for k in range(4)]
    return jnp.stack([jnp.where(high, even[k ^ 2], even[k]) for k in range(4)])


def weight_sum(own, sent):
    share, chan = own.shape[1], own.shape[2]
    total = own
    for step in range(1, sent.shape[0] + 1):
        total = total + swap(sent[step - 1], "sp", step).astype(F32)
    shape = total.shape
    total = total.reshape(-1, chan)
    count = lax.axis_size("rep")
    strides = []
    while RADIX ** len(strides) < count:
        strides.append(RADIX ** len(strides))
    scattered = strides[:2]
    for stride in scattered:
        digit = lax.axis_index("rep") // stride % RADIX
        pieces = total.reshape(RADIX, -1, chan)
        total = lax.dynamic_index_in_dim(pieces, digit, 0, False)
        met = [
            swap(lax.dynamic_index_in_dim(pieces, digit ^ k, 0, False).astype(BF16), "rep", k * stride)
            for k in range(1, RADIX)
        ]
        total = (total + met[0].astype(F32)) + (met[1].astype(F32) + met[2].astype(F32))
    total = total.astype(BF16)
    for stride in strides[2:]:
        met = [swap(total, "rep", k * stride).astype(F32) for k in range(1, RADIX)]
        total = ((total.astype(F32) + met[0]) + (met[1] + met[2])).astype(BF16)
    for stride in scattered[::-1]:
        digit = lax.axis_index("rep") // stride % RADIX
        met = [total] + [swap(total, "rep", k * stride) for k in range(1, RADIX)]
        total = digit_order(met, digit).reshape(-1, chan)
    return total.reshape(shape).astype(F32)


def local(level_four, level_six, conv_weight, bn_gain, bn_shift, cotan_four, cotan_six):
    sp_count, sp_index = lax.axis_size("sp"), lax.axis_index("sp")
    images = level_four.shape[0]
    four, six, cot_four, cot_six = (a[0] for a in (level_four, level_six, cotan_four, cotan_six))
    rows_four, cols_four, chan = four.shape
    rows_six, cols_six = six.shape[:2]
    pitch_four, pitch_six = pitch_of(cols_four), pitch_of(cols_six)
    counts = (
        float(images * GROUP * rows_four * sp_count * cols_four),
        float(images * GROUP * rows_six * sp_count * cols_six),
    )
    place = jnp.stack([sp_index > 0, sp_index < sp_count - 1, sp_index]).astype(jnp.int32)
    above, below = edges(four, six, cot_four, cot_six)
    smem = pl.BlockSpec(memory_space=pltpu.SMEM)
    vmem = pl.BlockSpec(memory_space=pltpu.VMEM)
    params = pltpu.CompilerParams(vmem_limit_bytes=VMEM_LIMIT)
    framed_four = jax.ShapeDtypeStruct((rows_four + 2, pitch_four, chan), BF16)
    framed_six = jax.ShapeDtypeStruct((rows_six + 2, pitch_six, chan), BF16)
    four_sums = jax.ShapeDtypeStruct((4, chan), F32)
    flops = 2 * 9 * chan * chan * (rows_four * cols_four + rows_six * cols_six)

    def cost(share, size):
        return pl.CostEstimate(flops=int(flops * share), bytes_accessed=size, transcendentals=0)

    conv_four, conv_six, moments = pl.pallas_call(
        forward_kernel,
        out_shape=(framed_four, framed_six, four_sums),
        in_specs=[smem] + [vmem] * 5,
        out_specs=(vmem, vmem, vmem),
        scratch_shapes=[
            pltpu.VMEM((rows_four + 4, pitch_four, 3 * chan), BF16),
            pltpu.VMEM((rows_six + 4, pitch_six, 3 * chan), BF16),
        ],
        compiler_params=params,
        cost_estimate=cost(1, 4 * four.size),
        name="forward",
    )(place, four, six, above, below, conv_weight)
    moments = group_sum(moments)

    slopes = pl.pallas_call(
        functools.partial(slope_kernel, counts),
        out_shape=four_sums,
        in_specs=[vmem] * 7,
        out_specs=vmem,
        compiler_params=params,
        cost_estimate=cost(0.01, 4 * four.size),
        name="slopes",
    )(conv_four, conv_six, cot_four, cot_six, moments, bn_gain, bn_shift)
    slopes = group_sum(slopes)

    share = chan // sp_count
    dconv_four, dconv_six, own, sent = pl.pallas_call(
        functools.partial(backward_kernel, counts),
        out_shape=(
            framed_four,
            framed_six,
            jax.ShapeDtypeStruct((9, share, chan), F32),
            jax.ShapeDtypeStruct((sp_count - 1, 9, share, chan), BF16),
        ),
        in_specs=[smem] + [vmem] * 12,
        out_specs=(vmem,) * 4,
        scratch_shapes=[
            pltpu.VMEM((rows_four + 2, pitch_four, 3 * chan), BF16),
            pltpu.VMEM((rows_six + 2, pitch_six, 3 * chan), BF16),
            pltpu.VMEM((3, chan, 3 * chan), F32),
        ],
        compiler_params=params,
        cost_estimate=cost(1.2, 8 * four.size),
        name="backward",
    )(
        place, four, six, conv_four, conv_six, cot_four, cot_six, above, below, moments, slopes, bn_gain, bn_shift
    )

    turned = conv_weight.reshape(3, 3, chan, chan).transpose(0, 1, 3, 2).reshape(3, 3 * chan, chan)
    grad_four, grad_six = pl.pallas_call(
        input_kernel,
        out_shape=(
            jax.ShapeDtypeStruct(four.shape, BF16),
            jax.ShapeDtypeStruct(six.shape, BF16),
        ),
        in_specs=[vmem] * 3,
        out_specs=(vmem, vmem),
        scratch_shapes=[
            pltpu.VMEM((rows_four + 2, pitch_four, 3 * chan), BF16),
            pltpu.VMEM((rows_six + 2, pitch_six, 3 * chan), BF16),
        ],
        compiler_params=params,
        cost_estimate=cost(1, 4 * four.size),
        name="inputs",
    )(dconv_four, dconv_six, turned)

    grad_weight = weight_sum(own, sent)
    totals = every_group(slopes)
    grad_gain = jnp.stack([totals[1], totals[3]])
    grad_shift = jnp.stack([totals[0], totals[2]])
    return (grad_four[None], grad_six[None], grad_weight, grad_gain, grad_shift)


def solution(mesh):
    placed = (
        P("rep", "sp", None, None),
        P("rep", "sp", None, None),
        P(),
        P(),
        P(),
        P("rep", "sp", None, None),
        P("rep", "sp", None, None),
    )
    return jax.shard_map(
        local,
        mesh=mesh,
        in_specs=placed,
        out_specs=(
            P("rep", "sp", None, None),
            P("rep", "sp", None, None),
            P(None, "sp", None),
            P(),
            P(),
        ),
        check_vma=False,
    )
```

```python
import functools

import jax
import jax.numpy as jnp
from jax import lax
from jax.experimental import pallas as pl
from jax.experimental.pallas import tpu as pltpu
from jax.sharding import PartitionSpec as P

GROUP = 16
RADIX = 4
EPSILON = 1e-05
F32 = jnp.float32
BF16 = jnp.bfloat16
VMEM_LIMIT = 40 * 1024 * 1024


def chunk_of(rows, most):
    return max(size for size in range(1, most + 1) if rows % size == 0)


def pitch_of(cols):
    return -(-cols // 16) * 16


def widen(cells, pitch):
    cells = cells.astype(F32)
    extra = pitch - cells.shape[0]
    if extra:
        cells = jnp.concatenate([cells, jnp.zeros((extra, cells.shape[1]), F32)], 0)
    return cells


def shifted(cells, cols):
    pitch = cells.shape[0]
    col = lax.broadcasted_iota(jnp.int32, cells.shape, 0)
    left = jnp.where(col == 0, 0.0, pltpu.roll(cells, 1, 0))
    right = jnp.where(col >= cols - 1, 0.0, pltpu.roll(cells, pitch - 1, 0))
    return left, right


def put_three(three, row, parts):
    chan = parts[0].shape[1]
    for place, part in enumerate(parts):
        three[row, :, place * chan : (place + 1) * chan] = part.astype(BF16)


def frame_row(three, row, cells, cols):
    cells = widen(cells, three.shape[1])
    left, right = shifted(cells, cols)
    put_three(three, row, (left, cells, right))


def level_coefs(moments, gain, shift, count):
    mean = moments[0:1] / count
    spread = moments[1:2] / count - mean * mean
    return mean, lax.rsqrt(spread + EPSILON), gain, shift


def slope_of(conv, cotan, coefs):
    mean, rstd, gain, shift = coefs
    scaled = (conv.astype(F32) - mean) * rstd
    normed = scaled * gain + shift
    sigm = 0.5 + 0.5 * jnp.tanh(0.5 * normed)
    return scaled, cotan.astype(F32) * sigm * (1.0 + normed * (1.0 - sigm))


def masked(cells, cols):
    if cells.shape[0] == cols:
        return cells
    col = lax.broadcasted_iota(jnp.int32, cells.shape, 0)
    return jnp.where(col < cols, cells, 0.0)


def forward_level(x_ref, top, bottom, valid, w_ref, conv_ref, three, cols, most):
    rows, chan = x_ref.shape[0], x_ref.shape[2]
    pitch = three.shape[1]
    for edge in range(2):
        frame_row(three, edge, top(edge) * valid[0], cols)
        frame_row(three, rows + 2 + edge, bottom(edge) * valid[1], cols)

    def fill(row, unused):
        frame_row(three, row + 2, x_ref[row], cols)
        return unused

    lax.fori_loop(0, rows, fill, 0)

    def taps(start, size):
        total = None
        for tap in range(3):
            lhs = three[pl.ds(start + tap, size)].reshape(size * pitch, 3 * chan)
            rhs = w_ref[3 * tap : 3 * tap + 3].reshape(3 * chan, chan)
            term = jnp.dot(lhs, rhs, preferred_element_type=F32)
            total = term if total is None else total + term
        return total.astype(BF16)

    for edge in (0, rows + 1):
        conv_ref[edge] = taps(edge, 1)

    size = chunk_of(rows, most)

    def step(index, sums):
        start = index * size + 1
        conv = taps(start, size)
        conv_ref[pl.ds(start, size)] = conv.reshape(size, pitch, chan)
        conv = conv.astype(F32)
        if pitch != cols:
            col = lax.broadcasted_iota(jnp.int32, conv.shape, 0) % pitch
            conv = jnp.where(col < cols, conv, 0.0)
        conv = conv.reshape(-1, 8, chan)
        return sums[0] + jnp.sum(conv, 0), sums[1] + jnp.sum(conv * conv, 0)

    zero = jnp.zeros((8, chan), F32)
    first, second = lax.fori_loop(0, rows // size, step, (zero, zero))
    return jnp.sum(first, 0, keepdims=True), jnp.sum(second, 0, keepdims=True)


def forward_kernel(
    valid_ref, four_ref, six_ref, above_ref, below_ref, w_ref,
    conv_four_ref, conv_six_ref, moments_ref, three_four, three_six,
):
    cols_four, cols_six = four_ref.shape[1], six_ref.shape[1]
    valid = (valid_ref[0].astype(F32), valid_ref[1].astype(F32))
    base, pitch_six = 3 * cols_four, three_six.shape[1]

    def reader(ref, start, pitch):
        return lambda edge: ref[start + edge * pitch : start + (edge + 1) * pitch].astype(F32)

    sums = forward_level(
        four_ref, reader(above_ref, 0, cols_four), reader(below_ref, 0, cols_four), valid, w_ref,
        conv_four_ref, three_four, cols_four, 16,
    )
    sums += forward_level(
        six_ref, reader(above_ref, base, pitch_six), reader(below_ref, base, pitch_six), valid, w_ref,
        conv_six_ref, three_six, cols_six, 16,
    )
    moments_ref[...] = jnp.concatenate(sums, 0)


def slope_level(conv_ref, cotan_ref, coefs):
    rows, cols, chan = cotan_ref.shape

    def step(row, sums):
        conv = conv_ref[row + 1][:cols]
        scaled, slope = slope_of(conv, cotan_ref[row], coefs)
        first = jnp.sum(slope.reshape(-1, 8, chan), 0)
        second = jnp.sum((slope * scaled).reshape(-1, 8, chan), 0)
        return sums[0] + first, sums[1] + second

    zero = jnp.zeros((8, chan), F32)
    first, second = lax.fori_loop(0, rows, step, (zero, zero))
    return jnp.sum(first, 0, keepdims=True), jnp.sum(second, 0, keepdims=True)


def slope_kernel(
    counts, conv_four_ref, conv_six_ref, cotan_four_ref, cotan_six_ref, moments_ref, gain_ref, shift_ref, slopes_ref
):
    sums = ()
    for level, (conv_ref, cotan_ref) in enumerate(
        ((conv_four_ref, cotan_four_ref), (conv_six_ref, cotan_six_ref))
    ):
        pair = moments_ref[2 * level : 2 * level + 2]
        here = slice(level, level + 1)
        coefs = level_coefs(pair, gain_ref[here], shift_ref[here], counts[level])
        sums += slope_level(conv_ref, cotan_ref, coefs)
    slopes_ref[...] = jnp.broadcast_to(jnp.concatenate(sums, 0)[None], slopes_ref.shape)


def backward_level(x_ref, conv_ref, cotan_ref, above, below, valid, coefs, slopes, count, dconv_ref, three, total, most, out_copy):
    rows, cols, chan = x_ref.shape
    pitch = three.shape[1]
    mean, rstd, gain, shift = coefs
    lead = gain * rstd
    first, second = slopes[0:1] / count, slopes[1:2] / count

    def put(row, cotan):
        conv = conv_ref[row]
        scaled, slope = slope_of(conv, widen(cotan, pitch), coefs)
        dconv = masked(lead * (slope - first - scaled * second), cols)
        return dconv

    def store(row, dconv):
        dconv = dconv.astype(BF16).astype(F32)
        dconv_ref[row] = dconv.astype(BF16)
        left, right = shifted(dconv, cols)
        put_three(three, row, (right, dconv, left))

    def step(row, unused):
        store(row + 1, put(row + 1, cotan_ref[row]))
        return unused

    lax.fori_loop(0, rows, step, 0)
    store(0, put(0, above) * valid[0])
    store(rows + 1, put(rows + 1, below) * valid[1])
    if out_copy is not None:
        out_copy.start()

    size = chunk_of(rows, most)

    def chunk(index, unused):
        start = index * size
        cells = x_ref[pl.ds(start, size)].astype(F32)
        if pitch != cols:
            cells = jnp.concatenate([cells, jnp.zeros((size, pitch - cols, chan), F32)], 1)
        lhs = cells.astype(BF16).reshape(size * pitch, chan)
        for tap in range(3):
            rhs = three[pl.ds(start + 2 - tap, size)].reshape(size * pitch, 3 * chan)
            total[tap] += lax.dot_general(lhs, rhs, (((0,), (0,)), ((), ())), preferred_element_type=F32)
        return unused

    lax.fori_loop(0, rows // size, chunk, 0)


def backward_kernel(
    counts, place_ref, four_ref, six_ref, conv_four_ref, conv_six_ref, cotan_four_ref, cotan_six_ref,
    above_ref, below_ref, moments_ref, near_ref, far_ref, gain_ref, shift_ref,
    dconv_four_ref, dconv_six_ref, own_ref, sent_ref, slopes_ref, three_four, three_six, total, framed_four, sem,
):
    valid = (place_ref[0].astype(F32), place_ref[1].astype(F32))
    total[...] = jnp.zeros_like(total)
    slopes_ref[...] = jnp.sum(near_ref[...], 0) + jnp.sum(far_ref[...], 0)
    cols_four = four_ref.shape[1]
    out_copy = pltpu.make_async_copy(framed_four, dconv_four_ref, sem)
    starts = (2 * cols_four, 3 * cols_four + 2 * three_six.shape[1])
    for level, (x_ref, conv_ref, cotan_ref, dconv_ref, three) in enumerate(
        (
            (four_ref, conv_four_ref, cotan_four_ref, framed_four, three_four),
            (six_ref, conv_six_ref, cotan_six_ref, dconv_six_ref, three_six),
        )
    ):
        cols = x_ref.shape[1]
        here = slice(level, level + 1)
        pair = slice(2 * level, 2 * level + 2)
        coefs = level_coefs(moments_ref[pair], gain_ref[here], shift_ref[here], counts[level])
        edge = slice(starts[level], starts[level] + three.shape[1])
        backward_level(
            x_ref, conv_ref, cotan_ref, above_ref[edge], below_ref[edge], valid, coefs, slopes_ref[pair],
            counts[level], dconv_ref, three, total, 16, out_copy if level == 0 else None,
        )
    chan = own_ref.shape[2]
    share = own_ref.shape[1]
    others = sent_ref.shape[0]
    for step in range(others + 1):
        begin = pl.multiple_of((place_ref[2] ^ step) * share, share)
        for tap in range(9):
            lanes = slice(tap % 3 * chan, (tap % 3 + 1) * chan)
            part = total[tap // 3, pl.ds(begin, share), lanes]
            if step == 0:
                own_ref[tap] = part
            else:
                sent_ref[step - 1, tap] = part.astype(BF16)
    out_copy.wait()


def input_level(dconv_ref, w_ref, grad_ref, three, most):
    rows, cols, chan = grad_ref.shape
    pitch = three.shape[1]

    def fill(row, unused):
        cells = dconv_ref[row].astype(F32)
        left, right = shifted(cells, cols)
        put_three(three, row, (right, cells, left))
        return unused

    lax.fori_loop(0, rows + 2, fill, 0)
    size = chunk_of(rows, most)

    def step(index, unused):
        start = index * size
        total = None
        for tap in range(3):
            lhs = three[pl.ds(start + 2 - tap, size)].reshape(size * pitch, 3 * chan)
            term = jnp.dot(lhs, w_ref[tap], preferred_element_type=F32)
            total = term if total is None else total + term
        total = total.reshape(size, pitch, chan)
        grad_ref[pl.ds(start, size)] = total[:, :cols].astype(BF16)
        return unused

    lax.fori_loop(0, rows // size, step, 0)


def input_kernel(
    dconv_four_ref, dconv_six_ref, w_ref, grad_four_ref, grad_six_ref, three_four, three_six, framed_four, sem
):
    copy = pltpu.make_async_copy(dconv_four_ref, framed_four, sem)
    copy.start()
    input_level(dconv_six_ref, w_ref, grad_six_ref, three_six, 16)
    copy.wait()
    input_level(framed_four, w_ref, grad_four_ref, three_four, 16)


def swap(array, axis, stride):
    count = lax.axis_size(axis)
    return lax.ppermute(array, axis, [(i, i ^ stride) for i in range(count)])


def edge_kernel(starts, place_ref, four_ref, six_ref, cotan_four_ref, cotan_six_ref, *rest):
    outs, sems = rest[:-1], rest[-1]
    rows_four, cols_four = four_ref.shape[:2]
    rows_six = six_ref.shape[0]
    pitch = pitch_of(six_ref.shape[1])
    copies = []
    for number, (start, out_ref) in enumerate(zip(starts, outs)):
        last = (1 - place_ref[0]) if start is None else start
        for part, (ref, row) in enumerate(
            (
                (four_ref, last * (rows_four - 2)),
                (four_ref, last * (rows_four - 2) + 1),
                (cotan_four_ref, last * (rows_four - 1)),
            )
        ):
            copy = pltpu.make_async_copy(
                ref.at[row], out_ref.at[part * cols_four : (part + 1) * cols_four], sems.at[number, part]
            )
            copy.start()
            copies.append(copy)
        for part, (ref, row) in enumerate(
            (
                (six_ref, last * (rows_six - 2)),
                (six_ref, last * (rows_six - 2) + 1),
                (cotan_six_ref, last * (rows_six - 1)),
            )
        ):
            begin = 3 * cols_four + part * pitch
            out_ref[begin : begin + pitch] = widen(ref[row], pitch).astype(BF16)
    for copy in copies:
        copy.wait()


def edges(place, four, six, cotan_four, cotan_six):
    count = lax.axis_size("sp")
    starts = (None,) if count == 2 else (0, 1)
    length = 3 * four.shape[1] + 3 * pitch_of(six.shape[1])
    vmem = pl.BlockSpec(memory_space=pltpu.VMEM)
    hbm = pl.BlockSpec(memory_space=pltpu.HBM)
    outs = pl.pallas_call(
        functools.partial(edge_kernel, starts),
        out_shape=tuple(jax.ShapeDtypeStruct((length, four.shape[2]), BF16) for _ in starts),
        in_specs=[pl.BlockSpec(memory_space=pltpu.SMEM), hbm, vmem, hbm, vmem],
        out_specs=tuple(vmem for _ in starts),
        scratch_shapes=[pltpu.SemaphoreType.DMA((len(starts), 3))],
        compiler_params=pltpu.CompilerParams(vmem_limit_bytes=4 * 1024 * 1024),
        name="edges",
    )(place, four, six, cotan_four, cotan_six)
    if count == 2:
        met = swap(outs[0], "sp", 1)
        return met, met
    above = lax.ppermute(outs[1], "sp", [(i, (i + 1) % count) for i in range(count)])
    below = lax.ppermute(outs[0], "sp", [((i + 1) % count, i) for i in range(count)])
    return above, below


def group_sum(sums):
    stride = 1
    while stride < lax.axis_size("sp"):
        sums = sums + swap(sums, "sp", stride)
        stride = 2 * stride
    stride = 1
    while stride < GROUP:
        met = [swap(sums, "rep", k * stride) for k in range(1, RADIX)]
        sums = (sums + met[0]) + (met[1] + met[2])
        stride = RADIX * stride
    return sums


def group_parts(copies):
    count = lax.axis_size("rep")
    groups = [list(range(base, base + GROUP)) for base in range(0, count, GROUP)]
    met = lax.all_to_all(copies, "rep", 0, 0, axis_index_groups=groups if count > GROUP else None, tiled=True)
    parts = [met]
    stride = 1
    while stride < lax.axis_size("sp"):
        if stride > 1:
            parts = [parts[0] + parts[1]]
        parts.append(swap(parts[0], "sp", stride))
        stride = 2 * stride
    return parts


def every_group(sums):
    stride = GROUP
    while stride < lax.axis_size("rep"):
        sums = sums + swap(sums, "rep", stride)
        stride = 2 * stride
    return sums


def digit_order(parts, digit):
    odd = digit % 2 == 1
    high = digit >= 2
    even = [jnp.where(odd, parts[k ^ 1], parts[k]) for k in range(4)]
    return jnp.stack([jnp.where(high, even[k ^ 2], even[k]) for k in range(4)])


def weight_pieces(own, sent):
    total = own
    for step in range(1, sent.shape[0] + 1):
        total = total + swap(sent[step - 1], "sp", step).astype(F32)
    total = total.reshape(RADIX, RADIX, -1, own.shape[2]).swapaxes(0, 1)
    return total.reshape(GROUP, -1, own.shape[2]).astype(BF16)


def weight_scatter(pieces):
    count = lax.axis_size("rep")
    groups = [list(range(base, base + GROUP)) for base in range(0, count, GROUP)]
    return lax.all_to_all(pieces, "rep", 0, 0, axis_index_groups=groups if count > GROUP else None, tiled=True)


def weight_gather(pieces):
    total = jnp.sum(pieces.astype(F32), 0).astype(BF16)
    chan = total.shape[1]
    stride = GROUP
    while stride < lax.axis_size("rep"):
        met = [swap(total, "rep", k * stride).astype(F32) for k in range(1, RADIX)]
        total = ((total.astype(F32) + met[0]) + (met[1] + met[2])).astype(BF16)
        stride = RADIX * stride
    stride = GROUP // RADIX
    while stride >= 1:
        digit = lax.axis_index("rep") // stride % RADIX
        met = [total] + [swap(total, "rep", k * stride) for k in range(1, RADIX)]
        total = digit_order(met, digit).reshape(-1, chan)
        stride = stride // RADIX
    return total.astype(F32)


def local(level_four, level_six, conv_weight, bn_gain, bn_shift, cotan_four, cotan_six):
    sp_count, sp_index = lax.axis_size("sp"), lax.axis_index("sp")
    images = level_four.shape[0]
    four, six, cot_four, cot_six = (a[0] for a in (level_four, level_six, cotan_four, cotan_six))
    rows_four, cols_four, chan = four.shape
    rows_six, cols_six = six.shape[:2]
    pitch_four, pitch_six = pitch_of(cols_four), pitch_of(cols_six)
    counts = (
        float(images * GROUP * rows_four * sp_count * cols_four),
        float(images * GROUP * rows_six * sp_count * cols_six),
    )
    place = jnp.stack([sp_index > 0, sp_index < sp_count - 1, sp_index]).astype(jnp.int32)
    above, below = edges(place, four, six, cot_four, cot_six)
    smem = pl.BlockSpec(memory_space=pltpu.SMEM)
    vmem = pl.BlockSpec(memory_space=pltpu.VMEM)
    hbm = pl.BlockSpec(memory_space=pltpu.HBM)
    params = pltpu.CompilerParams(vmem_limit_bytes=VMEM_LIMIT)
    framed_four = jax.ShapeDtypeStruct((rows_four + 2, pitch_four, chan), BF16)
    framed_six = jax.ShapeDtypeStruct((rows_six + 2, pitch_six, chan), BF16)
    four_sums = jax.ShapeDtypeStruct((4, chan), F32)
    flops = 2 * 9 * chan * chan * (rows_four * cols_four + rows_six * cols_six)

    def cost(share, size):
        return pl.CostEstimate(flops=int(flops * share), bytes_accessed=size, transcendentals=0)

    conv_four, conv_six, moments = pl.pallas_call(
        forward_kernel,
        out_shape=(framed_four, framed_six, four_sums),
        in_specs=[smem] + [vmem] * 5,
        out_specs=(vmem, vmem, vmem),
        scratch_shapes=[
            pltpu.VMEM((rows_four + 4, pitch_four, 3 * chan), BF16),
            pltpu.VMEM((rows_six + 4, pitch_six, 3 * chan), BF16),
        ],
        compiler_params=params,
        cost_estimate=cost(1, 4 * four.size),
        name="forward",
    )(place, four, six, above, below, conv_weight)
    moments = group_sum(moments)

    slopes = pl.pallas_call(
        functools.partial(slope_kernel, counts),
        out_shape=jax.ShapeDtypeStruct((GROUP, 4, chan), F32),
        in_specs=[vmem] * 7,
        out_specs=vmem,
        compiler_params=params,
        cost_estimate=cost(0.01, 4 * four.size),
        name="slopes",
    )(conv_four, conv_six, cot_four, cot_six, moments, bn_gain, bn_shift)
    slope_parts = group_parts(slopes)

    share = chan // sp_count
    dconv_four, dconv_six, own, sent, slopes = pl.pallas_call(
        functools.partial(backward_kernel, counts),
        out_shape=(
            framed_four,
            framed_six,
            jax.ShapeDtypeStruct((9, share, chan), F32),
            jax.ShapeDtypeStruct((sp_count - 1, 9, share, chan), BF16),
            four_sums,
        ),
        in_specs=[smem] + [vmem] * 13,
        out_specs=(hbm,) + (vmem,) * 4,
        scratch_shapes=[
            pltpu.VMEM((rows_four + 2, pitch_four, 3 * chan), BF16),
            pltpu.VMEM((rows_six + 2, pitch_six, 3 * chan), BF16),
            pltpu.VMEM((3, chan, 3 * chan), F32),
            pltpu.VMEM(framed_four.shape, BF16),
            pltpu.SemaphoreType.DMA,
        ],
        compiler_params=params,
        cost_estimate=cost(1.2, 8 * four.size),
        name="backward",
    )(
        place, four, six, conv_four, conv_six, cot_four, cot_six, above, below, moments, *slope_parts,
        bn_gain, bn_shift,
    )

    pieces = weight_pieces(own, sent)
    pieces, dconv_four = lax.optimization_barrier((pieces, dconv_four))
    pieces = weight_scatter(pieces)
    turned = conv_weight.reshape(3, 3, chan, chan).transpose(0, 1, 3, 2).reshape(3, 3 * chan, chan)
    grad_four, grad_six = pl.pallas_call(
        input_kernel,
        out_shape=(
            jax.ShapeDtypeStruct(four.shape, BF16),
            jax.ShapeDtypeStruct(six.shape, BF16),
        ),
        in_specs=[hbm, vmem, vmem],
        out_specs=(vmem, vmem),
        scratch_shapes=[
            pltpu.VMEM((rows_four + 2, pitch_four, 3 * chan), BF16),
            pltpu.VMEM((rows_six + 2, pitch_six, 3 * chan), BF16),
            pltpu.VMEM(framed_four.shape, BF16),
            pltpu.SemaphoreType.DMA,
        ],
        compiler_params=params,
        cost_estimate=cost(1, 4 * four.size),
        name="inputs",
    )(dconv_four, dconv_six, turned)

    pieces, grad_six = lax.optimization_barrier((pieces, grad_six))
    grad_weight = weight_gather(pieces).reshape(own.shape)
    totals = every_group(slopes)
    grad_gain = jnp.stack([totals[1], totals[3]])
    grad_shift = jnp.stack([totals[0], totals[2]])
    return (grad_four[None], grad_six[None], grad_weight, grad_gain, grad_shift)


def solution(mesh):
    placed = (
        P("rep", "sp", None, None),
        P("rep", "sp", None, None),
        P(),
        P(),
        P(),
        P("rep", "sp", None, None),
        P("rep", "sp", None, None),
    )
    return jax.shard_map(
        local,
        mesh=mesh,
        in_specs=placed,
        out_specs=(
            P("rep", "sp", None, None),
            P("rep", "sp", None, None),
            P(None, "sp", None),
            P(),
            P(),
        ),
        check_vma=False,
    )
```

```python
import functools

import jax
import jax.numpy as jnp
from jax import lax
from jax.experimental import pallas as pl
from jax.experimental.pallas import tpu as pltpu
from jax.sharding import PartitionSpec as P

GROUP = 16
RADIX = 4
EPSILON = 1e-05
F32 = jnp.float32
BF16 = jnp.bfloat16
VMEM_LIMIT = 40 * 1024 * 1024
EDGE_LIMIT = 60 * 1024 * 1024


def chunk_of(rows, most):
    return max(size for size in range(1, most + 1) if rows % size == 0)


def pitch_of(cols):
    return -(-cols // 16) * 16


def chunks_of(rows, most):
    size = chunk_of(rows, most)
    return [(start, start + size) for start in range(0, rows, size)]


def widen(cells, pitch):
    cells = cells.astype(F32)
    extra = pitch - cells.shape[0]
    if extra:
        cells = jnp.concatenate([cells, jnp.zeros((extra, cells.shape[1]), F32)], 0)
    return cells


def put_three(three, row, cells, cols, turned):
    pitch, chan = cells.shape
    col = lax.broadcasted_iota(jnp.int32, cells.shape, 0)
    left = jnp.where(col == 0, 0.0, pltpu.roll(cells, 1, 0))
    right = jnp.where(col >= cols - 1, 0.0, pltpu.roll(cells, pitch - 1, 0))
    parts = (right, cells, left) if turned else (left, cells, right)
    for place, part in enumerate(parts):
        three[row, :, place * chan : (place + 1) * chan] = part.astype(BF16)


def beside(three, starts, size):
    pitch, width = three.shape[1:]
    return jnp.concatenate([three[start : start + size].reshape(size * pitch, width) for start in starts], 1)


def level_coefs(moments, gain, shift, count):
    mean = moments[0:1] / count
    spread = moments[1:2] / count - mean * mean
    return mean, lax.rsqrt(spread + EPSILON), gain, shift


def slope_of(conv, cotan, coefs):
    mean, rstd, gain, shift = coefs
    centred = conv.astype(F32) - mean
    half = centred * (0.5 * rstd * gain) + 0.5 * shift
    turn = jnp.tanh(half)
    return centred, cotan.astype(F32) * ((1.0 + turn) * (1.0 + half * (1.0 - turn)))


def masked(cells, cols):
    if cells.shape[0] == cols:
        return cells
    col = lax.broadcasted_iota(jnp.int32, cells.shape, 0)
    return jnp.where(col < cols, cells, 0.0)


def staged(fills, dots):
    fills[0]()
    for index, dot in enumerate(dots):
        if index + 1 < len(fills):
            fills[index + 1]()
        dot()


def forward_level(x_ref, top, bottom, valid, w_ref, conv_ref, three, sums, most):
    rows, cols, chan = x_ref.shape
    pitch = three.shape[1]

    def fill_row(row):
        if row < 2:
            cells = top(row) * valid[0]
        elif row < rows + 2:
            cells = widen(x_ref[row - 2], pitch)
        else:
            cells = bottom(row - rows - 2) * valid[1]
        put_three(three, row, cells, cols, False)

    def dot(start, end, index):
        lhs = beside(three, (start, start + 1, start + 2), end - start)
        conv = jnp.dot(lhs, w_ref[...].reshape(9 * chan, chan), preferred_element_type=F32).astype(BF16)
        conv = conv.reshape(end - start, pitch, chan)
        conv_ref[start:end] = conv
        first, last = max(start, 1), min(end, rows + 1)
        conv = conv[first - start : last - start].astype(F32)
        if pitch != cols:
            conv = conv[:, :cols]
        conv = conv.reshape(-1, 8, chan)
        sums[0].append(jnp.sum(conv, 0))
        sums[1].append(jnp.sum(conv * conv, 0))

    chunks = [[start + 1, end + 1] for start, end in chunks_of(rows, most)]
    chunks[0][0] = 0
    chunks[-1][1] = rows + 2
    fills, dots, done = [], [], 0
    for index, (start, end) in enumerate(chunks):
        fills.append(lambda todo=range(done, end + 2): [fill_row(row) for row in todo])
        done = end + 2
        dots.append(functools.partial(dot, start, end, index))
    return fills, dots


def folded(parts):
    total = parts[0]
    for part in parts[1:]:
        total = total + part
    return jnp.sum(total, 0, keepdims=True)


def forward_kernel(
    valid_ref, four_ref, six_ref, above_ref, below_ref, w_ref,
    conv_four_ref, conv_six_ref, moments_ref, three_four, three_six,
):
    cols_four = four_ref.shape[1]
    valid = (valid_ref[0].astype(F32), valid_ref[1].astype(F32))
    base, pitch_six = 3 * cols_four, three_six.shape[1]

    def reader(ref, start, pitch):
        return lambda edge: ref[start + edge * pitch : start + (edge + 1) * pitch].astype(F32)

    sums_four, sums_six = ([], []), ([], [])
    fills_six, dots_six = forward_level(
        six_ref, reader(above_ref, base, pitch_six), reader(below_ref, base, pitch_six), valid, w_ref,
        conv_six_ref, three_six, sums_six, 12,
    )
    fills_four, dots_four = forward_level(
        four_ref, reader(above_ref, 0, cols_four), reader(below_ref, 0, cols_four), valid, w_ref,
        conv_four_ref, three_four, sums_four, 8,
    )
    staged(fills_six + fills_four, dots_six + dots_four)
    sums = [folded(parts) for parts in sums_four + sums_six]
    moments_ref[...] = jnp.concatenate(sums, 0)


def slope_level(conv_ref, cotan_ref, coefs):
    rows, cols, chan = cotan_ref.shape

    def step(row, sums):
        conv = conv_ref[row + 1][:cols]
        centred, slope = slope_of(conv, cotan_ref[row], coefs)
        first = jnp.sum(slope.reshape(-1, 8, chan), 0)
        second = jnp.sum((slope * centred).reshape(-1, 8, chan), 0)
        return sums[0] + first, sums[1] + second

    zero = jnp.zeros((8, chan), F32)
    first, second = lax.fori_loop(0, rows, step, (zero, zero), unroll=3)
    first = 0.5 * jnp.sum(first, 0, keepdims=True)
    return first, 0.5 * coefs[1] * jnp.sum(second, 0, keepdims=True)


def slope_kernel(
    counts, conv_four_ref, conv_six_ref, cotan_four_ref, cotan_six_ref, moments_ref, gain_ref, shift_ref, slopes_ref
):
    sums = ()
    for level, (conv_ref, cotan_ref) in enumerate(
        ((conv_four_ref, cotan_four_ref), (conv_six_ref, cotan_six_ref))
    ):
        pair = moments_ref[2 * level : 2 * level + 2]
        here = slice(level, level + 1)
        coefs = level_coefs(pair, gain_ref[here], shift_ref[here], counts[level])
        sums += slope_level(conv_ref, cotan_ref, coefs)
    slopes_ref[...] = jnp.concatenate(sums, 0)


def backward_level(x_ref, conv_ref, cotan_ref, above, below, valid, coefs, slopes, count, dconv_ref, three, put, most):
    rows, cols, chan = x_ref.shape
    pitch = three.shape[1]
    mean, rstd, gain, shift = coefs
    lead = gain * rstd
    offset, factor = lead * (slopes[0:1] / count), lead * rstd * (slopes[1:2] / count)

    def fill_row(row):
        if row == 0:
            cotan = above
        elif row == rows + 1:
            cotan = below
        else:
            cotan = cotan_ref[row - 1]
        centred, slope = slope_of(conv_ref[row], widen(cotan, pitch), coefs)
        dconv = masked((0.5 * lead) * slope - (offset + centred * factor), cols)
        if row == 0:
            dconv = dconv * valid[0]
        elif row == rows + 1:
            dconv = dconv * valid[1]
        dconv_ref[row] = dconv.astype(BF16)
        put_three(three, row, dconv, cols, True)

    def dot(start, end):
        size = end - start
        cells = x_ref[start:end]
        if pitch != cols:
            cells = cells.astype(F32)
            cells = jnp.concatenate([cells, jnp.zeros((size, pitch - cols, chan), F32)], 1).astype(BF16)
        lhs = cells.reshape(size * pitch, chan)
        rhs = beside(three, (start + 2, start + 1, start), size)
        put(lax.dot_general(lhs, rhs, (((0,), (0,)), ((), ())), preferred_element_type=F32))

    fills, dots, done = [], [], 0
    for start, end in chunks_of(rows, most):
        fills.append(lambda todo=range(done, end + 2): [fill_row(row) for row in todo])
        done = end + 2
        dots.append(functools.partial(dot, start, end))
    return fills, dots


def backward_kernel(
    counts, place_ref, four_ref, six_ref, conv_four_ref, conv_six_ref, cotan_four_ref, cotan_six_ref,
    above_ref, below_ref, moments_ref, slopes_ref, gain_ref, shift_ref,
    dconv_four_ref, dconv_six_ref, own_ref, sent_ref, three_four, three_six, total,
):
    valid = (place_ref[0].astype(F32), place_ref[1].astype(F32))
    cols_four = four_ref.shape[1]
    starts = (2 * cols_four, 3 * cols_four + 2 * three_six.shape[1])
    begun = []

    def put(term):
        total[...] = total[...] + term if begun else term
        begun.append(True)

    fills, dots = [], []
    for level, (x_ref, conv_ref, cotan_ref, dconv_ref, three, most) in reversed(
        list(
            enumerate(
                (
                    (four_ref, conv_four_ref, cotan_four_ref, dconv_four_ref, three_four, 8),
                    (six_ref, conv_six_ref, cotan_six_ref, dconv_six_ref, three_six, 12),
                )
            )
        )
    ):
        here = slice(level, level + 1)
        pair = slice(2 * level, 2 * level + 2)
        coefs = level_coefs(moments_ref[pair], gain_ref[here], shift_ref[here], counts[level])
        edge = slice(starts[level], starts[level] + three.shape[1])
        level_fills, level_dots = backward_level(
            x_ref, conv_ref, cotan_ref, above_ref[edge], below_ref[edge], valid, coefs, slopes_ref[pair],
            counts[level], dconv_ref, three, put, most,
        )
        fills += level_fills
        dots += level_dots
    staged(fills, dots)
    chan = own_ref.shape[2]
    share = own_ref.shape[1]
    others = sent_ref.shape[0]
    for step in range(others + 1):
        begin = pl.multiple_of((place_ref[2] ^ step) * share, share)
        for tap in range(9):
            part = total[pl.ds(begin, share), tap * chan : (tap + 1) * chan]
            if step == 0:
                own_ref[tap] = part
            else:
                sent_ref[step - 1, tap] = part.astype(BF16)


def input_level(dconv_ref, w_ref, grad_ref, three, most):
    rows, cols, chan = grad_ref.shape
    pitch = three.shape[1]

    def fill_row(row):
        put_three(three, row, dconv_ref[row].astype(F32), cols, True)

    def dot(start, end):
        size = end - start
        lhs = beside(three, (start + 2, start + 1, start), size)
        grad = jnp.dot(lhs, w_ref[...], preferred_element_type=F32)
        grad_ref[start:end] = grad.reshape(size, pitch, chan)[:, :cols].astype(BF16)

    fills, dots, done = [], [], 0
    for start, end in chunks_of(rows, most):
        fills.append(lambda todo=range(done, end + 2): [fill_row(row) for row in todo])
        done = end + 2
        dots.append(functools.partial(dot, start, end))
    return fills, dots


def input_kernel(dconv_four_ref, dconv_six_ref, w_ref, grad_four_ref, grad_six_ref, three_four, three_six):
    fills_six, dots_six = input_level(dconv_six_ref, w_ref, grad_six_ref, three_six, 12)
    fills_four, dots_four = input_level(dconv_four_ref, w_ref, grad_four_ref, three_four, 8)
    staged(fills_six + fills_four, dots_six + dots_four)


def swap(array, axis, stride):
    count = lax.axis_size(axis)
    return lax.ppermute(array, axis, [(i, i ^ stride) for i in range(count)])


def edge_kernel(starts, place_ref, four_ref, six_ref, cotan_four_ref, cotan_six_ref, *rest):
    outs, sems = rest[:-1], rest[-1]
    rows_four, cols_four = four_ref.shape[:2]
    rows_six = six_ref.shape[0]
    pitch = pitch_of(six_ref.shape[1])
    copies = []
    for number, (start, out_ref) in enumerate(zip(starts, outs)):
        last = (1 - place_ref[0]) if start is None else start
        for part, (ref, row) in enumerate(
            (
                (four_ref, last * (rows_four - 2)),
                (four_ref, last * (rows_four - 2) + 1),
                (cotan_four_ref, last * (rows_four - 1)),
            )
        ):
            copy = pltpu.make_async_copy(
                ref.at[row], out_ref.at[part * cols_four : (part + 1) * cols_four], sems.at[number, part]
            )
            copy.start()
            copies.append(copy)
        for part, (ref, row) in enumerate(
            (
                (six_ref, last * (rows_six - 2)),
                (six_ref, last * (rows_six - 2) + 1),
                (cotan_six_ref, last * (rows_six - 1)),
            )
        ):
            begin = 3 * cols_four + part * pitch
            out_ref[begin : begin + pitch] = widen(ref[row], pitch).astype(BF16)
    for copy in copies:
        copy.wait()


def edges(place, four, six, cotan_four, cotan_six):
    count = lax.axis_size("sp")
    starts = (None,) if count == 2 else (0, 1)
    length = 3 * four.shape[1] + 3 * pitch_of(six.shape[1])
    vmem = pl.BlockSpec(memory_space=pltpu.VMEM)
    hbm = pl.BlockSpec(memory_space=pltpu.HBM)
    outs = pl.pallas_call(
        functools.partial(edge_kernel, starts),
        out_shape=tuple(jax.ShapeDtypeStruct((length, four.shape[2]), BF16) for _ in starts),
        in_specs=[pl.BlockSpec(memory_space=pltpu.SMEM), hbm, vmem, hbm, vmem],
        out_specs=tuple(vmem for _ in starts),
        scratch_shapes=[pltpu.SemaphoreType.DMA((len(starts), 3))],
        compiler_params=pltpu.CompilerParams(vmem_limit_bytes=EDGE_LIMIT),
        name="edges",
    )(place, four, six, cotan_four, cotan_six)
    if count == 2:
        met = swap(outs[0], "sp", 1)
        return met, met
    above = lax.ppermute(outs[1], "sp", [(i, (i + 1) % count) for i in range(count)])
    below = lax.ppermute(outs[0], "sp", [((i + 1) % count, i) for i in range(count)])
    return above, below


def group_sum(sums):
    stride = 1
    while stride < lax.axis_size("sp"):
        sums = sums + swap(sums, "sp", stride)
        stride = 2 * stride
    stride = 1
    while stride < GROUP:
        met = [swap(sums, "rep", k * stride) for k in range(1, RADIX)]
        sums = (sums + met[0]) + (met[1] + met[2])
        stride = RADIX * stride
    return sums


def every_group(sums):
    stride = GROUP
    while stride < lax.axis_size("rep"):
        sums = sums + swap(sums, "rep", stride)
        stride = 2 * stride
    return sums


def digit_order(parts, digit):
    odd = digit % 2 == 1
    high = digit >= 2
    even = [jnp.where(odd, parts[k ^ 1], parts[k]) for k in range(4)]
    return jnp.stack([jnp.where(high, even[k ^ 2], even[k]) for k in range(4)])


def scatter_start(own, sent):
    met = [swap(sent[step], "sp", step + 1) for step in range(sent.shape[0])]
    chan = own.shape[2]
    parts = [part.reshape(RADIX, -1, chan) for part in [own] + met]
    digit = lax.axis_index("rep") % RADIX

    def piece(k):
        total = lax.dynamic_index_in_dim(parts[0], digit ^ k, 0, False)
        for part in parts[1:]:
            total = total + lax.dynamic_index_in_dim(part, digit ^ k, 0, False).astype(F32)
        return total

    return piece(0), [piece(k).astype(BF16) for k in range(1, RADIX)]


def added(own, met):
    return (own + met[0].astype(F32)) + (met[1].astype(F32) + met[2].astype(F32))


def weight_finish(total):
    chan = total.shape[1]
    digit = lax.axis_index("rep") // RADIX % RADIX
    pieces = total.reshape(RADIX, -1, chan)
    met = [
        swap(lax.dynamic_index_in_dim(pieces, digit ^ k, 0, False).astype(BF16), "rep", k * RADIX)
        for k in range(1, RADIX)
    ]
    total = added(lax.dynamic_index_in_dim(pieces, digit, 0, False), met).astype(BF16)
    stride = GROUP
    while stride < lax.axis_size("rep"):
        met = [swap(total, "rep", k * stride) for k in range(1, RADIX)]
        total = added(total.astype(F32), met).astype(BF16)
        stride = RADIX * stride
    for stride in (RADIX, 1):
        digit = lax.axis_index("rep") // stride % RADIX
        met = [total] + [swap(total, "rep", k * stride) for k in range(1, RADIX)]
        total = digit_order(met, digit).reshape(-1, chan)
    return total.astype(F32)


def local(level_four, level_six, conv_weight, bn_gain, bn_shift, cotan_four, cotan_six):
    sp_count, sp_index = lax.axis_size("sp"), lax.axis_index("sp")
    images = level_four.shape[0]
    four, six, cot_four, cot_six = (a[0] for a in (level_four, level_six, cotan_four, cotan_six))
    rows_four, cols_four, chan = four.shape
    rows_six, cols_six = six.shape[:2]
    pitch_four, pitch_six = pitch_of(cols_four), pitch_of(cols_six)
    counts = (
        float(images * GROUP * rows_four * sp_count * cols_four),
        float(images * GROUP * rows_six * sp_count * cols_six),
    )
    place = jnp.stack([sp_index > 0, sp_index < sp_count - 1, sp_index]).astype(jnp.int32)
    above, below = edges(place, four, six, cot_four, cot_six)
    smem = pl.BlockSpec(memory_space=pltpu.SMEM)
    vmem = pl.BlockSpec(memory_space=pltpu.VMEM)
    params = pltpu.CompilerParams(vmem_limit_bytes=VMEM_LIMIT)
    framed_four = jax.ShapeDtypeStruct((rows_four + 2, pitch_four, chan), BF16)
    framed_six = jax.ShapeDtypeStruct((rows_six + 2, pitch_six, chan), BF16)
    four_sums = jax.ShapeDtypeStruct((4, chan), F32)
    flops = 2 * 9 * chan * chan * (rows_four * cols_four + rows_six * cols_six)

    def cost(share, size):
        return pl.CostEstimate(flops=int(flops * share), bytes_accessed=size, transcendentals=0)

    conv_four, conv_six, moments = pl.pallas_call(
        forward_kernel,
        out_shape=(framed_four, framed_six, four_sums),
        in_specs=[smem] + [vmem] * 5,
        out_specs=(vmem, vmem, vmem),
        scratch_shapes=[
            pltpu.VMEM((rows_four + 4, pitch_four, 3 * chan), BF16),
            pltpu.VMEM((rows_six + 4, pitch_six, 3 * chan), BF16),
        ],
        compiler_params=params,
        cost_estimate=cost(1, 4 * four.size),
        name="forward",
    )(place, four, six, above, below, conv_weight)
    moments = group_sum(moments)

    slopes = pl.pallas_call(
        functools.partial(slope_kernel, counts),
        out_shape=four_sums,
        in_specs=[vmem] * 7,
        out_specs=vmem,
        compiler_params=params,
        cost_estimate=cost(0.01, 4 * four.size),
        name="slopes",
    )(conv_four, conv_six, cot_four, cot_six, moments, bn_gain, bn_shift)
    slopes = group_sum(slopes)

    share = chan // sp_count
    dconv_four, dconv_six, own, sent = pl.pallas_call(
        functools.partial(backward_kernel, counts),
        out_shape=(
            framed_four,
            framed_six,
            jax.ShapeDtypeStruct((9, share, chan), F32),
            jax.ShapeDtypeStruct((sp_count - 1, 9, share, chan), BF16),
        ),
        in_specs=[smem] + [vmem] * 12,
        out_specs=(vmem,) * 4,
        scratch_shapes=[
            pltpu.VMEM((rows_four + 2, pitch_four, 3 * chan), BF16),
            pltpu.VMEM((rows_six + 2, pitch_six, 3 * chan), BF16),
            pltpu.VMEM((chan, 9 * chan), F32),
        ],
        compiler_params=params,
        cost_estimate=cost(1.2, 8 * four.size),
        name="backward",
    )(
        place, four, six, conv_four, conv_six, cot_four, cot_six, above, below, moments, slopes,
        bn_gain, bn_shift,
    )

    piece, pieces = scatter_start(own, sent)
    pieces, dconv_four = lax.optimization_barrier((pieces, dconv_four))
    met = [swap(pieces[k - 1], "rep", k) for k in range(1, RADIX)]
    turned = conv_weight.reshape(3, 3, chan, chan).transpose(0, 1, 3, 2).reshape(9 * chan, chan)
    grad_four, grad_six = pl.pallas_call(
        input_kernel,
        out_shape=(
            jax.ShapeDtypeStruct(four.shape, BF16),
            jax.ShapeDtypeStruct(six.shape, BF16),
        ),
        in_specs=[vmem] * 3,
        out_specs=(vmem, vmem),
        scratch_shapes=[
            pltpu.VMEM((rows_four + 2, pitch_four, 3 * chan), BF16),
            pltpu.VMEM((rows_six + 2, pitch_six, 3 * chan), BF16),
        ],
        compiler_params=params,
        cost_estimate=cost(1, 4 * four.size),
        name="inputs",
    )(dconv_four, dconv_six, turned)

    met, grad_six = lax.optimization_barrier((met, grad_six))
    grad_weight = weight_finish(added(piece, met)).reshape(own.shape)
    totals = every_group(slopes)
    grad_gain = jnp.stack([totals[1], totals[3]])
    grad_shift = jnp.stack([totals[0], totals[2]])
    return (grad_four[None], grad_six[None], grad_weight, grad_gain, grad_shift)


def solution(mesh):
    placed = (
        P("rep", "sp", None, None),
        P("rep", "sp", None, None),
        P(),
        P(),
        P(),
        P("rep", "sp", None, None),
        P("rep", "sp", None, None),
    )
    return jax.shard_map(
        local,
        mesh=mesh,
        in_specs=placed,
        out_specs=(
            P("rep", "sp", None, None),
            P("rep", "sp", None, None),
            P(None, "sp", None),
            P(),
            P(),
        ),
        check_vma=False,
    )
```

```python
import functools

import jax
import jax.numpy as jnp
from jax import lax
from jax.experimental import pallas as pl
from jax.experimental.pallas import tpu as pltpu
from jax.sharding import PartitionSpec as P

GROUP = 16
RADIX = 4
EPSILON = 1e-05
F32 = jnp.float32
BF16 = jnp.bfloat16
VMEM_LIMIT = 20 * 1024 * 1024
EDGE_LIMIT = 60 * 1024 * 1024


def chunk_of(rows, most):
    return max(size for size in range(1, most + 1) if rows % size == 0)


def pitch_of(cols):
    return -(-cols // 16) * 16


def chunks_of(rows, most):
    size = chunk_of(rows, most)
    return [(start, start + size) for start in range(0, rows, size)]


def widen(cells, pitch):
    cells = cells.astype(F32)
    extra = pitch - cells.shape[0]
    if extra:
        cells = jnp.concatenate([cells, jnp.zeros((extra, cells.shape[1]), F32)], 0)
    return cells


def put_three(three, row, cells, cols, turned):
    pitch, chan = cells.shape
    col = lax.broadcasted_iota(jnp.int32, cells.shape, 0)
    left = jnp.where(col == 0, 0.0, pltpu.roll(cells, 1, 0))
    right = jnp.where(col >= cols - 1, 0.0, pltpu.roll(cells, pitch - 1, 0))
    parts = (right, cells, left) if turned else (left, cells, right)
    for place, part in enumerate(parts):
        three[row, :, place * chan : (place + 1) * chan] = part.astype(BF16)


def beside(three, starts, size):
    pitch, width = three.shape[1:]
    return jnp.concatenate([three[start : start + size].reshape(size * pitch, width) for start in starts], 1)


def edges_valid(sp_count):
    index = lax.axis_index("sp")
    return jnp.where(index > 0, 1.0, 0.0), jnp.where(index < sp_count - 1, 1.0, 0.0)


def level_coefs(moments, gain, shift, count):
    mean = moments[0:1] / count
    spread = moments[1:2] / count - mean * mean
    return mean, lax.rsqrt(spread + EPSILON), gain, shift


def slope_of(conv, cotan, coefs):
    mean, rstd, gain, shift = coefs
    centred = conv.astype(F32) - mean
    half = centred * (0.5 * rstd * gain) + 0.5 * shift
    turn = jnp.tanh(half)
    return centred, cotan.astype(F32) * ((1.0 + turn) * (1.0 + half * (1.0 - turn)))


def masked(cells, cols):
    if cells.shape[0] == cols:
        return cells
    col = lax.broadcasted_iota(jnp.int32, cells.shape, 0)
    return jnp.where(col < cols, cells, 0.0)


def staged(fills, dots):
    fills[0]()
    for index, dot in enumerate(dots):
        if index + 1 < len(fills):
            fills[index + 1]()
        dot()


def forward_level(x_ref, top, bottom, valid, w_ref, conv_ref, three, sums, most):
    rows, cols, chan = x_ref.shape
    pitch = three.shape[1]

    def fill_row(row):
        if row < 2:
            cells = top(row) * valid[0]
        elif row < rows + 2:
            cells = widen(x_ref[row - 2], pitch)
        else:
            cells = bottom(row - rows - 2) * valid[1]
        put_three(three, row, cells, cols, False)

    def dot(start, end, index):
        lhs = beside(three, (start, start + 1, start + 2), end - start)
        conv = jnp.dot(lhs, w_ref[...].reshape(9 * chan, chan), preferred_element_type=F32).astype(BF16)
        conv = conv.reshape(end - start, pitch, chan)
        conv_ref[start:end] = conv
        first, last = max(start, 1), min(end, rows + 1)
        conv = conv[first - start : last - start].astype(F32)
        if pitch != cols:
            conv = conv[:, :cols]
        conv = conv.reshape(-1, 8, chan)
        sums[0].append(jnp.sum(conv, 0))
        sums[1].append(jnp.sum(conv * conv, 0))

    chunks = [[start + 1, end + 1] for start, end in chunks_of(rows, most)]
    chunks[0][0] = 0
    chunks[-1][1] = rows + 2
    fills, dots, done = [], [], 0
    for index, (start, end) in enumerate(chunks):
        fills.append(lambda todo=range(done, end + 2): [fill_row(row) for row in todo])
        done = end + 2
        dots.append(functools.partial(dot, start, end, index))
    return fills, dots


def folded(parts):
    total = parts[0]
    for part in parts[1:]:
        total = total + part
    return jnp.sum(total, 0, keepdims=True)


def forward_kernel(
    sp_count, four_ref, six_ref, above_ref, below_ref, w_ref,
    conv_four_ref, conv_six_ref, moments_ref, three_four, three_six,
):
    cols_four = four_ref.shape[1]
    valid = edges_valid(sp_count)
    base, pitch_six = 3 * cols_four, three_six.shape[1]

    def reader(ref, start, pitch):
        return lambda edge: ref[start + edge * pitch : start + (edge + 1) * pitch].astype(F32)

    sums_four, sums_six = ([], []), ([], [])
    fills_six, dots_six = forward_level(
        six_ref, reader(above_ref, base, pitch_six), reader(below_ref, base, pitch_six), valid, w_ref,
        conv_six_ref, three_six, sums_six, 12,
    )
    fills_four, dots_four = forward_level(
        four_ref, reader(above_ref, 0, cols_four), reader(below_ref, 0, cols_four), valid, w_ref,
        conv_four_ref, three_four, sums_four, 8,
    )
    staged(fills_six + fills_four, dots_six + dots_four)
    sums = [folded(parts) for parts in sums_four + sums_six]
    moments_ref[...] = jnp.concatenate(sums, 0)


def slope_level(conv_ref, cotan_ref, above, below, coefs, slope_ref):
    rows, cols, chan = cotan_ref.shape
    pitch = conv_ref.shape[1]

    def put(row, cotan):
        centred, slope = slope_of(conv_ref[row], widen(cotan, pitch), coefs)
        slope_ref[row] = slope
        return centred, slope

    def step(row, sums):
        centred, slope = put(row + 1, cotan_ref[row])
        first = jnp.sum(slope.reshape(-1, 8, chan), 0)
        second = jnp.sum((slope * centred).reshape(-1, 8, chan), 0)
        return sums[0] + first, sums[1] + second

    put(0, above)
    put(rows + 1, below)
    zero = jnp.zeros((8, chan), F32)
    first, second = lax.fori_loop(0, rows, step, (zero, zero), unroll=3)
    first = 0.5 * jnp.sum(first, 0, keepdims=True)
    return first, 0.5 * coefs[1] * jnp.sum(second, 0, keepdims=True)


def slope_kernel(
    counts, conv_four_ref, conv_six_ref, cotan_four_ref, cotan_six_ref, above_ref, below_ref, moments_ref, gain_ref,
    shift_ref, slope_four_ref, slope_six_ref, slopes_ref,
):
    sums = ()
    cols_four = cotan_four_ref.shape[1]
    starts = (2 * cols_four, 3 * cols_four + 2 * conv_six_ref.shape[1])
    for level, (conv_ref, cotan_ref, slope_ref) in enumerate(
        ((conv_four_ref, cotan_four_ref, slope_four_ref), (conv_six_ref, cotan_six_ref, slope_six_ref))
    ):
        pair = moments_ref[2 * level : 2 * level + 2]
        here = slice(level, level + 1)
        edge = slice(starts[level], starts[level] + conv_ref.shape[1])
        coefs = level_coefs(pair, gain_ref[here], shift_ref[here], counts[level])
        sums += slope_level(conv_ref, cotan_ref, above_ref[edge], below_ref[edge], coefs, slope_ref)
    slopes_ref[...] = jnp.concatenate(sums, 0)


def backward_level(x_ref, conv_ref, slope_ref, valid, coefs, slopes, count, three, put, most):
    rows, cols, chan = x_ref.shape
    pitch = three.shape[1]
    mean, rstd, gain, shift = coefs
    lead = gain * rstd
    offset, factor = lead * (slopes[0:1] / count), lead * rstd * (slopes[1:2] / count)

    def fill_row(row):
        centred = conv_ref[row].astype(F32) - mean
        dconv = masked((0.5 * lead) * slope_ref[row] - (offset + centred * factor), cols)
        if row == 0:
            dconv = dconv * valid[0]
        elif row == rows + 1:
            dconv = dconv * valid[1]
        put_three(three, row, dconv, cols, True)

    def dot(start, end):
        size = end - start
        cells = x_ref[start:end]
        if pitch != cols:
            cells = cells.astype(F32)
            cells = jnp.concatenate([cells, jnp.zeros((size, pitch - cols, chan), F32)], 1).astype(BF16)
        lhs = cells.reshape(size * pitch, chan)
        rhs = beside(three, (start + 2, start + 1, start), size)
        put(lax.dot_general(lhs, rhs, (((0,), (0,)), ((), ())), preferred_element_type=F32))

    fills, dots, done = [], [], 0
    for start, end in chunks_of(rows, most):
        fills.append(lambda todo=range(done, end + 2): [fill_row(row) for row in todo])
        done = end + 2
        dots.append(functools.partial(dot, start, end))
    return fills, dots


def backward_kernel(
    counts, sp_count, four_ref, six_ref, conv_four_ref, conv_six_ref, slope_four_ref, slope_six_ref,
    moments_ref, slopes_ref, gain_ref, shift_ref, three_four, three_six, own_ref, sent_ref, total,
):
    valid = edges_valid(sp_count)
    begun = []

    def put(term):
        total[...] = total[...] + term if begun else term
        begun.append(True)

    fills, dots = [], []
    for level, x_ref, conv_ref, slope_ref, three, most in (
        (1, six_ref, conv_six_ref, slope_six_ref, three_six, 12),
        (0, four_ref, conv_four_ref, slope_four_ref, three_four, 8),
    ):
        here = slice(level, level + 1)
        pair = slice(2 * level, 2 * level + 2)
        coefs = level_coefs(moments_ref[pair], gain_ref[here], shift_ref[here], counts[level])
        level_fills, level_dots = backward_level(
            x_ref, conv_ref, slope_ref, valid, coefs, slopes_ref[pair], counts[level], three, put, most
        )
        fills += level_fills
        dots += level_dots
    staged(fills, dots)
    share, chan = own_ref.shape[1:]
    for step in range(sp_count):
        begin = pl.multiple_of((lax.axis_index("sp") ^ step) * share, share)
        for tap in range(9):
            part = total[pl.ds(begin, share), tap * chan : (tap + 1) * chan]
            if step == 0:
                own_ref[tap] = part
            else:
                sent_ref[step - 1, tap] = part.astype(BF16)


def input_level(three, w_ref, grad_ref, most):
    rows, cols, chan = grad_ref.shape
    pitch = three.shape[1]
    rhs = jnp.concatenate([w_ref[tap] for tap in range(9)], 1)
    for start, end in chunks_of(rows, most):
        size = end - start
        lhs = beside(three, (start + 2, start + 1, start), size)
        grad = lax.dot_general(lhs, rhs, (((1,), (1,)), ((), ())), preferred_element_type=F32)
        grad_ref[start:end] = grad.reshape(size, pitch, chan)[:, :cols].astype(BF16)


def input_kernel(three_four, three_six, w_ref, grad_four_ref, grad_six_ref):
    input_level(three_six, w_ref, grad_six_ref, 12)
    input_level(three_four, w_ref, grad_four_ref, 16)


def swap(array, axis, stride):
    count = lax.axis_size(axis)
    return lax.ppermute(array, axis, [(i, i ^ stride) for i in range(count)])


def edge_kernel(starts, four_ref, six_ref, cotan_four_ref, cotan_six_ref, *rest):
    outs, six_rows, sems = rest[:-2], rest[-2], rest[-1]
    rows_four, cols_four = four_ref.shape[:2]
    rows_six = six_ref.shape[0]
    pitch = pitch_of(six_ref.shape[1])
    copies = []
    for number, (start, out_ref) in enumerate(zip(starts, outs)):
        last = (1 - jnp.minimum(lax.axis_index("sp"), 1)) if start is None else start
        for part, (ref, row) in enumerate(
            (
                (four_ref, last * (rows_four - 2)),
                (four_ref, last * (rows_four - 2) + 1),
                (cotan_four_ref, last * (rows_four - 1)),
                (six_ref, last * (rows_six - 2)),
                (six_ref, last * (rows_six - 2) + 1),
                (cotan_six_ref, last * (rows_six - 1)),
            )
        ):
            if part < 3:
                target = out_ref.at[part * cols_four : (part + 1) * cols_four]
            else:
                target = six_rows.at[number, part - 3]
            copies.append(pltpu.make_async_copy(ref.at[row], target, sems.at[number, part]))
    for copy in copies:
        copy.start()
    for copy in copies:
        copy.wait()
    for number, out_ref in enumerate(outs):
        for part in range(3):
            begin = 3 * cols_four + part * pitch
            out_ref[begin : begin + pitch] = widen(six_rows[number, part], pitch).astype(BF16)


def edges(four, six, cotan_four, cotan_six):
    count = lax.axis_size("sp")
    starts = (None,) if count == 2 else (0, 1)
    length = 3 * four.shape[1] + 3 * pitch_of(six.shape[1])
    vmem = pl.BlockSpec(memory_space=pltpu.VMEM)
    hbm = pl.BlockSpec(memory_space=pltpu.HBM)
    outs = pl.pallas_call(
        functools.partial(edge_kernel, starts),
        out_shape=tuple(jax.ShapeDtypeStruct((length, four.shape[2]), BF16) for _ in starts),
        in_specs=[hbm] * 4,
        out_specs=tuple(vmem for _ in starts),
        scratch_shapes=[
            pltpu.VMEM((len(starts), 3) + six.shape[1:], BF16),
            pltpu.SemaphoreType.DMA((len(starts), 6)),
        ],
        compiler_params=pltpu.CompilerParams(vmem_limit_bytes=EDGE_LIMIT),
        name="edges",
    )(four, six, cotan_four, cotan_six)
    if count == 2:
        met = swap(outs[0], "sp", 1)
        return met, met
    above = lax.ppermute(outs[1], "sp", [(i, (i + 1) % count) for i in range(count)])
    below = lax.ppermute(outs[0], "sp", [((i + 1) % count, i) for i in range(count)])
    return above, below


def group_sum(sums):
    stride = 1
    while stride < lax.axis_size("sp"):
        sums = sums + swap(sums, "sp", stride)
        stride = 2 * stride
    stride = 1
    while stride < GROUP:
        met = [swap(sums, "rep", k * stride) for k in range(1, RADIX)]
        sums = (sums + met[0]) + (met[1] + met[2])
        stride = RADIX * stride
    return sums


def every_group(sums):
    stride = GROUP
    while stride < lax.axis_size("rep"):
        sums = sums + swap(sums, "rep", stride)
        stride = 2 * stride
    return sums


def digit_order(parts, digit):
    odd = digit % 2 == 1
    high = digit >= 2
    even = [jnp.where(odd, parts[k ^ 1], parts[k]) for k in range(4)]
    return jnp.stack([jnp.where(high, even[k ^ 2], even[k]) for k in range(4)])


def scatter_start(own, sent):
    met = [swap(sent[step], "sp", step + 1) for step in range(sent.shape[0])]
    chan = own.shape[2]
    parts = [part.reshape(RADIX, -1, chan) for part in [own] + met]
    digit = lax.axis_index("rep") % RADIX

    def piece(k):
        total = lax.dynamic_index_in_dim(parts[0], digit ^ k, 0, False)
        for part in parts[1:]:
            total = total + lax.dynamic_index_in_dim(part, digit ^ k, 0, False).astype(F32)
        return total

    return piece(0), [piece(k).astype(BF16) for k in range(1, RADIX)]


def added(own, met):
    return (own + met[0].astype(F32)) + (met[1].astype(F32) + met[2].astype(F32))


def weight_finish(total):
    chan = total.shape[1]
    digit = lax.axis_index("rep") // RADIX % RADIX
    pieces = total.reshape(RADIX, -1, chan)
    met = [
        swap(lax.dynamic_index_in_dim(pieces, digit ^ k, 0, False).astype(BF16), "rep", k * RADIX)
        for k in range(1, RADIX)
    ]
    total = added(lax.dynamic_index_in_dim(pieces, digit, 0, False), met).astype(BF16)
    stride = GROUP
    while stride < lax.axis_size("rep"):
        met = [swap(total, "rep", k * stride) for k in range(1, RADIX)]
        total = added(total.astype(F32), met).astype(BF16)
        stride = RADIX * stride
    for stride in (RADIX, 1):
        digit = lax.axis_index("rep") // stride % RADIX
        met = [total] + [swap(total, "rep", k * stride) for k in range(1, RADIX)]
        total = digit_order(met, digit).reshape(-1, chan)
    return total.astype(F32)


def local(level_four, level_six, conv_weight, bn_gain, bn_shift, cotan_four, cotan_six):
    sp_count = lax.axis_size("sp")
    images = level_four.shape[0]
    four, six, cot_four, cot_six = (a[0] for a in (level_four, level_six, cotan_four, cotan_six))
    rows_four, cols_four, chan = four.shape
    rows_six, cols_six = six.shape[:2]
    pitch_four, pitch_six = pitch_of(cols_four), pitch_of(cols_six)
    counts = (
        float(images * GROUP * rows_four * sp_count * cols_four),
        float(images * GROUP * rows_six * sp_count * cols_six),
    )
    above, below = edges(four, six, cot_four, cot_six)
    vmem = pl.BlockSpec(memory_space=pltpu.VMEM)
    params = pltpu.CompilerParams(vmem_limit_bytes=VMEM_LIMIT)
    framed_four = jax.ShapeDtypeStruct((rows_four + 2, pitch_four, chan), BF16)
    framed_six = jax.ShapeDtypeStruct((rows_six + 2, pitch_six, chan), BF16)
    four_sums = jax.ShapeDtypeStruct((4, chan), F32)
    flops = 2 * 9 * chan * chan * (rows_four * cols_four + rows_six * cols_six)

    def cost(share, size):
        return pl.CostEstimate(flops=int(flops * share), bytes_accessed=size, transcendentals=0)

    conv_four, conv_six, moments = pl.pallas_call(
        functools.partial(forward_kernel, sp_count),
        out_shape=(framed_four, framed_six, four_sums),
        in_specs=[vmem] * 5,
        out_specs=(vmem, vmem, vmem),
        scratch_shapes=[
            pltpu.VMEM((rows_four + 4, pitch_four, 3 * chan), BF16),
            pltpu.VMEM((rows_six + 4, pitch_six, 3 * chan), BF16),
        ],
        compiler_params=params,
        cost_estimate=cost(1, 4 * four.size),
        name="forward",
    )(four, six, above, below, conv_weight)
    moments = group_sum(moments)

    slope_four, slope_six, slopes = pl.pallas_call(
        functools.partial(slope_kernel, counts),
        out_shape=(
            jax.ShapeDtypeStruct(framed_four.shape, F32),
            jax.ShapeDtypeStruct(framed_six.shape, F32),
            four_sums,
        ),
        in_specs=[vmem] * 9,
        out_specs=(vmem,) * 3,
        compiler_params=params,
        cost_estimate=cost(0.01, 4 * four.size),
        name="slopes",
    )(conv_four, conv_six, cot_four, cot_six, above, below, moments, bn_gain, bn_shift)
    slopes = group_sum(slopes)

    share = chan // sp_count
    wide_four, wide_six = (
        jax.ShapeDtypeStruct(framed.shape[:2] + (3 * chan,), BF16) for framed in (framed_four, framed_six)
    )
    three_four, three_six, own, sent = pl.pallas_call(
        functools.partial(backward_kernel, counts, sp_count),
        out_shape=(
            wide_four,
            wide_six,
            jax.ShapeDtypeStruct((9, share, chan), F32),
            jax.ShapeDtypeStruct((sp_count - 1, 9, share, chan), BF16),
        ),
        in_specs=[vmem] * 10,
        out_specs=(vmem,) * 4,
        scratch_shapes=[pltpu.VMEM((chan, 9 * chan), F32)],
        compiler_params=params,
        cost_estimate=cost(1.2, 8 * four.size),
        name="backward",
    )(four, six, conv_four, conv_six, slope_four, slope_six, moments, slopes, bn_gain, bn_shift)

    piece, pieces = scatter_start(own, sent)
    pieces, three_four = lax.optimization_barrier((pieces, three_four))
    met = [swap(pieces[k - 1], "rep", k) for k in range(1, RADIX)]
    grad_four, grad_six = pl.pallas_call(
        input_kernel,
        out_shape=(
            jax.ShapeDtypeStruct(four.shape, BF16),
            jax.ShapeDtypeStruct(six.shape, BF16),
        ),
        in_specs=[vmem] * 3,
        out_specs=(vmem, vmem),
        compiler_params=params,
        cost_estimate=cost(1, 4 * four.size),
        name="inputs",
    )(three_four, three_six, conv_weight)
    met, grad_six = lax.optimization_barrier((met, grad_six))
    grad_weight = weight_finish(added(piece, met)).reshape(own.shape)
    totals = every_group(slopes)
    grad_gain = jnp.stack([totals[1], totals[3]])
    grad_shift = jnp.stack([totals[0], totals[2]])
    return (grad_four[None], grad_six[None], grad_weight, grad_gain, grad_shift)


def solution(mesh):
    placed = (
        P("rep", "sp", None, None),
        P("rep", "sp", None, None),
        P(),
        P(),
        P(),
        P("rep", "sp", None, None),
        P("rep", "sp", None, None),
    )
    return jax.shard_map(
        local,
        mesh=mesh,
        in_specs=placed,
        out_specs=(
            P("rep", "sp", None, None),
            P("rep", "sp", None, None),
            P(None, "sp", None),
            P(),
            P(),
        ),
        check_vma=False,
    )
```

```python
import functools

import jax
import jax.numpy as jnp
from jax import lax
from jax.experimental import pallas as pl
from jax.experimental.pallas import tpu as pltpu
from jax.sharding import PartitionSpec as P

GROUP = 16
RADIX = 4
EPSILON = 1e-05
F32 = jnp.float32
BF16 = jnp.bfloat16
VMEM_LIMIT = 20 * 1024 * 1024
EDGE_LIMIT = 62 * 1024 * 1024


def chunk_of(rows, most):
    return max(size for size in range(1, most + 1) if rows % size == 0)


def pitch_of(cols):
    return -(-cols // 16) * 16


def chunks_of(rows, most):
    size = chunk_of(rows, most)
    return [(start, start + size) for start in range(0, rows, size)]


def widen(cells, pitch):
    cells = cells.astype(F32)
    extra = pitch - cells.shape[0]
    if extra:
        cells = jnp.concatenate([cells, jnp.zeros((extra, cells.shape[1]), F32)], 0)
    return cells


def put_three(three, row, cells, cols, turned):
    pitch, chan = cells.shape
    left, right = pltpu.roll(cells, 1, 0), pltpu.roll(cells, pitch - 1, 0)
    if pitch == cols:
        col = lax.broadcasted_iota(jnp.int32, (8, chan), 0)
        left = jnp.concatenate([jnp.where(col == 0, 0.0, left[:8]), left[8:]], 0)
        right = jnp.concatenate([right[:-8], jnp.where(col == 7, 0.0, right[-8:])], 0)
    parts = (right, cells, left) if turned else (left, cells, right)
    for place, part in enumerate(parts):
        three[row, :, place * chan : (place + 1) * chan] = part.astype(BF16)


def beside(three, starts, size):
    pitch, width = three.shape[1:]
    return jnp.concatenate([three[start : start + size].reshape(size * pitch, width) for start in starts], 1)


def edges_valid(sp_count):
    index = lax.axis_index("sp")
    return jnp.where(index > 0, 1.0, 0.0), jnp.where(index < sp_count - 1, 1.0, 0.0)


def level_coefs(moments, gain, shift, count):
    mean = moments[0:1] / count
    spread = moments[1:2] / count - mean * mean
    return mean, lax.rsqrt(spread + EPSILON), gain, shift


def slope_of(conv, cotan, coefs):
    mean, rstd, gain, shift = coefs
    centred = conv.astype(F32) - mean
    half = centred * (0.5 * rstd * gain) + 0.5 * shift
    turn = jnp.tanh(half)
    return centred, cotan.astype(F32) * ((1.0 + turn) * (1.0 + half * (1.0 - turn)))


def masked(cells, cols):
    if cells.shape[0] == cols:
        return cells
    col = lax.broadcasted_iota(jnp.int32, cells.shape, 0)
    return jnp.where(col < cols, cells, 0.0)


def staged(fills, dots):
    fills[0]()
    for index, dot in enumerate(dots):
        if index + 1 < len(fills):
            fills[index + 1]()
        dot()


def forward_level(x_ref, top, bottom, valid, w_ref, conv_ref, three, sums, most):
    rows, cols, chan = x_ref.shape
    pitch = three.shape[1]

    def fill_row(row):
        if row < 2:
            cells = top(row) * valid[0]
        elif row < rows + 2:
            cells = widen(x_ref[row - 2], pitch)
        else:
            cells = bottom(row - rows - 2) * valid[1]
        put_three(three, row, cells, cols, False)

    def dot(start, end, index):
        lhs = beside(three, (start, start + 1, start + 2), end - start)
        conv = jnp.dot(lhs, w_ref[...].reshape(9 * chan, chan), preferred_element_type=F32).astype(BF16)
        conv = conv.reshape(end - start, pitch, chan)
        conv_ref[start:end] = conv
        first, last = max(start, 1), min(end, rows + 1)
        conv = conv[first - start : last - start].astype(F32)
        if pitch != cols:
            conv = conv[:, :cols]
        conv = conv.reshape(-1, 8, chan)
        sums[0].append(jnp.sum(conv, 0))
        sums[1].append(jnp.sum(conv * conv, 0))

    chunks = [[start + 1, end + 1] for start, end in chunks_of(rows, most)]
    chunks[0][0] = 0
    chunks[-1][1] = rows + 2
    fills, dots, done = [], [], 0
    for index, (start, end) in enumerate(chunks):
        fills.append(lambda todo=range(done, end + 2): [fill_row(row) for row in todo])
        done = end + 2
        dots.append(functools.partial(dot, start, end, index))
    return fills, dots


def folded(parts):
    total = parts[0]
    for part in parts[1:]:
        total = total + part
    return jnp.sum(total, 0, keepdims=True)


def forward_kernel(
    sp_count, four_ref, six_ref, above_ref, below_ref, w_ref,
    conv_four_ref, conv_six_ref, moments_ref, three_four, three_six,
):
    cols_four = four_ref.shape[1]
    valid = edges_valid(sp_count)
    base, pitch_six = 3 * cols_four, three_six.shape[1]

    def reader(ref, start, pitch):
        return lambda edge: ref[start + edge * pitch : start + (edge + 1) * pitch].astype(F32)

    sums_four, sums_six = ([], []), ([], [])
    fills_six, dots_six = forward_level(
        six_ref, reader(above_ref, base, pitch_six), reader(below_ref, base, pitch_six), valid, w_ref,
        conv_six_ref, three_six, sums_six, 12,
    )
    fills_four, dots_four = forward_level(
        four_ref, reader(above_ref, 0, cols_four), reader(below_ref, 0, cols_four), valid, w_ref,
        conv_four_ref, three_four, sums_four, 8,
    )
    staged(fills_six + fills_four, dots_six + dots_four)
    sums = [folded(parts) for parts in sums_four + sums_six]
    moments_ref[...] = jnp.concatenate(sums, 0)


def slope_level(conv_ref, cotan_ref, above, below, coefs, slope_ref):
    rows, cols, chan = cotan_ref.shape
    pitch = conv_ref.shape[1]

    def put(row, cotan):
        centred, slope = slope_of(conv_ref[row], widen(cotan, pitch), coefs)
        slope_ref[row] = slope
        return centred, slope

    def step(row, sums):
        centred, slope = put(row + 1, cotan_ref[row])
        first = jnp.sum(slope.reshape(-1, 8, chan), 0)
        second = jnp.sum((slope * centred).reshape(-1, 8, chan), 0)
        return sums[0] + first, sums[1] + second

    put(0, above)
    put(rows + 1, below)
    zero = jnp.zeros((8, chan), F32)
    first, second = lax.fori_loop(0, rows, step, (zero, zero), unroll=chunk_of(rows, 8))
    first = 0.5 * jnp.sum(first, 0, keepdims=True)
    return first, 0.5 * coefs[1] * jnp.sum(second, 0, keepdims=True)


def slope_kernel(
    counts, conv_four_ref, conv_six_ref, cotan_four_ref, cotan_six_ref, above_ref, below_ref, moments_ref, gain_ref,
    shift_ref, slope_four_ref, slope_six_ref, slopes_ref,
):
    sums = ()
    cols_four = cotan_four_ref.shape[1]
    starts = (2 * cols_four, 3 * cols_four + 2 * conv_six_ref.shape[1])
    for level, (conv_ref, cotan_ref, slope_ref) in enumerate(
        ((conv_four_ref, cotan_four_ref, slope_four_ref), (conv_six_ref, cotan_six_ref, slope_six_ref))
    ):
        pair = moments_ref[2 * level : 2 * level + 2]
        here = slice(level, level + 1)
        edge = slice(starts[level], starts[level] + conv_ref.shape[1])
        coefs = level_coefs(pair, gain_ref[here], shift_ref[here], counts[level])
        sums += slope_level(conv_ref, cotan_ref, above_ref[edge], below_ref[edge], coefs, slope_ref)
    slopes_ref[...] = jnp.concatenate(sums, 0)


def backward_level(x_ref, conv_ref, slope_ref, valid, coefs, slopes, count, three, put, most):
    rows, cols, chan = x_ref.shape
    pitch = three.shape[1]
    mean, rstd, gain, shift = coefs
    lead = gain * rstd
    offset, factor = lead * (slopes[0:1] / count), lead * rstd * (slopes[1:2] / count)

    def fill_row(row):
        centred = conv_ref[row].astype(F32) - mean
        dconv = masked((0.5 * lead) * slope_ref[row] - (offset + centred * factor), cols)
        if row == 0:
            dconv = dconv * valid[0]
        elif row == rows + 1:
            dconv = dconv * valid[1]
        put_three(three, row, dconv, cols, True)

    def dot(start, end):
        size = end - start
        cells = x_ref[start:end]
        if pitch != cols:
            cells = cells.astype(F32)
            cells = jnp.concatenate([cells, jnp.zeros((size, pitch - cols, chan), F32)], 1).astype(BF16)
        lhs = cells.reshape(size * pitch, chan)
        rhs = beside(three, (start + 2, start + 1, start), size)
        put(lax.dot_general(lhs, rhs, (((0,), (0,)), ((), ())), preferred_element_type=F32))

    fills, dots, done = [], [], 0
    for start, end in chunks_of(rows, most):
        fills.append(lambda todo=range(done, end + 2): [fill_row(row) for row in todo])
        done = end + 2
        dots.append(functools.partial(dot, start, end))
    return fills, dots


def backward_kernel(
    counts, sp_count, four_ref, six_ref, conv_four_ref, conv_six_ref, slope_four_ref, slope_six_ref,
    moments_ref, slopes_ref, gain_ref, shift_ref, three_four, three_six, own_ref, sent_ref, total,
):
    valid = edges_valid(sp_count)
    begun = []

    def put(term):
        total[...] = total[...] + term if begun else term
        begun.append(True)

    fills, dots = [], []
    for level, x_ref, conv_ref, slope_ref, three, most in (
        (1, six_ref, conv_six_ref, slope_six_ref, three_six, 12),
        (0, four_ref, conv_four_ref, slope_four_ref, three_four, 8),
    ):
        here = slice(level, level + 1)
        pair = slice(2 * level, 2 * level + 2)
        coefs = level_coefs(moments_ref[pair], gain_ref[here], shift_ref[here], counts[level])
        level_fills, level_dots = backward_level(
            x_ref, conv_ref, slope_ref, valid, coefs, slopes_ref[pair], counts[level], three, put, most
        )
        fills += level_fills
        dots += level_dots
    staged(fills, dots)
    share, chan = own_ref.shape[1:]
    for step in range(sp_count):
        begin = pl.multiple_of((lax.axis_index("sp") ^ step) * share, share)
        for tap in range(9):
            part = total[pl.ds(begin, share), tap * chan : (tap + 1) * chan]
            if step == 0:
                own_ref[tap] = part
            else:
                sent_ref[step - 1, tap] = part.astype(BF16)


def input_level(three, w_ref, grad_ref, most):
    rows, cols, chan = grad_ref.shape
    pitch = three.shape[1]
    rhs = jnp.concatenate([w_ref[tap] for tap in range(9)], 1)
    for start, end in chunks_of(rows, most):
        size = end - start
        lhs = beside(three, (start + 2, start + 1, start), size)
        grad = lax.dot_general(lhs, rhs, (((1,), (1,)), ((), ())), preferred_element_type=F32)
        grad_ref[start:end] = grad.reshape(size, pitch, chan)[:, :cols].astype(BF16)


def input_kernel(three_four, three_six, w_ref, grad_four_ref, grad_six_ref):
    input_level(three_six, w_ref, grad_six_ref, 12)
    input_level(three_four, w_ref, grad_four_ref, 16)


def swap(array, axis, stride):
    count = lax.axis_size(axis)
    return lax.ppermute(array, axis, [(i, i ^ stride) for i in range(count)])


def edge_kernel(starts, four_ref, six_ref, cotan_four_ref, cotan_six_ref, *rest):
    outs, six_rows, sems = rest[:-2], rest[-2], rest[-1]
    rows_four, cols_four = four_ref.shape[:2]
    rows_six = six_ref.shape[0]
    pitch = pitch_of(six_ref.shape[1])
    copies = []
    for number, (start, out_ref) in enumerate(zip(starts, outs)):
        last = (1 - jnp.minimum(lax.axis_index("sp"), 1)) if start is None else start
        for part, (ref, row) in enumerate(
            (
                (four_ref, last * (rows_four - 2)),
                (four_ref, last * (rows_four - 2) + 1),
                (cotan_four_ref, last * (rows_four - 1)),
                (six_ref, last * (rows_six - 2)),
                (six_ref, last * (rows_six - 2) + 1),
                (cotan_six_ref, last * (rows_six - 1)),
            )
        ):
            if part < 3:
                target = out_ref.at[part * cols_four : (part + 1) * cols_four]
            else:
                target = six_rows.at[number, part - 3]
            copies.append(pltpu.make_async_copy(ref.at[row], target, sems.at[number, part]))
    for copy in copies:
        copy.start()
    for copy in copies:
        copy.wait()
    for number, out_ref in enumerate(outs):
        for part in range(3):
            begin = 3 * cols_four + part * pitch
            out_ref[begin : begin + pitch] = widen(six_rows[number, part], pitch).astype(BF16)


def edges(four, six, cotan_four, cotan_six):
    count = lax.axis_size("sp")
    starts = (None,) if count == 2 else (0, 1)
    length = 3 * four.shape[1] + 3 * pitch_of(six.shape[1])
    vmem = pl.BlockSpec(memory_space=pltpu.VMEM)
    hbm = pl.BlockSpec(memory_space=pltpu.HBM)
    outs = pl.pallas_call(
        functools.partial(edge_kernel, starts),
        out_shape=tuple(jax.ShapeDtypeStruct((length, four.shape[2]), BF16) for _ in starts),
        in_specs=[hbm] * 4,
        out_specs=tuple(vmem for _ in starts),
        scratch_shapes=[
            pltpu.VMEM((len(starts), 3) + six.shape[1:], BF16),
            pltpu.SemaphoreType.DMA((len(starts), 6)),
        ],
        compiler_params=pltpu.CompilerParams(vmem_limit_bytes=EDGE_LIMIT),
        name="edges",
    )(four, six, cotan_four, cotan_six)
    if count == 2:
        met = swap(outs[0], "sp", 1)
        return met, met
    above = lax.ppermute(outs[1], "sp", [(i, (i + 1) % count) for i in range(count)])
    below = lax.ppermute(outs[0], "sp", [((i + 1) % count, i) for i in range(count)])
    return above, below


def group_sum(sums):
    stride = 1
    while stride < lax.axis_size("sp"):
        sums = sums + swap(sums, "sp", stride)
        stride = 2 * stride
    stride = 1
    while stride < GROUP:
        met = [swap(sums, "rep", k * stride) for k in range(1, RADIX)]
        sums = (sums + met[0]) + (met[1] + met[2])
        stride = RADIX * stride
    return sums


def every_group(sums):
    stride = GROUP
    while stride < lax.axis_size("rep"):
        sums = sums + swap(sums, "rep", stride)
        stride = 2 * stride
    return sums


def places():
    found = []
    for shift in (0, 2):
        digit = (lax.axis_index("rep") >> shift) & (RADIX - 1)
        found.append(([digit ^ k for k in range(RADIX)], (digit & 1) == 1, digit >= 2))
    return found


def digit_order(parts, place):
    unused, odd, high = place
    even = [jnp.where(odd, parts[k ^ 1], parts[k]) for k in range(RADIX)]
    return jnp.stack([jnp.where(high, even[k ^ 2], even[k]) for k in range(RADIX)])


def piece_of(pieces, index):
    sizes = (1,) + pieces.shape[1:]
    return lax.dynamic_slice(pieces, (index, 0, 0), sizes, allow_negative_indices=False)[0]


def scatter_start(own, sent, place):
    met = [swap(sent[step], "sp", step + 1) for step in range(sent.shape[0])]
    chan = own.shape[2]
    parts = [part.reshape(RADIX, -1, chan) for part in [own] + met]

    def piece(k):
        total = piece_of(parts[0], place[0][k])
        for part in parts[1:]:
            total = total + piece_of(part, place[0][k]).astype(F32)
        return total

    return piece(0), [piece(k).astype(BF16) for k in range(1, RADIX)]


def added(own, met):
    return (own + met[0].astype(F32)) + (met[1].astype(F32) + met[2].astype(F32))


def weight_finish(total, found):
    chan = total.shape[1]
    indices = found[1][0]
    pieces = total.reshape(RADIX, -1, chan)
    met = [
        swap(piece_of(pieces, indices[k]).astype(BF16), "rep", k * RADIX)
        for k in range(1, RADIX)
    ]
    total = added(piece_of(pieces, indices[0]), met).astype(BF16)
    stride = GROUP
    while stride < lax.axis_size("rep"):
        met = [swap(total, "rep", k * stride) for k in range(1, RADIX)]
        total = added(total.astype(F32), met).astype(BF16)
        stride = RADIX * stride
    for stride, place in ((RADIX, found[1]), (1, found[0])):
        met = [total] + [swap(total, "rep", k * stride) for k in range(1, RADIX)]
        total = digit_order(met, place).reshape(-1, chan)
    return total.astype(F32)


def local(level_four, level_six, conv_weight, bn_gain, bn_shift, cotan_four, cotan_six):
    sp_count = lax.axis_size("sp")
    images = level_four.shape[0]
    four, six, cot_four, cot_six = (a[0] for a in (level_four, level_six, cotan_four, cotan_six))
    rows_four, cols_four, chan = four.shape
    rows_six, cols_six = six.shape[:2]
    pitch_four, pitch_six = pitch_of(cols_four), pitch_of(cols_six)
    counts = (
        float(images * GROUP * rows_four * sp_count * cols_four),
        float(images * GROUP * rows_six * sp_count * cols_six),
    )
    found, four = lax.optimization_barrier((places(), four))
    above, below = edges(four, six, cot_four, cot_six)
    vmem = pl.BlockSpec(memory_space=pltpu.VMEM)
    params = pltpu.CompilerParams(vmem_limit_bytes=VMEM_LIMIT)
    framed_four = jax.ShapeDtypeStruct((rows_four + 2, pitch_four, chan), BF16)
    framed_six = jax.ShapeDtypeStruct((rows_six + 2, pitch_six, chan), BF16)
    four_sums = jax.ShapeDtypeStruct((4, chan), F32)
    flops = 2 * 9 * chan * chan * (rows_four * cols_four + rows_six * cols_six)

    def cost(share, size):
        return pl.CostEstimate(flops=int(flops * share), bytes_accessed=size, transcendentals=0)

    conv_four, conv_six, moments = pl.pallas_call(
        functools.partial(forward_kernel, sp_count),
        out_shape=(framed_four, framed_six, four_sums),
        in_specs=[vmem] * 5,
        out_specs=(vmem, vmem, vmem),
        scratch_shapes=[
            pltpu.VMEM((rows_four + 4, pitch_four, 3 * chan), BF16),
            pltpu.VMEM((rows_six + 4, pitch_six, 3 * chan), BF16),
        ],
        compiler_params=params,
        cost_estimate=cost(1, 4 * four.size),
        name="forward",
    )(four, six, above, below, conv_weight)
    moments = group_sum(moments)

    slope_four, slope_six, slopes = pl.pallas_call(
        functools.partial(slope_kernel, counts),
        out_shape=(
            jax.ShapeDtypeStruct(framed_four.shape, F32),
            jax.ShapeDtypeStruct(framed_six.shape, F32),
            four_sums,
        ),
        in_specs=[vmem] * 9,
        out_specs=(vmem,) * 3,
        compiler_params=params,
        cost_estimate=cost(0.01, 4 * four.size),
        name="slopes",
    )(conv_four, conv_six, cot_four, cot_six, above, below, moments, bn_gain, bn_shift)
    slopes = group_sum(slopes)

    share = chan // sp_count
    wide_four, wide_six = (
        jax.ShapeDtypeStruct(framed.shape[:2] + (3 * chan,), BF16) for framed in (framed_four, framed_six)
    )
    three_four, three_six, own, sent = pl.pallas_call(
        functools.partial(backward_kernel, counts, sp_count),
        out_shape=(
            wide_four,
            wide_six,
            jax.ShapeDtypeStruct((9, share, chan), F32),
            jax.ShapeDtypeStruct((sp_count - 1, 9, share, chan), BF16),
        ),
        in_specs=[vmem] * 10,
        out_specs=(vmem,) * 4,
        scratch_shapes=[pltpu.VMEM((chan, 9 * chan), F32)],
        compiler_params=params,
        cost_estimate=cost(1.2, 8 * four.size),
        name="backward",
    )(four, six, conv_four, conv_six, slope_four, slope_six, moments, slopes, bn_gain, bn_shift)

    piece, pieces = scatter_start(own, sent, found[0])
    pieces, three_four = lax.optimization_barrier((pieces, three_four))
    met = [swap(pieces[k - 1], "rep", k) for k in range(1, RADIX)]
    grad_four, grad_six = pl.pallas_call(
        input_kernel,
        out_shape=(
            jax.ShapeDtypeStruct(four.shape, BF16),
            jax.ShapeDtypeStruct(six.shape, BF16),
        ),
        in_specs=[vmem] * 3,
        out_specs=(vmem, vmem),
        compiler_params=params,
        cost_estimate=cost(1, 4 * four.size),
        name="inputs",
    )(three_four, three_six, conv_weight)
    met, grad_six = lax.optimization_barrier((met, grad_six))
    grad_weight = weight_finish(added(piece, met), found).reshape(own.shape)
    totals = every_group(slopes)
    grad_gain = jnp.stack([totals[1], totals[3]])
    grad_shift = jnp.stack([totals[0], totals[2]])
    return (grad_four[None], grad_six[None], grad_weight, grad_gain, grad_shift)


def solution(mesh):
    placed = (
        P("rep", "sp", None, None),
        P("rep", "sp", None, None),
        P(),
        P(),
        P(),
        P("rep", "sp", None, None),
        P("rep", "sp", None, None),
    )
    return jax.shard_map(
        local,
        mesh=mesh,
        in_specs=placed,
        out_specs=(
            P("rep", "sp", None, None),
            P("rep", "sp", None, None),
            P(None, "sp", None),
            P(),
            P(),
        ),
        check_vma=False,
    )
```

```python
import functools

import jax
import jax.numpy as jnp
from jax import lax
from jax.experimental import pallas as pl
from jax.experimental.pallas import tpu as pltpu
from jax.sharding import PartitionSpec as P

GROUP = 16
RADIX = 4
EPSILON = 1e-05
F32 = jnp.float32
BF16 = jnp.bfloat16
VMEM_LIMIT = 20 * 1024 * 1024
EDGE_LIMIT = 60 * 1024 * 1024


def chunk_of(rows, most):
    return max(size for size in range(1, most + 1) if rows % size == 0)


def pitch_of(cols):
    return -(-cols // 16) * 16


def chunks_of(rows, most):
    size = chunk_of(rows, most)
    return [(start, start + size) for start in range(0, rows, size)]


def widen(cells, pitch):
    cells = cells.astype(F32)
    extra = pitch - cells.shape[0]
    if extra:
        cells = jnp.concatenate([cells, jnp.zeros((extra, cells.shape[1]), F32)], 0)
    return cells


def put_three(three, row, cells, cols, turned):
    pitch, chan = cells.shape
    left, right = pltpu.roll(cells, 1, 0), pltpu.roll(cells, pitch - 1, 0)
    if pitch == cols:
        col = lax.broadcasted_iota(jnp.int32, (8, chan), 0)
        left = jnp.concatenate([jnp.where(col == 0, 0.0, left[:8]), left[8:]], 0)
        right = jnp.concatenate([right[:-8], jnp.where(col == 7, 0.0, right[-8:])], 0)
    parts = (right, cells, left) if turned else (left, cells, right)
    for place, part in enumerate(parts):
        three[row, :, place * chan : (place + 1) * chan] = part.astype(BF16)


def beside(three, starts, size):
    pitch, width = three.shape[1:]
    return jnp.concatenate([three[start : start + size].reshape(size * pitch, width) for start in starts], 1)


def edges_valid(sp_count):
    index = lax.axis_index("sp")
    return jnp.where(index > 0, 1.0, 0.0), jnp.where(index < sp_count - 1, 1.0, 0.0)


def level_coefs(moments, gain, shift, count):
    mean = moments[0:1] / count
    spread = moments[1:2] / count - mean * mean
    return mean, lax.rsqrt(spread + EPSILON), gain, shift


def slope_of(conv, cotan, coefs):
    mean, rstd, gain, shift = coefs
    centred = conv.astype(F32) - mean
    half = centred * (0.5 * rstd * gain) + 0.5 * shift
    turn = jnp.tanh(half)
    return centred, cotan.astype(F32) * ((1.0 + turn) * (1.0 + half * (1.0 - turn)))


def masked(cells, cols):
    if cells.shape[0] == cols:
        return cells
    col = lax.broadcasted_iota(jnp.int32, cells.shape, 0)
    return jnp.where(col < cols, cells, 0.0)


def staged(fills, dots):
    fills[0]()
    for index, dot in enumerate(dots):
        if index + 1 < len(fills):
            fills[index + 1]()
        dot()


def forward_level(x_ref, top, bottom, valid, w_ref, conv_ref, three, sums, most):
    rows, cols, chan = x_ref.shape
    pitch = three.shape[1]

    def fill_row(row):
        if row < 2:
            cells = top(row) * valid[0]
        elif row < rows + 2:
            cells = widen(x_ref[row - 2], pitch)
        else:
            cells = bottom(row - rows - 2) * valid[1]
        put_three(three, row, cells, cols, False)

    def dot(start, end, index):
        lhs = beside(three, (start, start + 1, start + 2), end - start)
        conv = jnp.dot(lhs, w_ref[...].reshape(9 * chan, chan), preferred_element_type=F32).astype(BF16)
        conv = conv.reshape(end - start, pitch, chan)
        conv_ref[start:end] = conv
        first, last = max(start, 1), min(end, rows + 1)
        conv = conv[first - start : last - start].astype(F32)
        if pitch != cols:
            conv = conv[:, :cols]
        conv = conv.reshape(-1, 8, chan)
        sums[0].append(jnp.sum(conv, 0))
        sums[1].append(jnp.sum(conv * conv, 0))

    chunks = [[start + 1, end + 1] for start, end in chunks_of(rows, most)]
    chunks[0][0] = 0
    chunks[-1][1] = rows + 2
    fills, dots, done = [], [], 0
    for index, (start, end) in enumerate(chunks):
        fills.append(lambda todo=range(done, end + 2): [fill_row(row) for row in todo])
        done = end + 2
        dots.append(functools.partial(dot, start, end, index))
    return fills, dots


def folded(parts):
    total = parts[0]
    for part in parts[1:]:
        total = total + part
    return jnp.sum(total, 0, keepdims=True)


def forward_kernel(
    sp_count, four_ref, six_ref, above_ref, below_ref, w_ref,
    conv_four_ref, conv_six_ref, moments_ref, three_four, three_six,
):
    cols_four = four_ref.shape[1]
    valid = edges_valid(sp_count)
    base, pitch_six = 3 * cols_four, three_six.shape[1]

    def reader(ref, start, pitch):
        return lambda edge: ref[start + edge * pitch : start + (edge + 1) * pitch].astype(F32)

    sums_four, sums_six = ([], []), ([], [])
    fills_six, dots_six = forward_level(
        six_ref, reader(above_ref, base, pitch_six), reader(below_ref, base, pitch_six), valid, w_ref,
        conv_six_ref, three_six, sums_six, 12,
    )
    fills_four, dots_four = forward_level(
        four_ref, reader(above_ref, 0, cols_four), reader(below_ref, 0, cols_four), valid, w_ref,
        conv_four_ref, three_four, sums_four, 8,
    )
    staged(fills_six + fills_four, dots_six + dots_four)
    sums = [folded(parts) for parts in sums_four + sums_six]
    moments_ref[...] = jnp.concatenate(sums, 0)


def slope_level(conv_ref, cotan_ref, above, below, coefs, slope_ref):
    rows, cols, chan = cotan_ref.shape
    pitch = conv_ref.shape[1]

    def put(row, cotan):
        centred, slope = slope_of(conv_ref[row], widen(cotan, pitch), coefs)
        slope_ref[row] = slope
        return centred, slope

    def step(row, sums):
        centred, slope = put(row + 1, cotan_ref[row])
        first = jnp.sum(slope.reshape(-1, 8, chan), 0)
        second = jnp.sum((slope * centred).reshape(-1, 8, chan), 0)
        return sums[0] + first, sums[1] + second

    put(0, above)
    put(rows + 1, below)
    zero = jnp.zeros((8, chan), F32)
    first, second = lax.fori_loop(0, rows, step, (zero, zero), unroll=chunk_of(rows, 8))
    first = 0.5 * jnp.sum(first, 0, keepdims=True)
    return first, 0.5 * coefs[1] * jnp.sum(second, 0, keepdims=True)


def slope_kernel(
    counts, conv_four_ref, conv_six_ref, cotan_four_ref, cotan_six_ref, above_ref, below_ref, moments_ref, gain_ref,
    shift_ref, slope_four_ref, slope_six_ref, slopes_ref,
):
    sums = ()
    cols_four = cotan_four_ref.shape[1]
    starts = (2 * cols_four, 3 * cols_four + 2 * conv_six_ref.shape[1])
    for level, (conv_ref, cotan_ref, slope_ref) in enumerate(
        ((conv_four_ref, cotan_four_ref, slope_four_ref), (conv_six_ref, cotan_six_ref, slope_six_ref))
    ):
        pair = moments_ref[2 * level : 2 * level + 2]
        here = slice(level, level + 1)
        edge = slice(starts[level], starts[level] + conv_ref.shape[1])
        coefs = level_coefs(pair, gain_ref[here], shift_ref[here], counts[level])
        sums += slope_level(conv_ref, cotan_ref, above_ref[edge], below_ref[edge], coefs, slope_ref)
    slopes_ref[...] = jnp.concatenate(sums, 0)


def backward_level(x_ref, conv_ref, slope_ref, valid, coefs, slopes, count, three, put, most):
    rows, cols, chan = x_ref.shape
    pitch = three.shape[1]
    mean, rstd, gain, shift = coefs
    lead = gain * rstd
    offset, factor = lead * (slopes[0:1] / count), lead * rstd * (slopes[1:2] / count)

    def fill_row(row):
        centred = conv_ref[row].astype(F32) - mean
        dconv = masked((0.5 * lead) * slope_ref[row] - (offset + centred * factor), cols)
        if row == 0:
            dconv = dconv * valid[0]
        elif row == rows + 1:
            dconv = dconv * valid[1]
        put_three(three, row, dconv, cols, True)

    def dot(start, end):
        size = end - start
        cells = x_ref[start:end]
        if pitch != cols:
            cells = cells.astype(F32)
            cells = jnp.concatenate([cells, jnp.zeros((size, pitch - cols, chan), F32)], 1).astype(BF16)
        lhs = cells.reshape(size * pitch, chan)
        rhs = beside(three, (start + 2, start + 1, start), size)
        put(lax.dot_general(lhs, rhs, (((0,), (0,)), ((), ())), preferred_element_type=F32))

    fills, dots, done = [], [], 0
    for start, end in chunks_of(rows, most):
        fills.append(lambda todo=range(done, end + 2): [fill_row(row) for row in todo])
        done = end + 2
        dots.append(functools.partial(dot, start, end))
    return fills, dots


def backward_kernel(
    counts, sp_count, four_ref, six_ref, conv_four_ref, conv_six_ref, slope_four_ref, slope_six_ref,
    moments_ref, slopes_ref, gain_ref, shift_ref, three_four, three_six, own_ref, sent_ref, total,
):
    valid = edges_valid(sp_count)
    begun = []

    def put(term):
        total[...] = total[...] + term if begun else term
        begun.append(True)

    fills, dots = [], []
    for level, x_ref, conv_ref, slope_ref, three, most in (
        (1, six_ref, conv_six_ref, slope_six_ref, three_six, 12),
        (0, four_ref, conv_four_ref, slope_four_ref, three_four, 8),
    ):
        here = slice(level, level + 1)
        pair = slice(2 * level, 2 * level + 2)
        coefs = level_coefs(moments_ref[pair], gain_ref[here], shift_ref[here], counts[level])
        level_fills, level_dots = backward_level(
            x_ref, conv_ref, slope_ref, valid, coefs, slopes_ref[pair], counts[level], three, put, most
        )
        fills += level_fills
        dots += level_dots
    staged(fills, dots)
    share, chan = own_ref.shape[1:]
    for step in range(sp_count):
        begin = pl.multiple_of((lax.axis_index("sp") ^ step) * share, share)
        for tap in range(9):
            part = total[pl.ds(begin, share), tap * chan : (tap + 1) * chan]
            if step == 0:
                own_ref[tap] = part
            else:
                sent_ref[step - 1, tap] = part.astype(BF16)


def input_level(three, turned, grad, grad_ref, sems, most):
    rows, cols, chan = grad.shape
    pitch = three.shape[1]
    copies = []
    for index, (start, end) in enumerate(chunks_of(rows, most)):
        size = end - start
        lhs = beside(three, (start + 2, start + 1, start), size)
        term = jnp.dot(lhs, turned[...], preferred_element_type=F32)
        grad[start:end] = term.reshape(size, pitch, chan)[:, :cols].astype(BF16)
        copies.append(pltpu.make_async_copy(grad.at[start:end], grad_ref.at[start:end], sems.at[index]))
        copies[-1].start()
    return copies


def input_kernel(
    three_four, three_six, w_ref, grad_four_ref, grad_six_ref, turned, grad_four, grad_six, sems_four, sems_six
):
    chan = w_ref.shape[1]
    for tap in range(9):
        turned[tap * chan : (tap + 1) * chan] = w_ref[tap].T
    copies = input_level(three_six, turned, grad_six, grad_six_ref, sems_six, 12)
    copies += input_level(three_four, turned, grad_four, grad_four_ref, sems_four, 8)
    for copy in copies:
        copy.wait()


def swap(array, axis, stride):
    count = lax.axis_size(axis)
    return lax.ppermute(array, axis, [(i, i ^ stride) for i in range(count)])


def edge_kernel(starts, four_ref, six_ref, cotan_four_ref, cotan_six_ref, *rest):
    outs, six_rows, sems = rest[:-2], rest[-2], rest[-1]
    rows_four, cols_four = four_ref.shape[:2]
    rows_six = six_ref.shape[0]
    pitch = pitch_of(six_ref.shape[1])
    copies = []
    for number, (start, out_ref) in enumerate(zip(starts, outs)):
        last = (1 - jnp.minimum(lax.axis_index("sp"), 1)) if start is None else start
        for part, (ref, row) in enumerate(
            (
                (four_ref, last * (rows_four - 2)),
                (four_ref, last * (rows_four - 2) + 1),
                (cotan_four_ref, last * (rows_four - 1)),
                (six_ref, last * (rows_six - 2)),
                (six_ref, last * (rows_six - 2) + 1),
                (cotan_six_ref, last * (rows_six - 1)),
            )
        ):
            if part < 3:
                target = out_ref.at[part * cols_four : (part + 1) * cols_four]
            else:
                target = six_rows.at[number, part - 3]
            copies.append(pltpu.make_async_copy(ref.at[row], target, sems.at[number, part]))
    for copy in copies:
        copy.start()
    for copy in copies:
        copy.wait()
    for number, out_ref in enumerate(outs):
        for part in range(3):
            begin = 3 * cols_four + part * pitch
            out_ref[begin : begin + pitch] = widen(six_rows[number, part], pitch).astype(BF16)


def edges(four, six, cotan_four, cotan_six):
    count = lax.axis_size("sp")
    starts = (None,) if count == 2 else (0, 1)
    length = 3 * four.shape[1] + 3 * pitch_of(six.shape[1])
    vmem = pl.BlockSpec(memory_space=pltpu.VMEM)
    hbm = pl.BlockSpec(memory_space=pltpu.HBM)
    outs = pl.pallas_call(
        functools.partial(edge_kernel, starts),
        out_shape=tuple(jax.ShapeDtypeStruct((length, four.shape[2]), BF16) for _ in starts),
        in_specs=[hbm] * 4,
        out_specs=tuple(vmem for _ in starts),
        scratch_shapes=[
            pltpu.VMEM((len(starts), 3) + six.shape[1:], BF16),
            pltpu.SemaphoreType.DMA((len(starts), 6)),
        ],
        compiler_params=pltpu.CompilerParams(vmem_limit_bytes=EDGE_LIMIT),
        name="edges",
    )(four, six, cotan_four, cotan_six)
    if count == 2:
        met = swap(outs[0], "sp", 1)
        return met, met
    above = lax.ppermute(outs[1], "sp", [(i, (i + 1) % count) for i in range(count)])
    below = lax.ppermute(outs[0], "sp", [((i + 1) % count, i) for i in range(count)])
    return above, below


def swap_odd(array, axis, stride):
    count, sp_count = lax.axis_size("rep"), lax.axis_size("sp")
    pairs = []
    for rep in range(count):
        for sp in range(1, sp_count, 2):
            other = (rep ^ stride) * sp_count + sp if axis == "rep" else rep * sp_count + (sp ^ stride)
            pairs.append((rep * sp_count + sp, other))
    return lax.ppermute(array, ("rep", "sp"), pairs)


def group_sum(sums, odd):
    sums = sums + swap(sums, "sp", 1)
    stride = 2
    while stride < lax.axis_size("sp"):
        sums = sums + swap_odd(sums, "sp", stride)
        stride = 2 * stride
    stride = 1
    while stride < GROUP:
        met = [swap_odd(sums, "rep", k * stride) for k in range(1, RADIX)]
        sums = (sums + met[0]) + (met[1] + met[2])
        stride = RADIX * stride
    return jnp.where(odd, sums, swap(sums, "sp", 1))


def every_group(sums):
    stride = GROUP
    while stride < lax.axis_size("rep"):
        sums = sums + swap(sums, "rep", stride)
        stride = 2 * stride
    return sums


def places():
    found = []
    for shift in (0, 2):
        digit = (lax.axis_index("rep") >> shift) & (RADIX - 1)
        found.append(([digit ^ k for k in range(RADIX)], (digit & 1) == 1, digit >= 2))
    return found + [(lax.axis_index("sp") & 1) == 1]


def digit_order(parts, place):
    unused, odd, high = place
    even = [jnp.where(odd, parts[k ^ 1], parts[k]) for k in range(RADIX)]
    return jnp.stack([jnp.where(high, even[k ^ 2], even[k]) for k in range(RADIX)])


def piece_of(pieces, index):
    sizes = (1,) + pieces.shape[1:]
    return lax.dynamic_slice(pieces, (index, 0, 0), sizes, allow_negative_indices=False)[0]


def scatter_start(own, sent, place):
    met = [swap(sent[step], "sp", step + 1) for step in range(sent.shape[0])]
    chan = own.shape[2]
    parts = [part.reshape(RADIX, -1, chan) for part in [own] + met]

    def piece(k):
        total = piece_of(parts[0], place[0][k])
        for part in parts[1:]:
            total = total + piece_of(part, place[0][k]).astype(F32)
        return total

    return piece(0), [piece(k).astype(BF16) for k in range(1, RADIX)]


def added(own, met):
    return (own + met[0].astype(F32)) + (met[1].astype(F32) + met[2].astype(F32))


def weight_finish(total, found):
    chan = total.shape[1]
    indices = found[1][0]
    pieces = total.reshape(RADIX, -1, chan)
    met = [
        swap(piece_of(pieces, indices[k]).astype(BF16), "rep", k * RADIX)
        for k in range(1, RADIX)
    ]
    total = added(piece_of(pieces, indices[0]), met).astype(BF16)
    stride = GROUP
    while stride < lax.axis_size("rep"):
        met = [swap(total, "rep", k * stride) for k in range(1, RADIX)]
        total = added(total.astype(F32), met).astype(BF16)
        stride = RADIX * stride
    met = [total] + [swap(total, "rep", k * RADIX) for k in range(1, RADIX)]
    total = digit_order(met, found[1]).reshape(-1, chan)
    met = [total] + [swap(total, "rep", k) for k in range(1, RADIX)]
    whole = jnp.zeros((RADIX,) + total.shape, F32)
    for k in range(RADIX):
        start = (found[0][0][k], 0, 0)
        whole = lax.dynamic_update_slice(whole, met[k][None].astype(F32), start, allow_negative_indices=False)
    return whole


def local(level_four, level_six, conv_weight, bn_gain, bn_shift, cotan_four, cotan_six):
    sp_count = lax.axis_size("sp")
    images = level_four.shape[0]
    four, six, cot_four, cot_six = (a[0] for a in (level_four, level_six, cotan_four, cotan_six))
    rows_four, cols_four, chan = four.shape
    rows_six, cols_six = six.shape[:2]
    pitch_four, pitch_six = pitch_of(cols_four), pitch_of(cols_six)
    counts = (
        float(images * GROUP * rows_four * sp_count * cols_four),
        float(images * GROUP * rows_six * sp_count * cols_six),
    )
    found, four = lax.optimization_barrier((places(), four))
    above, below = edges(four, six, cot_four, cot_six)
    vmem = pl.BlockSpec(memory_space=pltpu.VMEM)
    hbm = pl.BlockSpec(memory_space=pltpu.HBM)
    params = pltpu.CompilerParams(vmem_limit_bytes=VMEM_LIMIT)
    framed_four = jax.ShapeDtypeStruct((rows_four + 2, pitch_four, chan), BF16)
    framed_six = jax.ShapeDtypeStruct((rows_six + 2, pitch_six, chan), BF16)
    four_sums = jax.ShapeDtypeStruct((4, chan), F32)
    flops = 2 * 9 * chan * chan * (rows_four * cols_four + rows_six * cols_six)

    def cost(share, size):
        return pl.CostEstimate(flops=int(flops * share), bytes_accessed=size, transcendentals=0)

    conv_four, conv_six, moments = pl.pallas_call(
        functools.partial(forward_kernel, sp_count),
        out_shape=(framed_four, framed_six, four_sums),
        in_specs=[vmem] * 5,
        out_specs=(vmem, vmem, vmem),
        scratch_shapes=[
            pltpu.VMEM((rows_four + 4, pitch_four, 3 * chan), BF16),
            pltpu.VMEM((rows_six + 4, pitch_six, 3 * chan), BF16),
        ],
        compiler_params=params,
        cost_estimate=cost(1, 4 * four.size),
        name="forward",
    )(four, six, above, below, conv_weight)
    moments = group_sum(moments, found[2])

    slope_four, slope_six, slopes = pl.pallas_call(
        functools.partial(slope_kernel, counts),
        out_shape=(
            jax.ShapeDtypeStruct(framed_four.shape, F32),
            jax.ShapeDtypeStruct(framed_six.shape, F32),
            four_sums,
        ),
        in_specs=[vmem] * 9,
        out_specs=(vmem,) * 3,
        compiler_params=params,
        cost_estimate=cost(0.01, 4 * four.size),
        name="slopes",
    )(conv_four, conv_six, cot_four, cot_six, above, below, moments, bn_gain, bn_shift)
    slopes = group_sum(slopes, found[2])

    share = chan // sp_count
    wide_four, wide_six = (
        jax.ShapeDtypeStruct(framed.shape[:2] + (3 * chan,), BF16) for framed in (framed_four, framed_six)
    )
    three_four, three_six, own, sent = pl.pallas_call(
        functools.partial(backward_kernel, counts, sp_count),
        out_shape=(
            wide_four,
            wide_six,
            jax.ShapeDtypeStruct((9, share, chan), F32),
            jax.ShapeDtypeStruct((sp_count - 1, 9, share, chan), BF16),
        ),
        in_specs=[vmem] * 10,
        out_specs=(vmem,) * 4,
        scratch_shapes=[pltpu.VMEM((chan, 9 * chan), F32)],
        compiler_params=params,
        cost_estimate=cost(1.2, 8 * four.size),
        name="backward",
    )(four, six, conv_four, conv_six, slope_four, slope_six, moments, slopes, bn_gain, bn_shift)

    piece, pieces = scatter_start(own, sent, found[0])
    pieces, three_four = lax.optimization_barrier((pieces, three_four))
    met = [swap(pieces[k - 1], "rep", k) for k in range(1, RADIX)]
    grad_four, grad_six = pl.pallas_call(
        input_kernel,
        out_shape=(
            jax.ShapeDtypeStruct(four.shape, BF16),
            jax.ShapeDtypeStruct(six.shape, BF16),
        ),
        in_specs=[vmem] * 3,
        out_specs=(hbm, hbm),
        scratch_shapes=[
            pltpu.VMEM((9 * chan, chan), BF16),
            pltpu.VMEM(four.shape, BF16),
            pltpu.VMEM(six.shape, BF16),
            pltpu.SemaphoreType.DMA((len(chunks_of(rows_four, 8)),)),
            pltpu.SemaphoreType.DMA((len(chunks_of(rows_six, 12)),)),
        ],
        compiler_params=params,
        cost_estimate=cost(1, 4 * four.size),
        name="inputs",
    )(three_four, three_six, conv_weight)
    met, grad_six = lax.optimization_barrier((met, grad_six))
    grad_weight = weight_finish(added(piece, met), found).reshape(own.shape)
    totals = every_group(slopes)
    grad_gain = jnp.stack([totals[1], totals[3]])
    grad_shift = jnp.stack([totals[0], totals[2]])
    return (grad_four[None], grad_six[None], grad_weight, grad_gain, grad_shift)


def solution(mesh):
    placed = (
        P("rep", "sp", None, None),
        P("rep", "sp", None, None),
        P(),
        P(),
        P(),
        P("rep", "sp", None, None),
        P("rep", "sp", None, None),
    )
    return jax.shard_map(
        local,
        mesh=mesh,
        in_specs=placed,
        out_specs=(
            P("rep", "sp", None, None),
            P("rep", "sp", None, None),
            P(None, "sp", None),
            P(),
            P(),
        ),
        check_vma=False,
    )
```

```python
import functools

import jax
import jax.numpy as jnp
from jax import lax
from jax.experimental import pallas as pl
from jax.experimental.pallas import tpu as pltpu
from jax.sharding import PartitionSpec as P

GROUP = 16
RADIX = 4
EPSILON = 1e-05
F32 = jnp.float32
BF16 = jnp.bfloat16
VMEM_LIMIT = 20 * 1024 * 1024
EDGE_LIMIT = 60 * 1024 * 1024


def chunk_of(rows, most):
    return max(size for size in range(1, most + 1) if rows % size == 0)


def pitch_of(cols):
    return -(-cols // 16) * 16


def chunks_of(rows, most):
    size = chunk_of(rows, most)
    return [(start, start + size) for start in range(0, rows, size)]


def widen(cells, pitch):
    cells = cells.astype(F32)
    extra = pitch - cells.shape[0]
    if extra:
        cells = jnp.concatenate([cells, jnp.zeros((extra, cells.shape[1]), F32)], 0)
    return cells


def put_three(three, row, cells, cols, turned):
    pitch, chan = cells.shape
    left, right = pltpu.roll(cells, 1, 0), pltpu.roll(cells, pitch - 1, 0)
    if pitch == cols:
        col = lax.broadcasted_iota(jnp.int32, (8, chan), 0)
        left = jnp.concatenate([jnp.where(col == 0, 0.0, left[:8]), left[8:]], 0)
        right = jnp.concatenate([right[:-8], jnp.where(col == 7, 0.0, right[-8:])], 0)
    parts = (right, cells, left) if turned else (left, cells, right)
    for place, part in enumerate(parts):
        three[row, :, place * chan : (place + 1) * chan] = part.astype(BF16)


def beside(three, starts, size):
    pitch, width = three.shape[1:]
    return jnp.concatenate([three[start : start + size].reshape(size * pitch, width) for start in starts], 1)


def edges_valid(sp_count):
    index = lax.axis_index("sp")
    return jnp.where(index > 0, 1.0, 0.0), jnp.where(index < sp_count - 1, 1.0, 0.0)


def level_coefs(moments, gain, shift, count):
    mean = moments[0:1] / count
    spread = moments[1:2] / count - mean * mean
    return mean, lax.rsqrt(spread + EPSILON), gain, shift


def slope_of(conv, cotan, coefs):
    mean, rstd, gain, shift = coefs
    centred = conv.astype(F32) - mean
    half = centred * (0.5 * rstd * gain) + 0.5 * shift
    turn = jnp.tanh(half)
    return centred, cotan.astype(F32) * ((1.0 + turn) * (1.0 + half * (1.0 - turn)))


def masked(cells, cols):
    if cells.shape[0] == cols:
        return cells
    col = lax.broadcasted_iota(jnp.int32, cells.shape, 0)
    return jnp.where(col < cols, cells, 0.0)


def staged(fills, dots):
    fills[0]()
    for index, dot in enumerate(dots):
        if index + 1 < len(fills):
            fills[index + 1]()
        dot()


def forward_level(x_ref, top, bottom, valid, w_ref, conv_ref, three, sums, most):
    rows, cols, chan = x_ref.shape
    pitch = three.shape[1]

    def fill_row(row):
        if row < 2:
            cells = top(row) * valid[0]
        elif row < rows + 2:
            cells = widen(x_ref[row - 2], pitch)
        else:
            cells = bottom(row - rows - 2) * valid[1]
        put_three(three, row, cells, cols, False)

    def dot(start, end, index):
        lhs = beside(three, (start, start + 1, start + 2), end - start)
        conv = jnp.dot(lhs, w_ref[...].reshape(9 * chan, chan), preferred_element_type=F32).astype(BF16)
        conv = conv.reshape(end - start, pitch, chan)
        conv_ref[start:end] = conv
        first, last = max(start, 1), min(end, rows + 1)
        conv = conv[first - start : last - start].astype(F32)
        if pitch != cols:
            conv = conv[:, :cols]
        conv = conv.reshape(-1, 8, chan)
        sums[0].append(jnp.sum(conv, 0))
        sums[1].append(jnp.sum(conv * conv, 0))

    chunks = [[start + 1, end + 1] for start, end in chunks_of(rows, most)]
    chunks[0][0] = 0
    chunks[-1][1] = rows + 2
    fills, dots, done = [], [], 0
    for index, (start, end) in enumerate(chunks):
        fills.append(lambda todo=range(done, end + 2): [fill_row(row) for row in todo])
        done = end + 2
        dots.append(functools.partial(dot, start, end, index))
    return fills, dots


def folded(parts):
    total = parts[0]
    for part in parts[1:]:
        total = total + part
    return jnp.sum(total, 0, keepdims=True)


def forward_kernel(
    sp_count, four_ref, six_ref, above_ref, below_ref, w_ref,
    conv_four_ref, conv_six_ref, moments_ref, three_four, three_six,
):
    cols_four = four_ref.shape[1]
    valid = edges_valid(sp_count)
    base, pitch_six = 3 * cols_four, three_six.shape[1]

    def reader(ref, start, pitch):
        return lambda edge: ref[start + edge * pitch : start + (edge + 1) * pitch].astype(F32)

    sums_four, sums_six = ([], []), ([], [])
    fills_six, dots_six = forward_level(
        six_ref, reader(above_ref, base, pitch_six), reader(below_ref, base, pitch_six), valid, w_ref,
        conv_six_ref, three_six, sums_six, 12,
    )
    fills_four, dots_four = forward_level(
        four_ref, reader(above_ref, 0, cols_four), reader(below_ref, 0, cols_four), valid, w_ref,
        conv_four_ref, three_four, sums_four, 8,
    )
    staged(fills_six + fills_four, dots_six + dots_four)
    sums = [folded(parts) for parts in sums_four + sums_six]
    moments_ref[...] = jnp.concatenate(sums, 0)


def slope_level(conv_ref, cotan_ref, above, below, coefs, slope_ref):
    rows, cols, chan = cotan_ref.shape
    pitch = conv_ref.shape[1]

    def put(row, cotan):
        centred, slope = slope_of(conv_ref[row], widen(cotan, pitch), coefs)
        slope_ref[row] = slope
        return centred, slope

    def step(row, sums):
        centred, slope = put(row + 1, cotan_ref[row])
        first = jnp.sum(slope.reshape(-1, 8, chan), 0)
        second = jnp.sum((slope * centred).reshape(-1, 8, chan), 0)
        return sums[0] + first, sums[1] + second

    put(0, above)
    put(rows + 1, below)
    zero = jnp.zeros((8, chan), F32)
    first, second = lax.fori_loop(0, rows, step, (zero, zero), unroll=chunk_of(rows, 8))
    first = 0.5 * jnp.sum(first, 0, keepdims=True)
    return first, 0.5 * coefs[1] * jnp.sum(second, 0, keepdims=True)


def slope_kernel(
    counts, conv_four_ref, conv_six_ref, cotan_four_ref, cotan_six_ref, above_ref, below_ref, moments_ref, gain_ref,
    shift_ref, slope_four_ref, slope_six_ref, slopes_ref,
):
    sums = ()
    cols_four = cotan_four_ref.shape[1]
    starts = (2 * cols_four, 3 * cols_four + 2 * conv_six_ref.shape[1])
    for level, (conv_ref, cotan_ref, slope_ref) in enumerate(
        ((conv_four_ref, cotan_four_ref, slope_four_ref), (conv_six_ref, cotan_six_ref, slope_six_ref))
    ):
        pair = moments_ref[2 * level : 2 * level + 2]
        here = slice(level, level + 1)
        edge = slice(starts[level], starts[level] + conv_ref.shape[1])
        coefs = level_coefs(pair, gain_ref[here], shift_ref[here], counts[level])
        sums += slope_level(conv_ref, cotan_ref, above_ref[edge], below_ref[edge], coefs, slope_ref)
    slopes_ref[...] = jnp.concatenate(sums, 0)


def backward_level(x_ref, conv_ref, slope_ref, valid, coefs, slopes, count, three, put, most):
    rows, cols, chan = x_ref.shape
    pitch = three.shape[1]
    mean, rstd, gain, shift = coefs
    lead = gain * rstd
    offset, factor = lead * (slopes[0:1] / count), lead * rstd * (slopes[1:2] / count)

    def fill_row(row):
        centred = conv_ref[row].astype(F32) - mean
        dconv = masked((0.5 * lead) * slope_ref[row] - (offset + centred * factor), cols)
        if row == 0:
            dconv = dconv * valid[0]
        elif row == rows + 1:
            dconv = dconv * valid[1]
        put_three(three, row, dconv, cols, True)

    def dot(start, end):
        size = end - start
        cells = x_ref[start:end]
        if pitch != cols:
            cells = cells.astype(F32)
            cells = jnp.concatenate([cells, jnp.zeros((size, pitch - cols, chan), F32)], 1).astype(BF16)
        lhs = cells.reshape(size * pitch, chan)
        rhs = beside(three, (start + 2, start + 1, start), size)
        put(lax.dot_general(lhs, rhs, (((0,), (0,)), ((), ())), preferred_element_type=F32))

    fills, dots, done = [], [], 0
    for start, end in chunks_of(rows, most):
        fills.append(lambda todo=range(done, end + 2): [fill_row(row) for row in todo])
        done = end + 2
        dots.append(functools.partial(dot, start, end))
    return fills, dots


def backward_kernel(
    counts, sp_count, four_ref, six_ref, conv_four_ref, conv_six_ref, slope_four_ref, slope_six_ref,
    moments_ref, slopes_ref, gain_ref, shift_ref, three_four, three_six, own_ref, sent_ref, total,
):
    valid = edges_valid(sp_count)
    begun = []

    def put(term):
        total[...] = total[...] + term if begun else term
        begun.append(True)

    fills, dots = [], []
    for level, x_ref, conv_ref, slope_ref, three, most in (
        (1, six_ref, conv_six_ref, slope_six_ref, three_six, 12),
        (0, four_ref, conv_four_ref, slope_four_ref, three_four, 8),
    ):
        here = slice(level, level + 1)
        pair = slice(2 * level, 2 * level + 2)
        coefs = level_coefs(moments_ref[pair], gain_ref[here], shift_ref[here], counts[level])
        level_fills, level_dots = backward_level(
            x_ref, conv_ref, slope_ref, valid, coefs, slopes_ref[pair], counts[level], three, put, most
        )
        fills += level_fills
        dots += level_dots
    staged(fills, dots)
    share, chan = own_ref.shape[1:]
    for step in range(sp_count):
        begin = pl.multiple_of((lax.axis_index("sp") ^ step) * share, share)
        for tap in range(9):
            part = total[pl.ds(begin, share), tap * chan : (tap + 1) * chan]
            if step == 0:
                own_ref[tap] = part
            else:
                sent_ref[step - 1, tap] = part.astype(BF16)


def input_level(three, turned, grad, grad_ref, sems, most):
    rows, cols, chan = grad.shape
    pitch = three.shape[1]
    copies = []
    for index, (start, end) in enumerate(chunks_of(rows, most)):
        size = end - start
        lhs = beside(three, (start + 2, start + 1, start), size)
        term = jnp.dot(lhs, turned[...], preferred_element_type=F32)
        grad[start:end] = term.reshape(size, pitch, chan)[:, :cols].astype(BF16)
        copies.append(pltpu.make_async_copy(grad.at[start:end], grad_ref.at[start:end], sems.at[index]))
        copies[-1].start()
    return copies


def input_kernel(
    three_four, three_six, w_ref, grad_four_ref, grad_six_ref, turned, grad_four, grad_six, sems_four, sems_six
):
    chan = w_ref.shape[1]
    for tap in range(9):
        turned[tap * chan : (tap + 1) * chan] = w_ref[tap].T
    copies = input_level(three_six, turned, grad_six, grad_six_ref, sems_six, 12)
    copies += input_level(three_four, turned, grad_four, grad_four_ref, sems_four, 8)
    for copy in copies:
        copy.wait()


def swap(array, axis, stride):
    count = lax.axis_size(axis)
    return lax.ppermute(array, axis, [(i, i ^ stride) for i in range(count)])


def edge_kernel(starts, four_ref, six_ref, cotan_four_ref, cotan_six_ref, *rest):
    outs, six_rows, sems = rest[:-2], rest[-2], rest[-1]
    rows_four, cols_four = four_ref.shape[:2]
    rows_six = six_ref.shape[0]
    pitch = pitch_of(six_ref.shape[1])
    copies = []
    for number, (start, out_ref) in enumerate(zip(starts, outs)):
        last = (1 - jnp.minimum(lax.axis_index("sp"), 1)) if start is None else start
        for part, (ref, row) in enumerate(
            (
                (four_ref, last * (rows_four - 2)),
                (four_ref, last * (rows_four - 2) + 1),
                (cotan_four_ref, last * (rows_four - 1)),
                (six_ref, last * (rows_six - 2)),
                (six_ref, last * (rows_six - 2) + 1),
                (cotan_six_ref, last * (rows_six - 1)),
            )
        ):
            if part < 3:
                target = out_ref.at[part * cols_four : (part + 1) * cols_four]
            else:
                target = six_rows.at[number, part - 3]
            copies.append(pltpu.make_async_copy(ref.at[row], target, sems.at[number, part]))
    for copy in copies:
        copy.start()
    for copy in copies:
        copy.wait()
    for number, out_ref in enumerate(outs):
        for part in range(3):
            begin = 3 * cols_four + part * pitch
            out_ref[begin : begin + pitch] = widen(six_rows[number, part], pitch).astype(BF16)


def edges(four, six, cotan_four, cotan_six):
    count = lax.axis_size("sp")
    starts = (None,) if count == 2 else (0, 1)
    length = 3 * four.shape[1] + 3 * pitch_of(six.shape[1])
    vmem = pl.BlockSpec(memory_space=pltpu.VMEM)
    hbm = pl.BlockSpec(memory_space=pltpu.HBM)
    outs = pl.pallas_call(
        functools.partial(edge_kernel, starts),
        out_shape=tuple(jax.ShapeDtypeStruct((length, four.shape[2]), BF16) for _ in starts),
        in_specs=[hbm] * 4,
        out_specs=tuple(vmem for _ in starts),
        scratch_shapes=[
            pltpu.VMEM((len(starts), 3) + six.shape[1:], BF16),
            pltpu.SemaphoreType.DMA((len(starts), 6)),
        ],
        compiler_params=pltpu.CompilerParams(vmem_limit_bytes=EDGE_LIMIT),
        name="edges",
    )(four, six, cotan_four, cotan_six)
    if count == 2:
        met = swap(outs[0], "sp", 1)
        return met, met
    above = lax.ppermute(outs[1], "sp", [(i, (i + 1) % count) for i in range(count)])
    below = lax.ppermute(outs[0], "sp", [((i + 1) % count, i) for i in range(count)])
    return above, below


def swap_odd(array, axis, stride):
    count, sp_count = lax.axis_size("rep"), lax.axis_size("sp")
    pairs = []
    for rep in range(count):
        for sp in range(sp_count):
            other = rep * sp_count + sp
            if sp % 2 == 1:
                other = (rep ^ stride) * sp_count + sp if axis == "rep" else rep * sp_count + (sp ^ stride)
            pairs.append((rep * sp_count + sp, other))
    return lax.ppermute(array, ("rep", "sp"), pairs)


def group_sum(sums, odd):
    sums = sums + swap(sums, "sp", 1)
    stride = 2
    while stride < lax.axis_size("sp"):
        sums = sums + swap_odd(sums, "sp", stride)
        stride = 2 * stride
    stride = 1
    while stride < GROUP:
        met = [swap_odd(sums, "rep", k * stride) for k in range(1, RADIX)]
        sums = (sums + met[0]) + (met[1] + met[2])
        stride = RADIX * stride
    return jnp.where(odd, sums, swap(sums, "sp", 1))


def every_group(sums):
    stride = GROUP
    while stride < lax.axis_size("rep"):
        sums = sums + swap(sums, "rep", stride)
        stride = 2 * stride
    return sums


def places():
    found = []
    for shift in (0, 2):
        digit = (lax.axis_index("rep") >> shift) & (RADIX - 1)
        found.append(([digit ^ k for k in range(RADIX)], (digit & 1) == 1, digit >= 2))
    return found + [(lax.axis_index("sp") & 1) == 1]


def digit_order(parts, place):
    unused, odd, high = place
    even = [jnp.where(odd, parts[k ^ 1], parts[k]) for k in range(RADIX)]
    return jnp.stack([jnp.where(high, even[k ^ 2], even[k]) for k in range(RADIX)])


def piece_of(pieces, index):
    sizes = (1,) + pieces.shape[1:]
    return lax.dynamic_slice(pieces, (index, 0, 0), sizes, allow_negative_indices=False)[0]


def scatter_start(own, sent, place):
    met = [swap(sent[step], "sp", step + 1) for step in range(sent.shape[0])]
    chan = own.shape[2]
    parts = [part.reshape(RADIX, -1, chan) for part in [own] + met]

    def piece(k):
        total = piece_of(parts[0], place[0][k])
        for part in parts[1:]:
            total = total + piece_of(part, place[0][k]).astype(F32)
        return total

    return piece(0), [piece(k).astype(BF16) for k in range(1, RADIX)]


def added(own, met):
    return (own + met[0].astype(F32)) + (met[1].astype(F32) + met[2].astype(F32))


def weight_finish(total, found):
    chan = total.shape[1]
    indices = found[1][0]
    pieces = total.reshape(RADIX, -1, chan)
    met = [
        swap(piece_of(pieces, indices[k]).astype(BF16), "rep", k * RADIX)
        for k in range(1, RADIX)
    ]
    total = added(piece_of(pieces, indices[0]), met).astype(BF16)
    stride = GROUP
    while stride < lax.axis_size("rep"):
        met = [swap(total, "rep", k * stride) for k in range(1, RADIX)]
        total = added(total.astype(F32), met).astype(BF16)
        stride = RADIX * stride
    met = [total] + [swap(total, "rep", k * RADIX) for k in range(1, RADIX)]
    total = digit_order(met, found[1]).reshape(-1, chan)
    met = [total] + [swap(total, "rep", k) for k in range(1, RADIX)]
    whole = jnp.zeros((RADIX,) + total.shape, F32)
    for k in range(RADIX):
        start = (found[0][0][k], 0, 0)
        whole = lax.dynamic_update_slice(whole, met[k][None].astype(F32), start, allow_negative_indices=False)
    return whole


def local(level_four, level_six, conv_weight, bn_gain, bn_shift, cotan_four, cotan_six):
    sp_count = lax.axis_size("sp")
    images = level_four.shape[0]
    four, six, cot_four, cot_six = (a[0] for a in (level_four, level_six, cotan_four, cotan_six))
    rows_four, cols_four, chan = four.shape
    rows_six, cols_six = six.shape[:2]
    pitch_four, pitch_six = pitch_of(cols_four), pitch_of(cols_six)
    counts = (
        float(images * GROUP * rows_four * sp_count * cols_four),
        float(images * GROUP * rows_six * sp_count * cols_six),
    )
    found, four = lax.optimization_barrier((places(), four))
    above, below = edges(four, six, cot_four, cot_six)
    vmem = pl.BlockSpec(memory_space=pltpu.VMEM)
    hbm = pl.BlockSpec(memory_space=pltpu.HBM)
    params = pltpu.CompilerParams(vmem_limit_bytes=VMEM_LIMIT)
    framed_four = jax.ShapeDtypeStruct((rows_four + 2, pitch_four, chan), BF16)
    framed_six = jax.ShapeDtypeStruct((rows_six + 2, pitch_six, chan), BF16)
    four_sums = jax.ShapeDtypeStruct((4, chan), F32)
    flops = 2 * 9 * chan * chan * (rows_four * cols_four + rows_six * cols_six)

    def cost(share, size):
        return pl.CostEstimate(flops=int(flops * share), bytes_accessed=size, transcendentals=0)

    conv_four, conv_six, moments = pl.pallas_call(
        functools.partial(forward_kernel, sp_count),
        out_shape=(framed_four, framed_six, four_sums),
        in_specs=[vmem] * 5,
        out_specs=(vmem, vmem, vmem),
        scratch_shapes=[
            pltpu.VMEM((rows_four + 4, pitch_four, 3 * chan), BF16),
            pltpu.VMEM((rows_six + 4, pitch_six, 3 * chan), BF16),
        ],
        compiler_params=params,
        cost_estimate=cost(1, 4 * four.size),
        name="forward",
    )(four, six, above, below, conv_weight)
    moments = group_sum(moments, found[2])

    slope_four, slope_six, slopes = pl.pallas_call(
        functools.partial(slope_kernel, counts),
        out_shape=(
            jax.ShapeDtypeStruct(framed_four.shape, F32),
            jax.ShapeDtypeStruct(framed_six.shape, F32),
            four_sums,
        ),
        in_specs=[vmem] * 9,
        out_specs=(vmem,) * 3,
        compiler_params=params,
        cost_estimate=cost(0.01, 4 * four.size),
        name="slopes",
    )(conv_four, conv_six, cot_four, cot_six, above, below, moments, bn_gain, bn_shift)
    slopes = group_sum(slopes, found[2])

    share = chan // sp_count
    wide_four, wide_six = (
        jax.ShapeDtypeStruct(framed.shape[:2] + (3 * chan,), BF16) for framed in (framed_four, framed_six)
    )
    three_four, three_six, own, sent = pl.pallas_call(
        functools.partial(backward_kernel, counts, sp_count),
        out_shape=(
            wide_four,
            wide_six,
            jax.ShapeDtypeStruct((9, share, chan), F32),
            jax.ShapeDtypeStruct((sp_count - 1, 9, share, chan), BF16),
        ),
        in_specs=[vmem] * 10,
        out_specs=(vmem,) * 4,
        scratch_shapes=[pltpu.VMEM((chan, 9 * chan), F32)],
        compiler_params=params,
        cost_estimate=cost(1.2, 8 * four.size),
        name="backward",
    )(four, six, conv_four, conv_six, slope_four, slope_six, moments, slopes, bn_gain, bn_shift)

    piece, pieces = scatter_start(own, sent, found[0])
    pieces, three_four = lax.optimization_barrier((pieces, three_four))
    met = [swap(pieces[k - 1], "rep", k) for k in range(1, RADIX)]
    grad_four, grad_six = pl.pallas_call(
        input_kernel,
        out_shape=(
            jax.ShapeDtypeStruct(four.shape, BF16),
            jax.ShapeDtypeStruct(six.shape, BF16),
        ),
        in_specs=[vmem] * 3,
        out_specs=(hbm, hbm),
        scratch_shapes=[
            pltpu.VMEM((9 * chan, chan), BF16),
            pltpu.VMEM(four.shape, BF16),
            pltpu.VMEM(six.shape, BF16),
            pltpu.SemaphoreType.DMA((len(chunks_of(rows_four, 8)),)),
            pltpu.SemaphoreType.DMA((len(chunks_of(rows_six, 12)),)),
        ],
        compiler_params=params,
        cost_estimate=cost(1, 4 * four.size),
        name="inputs",
    )(three_four, three_six, conv_weight)
    met, grad_six = lax.optimization_barrier((met, grad_six))
    grad_weight = weight_finish(added(piece, met), found).reshape(own.shape)
    totals = every_group(slopes)
    grad_gain = jnp.stack([totals[1], totals[3]])
    grad_shift = jnp.stack([totals[0], totals[2]])
    return (grad_four[None], grad_six[None], grad_weight, grad_gain, grad_shift)


def solution(mesh):
    placed = (
        P("rep", "sp", None, None),
        P("rep", "sp", None, None),
        P(),
        P(),
        P(),
        P("rep", "sp", None, None),
        P("rep", "sp", None, None),
    )
    return jax.shard_map(
        local,
        mesh=mesh,
        in_specs=placed,
        out_specs=(
            P("rep", "sp", None, None),
            P("rep", "sp", None, None),
            P(None, "sp", None),
            P(),
            P(),
        ),
        check_vma=False,
    )
```

```python
import functools

import jax
import jax.numpy as jnp
from jax import lax
from jax.experimental import pallas as pl
from jax.experimental.pallas import tpu as pltpu
from jax.sharding import PartitionSpec as P

GROUP = 16
RADIX = 4
FAR_FIRST = (3, 2, 1)
EPSILON = 1e-05
F32 = jnp.float32
BF16 = jnp.bfloat16
VMEM_LIMIT = 20 * 1024 * 1024
EDGE_LIMIT = 60 * 1024 * 1024


def chunk_of(rows, most):
    return max(size for size in range(1, most + 1) if rows % size == 0)


def pitch_of(cols):
    return -(-cols // 16) * 16


def chunks_of(rows, most):
    size = chunk_of(rows, most)
    return [(start, start + size) for start in range(0, rows, size)]


def widen(cells, pitch):
    cells = cells.astype(F32)
    extra = pitch - cells.shape[0]
    if extra:
        cells = jnp.concatenate([cells, jnp.zeros((extra, cells.shape[1]), F32)], 0)
    return cells


def put_three(three, row, cells, cols, turned):
    pitch, chan = cells.shape
    left, right = pltpu.roll(cells, 1, 0), pltpu.roll(cells, pitch - 1, 0)
    if pitch == cols:
        col = lax.broadcasted_iota(jnp.int32, (8, chan), 0)
        left = jnp.concatenate([jnp.where(col == 0, 0.0, left[:8]), left[8:]], 0)
        right = jnp.concatenate([right[:-8], jnp.where(col == 7, 0.0, right[-8:])], 0)
    parts = (right, cells, left) if turned else (left, cells, right)
    for place, part in enumerate(parts):
        three[row, :, place * chan : (place + 1) * chan] = part.astype(BF16)


def beside(three, starts, size):
    pitch, width = three.shape[1:]
    return jnp.concatenate([three[start : start + size].reshape(size * pitch, width) for start in starts], 1)


def edges_valid(sp_count):
    index = lax.axis_index("sp")
    return jnp.where(index > 0, 1.0, 0.0), jnp.where(index < sp_count - 1, 1.0, 0.0)


def level_coefs(moments, gain, shift, count):
    mean = moments[0:1] / count
    spread = moments[1:2] / count - mean * mean
    return mean, lax.rsqrt(spread + EPSILON), gain, shift


def slope_of(conv, cotan, coefs):
    mean, rstd, gain, shift = coefs
    centred = conv.astype(F32) - mean
    half = centred * (0.5 * rstd * gain) + 0.5 * shift
    turn = jnp.tanh(half)
    return centred, cotan.astype(F32) * ((1.0 + turn) * (1.0 + half * (1.0 - turn)))


def masked(cells, cols):
    if cells.shape[0] == cols:
        return cells
    col = lax.broadcasted_iota(jnp.int32, cells.shape, 0)
    return jnp.where(col < cols, cells, 0.0)


def staged(fills, dots):
    fills[0]()
    for index, dot in enumerate(dots):
        if index + 1 < len(fills):
            fills[index + 1]()
        dot()


def forward_level(x_ref, top, bottom, valid, w_ref, conv_ref, three, sums, most):
    rows, cols, chan = x_ref.shape
    pitch = three.shape[1]

    def fill_row(row):
        if row < 2:
            cells = top(row) * valid[0]
        elif row < rows + 2:
            cells = widen(x_ref[row - 2], pitch)
        else:
            cells = bottom(row - rows - 2) * valid[1]
        put_three(three, row, cells, cols, False)

    def dot(start, end, index):
        lhs = beside(three, (start, start + 1, start + 2), end - start)
        conv = jnp.dot(lhs, w_ref[...].reshape(9 * chan, chan), preferred_element_type=F32).astype(BF16)
        conv = conv.reshape(end - start, pitch, chan)
        conv_ref[start:end] = conv
        first, last = max(start, 1), min(end, rows + 1)
        conv = conv[first - start : last - start].astype(F32)
        if pitch != cols:
            conv = conv[:, :cols]
        conv = conv.reshape(-1, 8, chan)
        sums[0].append(jnp.sum(conv, 0))
        sums[1].append(jnp.sum(conv * conv, 0))

    chunks = [[start + 1, end + 1] for start, end in chunks_of(rows, most)]
    chunks[0][0] = 0
    chunks[-1][1] = rows + 2
    fills, dots, done = [], [], 0
    for index, (start, end) in enumerate(chunks):
        fills.append(lambda todo=range(done, end + 2): [fill_row(row) for row in todo])
        done = end + 2
        dots.append(functools.partial(dot, start, end, index))
    return fills, dots


def folded(parts):
    total = parts[0]
    for part in parts[1:]:
        total = total + part
    return jnp.sum(total, 0, keepdims=True)


def forward_kernel(
    sp_count, four_ref, six_ref, above_ref, below_ref, w_ref,
    conv_four_ref, conv_six_ref, moments_ref, three_four, three_six,
):
    cols_four = four_ref.shape[1]
    valid = edges_valid(sp_count)
    base, pitch_six = 3 * cols_four, three_six.shape[1]

    def reader(ref, start, pitch):
        return lambda edge: ref[start + edge * pitch : start + (edge + 1) * pitch].astype(F32)

    sums_four, sums_six = ([], []), ([], [])
    fills_six, dots_six = forward_level(
        six_ref, reader(above_ref, base, pitch_six), reader(below_ref, base, pitch_six), valid, w_ref,
        conv_six_ref, three_six, sums_six, 12,
    )
    fills_four, dots_four = forward_level(
        four_ref, reader(above_ref, 0, cols_four), reader(below_ref, 0, cols_four), valid, w_ref,
        conv_four_ref, three_four, sums_four, 8,
    )
    staged(fills_six + fills_four, dots_six + dots_four)
    sums = [folded(parts) for parts in sums_four + sums_six]
    moments_ref[...] = jnp.concatenate(sums, 0)


def slope_level(conv_ref, cotan_ref, above, below, coefs, slope_ref):
    rows, cols, chan = cotan_ref.shape
    pitch = conv_ref.shape[1]

    def put(row, cotan):
        centred, slope = slope_of(conv_ref[row], widen(cotan, pitch), coefs)
        slope_ref[row] = slope
        return centred, slope

    def step(row, sums):
        centred, slope = put(row + 1, cotan_ref[row])
        first = jnp.sum(slope.reshape(-1, 8, chan), 0)
        second = jnp.sum((slope * centred).reshape(-1, 8, chan), 0)
        return sums[0] + first, sums[1] + second

    put(0, above)
    put(rows + 1, below)
    zero = jnp.zeros((8, chan), F32)
    first, second = lax.fori_loop(0, rows, step, (zero, zero), unroll=chunk_of(rows, 8))
    first = 0.5 * jnp.sum(first, 0, keepdims=True)
    return first, 0.5 * coefs[1] * jnp.sum(second, 0, keepdims=True)


def slope_kernel(
    counts, conv_four_ref, conv_six_ref, cotan_four_ref, cotan_six_ref, above_ref, below_ref, moments_ref, gain_ref,
    shift_ref, slope_four_ref, slope_six_ref, slopes_ref,
):
    sums = ()
    cols_four = cotan_four_ref.shape[1]
    starts = (2 * cols_four, 3 * cols_four + 2 * conv_six_ref.shape[1])
    for level, (conv_ref, cotan_ref, slope_ref) in enumerate(
        ((conv_four_ref, cotan_four_ref, slope_four_ref), (conv_six_ref, cotan_six_ref, slope_six_ref))
    ):
        pair = moments_ref[2 * level : 2 * level + 2]
        here = slice(level, level + 1)
        edge = slice(starts[level], starts[level] + conv_ref.shape[1])
        coefs = level_coefs(pair, gain_ref[here], shift_ref[here], counts[level])
        sums += slope_level(conv_ref, cotan_ref, above_ref[edge], below_ref[edge], coefs, slope_ref)
    slopes_ref[...] = jnp.concatenate(sums, 0)


def backward_level(x_ref, conv_ref, slope_ref, valid, coefs, slopes, count, three, put, most):
    rows, cols, chan = x_ref.shape
    pitch = three.shape[1]
    mean, rstd, gain, shift = coefs
    lead = gain * rstd
    offset, factor = lead * (slopes[0:1] / count), lead * rstd * (slopes[1:2] / count)

    def fill_row(row):
        centred = conv_ref[row].astype(F32) - mean
        dconv = masked((0.5 * lead) * slope_ref[row] - (offset + centred * factor), cols)
        if row == 0:
            dconv = dconv * valid[0]
        elif row == rows + 1:
            dconv = dconv * valid[1]
        put_three(three, row, dconv, cols, True)

    def dot(start, end):
        size = end - start
        cells = x_ref[start:end]
        if pitch != cols:
            cells = cells.astype(F32)
            cells = jnp.concatenate([cells, jnp.zeros((size, pitch - cols, chan), F32)], 1).astype(BF16)
        lhs = cells.reshape(size * pitch, chan)
        rhs = beside(three, (start + 2, start + 1, start), size)
        put(lax.dot_general(lhs, rhs, (((0,), (0,)), ((), ())), preferred_element_type=F32))

    fills, dots, done = [], [], 0
    for start, end in chunks_of(rows, most):
        fills.append(lambda todo=range(done, end + 2): [fill_row(row) for row in todo])
        done = end + 2
        dots.append(functools.partial(dot, start, end))
    return fills, dots


def backward_kernel(
    counts, sp_count, four_ref, six_ref, conv_four_ref, conv_six_ref, slope_four_ref, slope_six_ref,
    moments_ref, slopes_ref, gain_ref, shift_ref, three_four, three_six, own_ref, sent_ref, total,
):
    valid = edges_valid(sp_count)
    begun = []

    def put(term):
        total[...] = total[...] + term if begun else term
        begun.append(True)

    fills, dots = [], []
    for level, x_ref, conv_ref, slope_ref, three, most in (
        (1, six_ref, conv_six_ref, slope_six_ref, three_six, 12),
        (0, four_ref, conv_four_ref, slope_four_ref, three_four, 8),
    ):
        here = slice(level, level + 1)
        pair = slice(2 * level, 2 * level + 2)
        coefs = level_coefs(moments_ref[pair], gain_ref[here], shift_ref[here], counts[level])
        level_fills, level_dots = backward_level(
            x_ref, conv_ref, slope_ref, valid, coefs, slopes_ref[pair], counts[level], three, put, most
        )
        fills += level_fills
        dots += level_dots
    staged(fills, dots)
    share, chan = own_ref.shape[1:]
    for step in range(sp_count):
        begin = pl.multiple_of((lax.axis_index("sp") ^ step) * share, share)
        for tap in range(9):
            part = total[pl.ds(begin, share), tap * chan : (tap + 1) * chan]
            if step == 0:
                own_ref[tap] = part
            else:
                sent_ref[step - 1, tap] = part.astype(BF16)


def input_chunks(three, turned, grad, chunks, offset, sent=None):
    cols, chan = grad.shape[1:]
    pitch = three.shape[1]
    for index, (start, end) in enumerate(chunks):
        size = end - start
        lhs = beside(three, (start + 2, start + 1, start), size)
        term = jnp.dot(lhs, turned[...], preferred_element_type=F32)
        grad[start - offset : end - offset] = term.reshape(size, pitch, chan)[:, :cols].astype(BF16)
        if sent is not None:
            sent(index, start, end)


def input_first_kernel(chunks, three_four, w_ref, grad_ref, turned):
    chan = w_ref.shape[1]
    for tap in range(9):
        turned[tap * chan : (tap + 1) * chan] = w_ref[tap].T
    input_chunks(three_four, turned, grad_ref, chunks, 0)


def input_second_kernel(
    chunks, done, three_four, three_six, turned, first_ref, grad_four_ref, grad_six_ref,
    grad_four, grad_six, sem_first, sems_four, sems_six,
):
    copies = [pltpu.make_async_copy(first_ref, grad_four_ref.at[:done], sem_first)]
    copies[0].start()

    def sender(grad, grad_ref, offset, sems):
        def sent(index, start, end):
            copy = pltpu.make_async_copy(grad.at[start - offset : end - offset], grad_ref.at[start:end], sems.at[index])
            copy.start()
            copies.append(copy)

        return sent

    six_chunks = chunks_of(grad_six.shape[0], 12)
    input_chunks(three_six, turned, grad_six, six_chunks, 0, sender(grad_six, grad_six_ref, 0, sems_six))
    input_chunks(three_four, turned, grad_four, chunks, done, sender(grad_four, grad_four_ref, done, sems_four))
    for copy in copies:
        copy.wait()


def swap(array, axis, stride):
    count = lax.axis_size(axis)
    return lax.ppermute(array, axis, [(i, i ^ stride) for i in range(count)])


def edge_kernel(starts, four_ref, six_ref, cotan_four_ref, cotan_six_ref, *rest):
    outs, six_rows, sems = rest[:-2], rest[-2], rest[-1]
    rows_four, cols_four = four_ref.shape[:2]
    rows_six = six_ref.shape[0]
    pitch = pitch_of(six_ref.shape[1])
    copies = []
    for number, (start, out_ref) in enumerate(zip(starts, outs)):
        last = (1 - jnp.minimum(lax.axis_index("sp"), 1)) if start is None else start
        for part, (ref, row) in enumerate(
            (
                (four_ref, last * (rows_four - 2)),
                (four_ref, last * (rows_four - 2) + 1),
                (cotan_four_ref, last * (rows_four - 1)),
                (six_ref, last * (rows_six - 2)),
                (six_ref, last * (rows_six - 2) + 1),
                (cotan_six_ref, last * (rows_six - 1)),
            )
        ):
            if part < 3:
                target = out_ref.at[part * cols_four : (part + 1) * cols_four]
            else:
                target = six_rows.at[number, part - 3]
            copies.append(pltpu.make_async_copy(ref.at[row], target, sems.at[number, part]))
    for copy in copies:
        copy.start()
    for copy in copies:
        copy.wait()
    for number, out_ref in enumerate(outs):
        for part in range(3):
            begin = 3 * cols_four + part * pitch
            out_ref[begin : begin + pitch] = widen(six_rows[number, part], pitch).astype(BF16)


def edges(four, six, cotan_four, cotan_six):
    count = lax.axis_size("sp")
    starts = (None,) if count == 2 else (0, 1)
    length = 3 * four.shape[1] + 3 * pitch_of(six.shape[1])
    vmem = pl.BlockSpec(memory_space=pltpu.VMEM)
    hbm = pl.BlockSpec(memory_space=pltpu.HBM)
    outs = pl.pallas_call(
        functools.partial(edge_kernel, starts),
        out_shape=tuple(jax.ShapeDtypeStruct((length, four.shape[2]), BF16) for _ in starts),
        in_specs=[hbm] * 4,
        out_specs=tuple(vmem for _ in starts),
        scratch_shapes=[
            pltpu.VMEM((len(starts), 3) + six.shape[1:], BF16),
            pltpu.SemaphoreType.DMA((len(starts), 6)),
        ],
        compiler_params=pltpu.CompilerParams(vmem_limit_bytes=EDGE_LIMIT),
        name="edges",
    )(four, six, cotan_four, cotan_six)
    if count == 2:
        met = swap(outs[0], "sp", 1)
        return met, met
    above = lax.ppermute(outs[1], "sp", [(i, (i + 1) % count) for i in range(count)])
    below = lax.ppermute(outs[0], "sp", [((i + 1) % count, i) for i in range(count)])
    return above, below


def swap_across(array, axis, stride):
    count, sp_count = lax.axis_size("rep"), lax.axis_size("sp")
    rep_stride, sp_stride = (stride, 1) if axis == "rep" else (0, stride ^ 1)
    pairs = [
        (rep * sp_count + sp, (rep ^ rep_stride) * sp_count + (sp ^ sp_stride))
        for rep in range(count)
        for sp in range(sp_count)
    ]
    return lax.ppermute(array, ("rep", "sp"), pairs)


def group_sum(sums):
    sums = sums + swap(sums, "sp", 1)
    stride = 2
    while stride < lax.axis_size("sp"):
        sums = sums + swap_across(sums, "sp", stride)
        stride = 2 * stride
    stride = 1
    while stride < GROUP:
        met = [swap_across(sums, "rep", k * stride) for k in FAR_FIRST]
        sums = (sums + met[2]) + (met[1] + met[0])
        stride = RADIX * stride
    return sums


def every_group(sums):
    stride = GROUP
    while stride < lax.axis_size("rep"):
        sums = sums + swap(sums, "rep", stride)
        stride = 2 * stride
    return sums


def places():
    found = []
    for shift in (0, 2):
        digit = (lax.axis_index("rep") >> shift) & (RADIX - 1)
        found.append(([digit ^ k for k in range(RADIX)], (digit & 1) == 1, digit >= 2))
    return found


def digit_order(parts, place):
    unused, odd, high = place
    even = [jnp.where(odd, parts[k ^ 1], parts[k]) for k in range(RADIX)]
    return jnp.stack([jnp.where(high, even[k ^ 2], even[k]) for k in range(RADIX)])


def piece_of(pieces, index):
    sizes = (1,) + pieces.shape[1:]
    return lax.dynamic_slice(pieces, (index, 0, 0), sizes, allow_negative_indices=False)[0]


def scatter_start(own, sent, place):
    met = [swap(sent[step], "sp", step + 1) for step in range(sent.shape[0])]
    chan = own.shape[2]
    parts = [part.reshape(RADIX, -1, chan) for part in [own] + met]

    def piece(k):
        total = piece_of(parts[0], place[0][k])
        for part in parts[1:]:
            total = total + piece_of(part, place[0][k]).astype(F32)
        return total

    return piece(0), [piece(k).astype(BF16) for k in FAR_FIRST]


def added(own, met):
    return (own + met[2].astype(F32)) + (met[1].astype(F32) + met[0].astype(F32))


def fours(pieces, stride):
    return [swap(piece, "rep", k * stride) for k, piece in zip(FAR_FIRST, pieces)]


def scatter_next(total, place):
    pieces = total.reshape(RADIX, -1, total.shape[1])
    return piece_of(pieces, place[0][0]), [piece_of(pieces, place[0][k]).astype(BF16) for k in FAR_FIRST]


def weight_gather(total, found):
    chan = total.shape[1]
    total = total.astype(BF16)
    stride = GROUP
    while stride < lax.axis_size("rep"):
        total = added(total.astype(F32), fours([total] * 3, stride)).astype(BF16)
        stride = RADIX * stride
    met = [total] + fours([total] * 3, RADIX)[::-1]
    total = digit_order(met, found[1]).reshape(-1, chan)
    met = [total] + fours([total] * 3, 1)[::-1]
    whole = jnp.zeros((RADIX,) + total.shape, F32)
    for k in (0,) + FAR_FIRST:
        start = (found[0][0][k], 0, 0)
        whole = lax.dynamic_update_slice(whole, met[k][None].astype(F32), start, allow_negative_indices=False)
    return whole


def local(level_four, level_six, conv_weight, bn_gain, bn_shift, cotan_four, cotan_six):
    sp_count = lax.axis_size("sp")
    images = level_four.shape[0]
    four, six, cot_four, cot_six = (a[0] for a in (level_four, level_six, cotan_four, cotan_six))
    rows_four, cols_four, chan = four.shape
    rows_six, cols_six = six.shape[:2]
    pitch_four, pitch_six = pitch_of(cols_four), pitch_of(cols_six)
    counts = (
        float(images * GROUP * rows_four * sp_count * cols_four),
        float(images * GROUP * rows_six * sp_count * cols_six),
    )
    found, four = lax.optimization_barrier((places(), four))
    above, below = edges(four, six, cot_four, cot_six)
    vmem = pl.BlockSpec(memory_space=pltpu.VMEM)
    hbm = pl.BlockSpec(memory_space=pltpu.HBM)
    params = pltpu.CompilerParams(vmem_limit_bytes=VMEM_LIMIT)
    framed_four = jax.ShapeDtypeStruct((rows_four + 2, pitch_four, chan), BF16)
    framed_six = jax.ShapeDtypeStruct((rows_six + 2, pitch_six, chan), BF16)
    four_sums = jax.ShapeDtypeStruct((4, chan), F32)
    flops = 2 * 9 * chan * chan * (rows_four * cols_four + rows_six * cols_six)

    def cost(share, size):
        return pl.CostEstimate(flops=int(flops * share), bytes_accessed=size, transcendentals=0)

    conv_four, conv_six, moments = pl.pallas_call(
        functools.partial(forward_kernel, sp_count),
        out_shape=(framed_four, framed_six, four_sums),
        in_specs=[vmem] * 5,
        out_specs=(vmem, vmem, vmem),
        scratch_shapes=[
            pltpu.VMEM((rows_four + 4, pitch_four, 3 * chan), BF16),
            pltpu.VMEM((rows_six + 4, pitch_six, 3 * chan), BF16),
        ],
        compiler_params=params,
        cost_estimate=cost(1, 4 * four.size),
        name="forward",
    )(four, six, above, below, conv_weight)
    moments = group_sum(moments)

    slope_four, slope_six, slopes = pl.pallas_call(
        functools.partial(slope_kernel, counts),
        out_shape=(
            jax.ShapeDtypeStruct(framed_four.shape, F32),
            jax.ShapeDtypeStruct(framed_six.shape, F32),
            four_sums,
        ),
        in_specs=[vmem] * 9,
        out_specs=(vmem,) * 3,
        compiler_params=params,
        cost_estimate=cost(0.01, 4 * four.size),
        name="slopes",
    )(conv_four, conv_six, cot_four, cot_six, above, below, moments, bn_gain, bn_shift)
    slopes = group_sum(slopes)

    share = chan // sp_count
    wide_four, wide_six = (
        jax.ShapeDtypeStruct(framed.shape[:2] + (3 * chan,), BF16) for framed in (framed_four, framed_six)
    )
    three_four, three_six, own, sent = pl.pallas_call(
        functools.partial(backward_kernel, counts, sp_count),
        out_shape=(
            wide_four,
            wide_six,
            jax.ShapeDtypeStruct((9, share, chan), F32),
            jax.ShapeDtypeStruct((sp_count - 1, 9, share, chan), BF16),
        ),
        in_specs=[vmem] * 10,
        out_specs=(vmem,) * 4,
        scratch_shapes=[pltpu.VMEM((chan, 9 * chan), F32)],
        compiler_params=params,
        cost_estimate=cost(1.2, 8 * four.size),
        name="backward",
    )(four, six, conv_four, conv_six, slope_four, slope_six, moments, slopes, bn_gain, bn_shift)

    piece, pieces = scatter_start(own, sent, found[0])
    pieces, three_four = lax.optimization_barrier((pieces, three_four))
    met = fours(pieces, 1)
    chunks = chunks_of(rows_four, 8)
    split = -(-2 * len(chunks) // 3)
    done = chunks[split - 1][1]
    grad_first, turned = pl.pallas_call(
        functools.partial(input_first_kernel, chunks[:split]),
        out_shape=(
            jax.ShapeDtypeStruct((done, cols_four, chan), BF16),
            jax.ShapeDtypeStruct((9 * chan, chan), BF16),
        ),
        in_specs=[vmem] * 2,
        out_specs=(vmem, vmem),
        compiler_params=params,
        cost_estimate=cost(0.6, 3 * four.size),
        name="inputs_first",
    )(three_four, conv_weight)
    met, grad_first = lax.optimization_barrier((met, grad_first))

    piece, pieces = scatter_next(added(piece, met), found[1])
    pieces, three_six = lax.optimization_barrier((pieces, three_six))
    met = fours(pieces, RADIX)
    grad_four, grad_six = pl.pallas_call(
        functools.partial(input_second_kernel, chunks[split:], done),
        out_shape=(
            jax.ShapeDtypeStruct(four.shape, BF16),
            jax.ShapeDtypeStruct(six.shape, BF16),
        ),
        in_specs=[vmem] * 4,
        out_specs=(hbm, hbm),
        scratch_shapes=[
            pltpu.VMEM((max(rows_four - done, 1), cols_four, chan), BF16),
            pltpu.VMEM(six.shape, BF16),
            pltpu.SemaphoreType.DMA,
            pltpu.SemaphoreType.DMA((len(chunks),)),
            pltpu.SemaphoreType.DMA((len(chunks_of(rows_six, 12)),)),
        ],
        compiler_params=params,
        cost_estimate=cost(0.4, 2 * four.size),
        name="inputs_second",
    )(three_four, three_six, turned, grad_first)
    met, grad_six = lax.optimization_barrier((met, grad_six))
    grad_weight = weight_gather(added(piece, met), found).reshape(own.shape)
    totals = every_group(slopes)
    grad_gain = jnp.stack([totals[1], totals[3]])
    grad_shift = jnp.stack([totals[0], totals[2]])
    return (grad_four[None], grad_six[None], grad_weight, grad_gain, grad_shift)


def solution(mesh):
    placed = (
        P("rep", "sp", None, None),
        P("rep", "sp", None, None),
        P(),
        P(),
        P(),
        P("rep", "sp", None, None),
        P("rep", "sp", None, None),
    )
    return jax.shard_map(
        local,
        mesh=mesh,
        in_specs=placed,
        out_specs=(
            P("rep", "sp", None, None),
            P("rep", "sp", None, None),
            P(None, "sp", None),
            P(),
            P(),
        ),
        check_vma=False,
    )
```

```python
import functools

import jax
import jax.numpy as jnp
from jax import lax
from jax.experimental import pallas as pl
from jax.experimental.pallas import tpu as pltpu
from jax.sharding import PartitionSpec as P

GROUP = 16
RADIX = 4
FAR_FIRST = (3, 2, 1)
EPSILON = 1e-05
F32 = jnp.float32
BF16 = jnp.bfloat16
VMEM_LIMIT = 20 * 1024 * 1024
EDGE_LIMIT = 60 * 1024 * 1024


def chunk_of(rows, most, multiple=1):
    sizes = [size for size in range(1, most + 1) if rows % size == 0 and size % multiple == 0]
    return max(sizes) if sizes else rows


def pitch_of(cols):
    return -(-cols // 16) * 16


def chunks_of(rows, most, multiple=1):
    size = chunk_of(rows, most, multiple)
    return [(start, start + size) for start in range(0, rows, size)]


def widen(cells, pitch):
    cells = cells.astype(F32)
    extra = pitch - cells.shape[0]
    if extra:
        cells = jnp.concatenate([cells, jnp.zeros((extra, cells.shape[1]), F32)], 0)
    return cells


def put_three(three, row, cells, cols, turned):
    pitch, chan = cells.shape
    left, right = pltpu.roll(cells, 1, 0), pltpu.roll(cells, pitch - 1, 0)
    if pitch == cols:
        col = lax.broadcasted_iota(jnp.int32, (8, chan), 0)
        left = jnp.concatenate([jnp.where(col == 0, 0.0, left[:8]), left[8:]], 0)
        right = jnp.concatenate([right[:-8], jnp.where(col == 7, 0.0, right[-8:])], 0)
    parts = (right, cells, left) if turned else (left, cells, right)
    for place, part in enumerate(parts):
        three[row, :, place * chan : (place + 1) * chan] = part.astype(BF16)


def beside(three, starts, size):
    pitch, width = three.shape[1:]
    return jnp.concatenate([three[start : start + size].reshape(size * pitch, width) for start in starts], 1)


def edges_valid(sp_count):
    index = lax.axis_index("sp")
    return jnp.where(index > 0, 1.0, 0.0), jnp.where(index < sp_count - 1, 1.0, 0.0)


def level_coefs(moments, gain, shift, count):
    mean = moments[0:1] / count
    spread = moments[1:2] / count - mean * mean
    return mean, lax.rsqrt(spread + EPSILON), gain, shift


def slope_of(conv, cotan, coefs):
    mean, rstd, gain, shift = coefs
    centred = conv.astype(F32) - mean
    half = centred * (0.5 * rstd * gain) + 0.5 * shift
    turn = jnp.tanh(half)
    return centred, cotan.astype(F32) * ((1.0 + turn) * (1.0 + half * (1.0 - turn)))


def masked(cells, cols):
    if cells.shape[0] == cols:
        return cells
    col = lax.broadcasted_iota(jnp.int32, cells.shape, 0)
    return jnp.where(col < cols, cells, 0.0)


def staged(fills, dots):
    fills[0]()
    for index, dot in enumerate(dots):
        if index + 1 < len(fills):
            fills[index + 1]()
        dot()


def conv_rows(three, starts, size, w_ref):
    pitch, width = three.shape[1:]
    lhs = [beside(three, (start, start + 1, start + 2), size) for start in starts]
    lhs = jnp.concatenate(lhs, 0) if len(lhs) > 1 else lhs[0]
    conv = jnp.dot(lhs, w_ref[...].reshape(3 * width, -1), preferred_element_type=F32).astype(BF16)
    return conv.reshape(len(starts) * size, pitch, -1)


def add_moments(sums, conv, cols):
    chan = conv.shape[2]
    conv = conv.astype(F32)
    if conv.shape[1] != cols:
        conv = conv[:, :cols]
    conv = conv.reshape(-1, 8, chan)
    sums[0].append(jnp.sum(conv, 0))
    sums[1].append(jnp.sum(conv * conv, 0))


def folded(parts):
    total = parts[0]
    for part in parts[1:]:
        total = total + part
    return jnp.sum(total, 0, keepdims=True)


def inner_level(x_ref, w_ref, conv_ref, three, sums, most):
    rows, cols = x_ref.shape[:2]
    pitch = three.shape[1]

    def fill_row(row):
        put_three(three, row, widen(x_ref[row], pitch), cols, False)

    def dot(start, end):
        conv = conv_rows(three, (start,), end - start, w_ref)
        conv_ref[start:end] = conv
        add_moments(sums, conv, cols)

    inner = rows - 2
    count = max(1, inner // most)
    bounds = [index * inner // count for index in range(count + 1)]
    fills, dots, done = [], [], 0
    for start, end in zip(bounds[:-1], bounds[1:]):
        fills.append(lambda todo=range(done, end + 2): [fill_row(row) for row in todo])
        done = end + 2
        dots.append(functools.partial(dot, start, end))
    return fills, dots


def inner_kernel(four_ref, six_ref, w_ref, conv_four_ref, conv_six_ref, moments_ref, three_four, three_six):
    sums_four, sums_six = ([], []), ([], [])
    fills_six, dots_six = inner_level(six_ref, w_ref, conv_six_ref, three_six, sums_six, 10)
    fills_four, dots_four = inner_level(four_ref, w_ref, conv_four_ref, three_four, sums_four, 8)
    staged(fills_six + fills_four, dots_six + dots_four)
    moments_ref[...] = jnp.concatenate([folded(parts) for parts in sums_four + sums_six], 0)


def outer_level(x_ref, top, bottom, valid, w_ref, conv_ref, three, sums):
    rows, cols = x_ref.shape[:2]
    pitch = three.shape[1]
    for edge in range(2):
        put_three(three, edge, top(edge) * valid[0], cols, False)
        put_three(three, 2 + edge, widen(x_ref[edge], pitch), cols, False)
        put_three(three, 4 + edge, widen(x_ref[rows - 2 + edge], pitch), cols, False)
        put_three(three, 6 + edge, bottom(edge) * valid[1], cols, False)
    conv = conv_rows(three, (0, 4), 2, w_ref)
    conv_ref[...] = conv
    add_moments(sums, conv[1:3], cols)


def outer_kernel(
    sp_count, four_ref, six_ref, above_ref, below_ref, w_ref, inner_ref,
    conv_four_ref, conv_six_ref, moments_ref, three_four, three_six,
):
    cols_four = four_ref.shape[1]
    valid = edges_valid(sp_count)
    base, pitch_six = 3 * cols_four, three_six.shape[1]

    def reader(ref, start, pitch):
        return lambda edge: ref[start + edge * pitch : start + (edge + 1) * pitch].astype(F32)

    sums_four, sums_six = ([], []), ([], [])
    outer_level(
        six_ref, reader(above_ref, base, pitch_six), reader(below_ref, base, pitch_six), valid, w_ref,
        conv_six_ref, three_six, sums_six,
    )
    outer_level(
        four_ref, reader(above_ref, 0, cols_four), reader(below_ref, 0, cols_four), valid, w_ref,
        conv_four_ref, three_four, sums_four,
    )
    sums = [folded(parts) for parts in sums_four + sums_six]
    moments_ref[...] = inner_ref[...] + jnp.concatenate(sums, 0)


def turn_kernel(four_ref, six_ref, turned_ref):
    rows_four, cols_four, chan = four_ref.shape
    rows_six, cols_six = six_ref.shape[:2]
    pitch = pitch_of(cols_six)
    for start, end in chunks_of(rows_four, 8, 4):
        cells = four_ref[start:end].reshape((end - start) * cols_four, chan)
        turned_ref[:, start * cols_four : end * cols_four] = cells.T
    cells = six_ref[...].astype(F32)
    cells = jnp.concatenate([cells, jnp.zeros((rows_six, pitch - cols_six, chan), F32)], 1).astype(BF16)
    turned_ref[:, rows_four * cols_four :] = cells.reshape(rows_six * pitch, chan).T


def slope_level(inner_ref, outer_ref, cotan_ref, above, below, coefs, slope_ref):
    rows, cols, chan = cotan_ref.shape
    pitch = inner_ref.shape[1]

    def put(row, conv, cotan):
        centred, slope = slope_of(conv, widen(cotan, pitch), coefs)
        slope_ref[row] = slope
        return centred, slope

    def add(sums, pair):
        centred, slope = pair
        first = jnp.sum(slope.reshape(-1, 8, chan), 0)
        second = jnp.sum((slope * centred).reshape(-1, 8, chan), 0)
        return sums[0] + first, sums[1] + second

    def step(row, sums):
        return add(sums, put(row + 2, inner_ref[row], cotan_ref[row + 1]))

    put(0, outer_ref[0], above)
    put(rows + 1, outer_ref[3], below)
    zero = jnp.zeros((8, chan), F32)
    sums = add((zero, zero), put(1, outer_ref[1], cotan_ref[0]))
    sums = add(sums, put(rows, outer_ref[2], cotan_ref[rows - 1]))
    looped = (rows - 2) // 8 * 8
    if looped:
        sums = lax.fori_loop(0, looped, step, sums, unroll=8)
    for row in range(looped, rows - 2):
        sums = step(row, sums)
    first = 0.5 * jnp.sum(sums[0], 0, keepdims=True)
    return first, 0.5 * coefs[1] * jnp.sum(sums[1], 0, keepdims=True)


def slope_kernel(
    counts, inner_four_ref, inner_six_ref, outer_four_ref, outer_six_ref, cotan_four_ref, cotan_six_ref,
    above_ref, below_ref, moments_ref, gain_ref, shift_ref, slope_four_ref, slope_six_ref, slopes_ref,
):
    sums = ()
    cols_four = cotan_four_ref.shape[1]
    starts = (2 * cols_four, 3 * cols_four + 2 * inner_six_ref.shape[1])
    for level, (inner_ref, outer_ref, cotan_ref, slope_ref) in enumerate(
        (
            (inner_four_ref, outer_four_ref, cotan_four_ref, slope_four_ref),
            (inner_six_ref, outer_six_ref, cotan_six_ref, slope_six_ref),
        )
    ):
        pair = moments_ref[2 * level : 2 * level + 2]
        here = slice(level, level + 1)
        edge = slice(starts[level], starts[level] + inner_ref.shape[1])
        coefs = level_coefs(pair, gain_ref[here], shift_ref[here], counts[level])
        sums += slope_level(inner_ref, outer_ref, cotan_ref, above_ref[edge], below_ref[edge], coefs, slope_ref)
    slopes_ref[...] = jnp.concatenate(sums, 0)


def backward_level(
    turned_ref, first_cell, cols, inner_ref, outer_ref, slope_ref, valid, coefs, slopes, count, three, put, most
):
    rows = inner_ref.shape[0] + 2
    pitch = three.shape[1]
    mean, rstd, gain, shift = coefs
    lead = gain * rstd
    offset, factor = lead * (slopes[0:1] / count), lead * rstd * (slopes[1:2] / count)

    def fill_row(row):
        if 2 <= row < rows:
            conv = inner_ref[row - 2]
        else:
            conv = outer_ref[row if row < 2 else row - rows + 2]
        centred = conv.astype(F32) - mean
        dconv = masked((0.5 * lead) * slope_ref[row] - (offset + centred * factor), cols)
        if row == 0:
            dconv = dconv * valid[0]
        elif row == rows + 1:
            dconv = dconv * valid[1]
        put_three(three, row, dconv, cols, True)

    def dot(start, end):
        size = end - start
        lhs = turned_ref[:, first_cell + start * pitch : first_cell + end * pitch]
        rhs = beside(three, (start + 2, start + 1, start), size)
        put(jnp.dot(lhs, rhs, preferred_element_type=F32))

    fills, dots, done = [], [], 0
    for start, end in chunks_of(rows, most, 4):
        fills.append(lambda todo=range(done, end + 2): [fill_row(row) for row in todo])
        done = end + 2
        dots.append(functools.partial(dot, start, end))
    return fills, dots


def backward_kernel(
    counts, sp_count, cols, turned_ref, inner_four_ref, inner_six_ref, outer_four_ref, outer_six_ref,
    slope_four_ref, slope_six_ref, moments_ref, slopes_ref, gain_ref, shift_ref, three_four, three_six, own_ref, sent_ref, total,
):
    valid = edges_valid(sp_count)
    begun = []

    def put(term):
        total[...] = total[...] + term if begun else term
        begun.append(True)

    fills, dots = [], []
    cells_four = (three_four.shape[0] - 2) * three_four.shape[1]
    for level, first_cell, inner_ref, outer_ref, slope_ref, three, most in (
        (1, cells_four, inner_six_ref, outer_six_ref, slope_six_ref, three_six, 12),
        (0, 0, inner_four_ref, outer_four_ref, slope_four_ref, three_four, 8),
    ):
        here = slice(level, level + 1)
        pair = slice(2 * level, 2 * level + 2)
        coefs = level_coefs(moments_ref[pair], gain_ref[here], shift_ref[here], counts[level])
        level_fills, level_dots = backward_level(
            turned_ref, first_cell, cols[level], inner_ref, outer_ref, slope_ref, valid, coefs, slopes_ref[pair],
            counts[level], three, put, most,
        )
        fills += level_fills
        dots += level_dots
    staged(fills, dots)
    share, chan = own_ref.shape[1:]
    for step in range(sp_count):
        begin = pl.multiple_of((lax.axis_index("sp") ^ step) * share, share)
        for tap in range(9):
            part = total[pl.ds(begin, share), tap * chan : (tap + 1) * chan]
            if step == 0:
                own_ref[tap] = part
            else:
                sent_ref[step - 1, tap] = part.astype(BF16)


def input_chunks(three, turned, grad, chunks, offset, sent=None):
    cols, chan = grad.shape[1:]
    pitch = three.shape[1]
    for index, (start, end) in enumerate(chunks):
        size = end - start
        lhs = beside(three, (start + 2, start + 1, start), size)
        term = jnp.dot(lhs, turned[...], preferred_element_type=F32)
        grad[start - offset : end - offset] = term.reshape(size, pitch, chan)[:, :cols].astype(BF16)
        if sent is not None:
            sent(index, start, end)


def input_first_kernel(chunks, three_four, w_ref, grad_ref, turned):
    chan = w_ref.shape[1]
    for tap in range(9):
        turned[tap * chan : (tap + 1) * chan] = w_ref[tap].T
    input_chunks(three_four, turned, grad_ref, chunks, 0)


def input_second_kernel(
    chunks, done, three_four, three_six, turned, first_ref, grad_four_ref, grad_six_ref,
    grad_four, grad_six, sem_first, sems_four, sems_six,
):
    copies = [pltpu.make_async_copy(first_ref, grad_four_ref.at[:done], sem_first)]
    copies[0].start()

    def sender(grad, grad_ref, offset, sems):
        def sent(index, start, end):
            copy = pltpu.make_async_copy(grad.at[start - offset : end - offset], grad_ref.at[start:end], sems.at[index])
            copy.start()
            copies.append(copy)

        return sent

    six_chunks = chunks_of(grad_six.shape[0], 12)
    input_chunks(three_six, turned, grad_six, six_chunks, 0, sender(grad_six, grad_six_ref, 0, sems_six))
    input_chunks(three_four, turned, grad_four, chunks, done, sender(grad_four, grad_four_ref, done, sems_four))
    for copy in copies:
        copy.wait()


def swap(array, axis, stride):
    count = lax.axis_size(axis)
    return lax.ppermute(array, axis, [(i, i ^ stride) for i in range(count)])


def edge_kernel(starts, four_ref, six_ref, cotan_four_ref, cotan_six_ref, *rest):
    outs, six_rows, sems = rest[:-2], rest[-2], rest[-1]
    rows_four, cols_four = four_ref.shape[:2]
    rows_six = six_ref.shape[0]
    pitch = pitch_of(six_ref.shape[1])
    copies = []
    for number, (start, out_ref) in enumerate(zip(starts, outs)):
        last = (1 - jnp.minimum(lax.axis_index("sp"), 1)) if start is None else start
        for part, (ref, row) in enumerate(
            (
                (four_ref, last * (rows_four - 2)),
                (four_ref, last * (rows_four - 2) + 1),
                (cotan_four_ref, last * (rows_four - 1)),
                (six_ref, last * (rows_six - 2)),
                (six_ref, last * (rows_six - 2) + 1),
                (cotan_six_ref, last * (rows_six - 1)),
            )
        ):
            if part < 3:
                target = out_ref.at[part * cols_four : (part + 1) * cols_four]
            else:
                target = six_rows.at[number, part - 3]
            copies.append(pltpu.make_async_copy(ref.at[row], target, sems.at[number, part]))
    for copy in copies:
        copy.start()
    for copy in copies:
        copy.wait()
    for number, out_ref in enumerate(outs):
        for part in range(3):
            begin = 3 * cols_four + part * pitch
            out_ref[begin : begin + pitch] = widen(six_rows[number, part], pitch).astype(BF16)


def edges(four, six, cotan_four, cotan_six):
    count = lax.axis_size("sp")
    starts = (None,) if count == 2 else (0, 1)
    length = 3 * four.shape[1] + 3 * pitch_of(six.shape[1])
    vmem = pl.BlockSpec(memory_space=pltpu.VMEM)
    hbm = pl.BlockSpec(memory_space=pltpu.HBM)
    outs = pl.pallas_call(
        functools.partial(edge_kernel, starts),
        out_shape=tuple(jax.ShapeDtypeStruct((length, four.shape[2]), BF16) for _ in starts),
        in_specs=[hbm] * 4,
        out_specs=tuple(vmem for _ in starts),
        scratch_shapes=[
            pltpu.VMEM((len(starts), 3) + six.shape[1:], BF16),
            pltpu.SemaphoreType.DMA((len(starts), 6)),
        ],
        compiler_params=pltpu.CompilerParams(vmem_limit_bytes=EDGE_LIMIT),
        name="edges",
    )(four, six, cotan_four, cotan_six)
    if count == 2:
        met = swap(outs[0], "sp", 1)
        return met, met
    above = lax.ppermute(outs[1], "sp", [(i, (i + 1) % count) for i in range(count)])
    below = lax.ppermute(outs[0], "sp", [((i + 1) % count, i) for i in range(count)])
    return above, below


def swap_across(array, axis, stride):
    count, sp_count = lax.axis_size("rep"), lax.axis_size("sp")
    rep_stride, sp_stride = (stride, 1) if axis == "rep" else (0, stride ^ 1)
    pairs = [
        (rep * sp_count + sp, (rep ^ rep_stride) * sp_count + (sp ^ sp_stride))
        for rep in range(count)
        for sp in range(sp_count)
    ]
    return lax.ppermute(array, ("rep", "sp"), pairs)


def group_sum(sums):
    sums = sums + swap(sums, "sp", 1)
    stride = 2
    while stride < lax.axis_size("sp"):
        sums = sums + swap_across(sums, "sp", stride)
        stride = 2 * stride
    stride = 1
    while stride < GROUP:
        met = [swap_across(sums, "rep", k * stride) for k in FAR_FIRST]
        sums = (sums + met[2]) + (met[1] + met[0])
        stride = RADIX * stride
    return sums


def every_group(sums):
    stride = GROUP
    while stride < lax.axis_size("rep"):
        sums = sums + swap(sums, "rep", stride)
        stride = 2 * stride
    return sums


def places():
    found = []
    for shift in (0, 2):
        digit = (lax.axis_index("rep") >> shift) & (RADIX - 1)
        found.append(([digit ^ k for k in range(RADIX)], (digit & 1) == 1, digit >= 2))
    return found


def digit_order(parts, place):
    unused, odd, high = place
    even = [jnp.where(odd, parts[k ^ 1], parts[k]) for k in range(RADIX)]
    return jnp.stack([jnp.where(high, even[k ^ 2], even[k]) for k in range(RADIX)])


def piece_of(pieces, index):
    sizes = (1,) + pieces.shape[1:]
    return lax.dynamic_slice(pieces, (index, 0, 0), sizes, allow_negative_indices=False)[0]


def scatter_start(own, sent, place):
    met = [swap(sent[step], "sp", step + 1) for step in range(sent.shape[0])]
    chan = own.shape[2]
    parts = [part.reshape(RADIX, -1, chan) for part in [own] + met]

    def piece(k):
        total = piece_of(parts[0], place[0][k])
        for part in parts[1:]:
            total = total + piece_of(part, place[0][k]).astype(F32)
        return total

    return piece(0), [piece(k).astype(BF16) for k in FAR_FIRST]


def added(own, met):
    return (own + met[2].astype(F32)) + (met[1].astype(F32) + met[0].astype(F32))


def fours(pieces, stride):
    return [swap(piece, "rep", k * stride) for k, piece in zip(FAR_FIRST, pieces)]


def scatter_next(total, place):
    pieces = total.reshape(RADIX, -1, total.shape[1])
    return piece_of(pieces, place[0][0]), [piece_of(pieces, place[0][k]).astype(BF16) for k in FAR_FIRST]


def weight_gather(total, found):
    chan = total.shape[1]
    total = total.astype(BF16)
    stride = GROUP
    while stride < lax.axis_size("rep"):
        total = added(total.astype(F32), fours([total] * 3, stride)).astype(BF16)
        stride = RADIX * stride
    met = [total] + fours([total] * 3, RADIX)[::-1]
    total = digit_order(met, found[1]).reshape(-1, chan)
    met = [total] + fours([total] * 3, 1)[::-1]
    whole = jnp.zeros((RADIX,) + total.shape, F32)
    for k in (0,) + FAR_FIRST:
        start = (found[0][0][k], 0, 0)
        whole = lax.dynamic_update_slice(whole, met[k][None].astype(F32), start, allow_negative_indices=False)
    return whole


def local(level_four, level_six, conv_weight, bn_gain, bn_shift, cotan_four, cotan_six):
    sp_count = lax.axis_size("sp")
    images = level_four.shape[0]
    four, six, cot_four, cot_six = (a[0] for a in (level_four, level_six, cotan_four, cotan_six))
    rows_four, cols_four, chan = four.shape
    rows_six, cols_six = six.shape[:2]
    pitch_four, pitch_six = pitch_of(cols_four), pitch_of(cols_six)
    counts = (
        float(images * GROUP * rows_four * sp_count * cols_four),
        float(images * GROUP * rows_six * sp_count * cols_six),
    )
    found, four = lax.optimization_barrier((places(), four))
    above, below = edges(four, six, cot_four, cot_six)
    vmem = pl.BlockSpec(memory_space=pltpu.VMEM)
    hbm = pl.BlockSpec(memory_space=pltpu.HBM)
    params = pltpu.CompilerParams(vmem_limit_bytes=VMEM_LIMIT)
    framed_four = jax.ShapeDtypeStruct((rows_four + 2, pitch_four, chan), BF16)
    framed_six = jax.ShapeDtypeStruct((rows_six + 2, pitch_six, chan), BF16)
    four_sums = jax.ShapeDtypeStruct((4, chan), F32)
    flops = 2 * 9 * chan * chan * (rows_four * cols_four + rows_six * cols_six)

    def cost(share, size):
        return pl.CostEstimate(flops=int(flops * share), bytes_accessed=size, transcendentals=0)

    inner_four, inner_six, inner_moments = pl.pallas_call(
        inner_kernel,
        out_shape=(
            jax.ShapeDtypeStruct((rows_four - 2, pitch_four, chan), BF16),
            jax.ShapeDtypeStruct((rows_six - 2, pitch_six, chan), BF16),
            four_sums,
        ),
        in_specs=[vmem] * 3,
        out_specs=(vmem, vmem, vmem),
        scratch_shapes=[
            pltpu.VMEM((rows_four, pitch_four, 3 * chan), BF16),
            pltpu.VMEM((rows_six, pitch_six, 3 * chan), BF16),
        ],
        compiler_params=params,
        cost_estimate=cost(1, 4 * four.size),
        name="forward_inner",
    )(four, six, conv_weight)
    outer_four, outer_six, moments = pl.pallas_call(
        functools.partial(outer_kernel, sp_count),
        out_shape=(
            jax.ShapeDtypeStruct((4, pitch_four, chan), BF16),
            jax.ShapeDtypeStruct((4, pitch_six, chan), BF16),
            four_sums,
        ),
        in_specs=[vmem] * 6,
        out_specs=(vmem, vmem, vmem),
        scratch_shapes=[
            pltpu.VMEM((8, pitch_four, 3 * chan), BF16),
            pltpu.VMEM((8, pitch_six, 3 * chan), BF16),
        ],
        compiler_params=params,
        cost_estimate=cost(0.1, four.size),
        name="forward_outer",
    )(four, six, above, below, conv_weight, inner_moments)
    moments, four, six = lax.optimization_barrier((moments, four, six))
    turned_features = pl.pallas_call(
        turn_kernel,
        out_shape=jax.ShapeDtypeStruct((chan, rows_four * cols_four + rows_six * pitch_six), BF16),
        in_specs=[vmem] * 2,
        out_specs=vmem,
        compiler_params=params,
        cost_estimate=cost(0.3, 4 * four.size),
        name="turn",
    )(four, six)
    moments, turned_features = lax.optimization_barrier((group_sum(moments), turned_features))

    slope_four, slope_six, slopes = pl.pallas_call(
        functools.partial(slope_kernel, counts),
        out_shape=(
            jax.ShapeDtypeStruct(framed_four.shape, F32),
            jax.ShapeDtypeStruct(framed_six.shape, F32),
            four_sums,
        ),
        in_specs=[vmem] * 11,
        out_specs=(vmem,) * 3,
        compiler_params=params,
        cost_estimate=cost(0.01, 4 * four.size),
        name="slopes",
    )(
        inner_four, inner_six, outer_four, outer_six, cot_four, cot_six, above, below, moments, bn_gain, bn_shift
    )
    slopes = group_sum(slopes)

    share = chan // sp_count
    wide_four, wide_six = (
        jax.ShapeDtypeStruct(framed.shape[:2] + (3 * chan,), BF16) for framed in (framed_four, framed_six)
    )
    three_four, three_six, own, sent = pl.pallas_call(
        functools.partial(backward_kernel, counts, sp_count, (cols_four, cols_six)),
        out_shape=(
            wide_four,
            wide_six,
            jax.ShapeDtypeStruct((9, share, chan), F32),
            jax.ShapeDtypeStruct((sp_count - 1, 9, share, chan), BF16),
        ),
        in_specs=[vmem] * 11,
        out_specs=(vmem,) * 4,
        scratch_shapes=[pltpu.VMEM((chan, 9 * chan), F32)],
        compiler_params=params,
        cost_estimate=cost(1.2, 8 * four.size),
        name="backward",
    )(
        turned_features, inner_four, inner_six, outer_four, outer_six, slope_four, slope_six, moments, slopes,
        bn_gain, bn_shift,
    )

    piece, pieces = scatter_start(own, sent, found[0])
    pieces, three_four = lax.optimization_barrier((pieces, three_four))
    met = fours(pieces, 1)
    chunks = chunks_of(rows_four, 8)
    split = -(-2 * len(chunks) // 3)
    done = chunks[split - 1][1]
    grad_first, turned = pl.pallas_call(
        functools.partial(input_first_kernel, chunks[:split]),
        out_shape=(
            jax.ShapeDtypeStruct((done, cols_four, chan), BF16),
            jax.ShapeDtypeStruct((9 * chan, chan), BF16),
        ),
        in_specs=[vmem] * 2,
        out_specs=(vmem, vmem),
        compiler_params=params,
        cost_estimate=cost(0.6, 3 * four.size),
        name="inputs_first",
    )(three_four, conv_weight)
    met, grad_first = lax.optimization_barrier((met, grad_first))

    piece, pieces = scatter_next(added(piece, met), found[1])
    pieces, three_six = lax.optimization_barrier((pieces, three_six))
    met = fours(pieces, RADIX)
    grad_four, grad_six = pl.pallas_call(
        functools.partial(input_second_kernel, chunks[split:], done),
        out_shape=(
            jax.ShapeDtypeStruct(four.shape, BF16),
            jax.ShapeDtypeStruct(six.shape, BF16),
        ),
        in_specs=[vmem] * 4,
        out_specs=(hbm, hbm),
        scratch_shapes=[
            pltpu.VMEM((max(rows_four - done, 1), cols_four, chan), BF16),
            pltpu.VMEM(six.shape, BF16),
            pltpu.SemaphoreType.DMA,
            pltpu.SemaphoreType.DMA((len(chunks),)),
            pltpu.SemaphoreType.DMA((len(chunks_of(rows_six, 12)),)),
        ],
        compiler_params=params,
        cost_estimate=cost(0.4, 2 * four.size),
        name="inputs_second",
    )(three_four, three_six, turned, grad_first)
    met, grad_six = lax.optimization_barrier((met, grad_six))
    grad_weight = weight_gather(added(piece, met), found).reshape(own.shape)
    totals = every_group(slopes)
    grad_gain = jnp.stack([totals[1], totals[3]])
    grad_shift = jnp.stack([totals[0], totals[2]])
    return (grad_four[None], grad_six[None], grad_weight, grad_gain, grad_shift)


def solution(mesh):
    placed = (
        P("rep", "sp", None, None),
        P("rep", "sp", None, None),
        P(),
        P(),
        P(),
        P("rep", "sp", None, None),
        P("rep", "sp", None, None),
    )
    return jax.shard_map(
        local,
        mesh=mesh,
        in_specs=placed,
        out_specs=(
            P("rep", "sp", None, None),
            P("rep", "sp", None, None),
            P(None, "sp", None),
            P(),
            P(),
        ),
        check_vma=False,
    )
```

```python
import functools

import jax
import jax.numpy as jnp
from jax import lax
from jax.experimental import pallas as pl
from jax.experimental.pallas import tpu as pltpu
from jax.sharding import PartitionSpec as P

GROUP = 16
RADIX = 4
FAR_FIRST = (3, 2, 1)
EPSILON = 1e-05
F32 = jnp.float32
BF16 = jnp.bfloat16
VMEM_LIMIT = 20 * 1024 * 1024
EDGE_LIMIT = 60 * 1024 * 1024


def chunk_of(rows, most, multiple=1):
    sizes = [size for size in range(1, most + 1) if rows % size == 0 and size % multiple == 0]
    return max(sizes) if sizes else rows


def pitch_of(cols):
    return -(-cols // 16) * 16


def chunks_of(rows, most, multiple=1):
    size = chunk_of(rows, most, multiple)
    return [(start, start + size) for start in range(0, rows, size)]


def widen(cells, pitch):
    cells = cells.astype(F32)
    extra = pitch - cells.shape[0]
    if extra:
        cells = jnp.concatenate([cells, jnp.zeros((extra, cells.shape[1]), F32)], 0)
    return cells


def put_three(three, row, cells, cols, turned):
    pitch, chan = cells.shape
    left, right = pltpu.roll(cells, 1, 0), pltpu.roll(cells, pitch - 1, 0)
    if pitch == cols:
        col = lax.broadcasted_iota(jnp.int32, (8, chan), 0)
        left = jnp.concatenate([jnp.where(col == 0, 0.0, left[:8]), left[8:]], 0)
        right = jnp.concatenate([right[:-8], jnp.where(col == 7, 0.0, right[-8:])], 0)
    parts = (right, cells, left) if turned else (left, cells, right)
    for place, part in enumerate(parts):
        three[row, :, place * chan : (place + 1) * chan] = part.astype(BF16)


def beside(three, starts, size):
    pitch, width = three.shape[1:]
    return jnp.concatenate([three[start : start + size].reshape(size * pitch, width) for start in starts], 1)


def edges_valid(sp_count):
    index = lax.axis_index("sp")
    return jnp.where(index > 0, 1.0, 0.0), jnp.where(index < sp_count - 1, 1.0, 0.0)


def level_coefs(moments, gain, shift, count):
    mean = moments[0:1] / count
    spread = moments[1:2] / count - mean * mean
    return mean, lax.rsqrt(spread + EPSILON), gain, shift


def slope_of(conv, cotan, coefs):
    mean, rstd, gain, shift = coefs
    centred = conv.astype(F32) - mean
    half = centred * (0.5 * rstd * gain) + 0.5 * shift
    turn = jnp.tanh(half)
    return centred, cotan.astype(F32) * ((1.0 + turn) * (1.0 + half * (1.0 - turn)))


def masked(cells, cols):
    if cells.shape[0] == cols:
        return cells
    col = lax.broadcasted_iota(jnp.int32, cells.shape, 0)
    return jnp.where(col < cols, cells, 0.0)


def staged(fills, dots):
    fills[0]()
    for index, dot in enumerate(dots):
        if index + 1 < len(fills):
            fills[index + 1]()
        dot()


def conv_rows(three, starts, size, w_ref):
    pitch, width = three.shape[1:]
    lhs = [beside(three, (start, start + 1, start + 2), size) for start in starts]
    lhs = jnp.concatenate(lhs, 0) if len(lhs) > 1 else lhs[0]
    conv = jnp.dot(lhs, w_ref[...].reshape(3 * width, -1), preferred_element_type=F32).astype(BF16)
    return conv.reshape(len(starts) * size, pitch, -1)


def add_moments(sums, conv, cols):
    chan = conv.shape[2]
    conv = conv.astype(F32)
    if conv.shape[1] != cols:
        conv = conv[:, :cols]
    conv = conv.reshape(-1, 8, chan)
    sums[0].append(jnp.sum(conv, 0))
    sums[1].append(jnp.sum(conv * conv, 0))


def folded(parts):
    total = parts[0]
    for part in parts[1:]:
        total = total + part
    return jnp.sum(total, 0, keepdims=True)


def inner_level(x_ref, w_ref, conv_ref, three, sums, most):
    rows, cols = x_ref.shape[:2]
    pitch = three.shape[1]

    def fill_row(row):
        put_three(three, row, widen(x_ref[row], pitch), cols, False)

    def dot(start, end):
        conv = conv_rows(three, (start,), end - start, w_ref)
        conv_ref[start:end] = conv
        add_moments(sums, conv, cols)

    inner = rows - 2
    count = max(1, inner // most)
    bounds = [index * inner // count for index in range(count + 1)]
    fills, dots, done = [], [], 0
    for start, end in zip(bounds[:-1], bounds[1:]):
        fills.append(lambda todo=range(done, end + 2): [fill_row(row) for row in todo])
        done = end + 2
        dots.append(functools.partial(dot, start, end))
    return fills, dots


def inner_kernel(four_ref, six_ref, w_ref, conv_four_ref, conv_six_ref, moments_ref, three_four, three_six):
    sums_four, sums_six = ([], []), ([], [])
    fills_six, dots_six = inner_level(six_ref, w_ref, conv_six_ref, three_six, sums_six, 10)
    fills_four, dots_four = inner_level(four_ref, w_ref, conv_four_ref, three_four, sums_four, 8)
    staged(fills_six + fills_four, dots_six + dots_four)
    moments_ref[...] = jnp.concatenate([folded(parts) for parts in sums_four + sums_six], 0)


def outer_level(x_ref, top, bottom, valid, w_ref, conv_ref, three, sums):
    rows, cols = x_ref.shape[:2]
    pitch = three.shape[1]
    for edge in range(2):
        put_three(three, edge, top(edge) * valid[0], cols, False)
        put_three(three, 2 + edge, widen(x_ref[edge], pitch), cols, False)
        put_three(three, 4 + edge, widen(x_ref[rows - 2 + edge], pitch), cols, False)
        put_three(three, 6 + edge, bottom(edge) * valid[1], cols, False)
    conv = conv_rows(three, (0, 4), 2, w_ref)
    conv_ref[...] = conv
    add_moments(sums, conv[1:3], cols)


def outer_kernel(
    sp_count, four_ref, six_ref, above_ref, below_ref, w_ref, inner_ref,
    conv_four_ref, conv_six_ref, moments_ref, three_four, three_six,
):
    cols_four = four_ref.shape[1]
    valid = edges_valid(sp_count)
    base, pitch_six = 3 * cols_four, three_six.shape[1]

    def reader(ref, start, pitch):
        return lambda edge: ref[start + edge * pitch : start + (edge + 1) * pitch].astype(F32)

    sums_four, sums_six = ([], []), ([], [])
    outer_level(
        six_ref, reader(above_ref, base, pitch_six), reader(below_ref, base, pitch_six), valid, w_ref,
        conv_six_ref, three_six, sums_six,
    )
    outer_level(
        four_ref, reader(above_ref, 0, cols_four), reader(below_ref, 0, cols_four), valid, w_ref,
        conv_four_ref, three_four, sums_four,
    )
    sums = [folded(parts) for parts in sums_four + sums_six]
    moments_ref[...] = inner_ref[...] + jnp.concatenate(sums, 0)


def turn_kernel(four_ref, six_ref, turned_ref):
    rows_four, cols_four, chan = four_ref.shape
    rows_six, cols_six = six_ref.shape[:2]
    pitch = pitch_of(cols_six)
    for start, end in chunks_of(rows_four, 8, 4):
        cells = four_ref[start:end].reshape((end - start) * cols_four, chan)
        turned_ref[:, start * cols_four : end * cols_four] = cells.T
    cells = six_ref[...].astype(F32)
    cells = jnp.concatenate([cells, jnp.zeros((rows_six, pitch - cols_six, chan), F32)], 1).astype(BF16)
    turned_ref[:, rows_four * cols_four :] = cells.reshape(rows_six * pitch, chan).T


def slope_level(inner_ref, outer_ref, cotan_ref, above, below, coefs, slope_ref):
    rows, cols, chan = cotan_ref.shape
    pitch = inner_ref.shape[1]

    def put(row, conv, cotan):
        centred, slope = slope_of(conv, widen(cotan, pitch), coefs)
        slope_ref[row] = slope
        return centred, slope

    def add(sums, pair):
        centred, slope = pair
        first = jnp.sum(slope.reshape(-1, 8, chan), 0)
        second = jnp.sum((slope * centred).reshape(-1, 8, chan), 0)
        return sums[0] + first, sums[1] + second

    def step(row, sums):
        return add(sums, put(row + 2, inner_ref[row], cotan_ref[row + 1]))

    put(0, outer_ref[0], above)
    put(rows + 1, outer_ref[3], below)
    zero = jnp.zeros((8, chan), F32)
    sums = add((zero, zero), put(1, outer_ref[1], cotan_ref[0]))
    sums = add(sums, put(rows, outer_ref[2], cotan_ref[rows - 1]))
    looped = (rows - 2) // 8 * 8
    if looped:
        sums = lax.fori_loop(0, looped, step, sums, unroll=8)
    for row in range(looped, rows - 2):
        sums = step(row, sums)
    first = 0.5 * jnp.sum(sums[0], 0, keepdims=True)
    return first, 0.5 * coefs[1] * jnp.sum(sums[1], 0, keepdims=True)


def slope_kernel(
    counts, inner_four_ref, inner_six_ref, outer_four_ref, outer_six_ref, cotan_four_ref, cotan_six_ref,
    above_ref, below_ref, moments_ref, gain_ref, shift_ref, slope_four_ref, slope_six_ref, slopes_ref,
):
    sums = ()
    cols_four = cotan_four_ref.shape[1]
    starts = (2 * cols_four, 3 * cols_four + 2 * inner_six_ref.shape[1])
    for level, (inner_ref, outer_ref, cotan_ref, slope_ref) in enumerate(
        (
            (inner_four_ref, outer_four_ref, cotan_four_ref, slope_four_ref),
            (inner_six_ref, outer_six_ref, cotan_six_ref, slope_six_ref),
        )
    ):
        pair = moments_ref[2 * level : 2 * level + 2]
        here = slice(level, level + 1)
        edge = slice(starts[level], starts[level] + inner_ref.shape[1])
        coefs = level_coefs(pair, gain_ref[here], shift_ref[here], counts[level])
        sums += slope_level(inner_ref, outer_ref, cotan_ref, above_ref[edge], below_ref[edge], coefs, slope_ref)
    slopes_ref[...] = jnp.concatenate(sums, 0)


def backward_level(cols, inner_ref, outer_ref, slope_ref, valid, coefs, slopes, count, three):
    rows = inner_ref.shape[0] + 2
    pitch = three.shape[1]
    mean, rstd, gain, shift = coefs
    lead = gain * rstd
    offset, factor = lead * (slopes[0:1] / count), lead * rstd * (slopes[1:2] / count)

    def fill_row(row):
        if 2 <= row < rows:
            conv = inner_ref[row - 2]
        else:
            conv = outer_ref[row if row < 2 else row - rows + 2]
        centred = conv.astype(F32) - mean
        dconv = masked((0.5 * lead) * slope_ref[row] - (offset + centred * factor), cols)
        if row == 0:
            dconv = dconv * valid[0]
        elif row == rows + 1:
            dconv = dconv * valid[1]
        put_three(three, row, dconv, cols, True)

    def block(start, end):
        return beside(three, (start + 2, start + 1, start), end - start)

    return fill_row, block


def backward_bounds(rows):
    bounds = [0, min(8, rows)]
    while bounds[-1] < rows:
        bounds.append(min(bounds[-1] + 16, rows))
    return bounds


def backward_kernel(
    counts, sp_count, cols, turned_ref, inner_four_ref, inner_six_ref, outer_four_ref, outer_six_ref,
    slope_four_ref, slope_six_ref, moments_ref, slopes_ref, gain_ref, shift_ref, three_four, three_six, own_ref, sent_ref, total,
):
    valid = edges_valid(sp_count)
    parts = []
    for level, inner_ref, outer_ref, slope_ref, three in (
        (0, inner_four_ref, outer_four_ref, slope_four_ref, three_four),
        (1, inner_six_ref, outer_six_ref, slope_six_ref, three_six),
    ):
        here = slice(level, level + 1)
        pair = slice(2 * level, 2 * level + 2)
        coefs = level_coefs(moments_ref[pair], gain_ref[here], shift_ref[here], counts[level])
        parts.append(
            backward_level(
                cols[level], inner_ref, outer_ref, slope_ref, valid, coefs, slopes_ref[pair], counts[level], three
            )
        )
    (fill_four, block_four), (fill_six, block_six) = parts
    rows_four, rows_six = three_four.shape[0] - 2, three_six.shape[0] - 2
    pitch = three_four.shape[1]
    bounds = backward_bounds(rows_four)

    def dot(start, end):
        first, last = start * pitch, end * pitch
        rhs = block_four(start, end)
        if end == rows_four:
            rhs = jnp.concatenate([rhs, block_six(0, rows_six)], 0)
            last = turned_ref.shape[1]
        term = jnp.dot(turned_ref[:, first:last], rhs, preferred_element_type=F32)
        total[...] = total[...] + term if start else term

    fills, dots, done = [], [], 0
    for start, end in zip(bounds[:-1], bounds[1:]):
        todo = [functools.partial(fill_four, row) for row in range(done, end + 2)]
        if end == rows_four:
            todo += [functools.partial(fill_six, row) for row in range(rows_six + 2)]
        fills.append(lambda todo=todo: [fill() for fill in todo])
        done = end + 2
        dots.append(functools.partial(dot, start, end))
    staged(fills, dots)
    share, chan = own_ref.shape[1:]
    for step in range(sp_count):
        begin = pl.multiple_of((lax.axis_index("sp") ^ step) * share, share)
        for tap in range(9):
            part = total[pl.ds(begin, share), tap * chan : (tap + 1) * chan]
            if step == 0:
                own_ref[tap] = part
            else:
                sent_ref[step - 1, tap] = part.astype(BF16)


def input_chunks(three, turned, grad, chunks, offset, sent=None):
    cols, chan = grad.shape[1:]
    pitch = three.shape[1]
    for index, (start, end) in enumerate(chunks):
        size = end - start
        lhs = beside(three, (start + 2, start + 1, start), size)
        term = jnp.dot(lhs, turned[...], preferred_element_type=F32)
        grad[start - offset : end - offset] = term.reshape(size, pitch, chan)[:, :cols].astype(BF16)
        if sent is not None:
            sent(index, start, end)


def input_first_kernel(chunks, three_four, w_ref, grad_ref, turned):
    chan = w_ref.shape[1]
    for tap in range(9):
        turned[tap * chan : (tap + 1) * chan] = w_ref[tap].T
    input_chunks(three_four, turned, grad_ref, chunks, 0)


def input_second_kernel(
    chunks, done, three_four, three_six, turned, first_ref, grad_four_ref, grad_six_ref,
    grad_four, grad_six, sem_first, sems_four, sems_six,
):
    copies = [pltpu.make_async_copy(first_ref, grad_four_ref.at[:done], sem_first)]
    copies[0].start()

    def sender(grad, grad_ref, offset, sems):
        def sent(index, start, end):
            copy = pltpu.make_async_copy(grad.at[start - offset : end - offset], grad_ref.at[start:end], sems.at[index])
            copy.start()
            copies.append(copy)

        return sent

    six_chunks = chunks_of(grad_six.shape[0], 12)
    input_chunks(three_six, turned, grad_six, six_chunks, 0, sender(grad_six, grad_six_ref, 0, sems_six))
    input_chunks(three_four, turned, grad_four, chunks, done, sender(grad_four, grad_four_ref, done, sems_four))
    for copy in copies:
        copy.wait()


def swap(array, axis, stride):
    count = lax.axis_size(axis)
    return lax.ppermute(array, axis, [(i, i ^ stride) for i in range(count)])


def edge_kernel(starts, four_ref, six_ref, cotan_four_ref, cotan_six_ref, *rest):
    outs, six_rows, sems = rest[:-2], rest[-2], rest[-1]
    rows_four, cols_four = four_ref.shape[:2]
    rows_six = six_ref.shape[0]
    pitch = pitch_of(six_ref.shape[1])
    copies = []
    for number, (start, out_ref) in enumerate(zip(starts, outs)):
        last = (1 - jnp.minimum(lax.axis_index("sp"), 1)) if start is None else start
        for part, (ref, row) in enumerate(
            (
                (four_ref, last * (rows_four - 2)),
                (four_ref, last * (rows_four - 2) + 1),
                (cotan_four_ref, last * (rows_four - 1)),
                (six_ref, last * (rows_six - 2)),
                (six_ref, last * (rows_six - 2) + 1),
                (cotan_six_ref, last * (rows_six - 1)),
            )
        ):
            if part < 3:
                target = out_ref.at[part * cols_four : (part + 1) * cols_four]
            else:
                target = six_rows.at[number, part - 3]
            copies.append(pltpu.make_async_copy(ref.at[row], target, sems.at[number, part]))
    for copy in copies:
        copy.start()
    for copy in copies:
        copy.wait()
    for number, out_ref in enumerate(outs):
        for part in range(3):
            begin = 3 * cols_four + part * pitch
            out_ref[begin : begin + pitch] = widen(six_rows[number, part], pitch).astype(BF16)


def edges(four, six, cotan_four, cotan_six):
    count = lax.axis_size("sp")
    starts = (None,) if count == 2 else (0, 1)
    length = 3 * four.shape[1] + 3 * pitch_of(six.shape[1])
    vmem = pl.BlockSpec(memory_space=pltpu.VMEM)
    hbm = pl.BlockSpec(memory_space=pltpu.HBM)
    outs = pl.pallas_call(
        functools.partial(edge_kernel, starts),
        out_shape=tuple(jax.ShapeDtypeStruct((length, four.shape[2]), BF16) for _ in starts),
        in_specs=[hbm] * 4,
        out_specs=tuple(vmem for _ in starts),
        scratch_shapes=[
            pltpu.VMEM((len(starts), 3) + six.shape[1:], BF16),
            pltpu.SemaphoreType.DMA((len(starts), 6)),
        ],
        compiler_params=pltpu.CompilerParams(vmem_limit_bytes=EDGE_LIMIT),
        name="edges",
    )(four, six, cotan_four, cotan_six)
    if count == 2:
        met = swap(outs[0], "sp", 1)
        return met, met
    above = lax.ppermute(outs[1], "sp", [(i, (i + 1) % count) for i in range(count)])
    below = lax.ppermute(outs[0], "sp", [((i + 1) % count, i) for i in range(count)])
    return above, below


def swap_across(array, axis, stride):
    count, sp_count = lax.axis_size("rep"), lax.axis_size("sp")
    rep_stride, sp_stride = (stride, 1) if axis == "rep" else (0, stride ^ 1)
    pairs = [
        (rep * sp_count + sp, (rep ^ rep_stride) * sp_count + (sp ^ sp_stride))
        for rep in range(count)
        for sp in range(sp_count)
    ]
    return lax.ppermute(array, ("rep", "sp"), pairs)


def group_sum(sums):
    sums = sums + swap(sums, "sp", 1)
    stride = 2
    while stride < lax.axis_size("sp"):
        sums = sums + swap_across(sums, "sp", stride)
        stride = 2 * stride
    stride = 1
    while stride < GROUP:
        met = [swap_across(sums, "rep", k * stride) for k in FAR_FIRST]
        sums = (sums + met[2]) + (met[1] + met[0])
        stride = RADIX * stride
    return sums


def every_group(sums):
    stride = GROUP
    while stride < lax.axis_size("rep"):
        sums = sums + swap(sums, "rep", stride)
        stride = 2 * stride
    return sums


def places():
    digit = lax.axis_index("rep") & (RADIX - 1)
    return [digit ^ k for k in range(RADIX)]


def piece_of(pieces, index):
    sizes = (1,) + pieces.shape[1:]
    return lax.dynamic_slice(pieces, (index, 0, 0), sizes, allow_negative_indices=False)[0]


def scatter_start(own, sent, place):
    met = [swap(sent[step], "sp", step + 1) for step in range(sent.shape[0])]
    chan = own.shape[2]
    parts = [part.reshape(RADIX, -1, chan) for part in [own] + met]

    def piece(k):
        total = piece_of(parts[0], place[k])
        for part in parts[1:]:
            total = total + piece_of(part, place[k]).astype(F32)
        return total

    return piece(0), [piece(k).astype(BF16) for k in FAR_FIRST]


def added(own, met):
    return (own + met[2].astype(F32)) + (met[1].astype(F32) + met[0].astype(F32))


def fours(pieces, stride):
    return [swap(piece, "rep", k * stride) for k, piece in zip(FAR_FIRST, pieces)]


def swap_mixed(array, even, odd):
    count, sp_count = lax.axis_size("rep"), lax.axis_size("sp")
    pairs = [
        (rep * sp_count + sp, (rep ^ (odd if sp % 2 else even)) * sp_count + sp)
        for rep in range(count)
        for sp in range(sp_count)
    ]
    return lax.ppermute(array, ("rep", "sp"), pairs)


def both(own, met):
    return (own.astype(F32) + met.astype(F32)).astype(BF16)


def weight_gather(total, found):
    chan = total.shape[1]
    stride = GROUP
    while stride < lax.axis_size("rep"):
        total = added(total.astype(F32), fours([total] * 3, stride)).astype(BF16)
        stride = RADIX * stride
    met = [total] + fours([total] * 3, 1)[::-1]
    whole = jnp.zeros((RADIX,) + total.shape, F32)
    for k in (0,) + FAR_FIRST:
        start = (found[k], 0, 0)
        whole = lax.dynamic_update_slice(whole, met[k][None].astype(F32), start, allow_negative_indices=False)
    return whole


def local(level_four, level_six, conv_weight, bn_gain, bn_shift, cotan_four, cotan_six):
    sp_count = lax.axis_size("sp")
    images = level_four.shape[0]
    four, six, cot_four, cot_six = (a[0] for a in (level_four, level_six, cotan_four, cotan_six))
    rows_four, cols_four, chan = four.shape
    rows_six, cols_six = six.shape[:2]
    pitch_four, pitch_six = pitch_of(cols_four), pitch_of(cols_six)
    counts = (
        float(images * GROUP * rows_four * sp_count * cols_four),
        float(images * GROUP * rows_six * sp_count * cols_six),
    )
    found, four = lax.optimization_barrier((places(), four))
    above, below = edges(four, six, cot_four, cot_six)
    vmem = pl.BlockSpec(memory_space=pltpu.VMEM)
    hbm = pl.BlockSpec(memory_space=pltpu.HBM)
    params = pltpu.CompilerParams(vmem_limit_bytes=VMEM_LIMIT)
    framed_four = jax.ShapeDtypeStruct((rows_four + 2, pitch_four, chan), BF16)
    framed_six = jax.ShapeDtypeStruct((rows_six + 2, pitch_six, chan), BF16)
    four_sums = jax.ShapeDtypeStruct((4, chan), F32)
    flops = 2 * 9 * chan * chan * (rows_four * cols_four + rows_six * cols_six)

    def cost(share, size):
        return pl.CostEstimate(flops=int(flops * share), bytes_accessed=size, transcendentals=0)

    inner_four, inner_six, inner_moments = pl.pallas_call(
        inner_kernel,
        out_shape=(
            jax.ShapeDtypeStruct((rows_four - 2, pitch_four, chan), BF16),
            jax.ShapeDtypeStruct((rows_six - 2, pitch_six, chan), BF16),
            four_sums,
        ),
        in_specs=[vmem] * 3,
        out_specs=(vmem, vmem, vmem),
        scratch_shapes=[
            pltpu.VMEM((rows_four, pitch_four, 3 * chan), BF16),
            pltpu.VMEM((rows_six, pitch_six, 3 * chan), BF16),
        ],
        compiler_params=params,
        cost_estimate=cost(1, 4 * four.size),
        name="forward_inner",
    )(four, six, conv_weight)
    outer_four, outer_six, moments = pl.pallas_call(
        functools.partial(outer_kernel, sp_count),
        out_shape=(
            jax.ShapeDtypeStruct((4, pitch_four, chan), BF16),
            jax.ShapeDtypeStruct((4, pitch_six, chan), BF16),
            four_sums,
        ),
        in_specs=[vmem] * 6,
        out_specs=(vmem, vmem, vmem),
        scratch_shapes=[
            pltpu.VMEM((8, pitch_four, 3 * chan), BF16),
            pltpu.VMEM((8, pitch_six, 3 * chan), BF16),
        ],
        compiler_params=params,
        cost_estimate=cost(0.1, four.size),
        name="forward_outer",
    )(four, six, above, below, conv_weight, inner_moments)
    moments, four, six = lax.optimization_barrier((moments, four, six))
    turned_features = pl.pallas_call(
        turn_kernel,
        out_shape=jax.ShapeDtypeStruct((chan, rows_four * cols_four + rows_six * pitch_six), BF16),
        in_specs=[vmem] * 2,
        out_specs=vmem,
        compiler_params=params,
        cost_estimate=cost(0.3, 4 * four.size),
        name="turn",
    )(four, six)
    moments, turned_features = lax.optimization_barrier((group_sum(moments), turned_features))

    slope_four, slope_six, slopes = pl.pallas_call(
        functools.partial(slope_kernel, counts),
        out_shape=(
            jax.ShapeDtypeStruct(framed_four.shape, F32),
            jax.ShapeDtypeStruct(framed_six.shape, F32),
            four_sums,
        ),
        in_specs=[vmem] * 11,
        out_specs=(vmem,) * 3,
        compiler_params=params,
        cost_estimate=cost(0.01, 4 * four.size),
        name="slopes",
    )(
        inner_four, inner_six, outer_four, outer_six, cot_four, cot_six, above, below, moments, bn_gain, bn_shift
    )
    slopes = group_sum(slopes)

    share = chan // sp_count
    wide_four, wide_six = (
        jax.ShapeDtypeStruct(framed.shape[:2] + (3 * chan,), BF16) for framed in (framed_four, framed_six)
    )
    three_four, three_six, own, sent = pl.pallas_call(
        functools.partial(backward_kernel, counts, sp_count, (cols_four, cols_six)),
        out_shape=(
            wide_four,
            wide_six,
            jax.ShapeDtypeStruct((9, share, chan), F32),
            jax.ShapeDtypeStruct((sp_count - 1, 9, share, chan), BF16),
        ),
        in_specs=[vmem] * 11,
        out_specs=(vmem,) * 4,
        scratch_shapes=[pltpu.VMEM((chan, 9 * chan), F32)],
        compiler_params=params,
        cost_estimate=cost(1.2, 8 * four.size),
        name="backward",
    )(
        turned_features, inner_four, inner_six, outer_four, outer_six, slope_four, slope_six, moments, slopes,
        bn_gain, bn_shift,
    )

    piece, pieces = scatter_start(own, sent, found)
    pieces, three_four = lax.optimization_barrier((pieces, three_four))
    met = fours(pieces, 1)
    chunks = chunks_of(rows_four, 8)
    split = -(-2 * len(chunks) // 3)
    done = chunks[split - 1][1]
    grad_first, turned = pl.pallas_call(
        functools.partial(input_first_kernel, chunks[:split]),
        out_shape=(
            jax.ShapeDtypeStruct((done, cols_four, chan), BF16),
            jax.ShapeDtypeStruct((9 * chan, chan), BF16),
        ),
        in_specs=[vmem] * 2,
        out_specs=(vmem, vmem),
        compiler_params=params,
        cost_estimate=cost(0.6, 3 * four.size),
        name="inputs_first",
    )(three_four, conv_weight)
    met, grad_first = lax.optimization_barrier((met, grad_first))

    piece = added(piece, met).astype(BF16)
    piece, three_six = lax.optimization_barrier((piece, three_six))
    met = swap_mixed(piece, RADIX, 2 * RADIX)
    grad_four, grad_six = pl.pallas_call(
        functools.partial(input_second_kernel, chunks[split:], done),
        out_shape=(
            jax.ShapeDtypeStruct(four.shape, BF16),
            jax.ShapeDtypeStruct(six.shape, BF16),
        ),
        in_specs=[vmem] * 4,
        out_specs=(hbm, hbm),
        scratch_shapes=[
            pltpu.VMEM((max(rows_four - done, 1), cols_four, chan), BF16),
            pltpu.VMEM(six.shape, BF16),
            pltpu.SemaphoreType.DMA,
            pltpu.SemaphoreType.DMA((len(chunks),)),
            pltpu.SemaphoreType.DMA((len(chunks_of(rows_six, 12)),)),
        ],
        compiler_params=params,
        cost_estimate=cost(0.4, 2 * four.size),
        name="inputs_second",
    )(three_four, three_six, turned, grad_first)
    met, grad_six = lax.optimization_barrier((met, grad_six))
    piece = both(piece, met)
    piece = both(piece, swap_mixed(piece, 2 * RADIX, RADIX))
    grad_weight = weight_gather(piece, found).reshape(own.shape)
    totals = every_group(slopes)
    grad_gain = jnp.stack([totals[1], totals[3]])
    grad_shift = jnp.stack([totals[0], totals[2]])
    return (grad_four[None], grad_six[None], grad_weight, grad_gain, grad_shift)


def solution(mesh):
    placed = (
        P("rep", "sp", None, None),
        P("rep", "sp", None, None),
        P(),
        P(),
        P(),
        P("rep", "sp", None, None),
        P("rep", "sp", None, None),
    )
    return jax.shard_map(
        local,
        mesh=mesh,
        in_specs=placed,
        out_specs=(
            P("rep", "sp", None, None),
            P("rep", "sp", None, None),
            P(None, "sp", None),
            P(),
            P(),
        ),
        check_vma=False,
    )
```

```python
import functools

import jax
import jax.numpy as jnp
from jax import lax
from jax.experimental import pallas as pl
from jax.experimental.pallas import tpu as pltpu
from jax.sharding import PartitionSpec as P

GROUP = 16
RADIX = 4
FAR_FIRST = (3, 2, 1)
EPSILON = 1e-05
F32 = jnp.float32
BF16 = jnp.bfloat16
VMEM_LIMIT = 20 * 1024 * 1024
EDGE_LIMIT = 60 * 1024 * 1024


def chunk_of(rows, most, multiple=1):
    sizes = [size for size in range(1, most + 1) if rows % size == 0 and size % multiple == 0]
    return max(sizes) if sizes else rows


def pitch_of(cols):
    return -(-cols // 16) * 16


def parity(rep):
    return ((rep >> 2) ^ (rep >> 3)) & 1


def chunks_of(rows, most, multiple=1):
    size = chunk_of(rows, most, multiple)
    return [(start, start + size) for start in range(0, rows, size)]


def widen(cells, pitch):
    cells = cells.astype(F32)
    extra = pitch - cells.shape[0]
    if extra:
        cells = jnp.concatenate([cells, jnp.zeros((extra, cells.shape[1]), F32)], 0)
    return cells


def put_three(three, row, cells, cols, turned):
    pitch, chan = cells.shape
    left, right = pltpu.roll(cells, 1, 0), pltpu.roll(cells, pitch - 1, 0)
    if pitch == cols:
        col = lax.broadcasted_iota(jnp.int32, (8, chan), 0)
        left = jnp.concatenate([jnp.where(col == 0, 0.0, left[:8]), left[8:]], 0)
        right = jnp.concatenate([right[:-8], jnp.where(col == 7, 0.0, right[-8:])], 0)
    parts = (right, cells, left) if turned else (left, cells, right)
    for place, part in enumerate(parts):
        three[row, :, place * chan : (place + 1) * chan] = part.astype(BF16)


def beside(three, starts, size):
    pitch, width = three.shape[1:]
    return jnp.concatenate([three[start : start + size].reshape(size * pitch, width) for start in starts], 1)


def edges_valid(sp_count):
    index = lax.axis_index("sp")
    return jnp.where(index > 0, 1.0, 0.0), jnp.where(index < sp_count - 1, 1.0, 0.0)


def level_coefs(moments, gain, shift, count):
    mean = moments[0:1] / count
    spread = moments[1:2] / count - mean * mean
    return mean, lax.rsqrt(spread + EPSILON), gain, shift


def slope_of(conv, cotan, coefs):
    mean, rstd, gain, shift = coefs
    centred = conv.astype(F32) - mean
    half = centred * (0.5 * rstd * gain) + 0.5 * shift
    turn = jnp.tanh(half)
    return centred, cotan.astype(F32) * ((1.0 + turn) * (1.0 + half * (1.0 - turn)))


def masked(cells, cols):
    if cells.shape[0] == cols:
        return cells
    col = lax.broadcasted_iota(jnp.int32, cells.shape, 0)
    return jnp.where(col < cols, cells, 0.0)


def staged(fills, dots):
    fills[0]()
    for index, dot in enumerate(dots):
        if index + 1 < len(fills):
            fills[index + 1]()
        dot()


def conv_rows(three, starts, size, w_ref):
    pitch, width = three.shape[1:]
    lhs = [beside(three, (start, start + 1, start + 2), size) for start in starts]
    lhs = jnp.concatenate(lhs, 0) if len(lhs) > 1 else lhs[0]
    conv = jnp.dot(lhs, w_ref[...].reshape(3 * width, -1), preferred_element_type=F32).astype(BF16)
    return conv.reshape(len(starts) * size, pitch, -1)


def add_moments(sums, conv, cols):
    chan = conv.shape[2]
    conv = conv.astype(F32)
    if conv.shape[1] != cols:
        conv = conv[:, :cols]
    conv = conv.reshape(-1, 8, chan)
    sums[0].append(jnp.sum(conv, 0))
    sums[1].append(jnp.sum(conv * conv, 0))


def folded(parts):
    total = parts[0]
    for part in parts[1:]:
        total = total + part
    return jnp.sum(total, 0, keepdims=True)


def inner_level(x_ref, w_ref, conv_ref, three, sums, most):
    rows, cols = x_ref.shape[:2]
    pitch = three.shape[1]

    def fill_row(row):
        put_three(three, row, widen(x_ref[row], pitch), cols, False)

    def dot(start, end):
        conv = conv_rows(three, (start,), end - start, w_ref)
        conv_ref[start:end] = conv
        add_moments(sums, conv, cols)

    inner = rows - 2
    count = max(1, inner // most)
    bounds = [index * inner // count for index in range(count + 1)]
    fills, dots, done = [], [], 0
    for start, end in zip(bounds[:-1], bounds[1:]):
        fills.append(lambda todo=range(done, end + 2): [fill_row(row) for row in todo])
        done = end + 2
        dots.append(functools.partial(dot, start, end))
    return fills, dots


def inner_kernel(four_ref, six_ref, w_ref, conv_four_ref, conv_six_ref, moments_ref, three_four, three_six):
    sums_four, sums_six = ([], []), ([], [])
    fills_six, dots_six = inner_level(six_ref, w_ref, conv_six_ref, three_six, sums_six, 10)
    fills_four, dots_four = inner_level(four_ref, w_ref, conv_four_ref, three_four, sums_four, 8)
    staged(fills_six + fills_four, dots_six + dots_four)
    moments_ref[...] = jnp.concatenate([folded(parts) for parts in sums_four + sums_six], 0)


def outer_level(x_ref, top, bottom, valid, w_ref, conv_ref, three, sums):
    rows, cols = x_ref.shape[:2]
    pitch = three.shape[1]
    for edge in range(2):
        put_three(three, edge, top(edge) * valid[0], cols, False)
        put_three(three, 2 + edge, widen(x_ref[edge], pitch), cols, False)
        put_three(three, 4 + edge, widen(x_ref[rows - 2 + edge], pitch), cols, False)
        put_three(three, 6 + edge, bottom(edge) * valid[1], cols, False)
    conv = conv_rows(three, (0, 4), 2, w_ref)
    conv_ref[...] = conv
    add_moments(sums, conv[1:3], cols)


def outer_kernel(
    sp_count, four_ref, six_ref, above_ref, below_ref, w_ref, inner_ref,
    conv_four_ref, conv_six_ref, moments_ref, three_four, three_six,
):
    cols_four = four_ref.shape[1]
    valid = edges_valid(sp_count)
    base, pitch_six = 3 * cols_four, three_six.shape[1]

    def reader(ref, start, pitch):
        return lambda edge: ref[start + edge * pitch : start + (edge + 1) * pitch].astype(F32)

    sums_four, sums_six = ([], []), ([], [])
    outer_level(
        six_ref, reader(above_ref, base, pitch_six), reader(below_ref, base, pitch_six), valid, w_ref,
        conv_six_ref, three_six, sums_six,
    )
    outer_level(
        four_ref, reader(above_ref, 0, cols_four), reader(below_ref, 0, cols_four), valid, w_ref,
        conv_four_ref, three_four, sums_four,
    )
    sums = [folded(parts) for parts in sums_four + sums_six]
    moments_ref[...] = inner_ref[...] + jnp.concatenate(sums, 0)


def turn_kernel(four_ref, six_ref, turned_ref):
    rows_four, cols_four, chan = four_ref.shape
    rows_six, cols_six = six_ref.shape[:2]
    pitch = pitch_of(cols_six)
    for start, end in chunks_of(rows_four, 8, 4):
        cells = four_ref[start:end].reshape((end - start) * cols_four, chan)
        turned_ref[:, start * cols_four : end * cols_four] = cells.T
    cells = six_ref[...].astype(F32)
    cells = jnp.concatenate([cells, jnp.zeros((rows_six, pitch - cols_six, chan), F32)], 1).astype(BF16)
    turned_ref[:, rows_four * cols_four :] = cells.reshape(rows_six * pitch, chan).T


def slope_level(inner_ref, outer_ref, cotan_ref, above, below, coefs, slope_ref):
    rows, cols, chan = cotan_ref.shape
    pitch = inner_ref.shape[1]

    def put(row, conv, cotan):
        centred, slope = slope_of(conv, widen(cotan, pitch), coefs)
        slope_ref[row] = slope
        return centred, slope

    def add(sums, pair):
        centred, slope = pair
        first = jnp.sum(slope.reshape(-1, 8, chan), 0)
        second = jnp.sum((slope * centred).reshape(-1, 8, chan), 0)
        return sums[0] + first, sums[1] + second

    def step(row, sums):
        return add(sums, put(row + 2, inner_ref[row], cotan_ref[row + 1]))

    put(0, outer_ref[0], above)
    put(rows + 1, outer_ref[3], below)
    zero = jnp.zeros((8, chan), F32)
    sums = add((zero, zero), put(1, outer_ref[1], cotan_ref[0]))
    sums = add(sums, put(rows, outer_ref[2], cotan_ref[rows - 1]))
    looped = (rows - 2) // 8 * 8
    if looped:
        sums = lax.fori_loop(0, looped, step, sums, unroll=8)
    for row in range(looped, rows - 2):
        sums = step(row, sums)
    first = 0.5 * jnp.sum(sums[0], 0, keepdims=True)
    return first, 0.5 * coefs[1] * jnp.sum(sums[1], 0, keepdims=True)


def slope_kernel(
    counts, inner_four_ref, inner_six_ref, outer_four_ref, outer_six_ref, cotan_four_ref, cotan_six_ref,
    above_ref, below_ref, moments_ref, gain_ref, shift_ref, slope_four_ref, slope_six_ref, slopes_ref,
):
    sums = ()
    cols_four = cotan_four_ref.shape[1]
    starts = (2 * cols_four, 3 * cols_four + 2 * inner_six_ref.shape[1])
    for level, (inner_ref, outer_ref, cotan_ref, slope_ref) in enumerate(
        (
            (inner_four_ref, outer_four_ref, cotan_four_ref, slope_four_ref),
            (inner_six_ref, outer_six_ref, cotan_six_ref, slope_six_ref),
        )
    ):
        pair = moments_ref[2 * level : 2 * level + 2]
        here = slice(level, level + 1)
        edge = slice(starts[level], starts[level] + inner_ref.shape[1])
        coefs = level_coefs(pair, gain_ref[here], shift_ref[here], counts[level])
        sums += slope_level(inner_ref, outer_ref, cotan_ref, above_ref[edge], below_ref[edge], coefs, slope_ref)
    slopes_ref[...] = jnp.concatenate(sums, 0)


def backward_level(cols, inner_ref, outer_ref, slope_ref, valid, coefs, slopes, count, three):
    rows = inner_ref.shape[0] + 2
    pitch = three.shape[1]
    mean, rstd, gain, shift = coefs
    lead = gain * rstd
    offset, factor = lead * (slopes[0:1] / count), lead * rstd * (slopes[1:2] / count)

    def fill_row(row):
        if 2 <= row < rows:
            conv = inner_ref[row - 2]
        else:
            conv = outer_ref[row if row < 2 else row - rows + 2]
        centred = conv.astype(F32) - mean
        dconv = masked((0.5 * lead) * slope_ref[row] - (offset + centred * factor), cols)
        if row == 0:
            dconv = dconv * valid[0]
        elif row == rows + 1:
            dconv = dconv * valid[1]
        put_three(three, row, dconv, cols, True)

    def block(start, end):
        return beside(three, (start + 2, start + 1, start), end - start)

    return fill_row, block


def backward_bounds(rows):
    bounds = [0, min(8, rows)]
    while bounds[-1] < rows:
        bounds.append(min(bounds[-1] + 16, rows))
    return bounds


def backward_kernel(
    counts, sp_count, cols, turned_ref, inner_four_ref, inner_six_ref, outer_four_ref, outer_six_ref,
    slope_four_ref, slope_six_ref, moments_ref, slopes_ref, gain_ref, shift_ref, three_four, three_six, own_ref, sent_ref, total,
):
    valid = edges_valid(sp_count)
    parts = []
    for level, inner_ref, outer_ref, slope_ref, three in (
        (0, inner_four_ref, outer_four_ref, slope_four_ref, three_four),
        (1, inner_six_ref, outer_six_ref, slope_six_ref, three_six),
    ):
        here = slice(level, level + 1)
        pair = slice(2 * level, 2 * level + 2)
        coefs = level_coefs(moments_ref[pair], gain_ref[here], shift_ref[here], counts[level])
        parts.append(
            backward_level(
                cols[level], inner_ref, outer_ref, slope_ref, valid, coefs, slopes_ref[pair], counts[level], three
            )
        )
    (fill_four, block_four), (fill_six, block_six) = parts
    rows_four, rows_six = three_four.shape[0] - 2, three_six.shape[0] - 2
    pitch = three_four.shape[1]
    bounds = backward_bounds(rows_four)

    def dot(start, end):
        first, last = start * pitch, end * pitch
        rhs = block_four(start, end)
        if end == rows_four:
            rhs = jnp.concatenate([rhs, block_six(0, rows_six)], 0)
            last = turned_ref.shape[1]
        term = jnp.dot(turned_ref[:, first:last], rhs, preferred_element_type=F32)
        total[...] = total[...] + term if start else term

    fills, dots, done = [], [], 0
    for start, end in zip(bounds[:-1], bounds[1:]):
        todo = [functools.partial(fill_four, row) for row in range(done, end + 2)]
        if end == rows_four:
            todo += [functools.partial(fill_six, row) for row in range(rows_six + 2)]
        fills.append(lambda todo=todo: [fill() for fill in todo])
        done = end + 2
        dots.append(functools.partial(dot, start, end))
    staged(fills, dots)
    share, chan = own_ref.shape[1:]
    place = lax.axis_index("sp") ^ parity(lax.axis_index("rep"))
    for step in range(sp_count):
        begin = pl.multiple_of((place ^ step) * share, share)
        for tap in range(9):
            part = total[pl.ds(begin, share), tap * chan : (tap + 1) * chan]
            if step == 0:
                own_ref[tap] = part
            else:
                sent_ref[step - 1, tap] = part.astype(BF16)


def input_chunks(three, turned, grad, chunks, offset, sent=None):
    cols, chan = grad.shape[1:]
    pitch = three.shape[1]
    for index, (start, end) in enumerate(chunks):
        size = end - start
        lhs = beside(three, (start + 2, start + 1, start), size)
        term = jnp.dot(lhs, turned[...], preferred_element_type=F32)
        grad[start - offset : end - offset] = term.reshape(size, pitch, chan)[:, :cols].astype(BF16)
        if sent is not None:
            sent(index, start, end)


def input_first_kernel(chunks, three_four, w_ref, grad_ref, turned):
    chan = w_ref.shape[1]
    for tap in range(9):
        turned[tap * chan : (tap + 1) * chan] = w_ref[tap].T
    input_chunks(three_four, turned, grad_ref, chunks, 0)


def input_second_kernel(
    chunks, done, three_four, three_six, turned, first_ref, grad_four_ref, grad_six_ref,
    grad_four, grad_six, sem_first, sems_four, sems_six,
):
    copies = [pltpu.make_async_copy(first_ref, grad_four_ref.at[:done], sem_first)]
    copies[0].start()

    def sender(grad, grad_ref, offset, sems):
        def sent(index, start, end):
            copy = pltpu.make_async_copy(grad.at[start - offset : end - offset], grad_ref.at[start:end], sems.at[index])
            copy.start()
            copies.append(copy)

        return sent

    six_chunks = chunks_of(grad_six.shape[0], 12)
    input_chunks(three_six, turned, grad_six, six_chunks, 0, sender(grad_six, grad_six_ref, 0, sems_six))
    input_chunks(three_four, turned, grad_four, chunks, done, sender(grad_four, grad_four_ref, done, sems_four))
    for copy in copies:
        copy.wait()


def swap(array, axis, stride):
    count = lax.axis_size(axis)
    return lax.ppermute(array, axis, [(i, i ^ stride) for i in range(count)])


def edge_kernel(starts, four_ref, six_ref, cotan_four_ref, cotan_six_ref, *rest):
    outs, six_rows, sems = rest[:-2], rest[-2], rest[-1]
    rows_four, cols_four = four_ref.shape[:2]
    rows_six = six_ref.shape[0]
    pitch = pitch_of(six_ref.shape[1])
    copies = []
    for number, (start, out_ref) in enumerate(zip(starts, outs)):
        last = (1 - jnp.minimum(lax.axis_index("sp"), 1)) if start is None else start
        for part, (ref, row) in enumerate(
            (
                (four_ref, last * (rows_four - 2)),
                (four_ref, last * (rows_four - 2) + 1),
                (cotan_four_ref, last * (rows_four - 1)),
                (six_ref, last * (rows_six - 2)),
                (six_ref, last * (rows_six - 2) + 1),
                (cotan_six_ref, last * (rows_six - 1)),
            )
        ):
            if part < 3:
                target = out_ref.at[part * cols_four : (part + 1) * cols_four]
            else:
                target = six_rows.at[number, part - 3]
            copies.append(pltpu.make_async_copy(ref.at[row], target, sems.at[number, part]))
    for copy in copies:
        copy.start()
    for copy in copies:
        copy.wait()
    for number, out_ref in enumerate(outs):
        for part in range(3):
            begin = 3 * cols_four + part * pitch
            out_ref[begin : begin + pitch] = widen(six_rows[number, part], pitch).astype(BF16)


def edges(four, six, cotan_four, cotan_six):
    count = lax.axis_size("sp")
    starts = (None,) if count == 2 else (0, 1)
    length = 3 * four.shape[1] + 3 * pitch_of(six.shape[1])
    vmem = pl.BlockSpec(memory_space=pltpu.VMEM)
    hbm = pl.BlockSpec(memory_space=pltpu.HBM)
    outs = pl.pallas_call(
        functools.partial(edge_kernel, starts),
        out_shape=tuple(jax.ShapeDtypeStruct((length, four.shape[2]), BF16) for _ in starts),
        in_specs=[hbm] * 4,
        out_specs=tuple(vmem for _ in starts),
        scratch_shapes=[
            pltpu.VMEM((len(starts), 3) + six.shape[1:], BF16),
            pltpu.SemaphoreType.DMA((len(starts), 6)),
        ],
        compiler_params=pltpu.CompilerParams(vmem_limit_bytes=EDGE_LIMIT),
        name="edges",
    )(four, six, cotan_four, cotan_six)
    if count == 2:
        met = swap(outs[0], "sp", 1)
        return met, met
    above = lax.ppermute(outs[1], "sp", [(i, (i + 1) % count) for i in range(count)])
    below = lax.ppermute(outs[0], "sp", [((i + 1) % count, i) for i in range(count)])
    return above, below


def swap_across(array, axis, stride):
    count, sp_count = lax.axis_size("rep"), lax.axis_size("sp")
    rep_stride, sp_stride = (stride, 1) if axis == "rep" else (0, stride ^ 1)
    pairs = [
        (rep * sp_count + sp, (rep ^ rep_stride) * sp_count + (sp ^ sp_stride))
        for rep in range(count)
        for sp in range(sp_count)
    ]
    return lax.ppermute(array, ("rep", "sp"), pairs)


def group_sum(sums):
    sums = sums + swap(sums, "sp", 1)
    stride = 2
    while stride < lax.axis_size("sp"):
        sums = sums + swap_across(sums, "sp", stride)
        stride = 2 * stride
    stride = 1
    while stride < GROUP:
        met = [swap_across(sums, "rep", k * stride) for k in FAR_FIRST]
        sums = (sums + met[2]) + (met[1] + met[0])
        stride = RADIX * stride
    return sums


def every_group(sums):
    stride = GROUP
    while stride < lax.axis_size("rep"):
        sums = sums + swap(sums, "rep", stride)
        stride = 2 * stride
    return sums


def places():
    rep = lax.axis_index("rep")
    digit = rep & (RADIX - 1)
    return [digit ^ k for k in range(RADIX)], parity(rep) == 1


def piece_of(pieces, index):
    sizes = (1,) + pieces.shape[1:]
    return lax.dynamic_slice(pieces, (index, 0, 0), sizes, allow_negative_indices=False)[0]


def scatter_start(own, sent, place):
    met = [swap(sent[step], "sp", step + 1) for step in range(sent.shape[0])]
    chan = own.shape[2]
    parts = [part.reshape(RADIX, -1, chan) for part in [own] + met]

    def piece(k):
        total = piece_of(parts[0], place[k])
        for part in parts[1:]:
            total = total + piece_of(part, place[k]).astype(F32)
        return total

    return piece(0), [piece(k).astype(BF16) for k in FAR_FIRST]


def added(own, met):
    return (own + met[2].astype(F32)) + (met[1].astype(F32) + met[0].astype(F32))


def fours(pieces, stride):
    return [swap(piece, "rep", k * stride) for k, piece in zip(FAR_FIRST, pieces)]


def swap_high(array, even, odd):
    count, sp_count = lax.axis_size("rep"), lax.axis_size("sp")
    pairs = []
    for rep in range(count):
        for sp in range(sp_count):
            stride = odd if (sp ^ parity(rep)) & 1 else even
            pairs.append((rep * sp_count + sp, (rep ^ stride) * sp_count + (sp ^ 1)))
    return lax.ppermute(array, ("rep", "sp"), pairs)


def bring(array, k):
    count, sp_count = lax.axis_size("rep"), lax.axis_size("sp")
    pairs = [
        (rep * sp_count + sp, (rep ^ k) * sp_count + (sp ^ parity(rep)))
        for rep in range(count)
        for sp in range(sp_count)
    ]
    return lax.ppermute(array, ("rep", "sp"), pairs)


def both(own, met):
    return (own.astype(F32) + met.astype(F32)).astype(BF16)


def weight_gather(total, found):
    chan = total.shape[1]
    stride = GROUP
    while stride < lax.axis_size("rep"):
        total = added(total.astype(F32), fours([total] * 3, stride)).astype(BF16)
        stride = RADIX * stride
    met = {k: bring(total, k) for k in FAR_FIRST}
    met[0] = jnp.where(found[1], swap(total, "sp", 1), total)
    whole = jnp.zeros((RADIX,) + total.shape, F32)
    for k in (0,) + FAR_FIRST:
        start = (found[0][k], 0, 0)
        whole = lax.dynamic_update_slice(whole, met[k][None].astype(F32), start, allow_negative_indices=False)
    return whole


def local(level_four, level_six, conv_weight, bn_gain, bn_shift, cotan_four, cotan_six):
    sp_count = lax.axis_size("sp")
    images = level_four.shape[0]
    four, six, cot_four, cot_six = (a[0] for a in (level_four, level_six, cotan_four, cotan_six))
    rows_four, cols_four, chan = four.shape
    rows_six, cols_six = six.shape[:2]
    pitch_four, pitch_six = pitch_of(cols_four), pitch_of(cols_six)
    counts = (
        float(images * GROUP * rows_four * sp_count * cols_four),
        float(images * GROUP * rows_six * sp_count * cols_six),
    )
    found, four = lax.optimization_barrier((places(), four))
    above, below = edges(four, six, cot_four, cot_six)
    vmem = pl.BlockSpec(memory_space=pltpu.VMEM)
    hbm = pl.BlockSpec(memory_space=pltpu.HBM)
    params = pltpu.CompilerParams(vmem_limit_bytes=VMEM_LIMIT)
    framed_four = jax.ShapeDtypeStruct((rows_four + 2, pitch_four, chan), BF16)
    framed_six = jax.ShapeDtypeStruct((rows_six + 2, pitch_six, chan), BF16)
    four_sums = jax.ShapeDtypeStruct((4, chan), F32)
    flops = 2 * 9 * chan * chan * (rows_four * cols_four + rows_six * cols_six)

    def cost(share, size):
        return pl.CostEstimate(flops=int(flops * share), bytes_accessed=size, transcendentals=0)

    inner_four, inner_six, inner_moments = pl.pallas_call(
        inner_kernel,
        out_shape=(
            jax.ShapeDtypeStruct((rows_four - 2, pitch_four, chan), BF16),
            jax.ShapeDtypeStruct((rows_six - 2, pitch_six, chan), BF16),
            four_sums,
        ),
        in_specs=[vmem] * 3,
        out_specs=(vmem, vmem, vmem),
        scratch_shapes=[
            pltpu.VMEM((rows_four, pitch_four, 3 * chan), BF16),
            pltpu.VMEM((rows_six, pitch_six, 3 * chan), BF16),
        ],
        compiler_params=params,
        cost_estimate=cost(1, 4 * four.size),
        name="forward_inner",
    )(four, six, conv_weight)
    outer_four, outer_six, moments = pl.pallas_call(
        functools.partial(outer_kernel, sp_count),
        out_shape=(
            jax.ShapeDtypeStruct((4, pitch_four, chan), BF16),
            jax.ShapeDtypeStruct((4, pitch_six, chan), BF16),
            four_sums,
        ),
        in_specs=[vmem] * 6,
        out_specs=(vmem, vmem, vmem),
        scratch_shapes=[
            pltpu.VMEM((8, pitch_four, 3 * chan), BF16),
            pltpu.VMEM((8, pitch_six, 3 * chan), BF16),
        ],
        compiler_params=params,
        cost_estimate=cost(0.1, four.size),
        name="forward_outer",
    )(four, six, above, below, conv_weight, inner_moments)
    moments, four, six = lax.optimization_barrier((moments, four, six))
    turned_features = pl.pallas_call(
        turn_kernel,
        out_shape=jax.ShapeDtypeStruct((chan, rows_four * cols_four + rows_six * pitch_six), BF16),
        in_specs=[vmem] * 2,
        out_specs=vmem,
        compiler_params=params,
        cost_estimate=cost(0.3, 4 * four.size),
        name="turn",
    )(four, six)
    moments, turned_features = lax.optimization_barrier((group_sum(moments), turned_features))

    slope_four, slope_six, slopes = pl.pallas_call(
        functools.partial(slope_kernel, counts),
        out_shape=(
            jax.ShapeDtypeStruct(framed_four.shape, F32),
            jax.ShapeDtypeStruct(framed_six.shape, F32),
            four_sums,
        ),
        in_specs=[vmem] * 11,
        out_specs=(vmem,) * 3,
        compiler_params=params,
        cost_estimate=cost(0.01, 4 * four.size),
        name="slopes",
    )(
        inner_four, inner_six, outer_four, outer_six, cot_four, cot_six, above, below, moments, bn_gain, bn_shift
    )
    slopes = group_sum(slopes)

    share = chan // sp_count
    wide_four, wide_six = (
        jax.ShapeDtypeStruct(framed.shape[:2] + (3 * chan,), BF16) for framed in (framed_four, framed_six)
    )
    three_four, three_six, own, sent = pl.pallas_call(
        functools.partial(backward_kernel, counts, sp_count, (cols_four, cols_six)),
        out_shape=(
            wide_four,
            wide_six,
            jax.ShapeDtypeStruct((9, share, chan), F32),
            jax.ShapeDtypeStruct((sp_count - 1, 9, share, chan), BF16),
        ),
        in_specs=[vmem] * 11,
        out_specs=(vmem,) * 4,
        scratch_shapes=[pltpu.VMEM((chan, 9 * chan), F32)],
        compiler_params=params,
        cost_estimate=cost(1.2, 8 * four.size),
        name="backward",
    )(
        turned_features, inner_four, inner_six, outer_four, outer_six, slope_four, slope_six, moments, slopes,
        bn_gain, bn_shift,
    )

    piece, pieces = scatter_start(own, sent, found[0])
    pieces, three_four = lax.optimization_barrier((pieces, three_four))
    met = fours(pieces, 1)
    chunks = chunks_of(rows_four, 8)
    split = -(-2 * len(chunks) // 3)
    done = chunks[split - 1][1]
    grad_first, turned = pl.pallas_call(
        functools.partial(input_first_kernel, chunks[:split]),
        out_shape=(
            jax.ShapeDtypeStruct((done, cols_four, chan), BF16),
            jax.ShapeDtypeStruct((9 * chan, chan), BF16),
        ),
        in_specs=[vmem] * 2,
        out_specs=(vmem, vmem),
        compiler_params=params,
        cost_estimate=cost(0.6, 3 * four.size),
        name="inputs_first",
    )(three_four, conv_weight)
    totals = every_group(slopes)
    grad_gain = jnp.stack([totals[1], totals[3]])
    grad_shift = jnp.stack([totals[0], totals[2]])
    met, grad_first, grad_gain, grad_shift = lax.optimization_barrier((met, grad_first, grad_gain, grad_shift))

    piece = added(piece, met).astype(BF16)
    piece, three_six = lax.optimization_barrier((piece, three_six))
    met = swap_high(piece, RADIX, 2 * RADIX)
    grad_four, grad_six = pl.pallas_call(
        functools.partial(input_second_kernel, chunks[split:], done),
        out_shape=(
            jax.ShapeDtypeStruct(four.shape, BF16),
            jax.ShapeDtypeStruct(six.shape, BF16),
        ),
        in_specs=[vmem] * 4,
        out_specs=(hbm, hbm),
        scratch_shapes=[
            pltpu.VMEM((max(rows_four - done, 1), cols_four, chan), BF16),
            pltpu.VMEM(six.shape, BF16),
            pltpu.SemaphoreType.DMA,
            pltpu.SemaphoreType.DMA((len(chunks),)),
            pltpu.SemaphoreType.DMA((len(chunks_of(rows_six, 12)),)),
        ],
        compiler_params=params,
        cost_estimate=cost(0.4, 2 * four.size),
        name="inputs_second",
    )(three_four, three_six, turned, grad_first)
    met, grad_six = lax.optimization_barrier((met, grad_six))
    piece = both(piece, met)
    piece = both(piece, swap_high(piece, 2 * RADIX, RADIX))
    grad_weight = weight_gather(piece, found).reshape(own.shape)
    return (grad_four[None], grad_six[None], grad_weight, grad_gain, grad_shift)


def solution(mesh):
    placed = (
        P("rep", "sp", None, None),
        P("rep", "sp", None, None),
        P(),
        P(),
        P(),
        P("rep", "sp", None, None),
        P("rep", "sp", None, None),
    )
    return jax.shard_map(
        local,
        mesh=mesh,
        in_specs=placed,
        out_specs=(
            P("rep", "sp", None, None),
            P("rep", "sp", None, None),
            P(None, "sp", None),
            P(),
            P(),
        ),
        check_vma=False,
    )
```

```python
import functools
from typing import NamedTuple

import jax
import jax.numpy as jnp
from jax import lax
from jax.experimental import pallas as pl
from jax.experimental.pallas import tpu as pltpu
from jax.sharding import PartitionSpec as P

GROUP = 16
RADIX = 4
FAR_FIRST = (3, 2, 1)
FIRST_TAPS = 4
EPSILON = 1e-05
F32 = jnp.float32
BF16 = jnp.bfloat16
VMEM_LIMIT = 20 * 1024 * 1024
EDGE_LIMIT = 60 * 1024 * 1024


def chunk_of(rows, most, multiple=1):
    sizes = [size for size in range(1, most + 1) if rows % size == 0 and size % multiple == 0]
    return max(sizes) if sizes else rows


def pitch_of(cols):
    return -(-cols // 16) * 16


def parity(rep):
    return ((rep >> 2) ^ (rep >> 3)) & 1


def chunks_of(rows, most, multiple=1):
    size = chunk_of(rows, most, multiple)
    return [(start, start + size) for start in range(0, rows, size)]


def widen(cells, pitch):
    cells = cells.astype(F32)
    extra = pitch - cells.shape[0]
    if extra:
        cells = jnp.concatenate([cells, jnp.zeros((extra, cells.shape[1]), F32)], 0)
    return cells


def put_three(three, row, cells, cols, turned):
    pitch, chan = cells.shape
    left, right = pltpu.roll(cells, 1, 0), pltpu.roll(cells, pitch - 1, 0)
    if pitch == cols:
        col = lax.broadcasted_iota(jnp.int32, (8, chan), 0)
        left = jnp.concatenate([jnp.where(col == 0, 0.0, left[:8]), left[8:]], 0)
        right = jnp.concatenate([right[:-8], jnp.where(col == 7, 0.0, right[-8:])], 0)
    parts = (right, cells, left) if turned else (left, cells, right)
    for place, part in enumerate(parts):
        three[row, :, place * chan : (place + 1) * chan] = part.astype(BF16)


def beside(three, starts, size):
    pitch, width = three.shape[1:]
    return jnp.concatenate([three[start : start + size].reshape(size * pitch, width) for start in starts], 1)


def edges_valid(sp_count):
    index = lax.axis_index("sp")
    return jnp.where(index > 0, 1.0, 0.0), jnp.where(index < sp_count - 1, 1.0, 0.0)


def level_coefs(moments, gain, shift, count):
    mean = moments[0:1] / count
    spread = moments[1:2] / count - mean * mean
    return mean, lax.rsqrt(spread + EPSILON), gain, shift


def slope_of(conv, cotan, coefs):
    mean, rstd, gain, shift = coefs
    centred = conv.astype(F32) - mean
    half = centred * (0.5 * rstd * gain) + 0.5 * shift
    turn = jnp.tanh(half)
    return centred, cotan.astype(F32) * ((1.0 + turn) * (1.0 + half * (1.0 - turn)))


def masked(cells, cols):
    if cells.shape[0] == cols:
        return cells
    col = lax.broadcasted_iota(jnp.int32, cells.shape, 0)
    return jnp.where(col < cols, cells, 0.0)


def staged(fills, dots):
    fills[0]()
    for index, dot in enumerate(dots):
        if index + 1 < len(fills):
            fills[index + 1]()
        dot()


def conv_rows(three, starts, size, w_ref):
    pitch, width = three.shape[1:]
    lhs = [beside(three, (start, start + 1, start + 2), size) for start in starts]
    lhs = jnp.concatenate(lhs, 0) if len(lhs) > 1 else lhs[0]
    conv = jnp.dot(lhs, w_ref[...].reshape(3 * width, -1), preferred_element_type=F32).astype(BF16)
    return conv.reshape(len(starts) * size, pitch, -1)


def add_moments(sums, conv, cols):
    chan = conv.shape[2]
    conv = conv.astype(F32)
    if conv.shape[1] != cols:
        conv = conv[:, :cols]
    conv = conv.reshape(-1, 8, chan)
    sums[0].append(jnp.sum(conv, 0))
    sums[1].append(jnp.sum(conv * conv, 0))


def folded(parts):
    total = parts[0]
    for part in parts[1:]:
        total = total + part
    return jnp.sum(total, 0, keepdims=True)


def inner_level(x_ref, w_ref, conv_ref, three, sums, most):
    rows, cols = x_ref.shape[:2]
    pitch = three.shape[1]

    def fill_row(row):
        put_three(three, row, widen(x_ref[row], pitch), cols, False)

    def dot(start, end):
        conv = conv_rows(three, (start,), end - start, w_ref)
        conv_ref[start:end] = conv
        add_moments(sums, conv, cols)

    inner = rows - 2
    count = max(1, inner // most)
    bounds = [index * inner // count for index in range(count + 1)]
    fills, dots, done = [], [], 0
    for start, end in zip(bounds[:-1], bounds[1:]):
        fills.append(lambda todo=range(done, end + 2): [fill_row(row) for row in todo])
        done = end + 2
        dots.append(functools.partial(dot, start, end))
    return fills, dots


def inner_kernel(four_ref, six_ref, w_ref, conv_four_ref, conv_six_ref, moments_ref, three_four, three_six):
    sums_four, sums_six = ([], []), ([], [])
    fills_six, dots_six = inner_level(six_ref, w_ref, conv_six_ref, three_six, sums_six, 10)
    fills_four, dots_four = inner_level(four_ref, w_ref, conv_four_ref, three_four, sums_four, 8)
    staged(fills_six + fills_four, dots_six + dots_four)
    moments_ref[...] = jnp.concatenate([folded(parts) for parts in sums_four + sums_six], 0)


def outer_level(x_ref, top, bottom, valid, w_ref, conv_ref, three, sums):
    rows, cols = x_ref.shape[:2]
    pitch = three.shape[1]
    for edge in range(2):
        put_three(three, edge, top(edge) * valid[0], cols, False)
        put_three(three, 2 + edge, widen(x_ref[edge], pitch), cols, False)
        put_three(three, 4 + edge, widen(x_ref[rows - 2 + edge], pitch), cols, False)
        put_three(three, 6 + edge, bottom(edge) * valid[1], cols, False)
    conv = conv_rows(three, (0, 4), 2, w_ref)
    conv_ref[...] = conv
    add_moments(sums, conv[1:3], cols)


def outer_kernel(
    sp_count, four_ref, six_ref, above_ref, below_ref, w_ref, inner_ref,
    conv_four_ref, conv_six_ref, moments_ref, three_four, three_six,
):
    cols_four = four_ref.shape[1]
    valid = edges_valid(sp_count)
    base, pitch_six = 3 * cols_four, three_six.shape[1]

    def reader(ref, start, pitch):
        return lambda edge: ref[start + edge * pitch : start + (edge + 1) * pitch].astype(F32)

    sums_four, sums_six = ([], []), ([], [])
    outer_level(
        six_ref, reader(above_ref, base, pitch_six), reader(below_ref, base, pitch_six), valid, w_ref,
        conv_six_ref, three_six, sums_six,
    )
    outer_level(
        four_ref, reader(above_ref, 0, cols_four), reader(below_ref, 0, cols_four), valid, w_ref,
        conv_four_ref, three_four, sums_four,
    )
    sums = [folded(parts) for parts in sums_four + sums_six]
    moments_ref[...] = inner_ref[...] + jnp.concatenate(sums, 0)


def turn_kernel(four_ref, six_ref, w_ref, turned_ref, turned_w_ref):
    rows_four, cols_four, chan = four_ref.shape
    rows_six, cols_six = six_ref.shape[:2]
    pitch = pitch_of(cols_six)
    for start, end in chunks_of(rows_four, 8, 4):
        cells = four_ref[start:end].reshape((end - start) * cols_four, chan)
        turned_ref[:, start * cols_four : end * cols_four] = cells.T
    cells = six_ref[...].astype(F32)
    cells = jnp.concatenate([cells, jnp.zeros((rows_six, pitch - cols_six, chan), F32)], 1).astype(BF16)
    turned_ref[:, rows_four * cols_four :] = cells.reshape(rows_six * pitch, chan).T
    for tap in range(9):
        turned_w_ref[tap * chan : (tap + 1) * chan] = w_ref[tap].T


def slope_level(inner_ref, outer_ref, cotan_ref, above, below, coefs, slope_ref):
    rows, cols, chan = cotan_ref.shape
    pitch = inner_ref.shape[1]

    def put(row, conv, cotan):
        centred, slope = slope_of(conv, widen(cotan, pitch), coefs)
        slope_ref[row] = slope
        return centred, slope

    def add(sums, pair):
        centred, slope = pair
        first = jnp.sum(slope.reshape(-1, 8, chan), 0)
        second = jnp.sum((slope * centred).reshape(-1, 8, chan), 0)
        return sums[0] + first, sums[1] + second

    def step(row, sums):
        return add(sums, put(row + 2, inner_ref[row], cotan_ref[row + 1]))

    put(0, outer_ref[0], above)
    put(rows + 1, outer_ref[3], below)
    zero = jnp.zeros((8, chan), F32)
    sums = add((zero, zero), put(1, outer_ref[1], cotan_ref[0]))
    sums = add(sums, put(rows, outer_ref[2], cotan_ref[rows - 1]))
    looped = (rows - 2) // 8 * 8
    if looped:
        sums = lax.fori_loop(0, looped, step, sums, unroll=8)
    for row in range(looped, rows - 2):
        sums = step(row, sums)
    first = 0.5 * jnp.sum(sums[0], 0, keepdims=True)
    return first, 0.5 * coefs[1] * jnp.sum(sums[1], 0, keepdims=True)


def slope_kernel(
    counts, inner_four_ref, inner_six_ref, outer_four_ref, outer_six_ref, cotan_four_ref, cotan_six_ref,
    above_ref, below_ref, moments_ref, gain_ref, shift_ref, slope_four_ref, slope_six_ref, slopes_ref,
):
    sums = ()
    cols_four = cotan_four_ref.shape[1]
    starts = (2 * cols_four, 3 * cols_four + 2 * inner_six_ref.shape[1])
    for level, (inner_ref, outer_ref, cotan_ref, slope_ref) in enumerate(
        (
            (inner_four_ref, outer_four_ref, cotan_four_ref, slope_four_ref),
            (inner_six_ref, outer_six_ref, cotan_six_ref, slope_six_ref),
        )
    ):
        pair = moments_ref[2 * level : 2 * level + 2]
        here = slice(level, level + 1)
        edge = slice(starts[level], starts[level] + inner_ref.shape[1])
        coefs = level_coefs(pair, gain_ref[here], shift_ref[here], counts[level])
        sums += slope_level(inner_ref, outer_ref, cotan_ref, above_ref[edge], below_ref[edge], coefs, slope_ref)
    slopes_ref[...] = jnp.concatenate(sums, 0)


def backward_level(cols, inner_ref, outer_ref, slope_ref, valid, coefs, slopes, count, three):
    rows = inner_ref.shape[0] + 2
    pitch = three.shape[1]
    mean, rstd, gain, shift = coefs
    lead = gain * rstd
    offset, factor = lead * (slopes[0:1] / count), lead * rstd * (slopes[1:2] / count)

    def fill_row(row):
        if 2 <= row < rows:
            conv = inner_ref[row - 2]
        else:
            conv = outer_ref[row if row < 2 else row - rows + 2]
        centred = conv.astype(F32) - mean
        dconv = masked((0.5 * lead) * slope_ref[row] - (offset + centred * factor), cols)
        if row == 0:
            dconv = dconv * valid[0]
        elif row == rows + 1:
            dconv = dconv * valid[1]
        put_three(three, row, dconv, cols, True)

    return fill_row


def taps_beside(three, start, end, taps):
    pitch, width = three.shape[1:]
    chan = width // 3
    parts = []
    for row_tap in range(3):
        low, high = max(taps[0] - 3 * row_tap, 0), min(taps[1] - 3 * row_tap, 3)
        if low < high:
            first = start + 2 - row_tap
            rows = three[first : first + end - start, :, low * chan : high * chan]
            parts.append(rows.reshape((end - start) * pitch, (high - low) * chan))
    return jnp.concatenate(parts, 1)


def backward_bounds(rows):
    bounds = [0, min(8, rows)]
    while bounds[-1] < rows:
        bounds.append(min(bounds[-1] + 16, rows))
    return bounds


def weight_dot(turned_ref, three_four, three_six, total, taps, start, end):
    rows_four, rows_six = three_four.shape[0] - 2, three_six.shape[0] - 2
    pitch = three_four.shape[1]
    first, last = start * pitch, end * pitch
    rhs = taps_beside(three_four, start, end, taps)
    if end == rows_four:
        rhs = jnp.concatenate([rhs, taps_beside(three_six, 0, rows_six, taps)], 0)
        last = turned_ref.shape[1]
    term = jnp.dot(turned_ref[:, first:last], rhs, preferred_element_type=F32)
    total[...] = total[...] + term if start else term


def put_shares(total, sp_count, own_ref, sent_ref):
    taps, share, chan = own_ref.shape
    place = lax.axis_index("sp") ^ parity(lax.axis_index("rep"))
    for step in range(sp_count):
        begin = pl.multiple_of((place ^ step) * share, share)
        for tap in range(taps):
            part = total[pl.ds(begin, share), tap * chan : (tap + 1) * chan]
            if step == 0:
                own_ref[tap] = part
            else:
                sent_ref[step - 1, tap] = part.astype(BF16)


def backward_kernel(
    counts, sp_count, cols, turned_ref, inner_four_ref, inner_six_ref, outer_four_ref, outer_six_ref,
    slope_four_ref, slope_six_ref, moments_ref, slopes_ref, gain_ref, shift_ref, three_four, three_six, own_ref,
    sent_ref, grad_gain_ref, grad_shift_ref, total,
):
    valid = edges_valid(sp_count)
    grad_gain_ref[...] = jnp.concatenate([slopes_ref[1:2], slopes_ref[3:4]], 0)
    grad_shift_ref[...] = jnp.concatenate([slopes_ref[0:1], slopes_ref[2:3]], 0)
    parts = []
    for level, inner_ref, outer_ref, slope_ref, three in (
        (0, inner_four_ref, outer_four_ref, slope_four_ref, three_four),
        (1, inner_six_ref, outer_six_ref, slope_six_ref, three_six),
    ):
        here = slice(level, level + 1)
        pair = slice(2 * level, 2 * level + 2)
        coefs = level_coefs(moments_ref[pair], gain_ref[here], shift_ref[here], counts[level])
        parts.append(
            backward_level(
                cols[level], inner_ref, outer_ref, slope_ref, valid, coefs, slopes_ref[pair], counts[level], three
            )
        )
    fill_four, fill_six = parts
    rows_four, rows_six = three_four.shape[0] - 2, three_six.shape[0] - 2
    bounds = backward_bounds(rows_four)
    fills, dots, done = [], [], 0
    for start, end in zip(bounds[:-1], bounds[1:]):
        todo = [functools.partial(fill_four, row) for row in range(done, end + 2)]
        if end == rows_four:
            todo += [functools.partial(fill_six, row) for row in range(rows_six + 2)]
        fills.append(lambda todo=todo: [fill() for fill in todo])
        done = end + 2
        dots.append(
            functools.partial(weight_dot, turned_ref, three_four, three_six, total, (0, FIRST_TAPS), start, end)
        )
    staged(fills, dots)
    put_shares(total, sp_count, own_ref, sent_ref)


def weight_kernel(sp_count, turned_ref, three_four, three_six, own_ref, sent_ref, total):
    for start, end in chunks_of(three_four.shape[0] - 2, 16, 4):
        weight_dot(turned_ref, three_four, three_six, total, (FIRST_TAPS, 9), start, end)
    put_shares(total, sp_count, own_ref, sent_ref)


def input_chunks(three, turned, grad, chunks, offset, sent=None):
    cols, chan = grad.shape[1:]
    pitch = three.shape[1]
    for index, (start, end) in enumerate(chunks):
        size = end - start
        lhs = beside(three, (start + 2, start + 1, start), size)
        term = jnp.dot(lhs, turned[...], preferred_element_type=F32)
        grad[start - offset : end - offset] = term.reshape(size, pitch, chan)[:, :cols].astype(BF16)
        if sent is not None:
            sent(index, start, end)


def input_kernel(chunks, three_four, turned, grad_ref):
    input_chunks(three_four, turned, grad_ref, chunks, chunks[0][0])


def input_last_kernel(chunks, bounds, three_four, three_six, turned, *rest):
    count = len(bounds) - 1
    earlier, rest = rest[:count], rest[count:]
    grad_four_ref, grad_six_ref, grad_four, grad_six, sems, sems_four, sems_six = rest
    copies = [
        pltpu.make_async_copy(part, grad_four_ref.at[bounds[index] : bounds[index + 1]], sems.at[index])
        for index, part in enumerate(earlier)
    ]
    for copy in copies:
        copy.start()

    def sender(grad, grad_ref, offset, sems):
        def sent(index, start, end):
            copy = pltpu.make_async_copy(grad.at[start - offset : end - offset], grad_ref.at[start:end], sems.at[index])
            copy.start()
            copies.append(copy)

        return sent

    six_chunks = chunks_of(grad_six.shape[0], 12)
    input_chunks(three_six, turned, grad_six, six_chunks, 0, sender(grad_six, grad_six_ref, 0, sems_six))
    done = bounds[-1]
    input_chunks(three_four, turned, grad_four, chunks, done, sender(grad_four, grad_four_ref, done, sems_four))
    for copy in copies:
        copy.wait()


def swap(array, axis, stride):
    count = lax.axis_size(axis)
    return lax.ppermute(array, axis, [(i, i ^ stride) for i in range(count)])


def edge_kernel(starts, four_ref, six_ref, cotan_four_ref, cotan_six_ref, *rest):
    outs, six_rows, sems = rest[:-2], rest[-2], rest[-1]
    rows_four, cols_four = four_ref.shape[:2]
    rows_six = six_ref.shape[0]
    pitch = pitch_of(six_ref.shape[1])
    copies = []
    for number, (start, out_ref) in enumerate(zip(starts, outs)):
        last = (1 - jnp.minimum(lax.axis_index("sp"), 1)) if start is None else start
        for part, (ref, row) in enumerate(
            (
                (four_ref, last * (rows_four - 2)),
                (four_ref, last * (rows_four - 2) + 1),
                (cotan_four_ref, last * (rows_four - 1)),
                (six_ref, last * (rows_six - 2)),
                (six_ref, last * (rows_six - 2) + 1),
                (cotan_six_ref, last * (rows_six - 1)),
            )
        ):
            if part < 3:
                target = out_ref.at[part * cols_four : (part + 1) * cols_four]
            else:
                target = six_rows.at[number, part - 3]
            copies.append(pltpu.make_async_copy(ref.at[row], target, sems.at[number, part]))
    for copy in copies:
        copy.start()
    for copy in copies:
        copy.wait()
    for number, out_ref in enumerate(outs):
        for part in range(3):
            begin = 3 * cols_four + part * pitch
            out_ref[begin : begin + pitch] = widen(six_rows[number, part], pitch).astype(BF16)


def edges(four, six, cotan_four, cotan_six):
    count = lax.axis_size("sp")
    starts = (None,) if count == 2 else (0, 1)
    length = 3 * four.shape[1] + 3 * pitch_of(six.shape[1])
    vmem = pl.BlockSpec(memory_space=pltpu.VMEM)
    hbm = pl.BlockSpec(memory_space=pltpu.HBM)
    outs = pl.pallas_call(
        functools.partial(edge_kernel, starts),
        out_shape=tuple(jax.ShapeDtypeStruct((length, four.shape[2]), BF16) for _ in starts),
        in_specs=[hbm] * 4,
        out_specs=tuple(vmem for _ in starts),
        scratch_shapes=[
            pltpu.VMEM((len(starts), 3) + six.shape[1:], BF16),
            pltpu.SemaphoreType.DMA((len(starts), 6)),
        ],
        compiler_params=pltpu.CompilerParams(vmem_limit_bytes=EDGE_LIMIT),
        name="edges",
    )(four, six, cotan_four, cotan_six)
    if count == 2:
        met = swap(outs[0], "sp", 1)
        return met, met
    above = lax.ppermute(outs[1], "sp", [(i, (i + 1) % count) for i in range(count)])
    below = lax.ppermute(outs[0], "sp", [((i + 1) % count, i) for i in range(count)])
    return above, below


def swap_across(array, axis, stride):
    count, sp_count = lax.axis_size("rep"), lax.axis_size("sp")
    rep_stride, sp_stride = (stride, 1) if axis == "rep" else (0, stride ^ 1)
    pairs = [
        (rep * sp_count + sp, (rep ^ rep_stride) * sp_count + (sp ^ sp_stride))
        for rep in range(count)
        for sp in range(sp_count)
    ]
    return lax.ppermute(array, ("rep", "sp"), pairs)


def group_sum(sums):
    sums = sums + swap(sums, "sp", 1)
    stride = 2
    while stride < lax.axis_size("sp"):
        sums = sums + swap_across(sums, "sp", stride)
        stride = 2 * stride
    stride = 1
    while stride < GROUP:
        met = [swap_across(sums, "rep", k * stride) for k in FAR_FIRST]
        sums = (sums + met[2]) + (met[1] + met[0])
        stride = RADIX * stride
    return sums


def every_group(sums):
    stride = GROUP
    while stride < lax.axis_size("rep"):
        sums = sums + swap(sums, "rep", stride)
        stride = 2 * stride
    return sums


class Places(NamedTuple):
    digits: list
    first: list
    second: list
    odd: jax.Array


def places():
    rep = lax.axis_index("rep")
    digits = [(rep & (RADIX - 1)) ^ k for k in range(RADIX)]
    second = 9 - FIRST_TAPS
    return Places(
        digits,
        [FIRST_TAPS * digit for digit in digits],
        [RADIX * FIRST_TAPS + second * digit for digit in digits],
        parity(rep) == 1,
    )


def piece_of(pieces, index):
    sizes = (1,) + pieces.shape[1:]
    return lax.dynamic_slice(pieces, (index, 0, 0), sizes, allow_negative_indices=False)[0]


def scatter_pieces(own, met, found):
    chan = own.shape[2]
    parts = [part.reshape(RADIX, -1, chan) for part in [own] + met]

    def piece(k):
        total = piece_of(parts[0], found.digits[k])
        for part in parts[1:]:
            total = total + piece_of(part, found.digits[k]).astype(F32)
        return total

    return piece(0), [piece(k).astype(BF16) for k in FAR_FIRST]


def added(own, met):
    return (own + met[2].astype(F32)) + (met[1].astype(F32) + met[0].astype(F32))


def fours(pieces, stride):
    return [swap(piece, "rep", k * stride) for k, piece in zip(FAR_FIRST, pieces)]


def swap_high(array, even, odd):
    count, sp_count = lax.axis_size("rep"), lax.axis_size("sp")
    pairs = []
    for rep in range(count):
        for sp in range(sp_count):
            stride = odd if (sp ^ parity(rep)) & 1 else even
            pairs.append((rep * sp_count + sp, (rep ^ stride) * sp_count + (sp ^ 1)))
    return lax.ppermute(array, ("rep", "sp"), pairs)


def bring(array, k):
    count, sp_count = lax.axis_size("rep"), lax.axis_size("sp")
    pairs = [
        (rep * sp_count + sp, (rep ^ k) * sp_count + (sp ^ parity(rep)))
        for rep in range(count)
        for sp in range(sp_count)
    ]
    return lax.ppermute(array, ("rep", "sp"), pairs)


def both(own, met):
    return (own.astype(F32) + met.astype(F32)).astype(BF16)


def every_share(total):
    stride = GROUP
    while stride < lax.axis_size("rep"):
        total = added(total.astype(F32), fours([total] * 3, stride)).astype(BF16)
        stride = RADIX * stride
    return total


def gather(total, found):
    beside = swap(total, "sp", 1)
    return [bring(total, k) for k in FAR_FIRST] + [jnp.where(found.odd, beside, total)], beside


def put_pieces(whole, pieces, starts):
    for k, piece in zip(FAR_FIRST + (0,), pieces):
        piece = piece.reshape((-1,) + whole.shape[1:]).astype(F32)
        whole = lax.dynamic_update_slice(whole, piece, (starts[k], 0, 0), allow_negative_indices=False)
    return whole


def local(level_four, level_six, conv_weight, bn_gain, bn_shift, cotan_four, cotan_six):
    sp_count = lax.axis_size("sp")
    images = level_four.shape[0]
    four, six, cot_four, cot_six = (a[0] for a in (level_four, level_six, cotan_four, cotan_six))
    rows_four, cols_four, chan = four.shape
    rows_six, cols_six = six.shape[:2]
    pitch_four, pitch_six = pitch_of(cols_four), pitch_of(cols_six)
    counts = (
        float(images * GROUP * rows_four * sp_count * cols_four),
        float(images * GROUP * rows_six * sp_count * cols_six),
    )
    found, four = lax.optimization_barrier((places(), four))
    above, below = edges(four, six, cot_four, cot_six)
    vmem = pl.BlockSpec(memory_space=pltpu.VMEM)
    hbm = pl.BlockSpec(memory_space=pltpu.HBM)
    params = pltpu.CompilerParams(vmem_limit_bytes=VMEM_LIMIT)
    framed_four = jax.ShapeDtypeStruct((rows_four + 2, pitch_four, chan), BF16)
    framed_six = jax.ShapeDtypeStruct((rows_six + 2, pitch_six, chan), BF16)
    four_sums = jax.ShapeDtypeStruct((4, chan), F32)
    flops = 2 * 9 * chan * chan * (rows_four * cols_four + rows_six * cols_six)

    def cost(share, size):
        return pl.CostEstimate(flops=int(flops * share), bytes_accessed=size, transcendentals=0)

    inner_four, inner_six, inner_moments = pl.pallas_call(
        inner_kernel,
        out_shape=(
            jax.ShapeDtypeStruct((rows_four - 2, pitch_four, chan), BF16),
            jax.ShapeDtypeStruct((rows_six - 2, pitch_six, chan), BF16),
            four_sums,
        ),
        in_specs=[vmem] * 3,
        out_specs=(vmem, vmem, vmem),
        scratch_shapes=[
            pltpu.VMEM((rows_four, pitch_four, 3 * chan), BF16),
            pltpu.VMEM((rows_six, pitch_six, 3 * chan), BF16),
        ],
        compiler_params=params,
        cost_estimate=cost(1, 4 * four.size),
        name="forward_inner",
    )(four, six, conv_weight)
    outer_four, outer_six, moments = pl.pallas_call(
        functools.partial(outer_kernel, sp_count),
        out_shape=(
            jax.ShapeDtypeStruct((4, pitch_four, chan), BF16),
            jax.ShapeDtypeStruct((4, pitch_six, chan), BF16),
            four_sums,
        ),
        in_specs=[vmem] * 6,
        out_specs=(vmem, vmem, vmem),
        scratch_shapes=[
            pltpu.VMEM((8, pitch_four, 3 * chan), BF16),
            pltpu.VMEM((8, pitch_six, 3 * chan), BF16),
        ],
        compiler_params=params,
        cost_estimate=cost(0.1, four.size),
        name="forward_outer",
    )(four, six, above, below, conv_weight, inner_moments)
    moments, four, six = lax.optimization_barrier((moments, four, six))
    turned, turned_weight = pl.pallas_call(
        turn_kernel,
        out_shape=(
            jax.ShapeDtypeStruct((chan, rows_four * cols_four + rows_six * pitch_six), BF16),
            jax.ShapeDtypeStruct((9 * chan, chan), BF16),
        ),
        in_specs=[vmem] * 3,
        out_specs=(vmem, vmem),
        compiler_params=params,
        cost_estimate=cost(0.3, 4 * four.size),
        name="turn",
    )(four, six, conv_weight)
    moments, turned, turned_weight = lax.optimization_barrier((group_sum(moments), turned, turned_weight))

    slope_four, slope_six, slopes = pl.pallas_call(
        functools.partial(slope_kernel, counts),
        out_shape=(
            jax.ShapeDtypeStruct(framed_four.shape, F32),
            jax.ShapeDtypeStruct(framed_six.shape, F32),
            four_sums,
        ),
        in_specs=[vmem] * 11,
        out_specs=(vmem,) * 3,
        compiler_params=params,
        cost_estimate=cost(0.01, 4 * four.size),
        name="slopes",
    )(
        inner_four, inner_six, outer_four, outer_six, cot_four, cot_six, above, below, moments, bn_gain, bn_shift
    )
    slopes = group_sum(slopes)

    share = chan // sp_count
    wide_four, wide_six = (
        jax.ShapeDtypeStruct(framed.shape[:2] + (3 * chan,), BF16) for framed in (framed_four, framed_six)
    )
    def shares(taps):
        return (
            jax.ShapeDtypeStruct((taps, share, chan), F32),
            jax.ShapeDtypeStruct((sp_count - 1, taps, share, chan), BF16),
        )

    three_four, three_six, own_a, sent_a, grad_gain, grad_shift = pl.pallas_call(
        functools.partial(backward_kernel, counts, sp_count, (cols_four, cols_six)),
        out_shape=(wide_four, wide_six) + shares(FIRST_TAPS) + (jax.ShapeDtypeStruct((2, chan), F32),) * 2,
        in_specs=[vmem] * 11,
        out_specs=(vmem,) * 6,
        scratch_shapes=[pltpu.VMEM((chan, FIRST_TAPS * chan), F32)],
        compiler_params=params,
        cost_estimate=cost(0.6, 8 * four.size),
        name="backward",
    )(
        turned, inner_four, inner_six, outer_four, outer_six, slope_four, slope_six, moments, slopes,
        bn_gain, bn_shift,
    )
    sent_a, three_six = lax.optimization_barrier((sent_a, three_six))
    met_a = [swap(sent_a[step], "sp", step + 1) for step in range(sp_count - 1)]
    own_b, sent_b = pl.pallas_call(
        functools.partial(weight_kernel, sp_count),
        out_shape=shares(9 - FIRST_TAPS),
        in_specs=[vmem] * 3,
        out_specs=(vmem, vmem),
        scratch_shapes=[pltpu.VMEM((chan, (9 - FIRST_TAPS) * chan), F32)],
        compiler_params=params,
        cost_estimate=cost(0.6, 8 * four.size),
        name="weights",
    )(turned, three_four, three_six)
    met_a, sent_b = lax.optimization_barrier((met_a, sent_b))
    met_b = [swap(sent_b[step], "sp", step + 1) for step in range(sp_count - 1)]

    chunks = chunks_of(rows_four, 8)
    cuts = [part * len(chunks) // 3 for part in range(4)]
    groups = [chunks[low:high] for low, high in zip(cuts[:-1], cuts[1:]) if low < high]
    bounds = [group[0][0] for group in groups]

    def inputs(group, three):
        return pl.pallas_call(
            functools.partial(input_kernel, group),
            out_shape=jax.ShapeDtypeStruct((group[-1][1] - group[0][0], cols_four, chan), BF16),
            in_specs=[vmem] * 2,
            out_specs=vmem,
            compiler_params=params,
            cost_estimate=cost(0.3, four.size),
            name="inputs",
        )(three, turned_weight)

    grad_gain, grad_shift = every_group(grad_gain), every_group(grad_shift)

    piece_a, pieces_a = scatter_pieces(own_a, met_a, found)
    met_a = fours(pieces_a, 1)
    piece_b, pieces_b = scatter_pieces(own_b, met_b, found)
    met_b = fours(pieces_b, 1)
    met_a, unused = lax.optimization_barrier((met_a, pieces_b))

    piece_a = added(piece_a, met_a).astype(BF16)
    piece_a, three_four = lax.optimization_barrier((piece_a, three_four))
    met_a = swap_high(piece_a, RADIX, 2 * RADIX)
    earlier = [inputs(groups[0], three_four)] if len(groups) > 1 else []
    met_b, earlier = lax.optimization_barrier((met_b, earlier))

    piece_b = added(piece_b, met_b).astype(BF16)
    met_b = swap_high(piece_b, RADIX, 2 * RADIX)
    met_a, unused = lax.optimization_barrier((met_a, piece_b))

    piece_a = both(piece_a, met_a)
    piece_a, three_four = lax.optimization_barrier((piece_a, three_four))
    met_a = swap_high(piece_a, 2 * RADIX, RADIX)
    if len(groups) > 2:
        earlier = earlier + [inputs(groups[1], three_four)]
    met_b, earlier = lax.optimization_barrier((met_b, earlier))

    piece_b = both(piece_b, met_b)
    met_b = swap_high(piece_b, 2 * RADIX, RADIX)
    met_a, unused = lax.optimization_barrier((met_a, piece_b))

    pieces_a, unused = gather(every_share(both(piece_a, met_a)), found)
    piece_b = every_share(both(piece_b, met_b))
    pieces_b, beside = gather(piece_b, found)
    unused, three_four = lax.optimization_barrier((beside, three_four))
    done = bounds[-1]
    grad_four, grad_six = pl.pallas_call(
        functools.partial(input_last_kernel, groups[-1], bounds),
        out_shape=(
            jax.ShapeDtypeStruct(four.shape, BF16),
            jax.ShapeDtypeStruct(six.shape, BF16),
        ),
        in_specs=[vmem] * (3 + len(earlier)),
        out_specs=(hbm, hbm),
        scratch_shapes=[
            pltpu.VMEM((rows_four - done, cols_four, chan), BF16),
            pltpu.VMEM(six.shape, BF16),
            pltpu.SemaphoreType.DMA((len(groups),)),
            pltpu.SemaphoreType.DMA((len(chunks),)),
            pltpu.SemaphoreType.DMA((len(chunks_of(rows_six, 12)),)),
        ],
        compiler_params=params,
        cost_estimate=cost(0.4, 2 * four.size),
        name="inputs_last",
    )(three_four, three_six, turned_weight, *earlier)
    pieces_a, pieces_b, grad_six = lax.optimization_barrier((pieces_a, pieces_b, grad_six))
    whole = jnp.zeros((9 * RADIX, share // RADIX, chan), F32)
    whole = put_pieces(whole, pieces_a, found.first)
    whole = put_pieces(whole, pieces_b, found.second)
    grad_weight = whole.reshape(9, share, chan)
    return (grad_four[None], grad_six[None], grad_weight, grad_gain, grad_shift)


def solution(mesh):
    placed = (
        P("rep", "sp", None, None),
        P("rep", "sp", None, None),
        P(),
        P(),
        P(),
        P("rep", "sp", None, None),
        P("rep", "sp", None, None),
    )
    return jax.shard_map(
        local,
        mesh=mesh,
        in_specs=placed,
        out_specs=(
            P("rep", "sp", None, None),
            P("rep", "sp", None, None),
            P(None, "sp", None),
            P(),
            P(),
        ),
        check_vma=False,
    )
```

```python
import functools
from typing import NamedTuple

import jax
import jax.numpy as jnp
from jax import lax
from jax.experimental import pallas as pl
from jax.experimental.pallas import tpu as pltpu
from jax.sharding import PartitionSpec as P

GROUP = 16
RADIX = 4
FAR_FIRST = (3, 2, 1)
FIRST_TAPS = 4
EARLY_TAPS = 6
EPSILON = 1e-05
F32 = jnp.float32
BF16 = jnp.bfloat16
VMEM_LIMIT = 20 * 1024 * 1024
EDGE_LIMIT = 60 * 1024 * 1024


def chunk_of(rows, most, multiple=1):
    sizes = [size for size in range(1, most + 1) if rows % size == 0 and size % multiple == 0]
    return max(sizes) if sizes else rows


def pitch_of(cols):
    return -(-cols // 16) * 16


def parity(rep):
    return ((rep >> 2) ^ (rep >> 3)) & 1


def chunks_of(rows, most, multiple=1):
    size = chunk_of(rows, most, multiple)
    return [(start, start + size) for start in range(0, rows, size)]


def widen(cells, pitch):
    cells = cells.astype(F32)
    extra = pitch - cells.shape[0]
    if extra:
        cells = jnp.concatenate([cells, jnp.zeros((extra, cells.shape[1]), F32)], 0)
    return cells


def put_three(three, row, cells, cols, turned):
    pitch, chan = cells.shape
    left, right = pltpu.roll(cells, 1, 0), pltpu.roll(cells, pitch - 1, 0)
    if pitch == cols:
        col = lax.broadcasted_iota(jnp.int32, (8, chan), 0)
        left = jnp.concatenate([jnp.where(col == 0, 0.0, left[:8]), left[8:]], 0)
        right = jnp.concatenate([right[:-8], jnp.where(col == 7, 0.0, right[-8:])], 0)
    parts = (right, cells, left) if turned else (left, cells, right)
    for place, part in enumerate(parts):
        three[row, :, place * chan : (place + 1) * chan] = part.astype(BF16)


def beside(three, starts, size):
    pitch, width = three.shape[1:]
    return jnp.concatenate([three[start : start + size].reshape(size * pitch, width) for start in starts], 1)


def edges_valid(sp_count):
    index = lax.axis_index("sp")
    return jnp.where(index > 0, 1.0, 0.0), jnp.where(index < sp_count - 1, 1.0, 0.0)


def level_coefs(moments, gain, shift, count):
    mean = moments[0:1] / count
    spread = moments[1:2] / count - mean * mean
    return mean, lax.rsqrt(spread + EPSILON), gain, shift


def slope_of(conv, cotan, coefs):
    mean, rstd, gain, shift = coefs
    centred = conv.astype(F32) - mean
    half = centred * (0.5 * rstd * gain) + 0.5 * shift
    turn = jnp.tanh(half)
    return centred, cotan.astype(F32) * ((1.0 + turn) * (1.0 + half * (1.0 - turn)))


def masked(cells, cols):
    if cells.shape[0] == cols:
        return cells
    col = lax.broadcasted_iota(jnp.int32, cells.shape, 0)
    return jnp.where(col < cols, cells, 0.0)


def staged(fills, dots):
    fills[0]()
    for index, dot in enumerate(dots):
        if index + 1 < len(fills):
            fills[index + 1]()
        dot()


def conv_rows(three, starts, size, w_ref):
    pitch, width = three.shape[1:]
    lhs = [beside(three, (start, start + 1, start + 2), size) for start in starts]
    lhs = jnp.concatenate(lhs, 0) if len(lhs) > 1 else lhs[0]
    conv = jnp.dot(lhs, w_ref[...].reshape(3 * width, -1), preferred_element_type=F32).astype(BF16)
    return conv.reshape(len(starts) * size, pitch, -1)


def add_moments(sums, conv, cols):
    chan = conv.shape[2]
    conv = conv.astype(F32)
    if conv.shape[1] != cols:
        conv = conv[:, :cols]
    conv = conv.reshape(-1, 8, chan)
    sums[0].append(jnp.sum(conv, 0))
    sums[1].append(jnp.sum(conv * conv, 0))


def folded(parts):
    total = parts[0]
    for part in parts[1:]:
        total = total + part
    return jnp.sum(total, 0, keepdims=True)


def inner_level(x_ref, w_ref, conv_ref, three, sums, most):
    rows, cols = x_ref.shape[:2]
    pitch = three.shape[1]

    def fill_row(row):
        put_three(three, row, widen(x_ref[row], pitch), cols, False)

    def dot(start, end):
        conv = conv_rows(three, (start,), end - start, w_ref)
        conv_ref[start:end] = conv
        add_moments(sums, conv, cols)

    inner = rows - 2
    count = max(1, inner // most)
    bounds = [index * inner // count for index in range(count + 1)]
    fills, dots, done = [], [], 0
    for start, end in zip(bounds[:-1], bounds[1:]):
        fills.append(lambda todo=range(done, end + 2): [fill_row(row) for row in todo])
        done = end + 2
        dots.append(functools.partial(dot, start, end))
    return fills, dots


def inner_kernel(four_ref, six_ref, w_ref, conv_four_ref, conv_six_ref, moments_ref, three_four, three_six):
    sums_four, sums_six = ([], []), ([], [])
    fills_six, dots_six = inner_level(six_ref, w_ref, conv_six_ref, three_six, sums_six, 10)
    fills_four, dots_four = inner_level(four_ref, w_ref, conv_four_ref, three_four, sums_four, 8)
    staged(fills_six + fills_four, dots_six + dots_four)
    moments_ref[...] = jnp.concatenate([folded(parts) for parts in sums_four + sums_six], 0)


def outer_level(x_ref, top, bottom, valid, w_ref, conv_ref, three, sums):
    rows, cols = x_ref.shape[:2]
    pitch = three.shape[1]
    for edge in range(2):
        put_three(three, edge, top(edge) * valid[0], cols, False)
        put_three(three, 2 + edge, widen(x_ref[edge], pitch), cols, False)
        put_three(three, 4 + edge, widen(x_ref[rows - 2 + edge], pitch), cols, False)
        put_three(three, 6 + edge, bottom(edge) * valid[1], cols, False)
    conv = conv_rows(three, (0, 4), 2, w_ref)
    conv_ref[...] = conv
    add_moments(sums, conv[1:3], cols)


def outer_kernel(
    sp_count, four_ref, six_ref, above_ref, below_ref, w_ref, inner_ref,
    conv_four_ref, conv_six_ref, moments_ref, three_four, three_six,
):
    cols_four = four_ref.shape[1]
    valid = edges_valid(sp_count)
    base, pitch_six = 3 * cols_four, three_six.shape[1]

    def reader(ref, start, pitch):
        return lambda edge: ref[start + edge * pitch : start + (edge + 1) * pitch].astype(F32)

    sums_four, sums_six = ([], []), ([], [])
    outer_level(
        six_ref, reader(above_ref, base, pitch_six), reader(below_ref, base, pitch_six), valid, w_ref,
        conv_six_ref, three_six, sums_six,
    )
    outer_level(
        four_ref, reader(above_ref, 0, cols_four), reader(below_ref, 0, cols_four), valid, w_ref,
        conv_four_ref, three_four, sums_four,
    )
    sums = [folded(parts) for parts in sums_four + sums_six]
    moments_ref[...] = inner_ref[...] + jnp.concatenate(sums, 0)


def turn_kernel(four_ref, six_ref, w_ref, turned_ref, turned_w_ref):
    rows_four, cols_four, chan = four_ref.shape
    rows_six, cols_six = six_ref.shape[:2]
    pitch = pitch_of(cols_six)
    for start, end in chunks_of(rows_four, 8, 4):
        cells = four_ref[start:end].reshape((end - start) * cols_four, chan)
        turned_ref[:, start * cols_four : end * cols_four] = cells.T
    cells = six_ref[...].astype(F32)
    cells = jnp.concatenate([cells, jnp.zeros((rows_six, pitch - cols_six, chan), F32)], 1).astype(BF16)
    turned_ref[:, rows_four * cols_four :] = cells.reshape(rows_six * pitch, chan).T
    for tap in range(9):
        turned_w_ref[tap * chan : (tap + 1) * chan] = w_ref[tap].T


def slope_level(inner_ref, outer_ref, cotan_ref, above, below, coefs, slope_ref):
    rows, cols, chan = cotan_ref.shape
    pitch = inner_ref.shape[1]

    def put(row, conv, cotan):
        centred, slope = slope_of(conv, widen(cotan, pitch), coefs)
        slope_ref[row] = slope
        return centred, slope

    def add(sums, pair):
        centred, slope = pair
        first = jnp.sum(slope.reshape(-1, 8, chan), 0)
        second = jnp.sum((slope * centred).reshape(-1, 8, chan), 0)
        return sums[0] + first, sums[1] + second

    def step(row, sums):
        return add(sums, put(row + 2, inner_ref[row], cotan_ref[row + 1]))

    put(0, outer_ref[0], above)
    put(rows + 1, outer_ref[3], below)
    zero = jnp.zeros((8, chan), F32)
    sums = add((zero, zero), put(1, outer_ref[1], cotan_ref[0]))
    sums = add(sums, put(rows, outer_ref[2], cotan_ref[rows - 1]))
    looped = (rows - 2) // 8 * 8
    if looped:
        sums = lax.fori_loop(0, looped, step, sums, unroll=8)
    for row in range(looped, rows - 2):
        sums = step(row, sums)
    first = 0.5 * jnp.sum(sums[0], 0, keepdims=True)
    return first, 0.5 * coefs[1] * jnp.sum(sums[1], 0, keepdims=True)


def slope_kernel(
    counts, inner_four_ref, inner_six_ref, outer_four_ref, outer_six_ref, cotan_four_ref, cotan_six_ref,
    above_ref, below_ref, moments_ref, gain_ref, shift_ref, slope_four_ref, slope_six_ref, slopes_ref,
):
    sums = ()
    cols_four = cotan_four_ref.shape[1]
    starts = (2 * cols_four, 3 * cols_four + 2 * inner_six_ref.shape[1])
    for level, (inner_ref, outer_ref, cotan_ref, slope_ref) in enumerate(
        (
            (inner_four_ref, outer_four_ref, cotan_four_ref, slope_four_ref),
            (inner_six_ref, outer_six_ref, cotan_six_ref, slope_six_ref),
        )
    ):
        pair = moments_ref[2 * level : 2 * level + 2]
        here = slice(level, level + 1)
        edge = slice(starts[level], starts[level] + inner_ref.shape[1])
        coefs = level_coefs(pair, gain_ref[here], shift_ref[here], counts[level])
        sums += slope_level(inner_ref, outer_ref, cotan_ref, above_ref[edge], below_ref[edge], coefs, slope_ref)
    slopes_ref[...] = jnp.concatenate(sums, 0)


def backward_level(cols, inner_ref, outer_ref, slope_ref, valid, coefs, slopes, count, three):
    rows = inner_ref.shape[0] + 2
    pitch = three.shape[1]
    mean, rstd, gain, shift = coefs
    lead = gain * rstd
    offset, factor = lead * (slopes[0:1] / count), lead * rstd * (slopes[1:2] / count)

    def fill_row(row):
        if 2 <= row < rows:
            conv = inner_ref[row - 2]
        else:
            conv = outer_ref[row if row < 2 else row - rows + 2]
        centred = conv.astype(F32) - mean
        dconv = masked((0.5 * lead) * slope_ref[row] - (offset + centred * factor), cols)
        if row == 0:
            dconv = dconv * valid[0]
        elif row == rows + 1:
            dconv = dconv * valid[1]
        put_three(three, row, dconv, cols, True)

    return fill_row


def taps_beside(three, start, end, taps):
    pitch, width = three.shape[1:]
    chan = width // 3
    parts = []
    for row_tap in range(3):
        low, high = max(taps[0] - 3 * row_tap, 0), min(taps[1] - 3 * row_tap, 3)
        if low < high:
            first = start + 2 - row_tap
            rows = three[first : first + end - start, :, low * chan : high * chan]
            parts.append(rows.reshape((end - start) * pitch, (high - low) * chan))
    return jnp.concatenate(parts, 1)


def backward_bounds(rows):
    bounds = [0, min(8, rows)]
    while bounds[-1] < rows:
        bounds.append(min(bounds[-1] + 16, rows))
    return bounds


def weight_dot(turned_ref, three_four, three_six, total, taps, start, end):
    rows_four, rows_six = three_four.shape[0] - 2, three_six.shape[0] - 2
    pitch = three_four.shape[1]
    first, last = start * pitch, end * pitch
    rhs = taps_beside(three_four, start, end, taps)
    if end == rows_four:
        rhs = jnp.concatenate([rhs, taps_beside(three_six, 0, rows_six, taps)], 0)
        last = turned_ref.shape[1]
    term = jnp.dot(turned_ref[:, first:last], rhs, preferred_element_type=F32)
    total[...] = total[...] + term if start else term


def put_shares(totals, sp_count, own_ref, sent_ref):
    taps, share, chan = own_ref.shape
    places = [(total, start) for total in totals for start in range(0, total.shape[1], chan)][:taps]
    place = lax.axis_index("sp") ^ parity(lax.axis_index("rep"))
    for step in range(sp_count):
        begin = pl.multiple_of((place ^ step) * share, share)
        for tap, (total, start) in enumerate(places):
            part = total[pl.ds(begin, share), start : start + chan]
            if step == 0:
                own_ref[tap] = part
            else:
                sent_ref[step - 1, tap] = part.astype(BF16)


def backward_kernel(
    counts, sp_count, cols, turned_ref, inner_four_ref, inner_six_ref, outer_four_ref, outer_six_ref,
    slope_four_ref, slope_six_ref, moments_ref, slopes_ref, gain_ref, shift_ref, three_four, three_six, own_ref,
    sent_ref, rest_ref, grad_gain_ref, grad_shift_ref, total,
):
    valid = edges_valid(sp_count)
    grad_gain_ref[...] = jnp.concatenate([slopes_ref[1:2], slopes_ref[3:4]], 0)
    grad_shift_ref[...] = jnp.concatenate([slopes_ref[0:1], slopes_ref[2:3]], 0)
    parts = []
    for level, inner_ref, outer_ref, slope_ref, three in (
        (0, inner_four_ref, outer_four_ref, slope_four_ref, three_four),
        (1, inner_six_ref, outer_six_ref, slope_six_ref, three_six),
    ):
        here = slice(level, level + 1)
        pair = slice(2 * level, 2 * level + 2)
        coefs = level_coefs(moments_ref[pair], gain_ref[here], shift_ref[here], counts[level])
        parts.append(
            backward_level(
                cols[level], inner_ref, outer_ref, slope_ref, valid, coefs, slopes_ref[pair], counts[level], three
            )
        )
    fill_four, fill_six = parts
    rows_four, rows_six = three_four.shape[0] - 2, three_six.shape[0] - 2
    bounds = backward_bounds(rows_four)
    fills, dots, done = [], [], 0
    for start, end in zip(bounds[:-1], bounds[1:]):
        todo = [functools.partial(fill_four, row) for row in range(done, end + 2)]
        if end == rows_four:
            todo += [functools.partial(fill_six, row) for row in range(rows_six + 2)]
        fills.append(lambda todo=todo: [fill() for fill in todo])
        done = end + 2
        dots.append(
            functools.partial(weight_dot, turned_ref, three_four, three_six, total, (0, EARLY_TAPS), start, end)
        )
    staged(fills, dots)
    put_shares([total], sp_count, own_ref, sent_ref)
    rest_ref[...] = total[:, FIRST_TAPS * rest_ref.shape[0] :]


def weight_kernel(sp_count, turned_ref, three_four, three_six, rest_ref, own_ref, sent_ref, total):
    for start, end in chunks_of(three_four.shape[0] - 2, 16, 4):
        weight_dot(turned_ref, three_four, three_six, total, (EARLY_TAPS, 9), start, end)
    put_shares([rest_ref, total], sp_count, own_ref, sent_ref)


def input_chunks(three, turned, grad, chunks, offset, sent=None):
    cols, chan = grad.shape[1:]
    pitch = three.shape[1]
    for index, (start, end) in enumerate(chunks):
        size = end - start
        lhs = beside(three, (start + 2, start + 1, start), size)
        term = jnp.dot(lhs, turned[...], preferred_element_type=F32)
        grad[start - offset : end - offset] = term.reshape(size, pitch, chan)[:, :cols].astype(BF16)
        if sent is not None:
            sent(index, start, end)


def input_kernel(chunks, three_four, turned, grad_ref):
    input_chunks(three_four, turned, grad_ref, chunks, chunks[0][0])


def input_last_kernel(chunks, bounds, three_four, three_six, turned, *rest):
    count = len(bounds) - 1
    earlier, rest = rest[:count], rest[count:]
    grad_four_ref, grad_six_ref, grad_four, grad_six, sems, sems_four, sems_six = rest
    copies = [
        pltpu.make_async_copy(part, grad_four_ref.at[bounds[index] : bounds[index + 1]], sems.at[index])
        for index, part in enumerate(earlier)
    ]
    for copy in copies:
        copy.start()

    def sender(grad, grad_ref, offset, sems):
        def sent(index, start, end):
            copy = pltpu.make_async_copy(grad.at[start - offset : end - offset], grad_ref.at[start:end], sems.at[index])
            copy.start()
            copies.append(copy)

        return sent

    six_chunks = chunks_of(grad_six.shape[0], 12)
    input_chunks(three_six, turned, grad_six, six_chunks, 0, sender(grad_six, grad_six_ref, 0, sems_six))
    done = bounds[-1]
    input_chunks(three_four, turned, grad_four, chunks, done, sender(grad_four, grad_four_ref, done, sems_four))
    for copy in copies:
        copy.wait()


def swap(array, axis, stride):
    count = lax.axis_size(axis)
    return lax.ppermute(array, axis, [(i, i ^ stride) for i in range(count)])


def edge_kernel(starts, four_ref, six_ref, cotan_four_ref, cotan_six_ref, *rest):
    outs, six_rows, sems = rest[:-2], rest[-2], rest[-1]
    rows_four, cols_four = four_ref.shape[:2]
    rows_six = six_ref.shape[0]
    pitch = pitch_of(six_ref.shape[1])
    copies = []
    for number, (start, out_ref) in enumerate(zip(starts, outs)):
        last = (1 - jnp.minimum(lax.axis_index("sp"), 1)) if start is None else start
        for part, (ref, row) in enumerate(
            (
                (four_ref, last * (rows_four - 2)),
                (four_ref, last * (rows_four - 2) + 1),
                (cotan_four_ref, last * (rows_four - 1)),
                (six_ref, last * (rows_six - 2)),
                (six_ref, last * (rows_six - 2) + 1),
                (cotan_six_ref, last * (rows_six - 1)),
            )
        ):
            if part < 3:
                target = out_ref.at[part * cols_four : (part + 1) * cols_four]
            else:
                target = six_rows.at[number, part - 3]
            copies.append(pltpu.make_async_copy(ref.at[row], target, sems.at[number, part]))
    for copy in copies:
        copy.start()
    for copy in copies:
        copy.wait()
    for number, out_ref in enumerate(outs):
        for part in range(3):
            begin = 3 * cols_four + part * pitch
            out_ref[begin : begin + pitch] = widen(six_rows[number, part], pitch).astype(BF16)


def edges(four, six, cotan_four, cotan_six):
    count = lax.axis_size("sp")
    starts = (None,) if count == 2 else (0, 1)
    length = 3 * four.shape[1] + 3 * pitch_of(six.shape[1])
    vmem = pl.BlockSpec(memory_space=pltpu.VMEM)
    hbm = pl.BlockSpec(memory_space=pltpu.HBM)
    outs = pl.pallas_call(
        functools.partial(edge_kernel, starts),
        out_shape=tuple(jax.ShapeDtypeStruct((length, four.shape[2]), BF16) for _ in starts),
        in_specs=[hbm] * 4,
        out_specs=tuple(vmem for _ in starts),
        scratch_shapes=[
            pltpu.VMEM((len(starts), 3) + six.shape[1:], BF16),
            pltpu.SemaphoreType.DMA((len(starts), 6)),
        ],
        compiler_params=pltpu.CompilerParams(vmem_limit_bytes=EDGE_LIMIT),
        name="edges",
    )(four, six, cotan_four, cotan_six)
    if count == 2:
        met = swap(outs[0], "sp", 1)
        return met, met
    above = lax.ppermute(outs[1], "sp", [(i, (i + 1) % count) for i in range(count)])
    below = lax.ppermute(outs[0], "sp", [((i + 1) % count, i) for i in range(count)])
    return above, below


def swap_across(array, axis, stride):
    count, sp_count = lax.axis_size("rep"), lax.axis_size("sp")
    rep_stride, sp_stride = (stride, 1) if axis == "rep" else (0, stride ^ 1)
    pairs = [
        (rep * sp_count + sp, (rep ^ rep_stride) * sp_count + (sp ^ sp_stride))
        for rep in range(count)
        for sp in range(sp_count)
    ]
    return lax.ppermute(array, ("rep", "sp"), pairs)


def group_sum(sums):
    sums = sums + swap(sums, "sp", 1)
    stride = 2
    while stride < lax.axis_size("sp"):
        sums = sums + swap_across(sums, "sp", stride)
        stride = 2 * stride
    stride = 1
    while stride < GROUP:
        met = lax.optimization_barrier([swap_across(sums, "rep", k * stride) for k in FAR_FIRST])
        sums = (sums + met[2]) + (met[1] + met[0])
        stride = RADIX * stride
    return sums


def every_group(sums):
    stride = GROUP
    while stride < lax.axis_size("rep"):
        sums = sums + swap(sums, "rep", stride)
        stride = 2 * stride
    return sums


class Places(NamedTuple):
    digits: list
    first: list
    second: list
    odd: jax.Array


def places():
    rep = lax.axis_index("rep")
    digits = [(rep & (RADIX - 1)) ^ k for k in range(RADIX)]
    second = 9 - FIRST_TAPS
    return Places(
        digits,
        [FIRST_TAPS * digit for digit in digits],
        [RADIX * FIRST_TAPS + second * digit for digit in digits],
        parity(rep) == 1,
    )


def piece_of(pieces, index):
    sizes = (1,) + pieces.shape[1:]
    return lax.dynamic_slice(pieces, (index, 0, 0), sizes, allow_negative_indices=False)[0]


def scatter_pieces(own, met, found):
    chan = own.shape[2]
    parts = [part.reshape(RADIX, -1, chan) for part in [own] + met]

    def piece(k):
        total = piece_of(parts[0], found.digits[k])
        for part in parts[1:]:
            total = total + piece_of(part, found.digits[k]).astype(F32)
        return total

    return piece(0), [piece(k).astype(BF16) for k in FAR_FIRST]


def added(own, met):
    return (own + met[2].astype(F32)) + (met[1].astype(F32) + met[0].astype(F32))


def fours(pieces, stride):
    return [swap(piece, "rep", k * stride) for k, piece in zip(FAR_FIRST, pieces)]


def swap_high(array, even, odd):
    count, sp_count = lax.axis_size("rep"), lax.axis_size("sp")
    pairs = []
    for rep in range(count):
        for sp in range(sp_count):
            stride = odd if (sp ^ parity(rep)) & 1 else even
            pairs.append((rep * sp_count + sp, (rep ^ stride) * sp_count + (sp ^ 1)))
    return lax.ppermute(array, ("rep", "sp"), pairs)


def bring(array, k):
    count, sp_count = lax.axis_size("rep"), lax.axis_size("sp")
    pairs = [
        (rep * sp_count + sp, (rep ^ k) * sp_count + (sp ^ parity(rep)))
        for rep in range(count)
        for sp in range(sp_count)
    ]
    return lax.ppermute(array, ("rep", "sp"), pairs)


def both(own, met):
    return (own.astype(F32) + met.astype(F32)).astype(BF16)


def every_share(total):
    stride = GROUP
    while stride < lax.axis_size("rep"):
        total = added(total.astype(F32), fours([total] * 3, stride)).astype(BF16)
        stride = RADIX * stride
    return total


def gather(total, found):
    beside = swap(total, "sp", 1)
    return [bring(total, k) for k in FAR_FIRST] + [jnp.where(found.odd, beside, total)], beside


def put_pieces(whole, pieces, starts):
    for k, piece in zip(FAR_FIRST + (0,), pieces):
        piece = piece.reshape((-1,) + whole.shape[1:]).astype(F32)
        whole = lax.dynamic_update_slice(whole, piece, (starts[k], 0, 0), allow_negative_indices=False)
    return whole


def local(level_four, level_six, conv_weight, bn_gain, bn_shift, cotan_four, cotan_six):
    sp_count = lax.axis_size("sp")
    images = level_four.shape[0]
    four, six, cot_four, cot_six = (a[0] for a in (level_four, level_six, cotan_four, cotan_six))
    rows_four, cols_four, chan = four.shape
    rows_six, cols_six = six.shape[:2]
    pitch_four, pitch_six = pitch_of(cols_four), pitch_of(cols_six)
    counts = (
        float(images * GROUP * rows_four * sp_count * cols_four),
        float(images * GROUP * rows_six * sp_count * cols_six),
    )
    found, four = lax.optimization_barrier((places(), four))
    above, below = edges(four, six, cot_four, cot_six)
    vmem = pl.BlockSpec(memory_space=pltpu.VMEM)
    hbm = pl.BlockSpec(memory_space=pltpu.HBM)
    params = pltpu.CompilerParams(vmem_limit_bytes=VMEM_LIMIT)
    framed_four = jax.ShapeDtypeStruct((rows_four + 2, pitch_four, chan), BF16)
    framed_six = jax.ShapeDtypeStruct((rows_six + 2, pitch_six, chan), BF16)
    four_sums = jax.ShapeDtypeStruct((4, chan), F32)
    flops = 2 * 9 * chan * chan * (rows_four * cols_four + rows_six * cols_six)

    def cost(share, size):
        return pl.CostEstimate(flops=int(flops * share), bytes_accessed=size, transcendentals=0)

    inner_four, inner_six, inner_moments = pl.pallas_call(
        inner_kernel,
        out_shape=(
            jax.ShapeDtypeStruct((rows_four - 2, pitch_four, chan), BF16),
            jax.ShapeDtypeStruct((rows_six - 2, pitch_six, chan), BF16),
            four_sums,
        ),
        in_specs=[vmem] * 3,
        out_specs=(vmem, vmem, vmem),
        scratch_shapes=[
            pltpu.VMEM((rows_four, pitch_four, 3 * chan), BF16),
            pltpu.VMEM((rows_six, pitch_six, 3 * chan), BF16),
        ],
        compiler_params=params,
        cost_estimate=cost(1, 4 * four.size),
        name="forward_inner",
    )(four, six, conv_weight)
    outer_four, outer_six, moments = pl.pallas_call(
        functools.partial(outer_kernel, sp_count),
        out_shape=(
            jax.ShapeDtypeStruct((4, pitch_four, chan), BF16),
            jax.ShapeDtypeStruct((4, pitch_six, chan), BF16),
            four_sums,
        ),
        in_specs=[vmem] * 6,
        out_specs=(vmem, vmem, vmem),
        scratch_shapes=[
            pltpu.VMEM((8, pitch_four, 3 * chan), BF16),
            pltpu.VMEM((8, pitch_six, 3 * chan), BF16),
        ],
        compiler_params=params,
        cost_estimate=cost(0.1, four.size),
        name="forward_outer",
    )(four, six, above, below, conv_weight, inner_moments)
    moments, four, six = lax.optimization_barrier((moments, four, six))
    turned, turned_weight = pl.pallas_call(
        turn_kernel,
        out_shape=(
            jax.ShapeDtypeStruct((chan, rows_four * cols_four + rows_six * pitch_six), BF16),
            jax.ShapeDtypeStruct((9 * chan, chan), BF16),
        ),
        in_specs=[vmem] * 3,
        out_specs=(vmem, vmem),
        compiler_params=params,
        cost_estimate=cost(0.3, 4 * four.size),
        name="turn",
    )(four, six, conv_weight)
    moments, turned, turned_weight = lax.optimization_barrier((group_sum(moments), turned, turned_weight))

    slope_four, slope_six, slopes = pl.pallas_call(
        functools.partial(slope_kernel, counts),
        out_shape=(
            jax.ShapeDtypeStruct(framed_four.shape, F32),
            jax.ShapeDtypeStruct(framed_six.shape, F32),
            four_sums,
        ),
        in_specs=[vmem] * 11,
        out_specs=(vmem,) * 3,
        compiler_params=params,
        cost_estimate=cost(0.01, 4 * four.size),
        name="slopes",
    )(
        inner_four, inner_six, outer_four, outer_six, cot_four, cot_six, above, below, moments, bn_gain, bn_shift
    )
    slopes = group_sum(slopes)

    share = chan // sp_count
    wide_four, wide_six = (
        jax.ShapeDtypeStruct(framed.shape[:2] + (3 * chan,), BF16) for framed in (framed_four, framed_six)
    )
    def shares(taps):
        return (
            jax.ShapeDtypeStruct((taps, share, chan), F32),
            jax.ShapeDtypeStruct((sp_count - 1, taps, share, chan), BF16),
        )

    three_four, three_six, own_a, sent_a, rest, grad_gain, grad_shift = pl.pallas_call(
        functools.partial(backward_kernel, counts, sp_count, (cols_four, cols_six)),
        out_shape=(wide_four, wide_six)
        + shares(FIRST_TAPS)
        + (jax.ShapeDtypeStruct((chan, (EARLY_TAPS - FIRST_TAPS) * chan), F32),)
        + (jax.ShapeDtypeStruct((2, chan), F32),) * 2,
        in_specs=[vmem] * 11,
        out_specs=(vmem,) * 7,
        scratch_shapes=[pltpu.VMEM((chan, EARLY_TAPS * chan), F32)],
        compiler_params=params,
        cost_estimate=cost(0.6, 8 * four.size),
        name="backward",
    )(
        turned, inner_four, inner_six, outer_four, outer_six, slope_four, slope_six, moments, slopes,
        bn_gain, bn_shift,
    )
    sent_a, three_six = lax.optimization_barrier((sent_a, three_six))
    met_a = [swap(sent_a[step], "sp", step + 1) for step in range(sp_count - 1)]
    own_b, sent_b = pl.pallas_call(
        functools.partial(weight_kernel, sp_count),
        out_shape=shares(9 - FIRST_TAPS),
        in_specs=[vmem] * 4,
        out_specs=(vmem, vmem),
        scratch_shapes=[pltpu.VMEM((chan, (9 - EARLY_TAPS) * chan), F32)],
        compiler_params=params,
        cost_estimate=cost(0.6, 8 * four.size),
        name="weights",
    )(turned, three_four, three_six, rest)
    met_a, sent_b = lax.optimization_barrier((met_a, sent_b))
    met_b = [swap(sent_b[step], "sp", step + 1) for step in range(sp_count - 1)]

    chunks = chunks_of(rows_four, 8)
    cuts = [part * len(chunks) // 3 for part in range(4)]
    groups = [chunks[low:high] for low, high in zip(cuts[:-1], cuts[1:]) if low < high]
    bounds = [group[0][0] for group in groups]

    def inputs(group, three):
        return pl.pallas_call(
            functools.partial(input_kernel, group),
            out_shape=jax.ShapeDtypeStruct((group[-1][1] - group[0][0], cols_four, chan), BF16),
            in_specs=[vmem] * 2,
            out_specs=vmem,
            compiler_params=params,
            cost_estimate=cost(0.3, four.size),
            name="inputs",
        )(three, turned_weight)

    grad_gain, grad_shift = every_group(grad_gain), every_group(grad_shift)

    piece_a, pieces_a = scatter_pieces(own_a, met_a, found)
    met_a = fours(pieces_a, 1)
    piece_b, pieces_b = scatter_pieces(own_b, met_b, found)
    met_b = fours(pieces_b, 1)
    met_a, unused = lax.optimization_barrier((met_a, pieces_b))

    piece_a = added(piece_a, met_a).astype(BF16)
    piece_a, three_four = lax.optimization_barrier((piece_a, three_four))
    met_a = swap_high(piece_a, RADIX, 2 * RADIX)
    earlier = [inputs(groups[0], three_four)] if len(groups) > 1 else []
    met_b, earlier = lax.optimization_barrier((met_b, earlier))

    piece_b = added(piece_b, met_b).astype(BF16)
    met_b = swap_high(piece_b, RADIX, 2 * RADIX)
    met_a, unused = lax.optimization_barrier((met_a, piece_b))

    piece_a = both(piece_a, met_a)
    piece_a, three_four = lax.optimization_barrier((piece_a, three_four))
    met_a = swap_high(piece_a, 2 * RADIX, RADIX)
    if len(groups) > 2:
        earlier = earlier + [inputs(groups[1], three_four)]
    met_b, earlier = lax.optimization_barrier((met_b, earlier))

    piece_b = both(piece_b, met_b)
    met_b = swap_high(piece_b, 2 * RADIX, RADIX)
    met_a, unused = lax.optimization_barrier((met_a, piece_b))

    piece_a = every_share(both(piece_a, met_a))
    pieces_a, unused = gather(piece_a, found)
    piece_b = every_share(both(piece_b, met_b))
    pieces_b, beside = gather(piece_b, found)
    unused, three_four = lax.optimization_barrier((beside, three_four))
    done = bounds[-1]
    grad_four, grad_six = pl.pallas_call(
        functools.partial(input_last_kernel, groups[-1], bounds),
        out_shape=(
            jax.ShapeDtypeStruct(four.shape, BF16),
            jax.ShapeDtypeStruct(six.shape, BF16),
        ),
        in_specs=[vmem] * (3 + len(earlier)),
        out_specs=(hbm, hbm),
        scratch_shapes=[
            pltpu.VMEM((rows_four - done, cols_four, chan), BF16),
            pltpu.VMEM(six.shape, BF16),
            pltpu.SemaphoreType.DMA((len(groups),)),
            pltpu.SemaphoreType.DMA((len(chunks),)),
            pltpu.SemaphoreType.DMA((len(chunks_of(rows_six, 12)),)),
        ],
        compiler_params=params,
        cost_estimate=cost(0.4, 2 * four.size),
        name="inputs_last",
    )(three_four, three_six, turned_weight, *earlier)
    pieces_a, pieces_b, grad_six = lax.optimization_barrier((pieces_a, pieces_b, grad_six))
    whole = jnp.zeros((9 * RADIX, share // RADIX, chan), F32)
    whole = put_pieces(whole, pieces_a, found.first)
    whole = put_pieces(whole, pieces_b, found.second)
    grad_weight = whole.reshape(9, share, chan)
    return (grad_four[None], grad_six[None], grad_weight, grad_gain, grad_shift)


def solution(mesh):
    placed = (
        P("rep", "sp", None, None),
        P("rep", "sp", None, None),
        P(),
        P(),
        P(),
        P("rep", "sp", None, None),
        P("rep", "sp", None, None),
    )
    return jax.shard_map(
        local,
        mesh=mesh,
        in_specs=placed,
        out_specs=(
            P("rep", "sp", None, None),
            P("rep", "sp", None, None),
            P(None, "sp", None),
            P(),
            P(),
        ),
        check_vma=False,
    )
```

```python
import functools
from typing import NamedTuple

import jax
import jax.numpy as jnp
from jax import lax
from jax.experimental import pallas as pl
from jax.experimental.pallas import tpu as pltpu
from jax.sharding import PartitionSpec as P

GROUP = 16
RADIX = 4
FAR_FIRST = (3, 2, 1)
FIRST_TAPS = 4
EARLY_TAPS = 6
EPSILON = 1e-05
F32 = jnp.float32
BF16 = jnp.bfloat16
VMEM_LIMIT = 20 * 1024 * 1024
EDGE_LIMIT = 60 * 1024 * 1024


def chunk_of(rows, most, multiple=1):
    sizes = [size for size in range(1, most + 1) if rows % size == 0 and size % multiple == 0]
    return max(sizes) if sizes else rows


def pitch_of(cols):
    return -(-cols // 16) * 16


def parity(rep):
    return ((rep >> 2) ^ (rep >> 3)) & 1


def chunks_of(rows, most, multiple=1):
    size = chunk_of(rows, most, multiple)
    return [(start, start + size) for start in range(0, rows, size)]


def widen(cells, pitch):
    cells = cells.astype(F32)
    extra = pitch - cells.shape[0]
    if extra:
        cells = jnp.concatenate([cells, jnp.zeros((extra, cells.shape[1]), F32)], 0)
    return cells


def put_three(three, row, cells, cols, turned):
    pitch, chan = cells.shape
    left, right = pltpu.roll(cells, 1, 0), pltpu.roll(cells, pitch - 1, 0)
    if pitch == cols:
        col = lax.broadcasted_iota(jnp.int32, (8, chan), 0)
        left = jnp.concatenate([jnp.where(col == 0, 0.0, left[:8]), left[8:]], 0)
        right = jnp.concatenate([right[:-8], jnp.where(col == 7, 0.0, right[-8:])], 0)
    parts = (right, cells, left) if turned else (left, cells, right)
    for place, part in enumerate(parts):
        three[row, :, place * chan : (place + 1) * chan] = part.astype(BF16)


def beside(three, starts, size):
    pitch, width = three.shape[1:]
    return jnp.concatenate([three[start : start + size].reshape(size * pitch, width) for start in starts], 1)


def edges_valid(sp_count):
    index = lax.axis_index("sp")
    return jnp.where(index > 0, 1.0, 0.0), jnp.where(index < sp_count - 1, 1.0, 0.0)


def level_coefs(moments, gain, shift, count):
    mean = moments[0:1] / count
    spread = moments[1:2] / count - mean * mean
    return mean, lax.rsqrt(spread + EPSILON), gain, shift


def slope_of(conv, cotan, coefs):
    mean, rstd, gain, shift = coefs
    centred = conv.astype(F32) - mean
    half = centred * (0.5 * rstd * gain) + 0.5 * shift
    turn = jnp.tanh(half)
    return centred, cotan.astype(F32) * ((1.0 + turn) * (1.0 + half * (1.0 - turn)))


def masked(cells, cols):
    if cells.shape[0] == cols:
        return cells
    col = lax.broadcasted_iota(jnp.int32, cells.shape, 0)
    return jnp.where(col < cols, cells, 0.0)


def staged(fills, dots):
    fills[0]()
    for index, dot in enumerate(dots):
        if index + 1 < len(fills):
            fills[index + 1]()
        dot()


def conv_rows(lhs, w_ref):
    return jnp.dot(lhs, w_ref[...].reshape(lhs.shape[1], -1), preferred_element_type=F32).astype(BF16)


def add_moments(sums, conv, cols):
    chan = conv.shape[2]
    conv = conv.astype(F32)
    if conv.shape[1] != cols:
        conv = conv[:, :cols]
    conv = conv.reshape(-1, 8, chan)
    sums[0].append(jnp.sum(conv, 0))
    sums[1].append(jnp.sum(conv * conv, 0))


def folded(parts):
    total = parts[0]
    for part in parts[1:]:
        total = total + part
    return jnp.sum(total, 0, keepdims=True)


def inner_level(x_ref, w_ref, conv_ref, three, sums, most):
    rows, cols = x_ref.shape[:2]
    pitch = three.shape[1]

    def fill_row(row):
        put_three(three, row, widen(x_ref[row], pitch), cols, False)

    def dot(start, end):
        conv = conv_rows(beside(three, (start, start + 1, start + 2), end - start), w_ref)
        conv = conv.reshape(end - start, pitch, -1)
        conv_ref[start:end] = conv
        add_moments(sums, conv, cols)

    inner = rows - 2
    count = max(1, inner // most)
    bounds = [index * inner // count for index in range(count + 1)]
    fills, dots, done = [], [], 0
    for start, end in zip(bounds[:-1], bounds[1:]):
        fills.append(lambda todo=range(done, end + 2): [fill_row(row) for row in todo])
        done = end + 2
        dots.append(functools.partial(dot, start, end))
    return fills, dots


def inner_kernel(four_ref, six_ref, w_ref, conv_four_ref, conv_six_ref, moments_ref, three_four, three_six):
    sums_four, sums_six = ([], []), ([], [])
    fills_six, dots_six = inner_level(six_ref, w_ref, conv_six_ref, three_six, sums_six, 10)
    fills_four, dots_four = inner_level(four_ref, w_ref, conv_four_ref, three_four, sums_four, 8)
    staged(fills_six + fills_four, dots_six + dots_four)
    moments_ref[...] = jnp.concatenate([folded(parts) for parts in sums_four + sums_six], 0)


def outer_level(x_ref, top, bottom, valid, three):
    rows, cols = x_ref.shape[:2]
    pitch = three.shape[1]
    for edge in range(2):
        put_three(three, edge, top(edge) * valid[0], cols, False)
        put_three(three, 2 + edge, widen(x_ref[edge], pitch), cols, False)
        put_three(three, 4 + edge, widen(x_ref[rows - 2 + edge], pitch), cols, False)
        put_three(three, 6 + edge, bottom(edge) * valid[1], cols, False)
    return [beside(three, (start, start + 1, start + 2), 2) for start in (0, 4)]


def outer_kernel(
    sp_count, four_ref, six_ref, above_ref, below_ref, w_ref, inner_ref,
    conv_four_ref, conv_six_ref, moments_ref, three_four, three_six,
):
    cols_four = four_ref.shape[1]
    valid = edges_valid(sp_count)
    base, pitch_six = 3 * cols_four, three_six.shape[1]

    def reader(ref, start, pitch):
        return lambda edge: ref[start + edge * pitch : start + (edge + 1) * pitch].astype(F32)

    lhs = outer_level(
        four_ref, reader(above_ref, 0, cols_four), reader(below_ref, 0, cols_four), valid, three_four
    ) + outer_level(
        six_ref, reader(above_ref, base, pitch_six), reader(below_ref, base, pitch_six), valid, three_six
    )
    conv = conv_rows(jnp.concatenate(lhs, 0), w_ref)
    sums, begin = [], 0
    for conv_ref, cols in ((conv_four_ref, cols_four), (conv_six_ref, six_ref.shape[1])):
        cells = conv_ref.shape[0] * conv_ref.shape[1]
        rows = conv[begin : begin + cells].reshape(conv_ref.shape)
        begin += cells
        conv_ref[...] = rows
        parts = ([], [])
        add_moments(parts, rows[1:3], cols)
        sums += [folded(part) for part in parts]
    moments_ref[...] = inner_ref[...] + jnp.concatenate(sums, 0)


def turn_kernel(four_ref, six_ref, w_ref, turned_ref, turned_w_ref):
    rows_four, cols_four, chan = four_ref.shape
    rows_six, cols_six = six_ref.shape[:2]
    pitch = pitch_of(cols_six)
    for start, end in chunks_of(rows_four, 8, 4):
        cells = four_ref[start:end].reshape((end - start) * cols_four, chan)
        turned_ref[:, start * cols_four : end * cols_four] = cells.T
    cells = six_ref[...].astype(F32)
    cells = jnp.concatenate([cells, jnp.zeros((rows_six, pitch - cols_six, chan), F32)], 1).astype(BF16)
    turned_ref[:, rows_four * cols_four :] = cells.reshape(rows_six * pitch, chan).T
    for tap in range(9):
        turned_w_ref[tap * chan : (tap + 1) * chan] = w_ref[tap].T


def slope_level(inner_ref, outer_ref, cotan_ref, above, below, coefs, slope_ref):
    rows, cols, chan = cotan_ref.shape
    pitch = inner_ref.shape[1]

    def put(row, conv, cotan):
        centred, slope = slope_of(conv, widen(cotan, pitch), coefs)
        slope_ref[row] = slope
        return centred, slope

    def add(sums, pair):
        centred, slope = pair
        first = jnp.sum(slope.reshape(-1, 8, chan), 0)
        second = jnp.sum((slope * centred).reshape(-1, 8, chan), 0)
        return sums[0] + first, sums[1] + second

    def step(row, sums):
        return add(sums, put(row + 2, inner_ref[row], cotan_ref[row + 1]))

    put(0, outer_ref[0], above)
    put(rows + 1, outer_ref[3], below)
    zero = jnp.zeros((8, chan), F32)
    sums = add((zero, zero), put(1, outer_ref[1], cotan_ref[0]))
    sums = add(sums, put(rows, outer_ref[2], cotan_ref[rows - 1]))
    for row in range(rows - 2):
        sums = step(row, sums)
    first = 0.5 * jnp.sum(sums[0], 0, keepdims=True)
    return first, 0.5 * coefs[1] * jnp.sum(sums[1], 0, keepdims=True)


def slope_kernel(
    counts, inner_four_ref, inner_six_ref, outer_four_ref, outer_six_ref, cotan_four_ref, cotan_six_ref,
    above_ref, below_ref, moments_ref, gain_ref, shift_ref, slope_four_ref, slope_six_ref, slopes_ref,
):
    sums = ()
    cols_four = cotan_four_ref.shape[1]
    starts = (2 * cols_four, 3 * cols_four + 2 * inner_six_ref.shape[1])
    for level, (inner_ref, outer_ref, cotan_ref, slope_ref) in enumerate(
        (
            (inner_four_ref, outer_four_ref, cotan_four_ref, slope_four_ref),
            (inner_six_ref, outer_six_ref, cotan_six_ref, slope_six_ref),
        )
    ):
        pair = moments_ref[2 * level : 2 * level + 2]
        here = slice(level, level + 1)
        edge = slice(starts[level], starts[level] + inner_ref.shape[1])
        coefs = level_coefs(pair, gain_ref[here], shift_ref[here], counts[level])
        sums += slope_level(inner_ref, outer_ref, cotan_ref, above_ref[edge], below_ref[edge], coefs, slope_ref)
    slopes_ref[...] = jnp.concatenate(sums, 0)


def backward_level(cols, inner_ref, outer_ref, slope_ref, valid, coefs, slopes, count, three):
    rows = inner_ref.shape[0] + 2
    pitch = three.shape[1]
    mean, rstd, gain, shift = coefs
    lead = gain * rstd
    offset, factor = lead * (slopes[0:1] / count), lead * rstd * (slopes[1:2] / count)

    def fill_row(row):
        if 2 <= row < rows:
            conv = inner_ref[row - 2]
        else:
            conv = outer_ref[row if row < 2 else row - rows + 2]
        centred = conv.astype(F32) - mean
        dconv = masked((0.5 * lead) * slope_ref[row] - (offset + centred * factor), cols)
        if row == 0:
            dconv = dconv * valid[0]
        elif row == rows + 1:
            dconv = dconv * valid[1]
        put_three(three, row, dconv, cols, True)

    return fill_row


def taps_beside(three, start, end, taps):
    pitch, width = three.shape[1:]
    chan = width // 3
    parts = []
    for row_tap in range(3):
        low, high = max(taps[0] - 3 * row_tap, 0), min(taps[1] - 3 * row_tap, 3)
        if low < high:
            first = start + 2 - row_tap
            rows = three[first : first + end - start, :, low * chan : high * chan]
            parts.append(rows.reshape((end - start) * pitch, (high - low) * chan))
    return jnp.concatenate(parts, 1)


def backward_bounds(rows):
    bounds = [0, min(4, rows), min(16, rows)]
    while bounds[-1] < rows:
        bounds.append(min(bounds[-1] + 16, rows))
    return sorted(set(bounds))


def weight_dot(turned_ref, three_four, three_six, total, taps, start, end):
    rows_four, rows_six = three_four.shape[0] - 2, three_six.shape[0] - 2
    pitch = three_four.shape[1]
    first, last = start * pitch, end * pitch
    rhs = taps_beside(three_four, start, end, taps)
    if end == rows_four:
        rhs = jnp.concatenate([rhs, taps_beside(three_six, 0, rows_six, taps)], 0)
        last = turned_ref.shape[1]
    term = jnp.dot(turned_ref[:, first:last], rhs, preferred_element_type=F32)
    total[...] = total[...] + term if start else term


def put_shares(totals, sp_count, own_ref, sent_ref):
    taps, share, chan = own_ref.shape
    places = [(total, start) for total in totals for start in range(0, total.shape[1], chan)][:taps]
    place = lax.axis_index("sp") ^ parity(lax.axis_index("rep"))
    for step in range(sp_count):
        begin = pl.multiple_of((place ^ step) * share, share)
        for tap, (total, start) in enumerate(places):
            part = total[pl.ds(begin, share), start : start + chan]
            if step == 0:
                own_ref[tap] = part
            else:
                sent_ref[step - 1, tap] = part


def backward_kernel(
    counts, sp_count, cols, turned_ref, inner_four_ref, inner_six_ref, outer_four_ref, outer_six_ref,
    slope_four_ref, slope_six_ref, moments_ref, slopes_ref, gain_ref, shift_ref, three_four, three_six, own_ref,
    sent_ref, rest_ref, grad_gain_ref, grad_shift_ref, total,
):
    valid = edges_valid(sp_count)
    grad_gain_ref[...] = jnp.concatenate([slopes_ref[1:2], slopes_ref[3:4]], 0)
    grad_shift_ref[...] = jnp.concatenate([slopes_ref[0:1], slopes_ref[2:3]], 0)
    parts = []
    for level, inner_ref, outer_ref, slope_ref, three in (
        (0, inner_four_ref, outer_four_ref, slope_four_ref, three_four),
        (1, inner_six_ref, outer_six_ref, slope_six_ref, three_six),
    ):
        here = slice(level, level + 1)
        pair = slice(2 * level, 2 * level + 2)
        coefs = level_coefs(moments_ref[pair], gain_ref[here], shift_ref[here], counts[level])
        parts.append(
            backward_level(
                cols[level], inner_ref, outer_ref, slope_ref, valid, coefs, slopes_ref[pair], counts[level], three
            )
        )
    fill_four, fill_six = parts
    rows_four, rows_six = three_four.shape[0] - 2, three_six.shape[0] - 2
    bounds = backward_bounds(rows_four)
    fills, dots, done = [], [], 0
    for start, end in zip(bounds[:-1], bounds[1:]):
        todo = [functools.partial(fill_four, row) for row in range(done, end + 2)]
        if end == rows_four:
            todo += [functools.partial(fill_six, row) for row in range(rows_six + 2)]
        fills.append(lambda todo=todo: [fill() for fill in todo])
        done = end + 2
        dots.append(
            functools.partial(weight_dot, turned_ref, three_four, three_six, total, (0, EARLY_TAPS), start, end)
        )
    staged(fills, dots)
    put_shares([total], sp_count, own_ref, sent_ref)
    rest_ref[...] = total[:, FIRST_TAPS * rest_ref.shape[0] :]


def weight_kernel(sp_count, turned_ref, three_four, three_six, rest_ref, own_ref, sent_ref, total):
    for start, end in chunks_of(three_four.shape[0] - 2, 16, 4):
        weight_dot(turned_ref, three_four, three_six, total, (EARLY_TAPS, 9), start, end)
    put_shares([rest_ref, total], sp_count, own_ref, sent_ref)


def input_chunks(three, turned, grad, chunks, offset, sent=None):
    cols, chan = grad.shape[1:]
    pitch = three.shape[1]
    for index, (start, end) in enumerate(chunks):
        size = end - start
        lhs = beside(three, (start + 2, start + 1, start), size)
        term = jnp.dot(lhs, turned[...], preferred_element_type=F32)
        grad[start - offset : end - offset] = term.reshape(size, pitch, chan)[:, :cols].astype(BF16)
        if sent is not None:
            sent(index, start, end)


def input_kernel(chunks, three_four, turned, grad_ref):
    input_chunks(three_four, turned, grad_ref, chunks, chunks[0][0])


def input_last_kernel(chunks, bounds, three_four, three_six, turned, *rest):
    count = len(bounds) - 1
    earlier, rest = rest[:count], rest[count:]
    grad_four_ref, grad_six_ref, grad_four, grad_six, sems, sems_four, sems_six = rest
    copies = [
        pltpu.make_async_copy(part, grad_four_ref.at[bounds[index] : bounds[index + 1]], sems.at[index])
        for index, part in enumerate(earlier)
    ]
    for copy in copies:
        copy.start()

    def sender(grad, grad_ref, offset, sems):
        def sent(index, start, end):
            copy = pltpu.make_async_copy(grad.at[start - offset : end - offset], grad_ref.at[start:end], sems.at[index])
            copy.start()
            copies.append(copy)

        return sent

    six_chunks = chunks_of(grad_six.shape[0], 12)
    input_chunks(three_six, turned, grad_six, six_chunks, 0, sender(grad_six, grad_six_ref, 0, sems_six))
    done = bounds[-1]
    input_chunks(three_four, turned, grad_four, chunks, done, sender(grad_four, grad_four_ref, done, sems_four))
    for copy in copies:
        copy.wait()


def swap(array, axis, stride):
    count = lax.axis_size(axis)
    return lax.ppermute(array, axis, [(i, i ^ stride) for i in range(count)])


def edge_kernel(starts, four_ref, six_ref, cotan_four_ref, cotan_six_ref, *rest):
    outs, six_rows, sems = rest[:-2], rest[-2], rest[-1]
    rows_four, cols_four = four_ref.shape[:2]
    rows_six = six_ref.shape[0]
    pitch = pitch_of(six_ref.shape[1])
    copies = []
    for number, (start, out_ref) in enumerate(zip(starts, outs)):
        last = (1 - jnp.minimum(lax.axis_index("sp"), 1)) if start is None else start
        for part, (ref, row) in enumerate(
            (
                (four_ref, last * (rows_four - 2)),
                (four_ref, last * (rows_four - 2) + 1),
                (cotan_four_ref, last * (rows_four - 1)),
                (six_ref, last * (rows_six - 2)),
                (six_ref, last * (rows_six - 2) + 1),
                (cotan_six_ref, last * (rows_six - 1)),
            )
        ):
            if part < 3:
                target = out_ref.at[part * cols_four : (part + 1) * cols_four]
            else:
                target = six_rows.at[number, part - 3]
            copies.append(pltpu.make_async_copy(ref.at[row], target, sems.at[number, part]))
    for copy in copies:
        copy.start()
    for copy in copies:
        copy.wait()
    for number, out_ref in enumerate(outs):
        for part in range(3):
            begin = 3 * cols_four + part * pitch
            out_ref[begin : begin + pitch] = widen(six_rows[number, part], pitch).astype(BF16)


def edges(four, six, cotan_four, cotan_six):
    count = lax.axis_size("sp")
    starts = (None,) if count == 2 else (0, 1)
    length = 3 * four.shape[1] + 3 * pitch_of(six.shape[1])
    vmem = pl.BlockSpec(memory_space=pltpu.VMEM)
    hbm = pl.BlockSpec(memory_space=pltpu.HBM)
    outs = pl.pallas_call(
        functools.partial(edge_kernel, starts),
        out_shape=tuple(jax.ShapeDtypeStruct((length, four.shape[2]), BF16) for _ in starts),
        in_specs=[hbm] * 4,
        out_specs=tuple(vmem for _ in starts),
        scratch_shapes=[
            pltpu.VMEM((len(starts), 3) + six.shape[1:], BF16),
            pltpu.SemaphoreType.DMA((len(starts), 6)),
        ],
        compiler_params=pltpu.CompilerParams(vmem_limit_bytes=EDGE_LIMIT),
        name="edges",
    )(four, six, cotan_four, cotan_six)
    if count == 2:
        met = swap(outs[0], "sp", 1)
        return met, met
    above = lax.ppermute(outs[1], "sp", [(i, (i + 1) % count) for i in range(count)])
    below = lax.ppermute(outs[0], "sp", [((i + 1) % count, i) for i in range(count)])
    return above, below


def swap_across(array, axis, stride):
    count, sp_count = lax.axis_size("rep"), lax.axis_size("sp")
    rep_stride, sp_stride = (stride, 1) if axis == "rep" else (0, stride ^ 1)
    pairs = [
        (rep * sp_count + sp, (rep ^ rep_stride) * sp_count + (sp ^ sp_stride))
        for rep in range(count)
        for sp in range(sp_count)
    ]
    return lax.ppermute(array, ("rep", "sp"), pairs)


def group_sum(sums):
    sums = sums + swap(sums, "sp", 1)
    stride = 2
    while stride < lax.axis_size("sp"):
        sums = sums + swap_across(sums, "sp", stride)
        stride = 2 * stride
    stride = 1
    while stride < GROUP:
        met = lax.optimization_barrier([swap_across(sums, "rep", k * stride) for k in FAR_FIRST])
        sums = (sums + met[2]) + (met[1] + met[0])
        stride = RADIX * stride
    return sums


def every_group(sums):
    stride = GROUP
    while stride < lax.axis_size("rep"):
        sums = sums + swap(sums, "rep", stride)
        stride = 2 * stride
    return sums


class Places(NamedTuple):
    digits: list
    first: list
    second: list
    odd: jax.Array


def places():
    rep = lax.axis_index("rep")
    digits = [(rep & (RADIX - 1)) ^ k for k in range(RADIX)]
    second = 9 - FIRST_TAPS
    return Places(
        digits,
        [FIRST_TAPS * digit for digit in digits],
        [RADIX * FIRST_TAPS + second * digit for digit in digits],
        parity(rep) == 1,
    )


def piece_of(pieces, index):
    sizes = (1,) + pieces.shape[1:]
    return lax.dynamic_slice(pieces, (index, 0, 0), sizes, allow_negative_indices=False)[0]


def scatter_pieces(own, met, found):
    chan = own.shape[2]
    parts = [part.reshape(RADIX, -1, chan) for part in [own] + met]

    def piece(k):
        total = piece_of(parts[0], found.digits[k])
        for part in parts[1:]:
            total = total + piece_of(part, found.digits[k])
        return total

    return piece(0), [piece(k).astype(BF16) for k in FAR_FIRST]


def added(own, met):
    return (own + met[2].astype(F32)) + (met[1].astype(F32) + met[0].astype(F32))


def fours(pieces, stride):
    return [swap(piece, "rep", k * stride) for k, piece in zip(FAR_FIRST, pieces)]


def swap_high(array, even, odd):
    count, sp_count = lax.axis_size("rep"), lax.axis_size("sp")
    pairs = []
    for rep in range(count):
        for sp in range(sp_count):
            stride = odd if (sp ^ parity(rep)) & 1 else even
            pairs.append((rep * sp_count + sp, (rep ^ stride) * sp_count + (sp ^ 1)))
    return lax.ppermute(array, ("rep", "sp"), pairs)


def bring(array, k):
    count, sp_count = lax.axis_size("rep"), lax.axis_size("sp")
    pairs = [
        (rep * sp_count + sp, (rep ^ k) * sp_count + (sp ^ parity(rep)))
        for rep in range(count)
        for sp in range(sp_count)
    ]
    return lax.ppermute(array, ("rep", "sp"), pairs)


def both(own, met):
    return (own.astype(F32) + met.astype(F32)).astype(BF16)


def every_share(total):
    stride = GROUP
    while stride < lax.axis_size("rep"):
        total = added(total.astype(F32), fours([total] * 3, stride)).astype(BF16)
        stride = RADIX * stride
    return total


def gather(total, found):
    beside = swap(total, "sp", 1)
    return [bring(total, k) for k in FAR_FIRST] + [jnp.where(found.odd, beside, total)], beside


def put_pieces(whole, pieces, starts):
    for k, piece in zip(FAR_FIRST + (0,), pieces):
        piece = piece.reshape((-1,) + whole.shape[1:]).astype(F32)
        whole = lax.dynamic_update_slice(whole, piece, (starts[k], 0, 0), allow_negative_indices=False)
    return whole


def local(level_four, level_six, conv_weight, bn_gain, bn_shift, cotan_four, cotan_six):
    sp_count = lax.axis_size("sp")
    images = level_four.shape[0]
    four, six, cot_four, cot_six = (a[0] for a in (level_four, level_six, cotan_four, cotan_six))
    rows_four, cols_four, chan = four.shape
    rows_six, cols_six = six.shape[:2]
    pitch_four, pitch_six = pitch_of(cols_four), pitch_of(cols_six)
    counts = (
        float(images * GROUP * rows_four * sp_count * cols_four),
        float(images * GROUP * rows_six * sp_count * cols_six),
    )
    found, four = lax.optimization_barrier((places(), four))
    above, below = edges(four, six, cot_four, cot_six)
    vmem = pl.BlockSpec(memory_space=pltpu.VMEM)
    hbm = pl.BlockSpec(memory_space=pltpu.HBM)
    params = pltpu.CompilerParams(vmem_limit_bytes=VMEM_LIMIT)
    framed_four = jax.ShapeDtypeStruct((rows_four + 2, pitch_four, chan), BF16)
    framed_six = jax.ShapeDtypeStruct((rows_six + 2, pitch_six, chan), BF16)
    four_sums = jax.ShapeDtypeStruct((4, chan), F32)
    flops = 2 * 9 * chan * chan * (rows_four * cols_four + rows_six * cols_six)

    def cost(share, size):
        return pl.CostEstimate(flops=int(flops * share), bytes_accessed=size, transcendentals=0)

    inner_four, inner_six, inner_moments = pl.pallas_call(
        inner_kernel,
        out_shape=(
            jax.ShapeDtypeStruct((rows_four - 2, pitch_four, chan), BF16),
            jax.ShapeDtypeStruct((rows_six - 2, pitch_six, chan), BF16),
            four_sums,
        ),
        in_specs=[vmem] * 3,
        out_specs=(vmem, vmem, vmem),
        scratch_shapes=[
            pltpu.VMEM((rows_four, pitch_four, 3 * chan), BF16),
            pltpu.VMEM((rows_six, pitch_six, 3 * chan), BF16),
        ],
        compiler_params=params,
        cost_estimate=cost(1, 4 * four.size),
        name="forward_inner",
    )(four, six, conv_weight)
    outer_four, outer_six, moments = pl.pallas_call(
        functools.partial(outer_kernel, sp_count),
        out_shape=(
            jax.ShapeDtypeStruct((4, pitch_four, chan), BF16),
            jax.ShapeDtypeStruct((4, pitch_six, chan), BF16),
            four_sums,
        ),
        in_specs=[vmem] * 6,
        out_specs=(vmem, vmem, vmem),
        scratch_shapes=[
            pltpu.VMEM((8, pitch_four, 3 * chan), BF16),
            pltpu.VMEM((8, pitch_six, 3 * chan), BF16),
        ],
        compiler_params=params,
        cost_estimate=cost(0.1, four.size),
        name="forward_outer",
    )(four, six, above, below, conv_weight, inner_moments)
    moments, four, six = lax.optimization_barrier((moments, four, six))
    turned, turned_weight = pl.pallas_call(
        turn_kernel,
        out_shape=(
            jax.ShapeDtypeStruct((chan, rows_four * cols_four + rows_six * pitch_six), BF16),
            jax.ShapeDtypeStruct((9 * chan, chan), BF16),
        ),
        in_specs=[vmem] * 3,
        out_specs=(vmem, vmem),
        compiler_params=params,
        cost_estimate=cost(0.3, 4 * four.size),
        name="turn",
    )(four, six, conv_weight)
    moments, turned, turned_weight = lax.optimization_barrier((group_sum(moments), turned, turned_weight))

    slope_four, slope_six, slopes = pl.pallas_call(
        functools.partial(slope_kernel, counts),
        out_shape=(
            jax.ShapeDtypeStruct(framed_four.shape, F32),
            jax.ShapeDtypeStruct(framed_six.shape, F32),
            four_sums,
        ),
        in_specs=[vmem] * 11,
        out_specs=(vmem,) * 3,
        compiler_params=params,
        cost_estimate=cost(0.01, 4 * four.size),
        name="slopes",
    )(
        inner_four, inner_six, outer_four, outer_six, cot_four, cot_six, above, below, moments, bn_gain, bn_shift
    )
    slopes = group_sum(slopes)

    share = chan // sp_count
    wide_four, wide_six = (
        jax.ShapeDtypeStruct(framed.shape[:2] + (3 * chan,), BF16) for framed in (framed_four, framed_six)
    )
    def shares(taps):
        return (
            jax.ShapeDtypeStruct((taps, share, chan), F32),
            jax.ShapeDtypeStruct((sp_count - 1, taps, share, chan), F32),
        )

    three_four, three_six, own_a, sent_a, rest, grad_gain, grad_shift = pl.pallas_call(
        functools.partial(backward_kernel, counts, sp_count, (cols_four, cols_six)),
        out_shape=(wide_four, wide_six)
        + shares(FIRST_TAPS)
        + (jax.ShapeDtypeStruct((chan, (EARLY_TAPS - FIRST_TAPS) * chan), F32),)
        + (jax.ShapeDtypeStruct((2, chan), F32),) * 2,
        in_specs=[vmem] * 11,
        out_specs=(vmem,) * 7,
        scratch_shapes=[pltpu.VMEM((chan, EARLY_TAPS * chan), F32)],
        compiler_params=params,
        cost_estimate=cost(0.6, 8 * four.size),
        name="backward",
    )(
        turned, inner_four, inner_six, outer_four, outer_six, slope_four, slope_six, moments, slopes,
        bn_gain, bn_shift,
    )
    sent_a, three_six = lax.optimization_barrier((sent_a, three_six))
    met_a = [swap(sent_a[step], "sp", step + 1) for step in range(sp_count - 1)]
    own_b, sent_b = pl.pallas_call(
        functools.partial(weight_kernel, sp_count),
        out_shape=shares(9 - FIRST_TAPS),
        in_specs=[vmem] * 4,
        out_specs=(vmem, vmem),
        scratch_shapes=[pltpu.VMEM((chan, (9 - EARLY_TAPS) * chan), F32)],
        compiler_params=params,
        cost_estimate=cost(0.6, 8 * four.size),
        name="weights",
    )(turned, three_four, three_six, rest)
    met_a, sent_b = lax.optimization_barrier((met_a, sent_b))
    met_b = [swap(sent_b[step], "sp", step + 1) for step in range(sp_count - 1)]

    chunks = chunks_of(rows_four, 8)
    cuts = [part * len(chunks) // 3 for part in range(4)]
    groups = [chunks[low:high] for low, high in zip(cuts[:-1], cuts[1:]) if low < high]
    bounds = [group[0][0] for group in groups]

    def inputs(group, three):
        return pl.pallas_call(
            functools.partial(input_kernel, group),
            out_shape=jax.ShapeDtypeStruct((group[-1][1] - group[0][0], cols_four, chan), BF16),
            in_specs=[vmem] * 2,
            out_specs=vmem,
            compiler_params=params,
            cost_estimate=cost(0.3, four.size),
            name="inputs",
        )(three, turned_weight)

    grad_gain, grad_shift = every_group(grad_gain), every_group(grad_shift)

    piece_a, pieces_a = scatter_pieces(own_a, met_a, found)
    met_a = fours(pieces_a, 1)
    piece_b, pieces_b = scatter_pieces(own_b, met_b, found)
    met_b = fours(pieces_b, 1)
    met_a, unused = lax.optimization_barrier((met_a, pieces_b))

    piece_a = added(piece_a, met_a).astype(BF16)
    piece_a, three_four = lax.optimization_barrier((piece_a, three_four))
    met_a = swap_high(piece_a, RADIX, 2 * RADIX)
    earlier = [inputs(groups[0], three_four)] if len(groups) > 1 else []
    met_b, earlier = lax.optimization_barrier((met_b, earlier))

    piece_b = added(piece_b, met_b).astype(BF16)
    met_b = swap_high(piece_b, RADIX, 2 * RADIX)
    met_a, unused = lax.optimization_barrier((met_a, piece_b))

    piece_a = both(piece_a, met_a)
    piece_a, three_four = lax.optimization_barrier((piece_a, three_four))
    met_a = swap_high(piece_a, 2 * RADIX, RADIX)
    if len(groups) > 2:
        earlier = earlier + [inputs(groups[1], three_four)]
    met_b, earlier = lax.optimization_barrier((met_b, earlier))

    piece_b = both(piece_b, met_b)
    met_b = swap_high(piece_b, 2 * RADIX, RADIX)
    met_a, unused = lax.optimization_barrier((met_a, piece_b))

    piece_a = every_share(both(piece_a, met_a))
    pieces_a, unused = gather(piece_a, found)
    piece_b = every_share(both(piece_b, met_b))
    pieces_b, beside = gather(piece_b, found)
    unused, three_four = lax.optimization_barrier(((beside, pieces_a[0]), three_four))
    done = bounds[-1]
    grad_four, grad_six = pl.pallas_call(
        functools.partial(input_last_kernel, groups[-1], bounds),
        out_shape=(
            jax.ShapeDtypeStruct(four.shape, BF16),
            jax.ShapeDtypeStruct(six.shape, BF16),
        ),
        in_specs=[vmem] * (3 + len(earlier)),
        out_specs=(hbm, hbm),
        scratch_shapes=[
            pltpu.VMEM((rows_four - done, cols_four, chan), BF16),
            pltpu.VMEM(six.shape, BF16),
            pltpu.SemaphoreType.DMA((len(groups),)),
            pltpu.SemaphoreType.DMA((len(chunks),)),
            pltpu.SemaphoreType.DMA((len(chunks_of(rows_six, 12)),)),
        ],
        compiler_params=params,
        cost_estimate=cost(0.4, 2 * four.size),
        name="inputs_last",
    )(three_four, three_six, turned_weight, *earlier)
    pieces_a, grad_six = lax.optimization_barrier((pieces_a, grad_six))
    whole = jnp.zeros((9 * RADIX, share // RADIX, chan), F32)
    whole = put_pieces(whole, pieces_a, found.first)
    whole = put_pieces(whole, pieces_b, found.second)
    grad_weight = whole.reshape(9, share, chan)
    return (grad_four[None], grad_six[None], grad_weight, grad_gain, grad_shift)


def solution(mesh):
    placed = (
        P("rep", "sp", None, None),
        P("rep", "sp", None, None),
        P(),
        P(),
        P(),
        P("rep", "sp", None, None),
        P("rep", "sp", None, None),
    )
    return jax.shard_map(
        local,
        mesh=mesh,
        in_specs=placed,
        out_specs=(
            P("rep", "sp", None, None),
            P("rep", "sp", None, None),
            P(None, "sp", None),
            P(),
            P(),
        ),
        check_vma=False,
    )
```

```python
import functools
from typing import NamedTuple

import jax
import jax.numpy as jnp
from jax import lax
from jax.experimental import pallas as pl
from jax.experimental.pallas import tpu as pltpu
from jax.sharding import PartitionSpec as P

GROUP = 16
RADIX = 4
FAR_FIRST = (3, 2, 1)
FIRST_TAPS = 4
EARLY_TAPS = 6
EPSILON = 1e-05
F32 = jnp.float32
BF16 = jnp.bfloat16
VMEM_LIMIT = 20 * 1024 * 1024
EDGE_LIMIT = 60 * 1024 * 1024


def chunk_of(rows, most, multiple=1):
    sizes = [size for size in range(1, most + 1) if rows % size == 0 and size % multiple == 0]
    return max(sizes) if sizes else rows


def pitch_of(cols):
    return -(-cols // 16) * 16


def parity(rep):
    return ((rep >> 2) ^ (rep >> 3)) & 1


def chunks_of(rows, most, multiple=1):
    size = chunk_of(rows, most, multiple)
    return [(start, start + size) for start in range(0, rows, size)]


def widen(cells, pitch):
    cells = cells.astype(F32)
    extra = pitch - cells.shape[0]
    if extra:
        cells = jnp.concatenate([cells, jnp.zeros((extra, cells.shape[1]), F32)], 0)
    return cells


def put_three(three, row, cells, cols, turned):
    pitch, chan = cells.shape
    left, right = pltpu.roll(cells, 1, 0), pltpu.roll(cells, pitch - 1, 0)
    if pitch == cols:
        col = lax.broadcasted_iota(jnp.int32, (8, chan), 0)
        left = jnp.concatenate([jnp.where(col == 0, 0.0, left[:8]), left[8:]], 0)
        right = jnp.concatenate([right[:-8], jnp.where(col == 7, 0.0, right[-8:])], 0)
    parts = (right, cells, left) if turned else (left, cells, right)
    for place, part in enumerate(parts):
        three[row, :, place * chan : (place + 1) * chan] = part.astype(BF16)


def beside(three, starts, size):
    pitch, width = three.shape[1:]
    return jnp.concatenate([three[start : start + size].reshape(size * pitch, width) for start in starts], 1)


def edges_valid(sp_count):
    index = lax.axis_index("sp")
    return jnp.where(index > 0, 1.0, 0.0), jnp.where(index < sp_count - 1, 1.0, 0.0)


def level_coefs(moments, gain, shift, count):
    mean = moments[0:1] / count
    spread = moments[1:2] / count - mean * mean
    return mean, lax.rsqrt(spread + EPSILON), gain, shift


def slope_of(conv, cotan, coefs):
    mean, rstd, gain, shift = coefs
    centred = conv.astype(F32) - mean
    half = centred * (0.5 * rstd * gain) + 0.5 * shift
    turn = jnp.tanh(half)
    return centred, cotan.astype(F32) * ((1.0 + turn) * (1.0 + half * (1.0 - turn)))


def masked(cells, cols):
    if cells.shape[0] == cols:
        return cells
    col = lax.broadcasted_iota(jnp.int32, cells.shape, 0)
    return jnp.where(col < cols, cells, 0.0)


def staged(fills, dots):
    fills[0]()
    for index, dot in enumerate(dots):
        if index + 1 < len(fills):
            fills[index + 1]()
        dot()


def conv_rows(lhs, w_ref):
    return jnp.dot(lhs, w_ref[...].reshape(lhs.shape[1], -1), preferred_element_type=F32).astype(BF16)


def add_moments(sums, conv, cols):
    chan = conv.shape[2]
    conv = conv.astype(F32)
    if conv.shape[1] != cols:
        conv = conv[:, :cols]
    conv = conv.reshape(-1, 8, chan)
    sums[0].append(jnp.sum(conv, 0))
    sums[1].append(jnp.sum(conv * conv, 0))


def folded(parts):
    total = parts[0]
    for part in parts[1:]:
        total = total + part
    return jnp.sum(total, 0, keepdims=True)


def inner_kernel(four_ref, six_ref, w_ref, conv_four_ref, conv_six_ref, moments_ref, three_four, three_six):
    rows_four, cols_four = four_ref.shape[:2]
    rows_six, cols_six = six_ref.shape[:2]
    pitch_four, pitch_six = three_four.shape[1], three_six.shape[1]
    sums_four, sums_six = ([], []), ([], [])
    inner = rows_four - 2
    count = max(1, inner // 9)
    bounds = [index * inner // count for index in range(count + 1)]

    def fill_four(row):
        put_three(three_four, row, four_ref[row].astype(F32), cols_four, False)

    def fill_six(row):
        put_three(three_six, row, widen(six_ref[row], pitch_six), cols_six, False)

    def dot(start, end):
        lhs = beside(three_four, (start, start + 1, start + 2), end - start)
        cells = lhs.shape[0]
        if end == inner:
            lhs = jnp.concatenate([lhs, beside(three_six, (0, 1, 2), rows_six - 2)], 0)
        conv = conv_rows(lhs, w_ref)
        four = conv[:cells].reshape(end - start, pitch_four, -1)
        conv_four_ref[start:end] = four
        add_moments(sums_four, four, cols_four)
        if end == inner:
            six = conv[cells:].reshape(rows_six - 2, pitch_six, -1)
            conv_six_ref[...] = six
            add_moments(sums_six, six, cols_six)

    fills, dots, done = [], [], 0
    for start, end in zip(bounds[:-1], bounds[1:]):
        todo = [functools.partial(fill_four, row) for row in range(done, end + 2)]
        if end == inner:
            todo += [functools.partial(fill_six, row) for row in range(rows_six)]
        fills.append(lambda todo=todo: [fill() for fill in todo])
        done = end + 2
        dots.append(functools.partial(dot, start, end))
    staged(fills, dots)
    moments_ref[...] = jnp.concatenate([folded(parts) for parts in sums_four + sums_six], 0)


def outer_level(x_ref, top, bottom, valid, three):
    rows, cols = x_ref.shape[:2]
    pitch = three.shape[1]
    for edge in range(2):
        put_three(three, edge, top(edge) * valid[0], cols, False)
        put_three(three, 2 + edge, widen(x_ref[edge], pitch), cols, False)
        put_three(three, 4 + edge, widen(x_ref[rows - 2 + edge], pitch), cols, False)
        put_three(three, 6 + edge, bottom(edge) * valid[1], cols, False)
    return [beside(three, (start, start + 1, start + 2), 2) for start in (0, 4)]


def outer_kernel(
    sp_count, four_ref, six_ref, above_ref, below_ref, w_ref, inner_ref,
    conv_four_ref, conv_six_ref, moments_ref, three_four, three_six,
):
    cols_four = four_ref.shape[1]
    valid = edges_valid(sp_count)
    base, pitch_six = 3 * cols_four, three_six.shape[1]

    def reader(ref, start, pitch):
        return lambda edge: ref[start + edge * pitch : start + (edge + 1) * pitch].astype(F32)

    lhs = outer_level(
        four_ref, reader(above_ref, 0, cols_four), reader(below_ref, 0, cols_four), valid, three_four
    ) + outer_level(
        six_ref, reader(above_ref, base, pitch_six), reader(below_ref, base, pitch_six), valid, three_six
    )
    conv = conv_rows(jnp.concatenate(lhs, 0), w_ref)
    sums, begin = [], 0
    for conv_ref, cols in ((conv_four_ref, cols_four), (conv_six_ref, six_ref.shape[1])):
        cells = conv_ref.shape[0] * conv_ref.shape[1]
        rows = conv[begin : begin + cells].reshape(conv_ref.shape)
        begin += cells
        conv_ref[...] = rows
        parts = ([], [])
        add_moments(parts, rows[1:3], cols)
        sums += [folded(part) for part in parts]
    moments_ref[...] = inner_ref[...] + jnp.concatenate(sums, 0)


def turn_kernel(four_ref, six_ref, w_ref, turned_ref, turned_w_ref):
    rows_four, cols_four, chan = four_ref.shape
    rows_six, cols_six = six_ref.shape[:2]
    pitch = pitch_of(cols_six)
    for start, end in chunks_of(rows_four, 8, 4):
        cells = four_ref[start:end].reshape((end - start) * cols_four, chan)
        turned_ref[:, start * cols_four : end * cols_four] = cells.T
    cells = six_ref[...].astype(F32)
    cells = jnp.concatenate([cells, jnp.zeros((rows_six, pitch - cols_six, chan), F32)], 1).astype(BF16)
    turned_ref[:, rows_four * cols_four :] = cells.reshape(rows_six * pitch, chan).T
    for tap in range(9):
        turned_w_ref[tap * chan : (tap + 1) * chan] = w_ref[tap].T


def slope_level(inner_ref, outer_ref, cotan_ref, above, below, coefs, slope_ref):
    rows, cols, chan = cotan_ref.shape
    pitch = inner_ref.shape[1]

    def put(row, conv, cotan):
        centred, slope = slope_of(conv, widen(cotan, pitch), coefs)
        slope_ref[row] = slope
        return centred, slope

    def add(sums, pair):
        centred, slope = pair
        first = jnp.sum(slope.reshape(-1, 8, chan), 0)
        second = jnp.sum((slope * centred).reshape(-1, 8, chan), 0)
        return sums[0] + first, sums[1] + second

    def step(row, sums):
        return add(sums, put(row + 2, inner_ref[row], cotan_ref[row + 1]))

    put(0, outer_ref[0], above)
    put(rows + 1, outer_ref[3], below)
    zero = jnp.zeros((8, chan), F32)
    sums = add((zero, zero), put(1, outer_ref[1], cotan_ref[0]))
    sums = add(sums, put(rows, outer_ref[2], cotan_ref[rows - 1]))
    for row in range(rows - 2):
        sums = step(row, sums)
    first = 0.5 * jnp.sum(sums[0], 0, keepdims=True)
    return first, 0.5 * coefs[1] * jnp.sum(sums[1], 0, keepdims=True)


def slope_kernel(
    counts, inner_four_ref, inner_six_ref, outer_four_ref, outer_six_ref, cotan_four_ref, cotan_six_ref,
    above_ref, below_ref, moments_ref, gain_ref, shift_ref, slope_four_ref, slope_six_ref, slopes_ref,
):
    sums = ()
    cols_four = cotan_four_ref.shape[1]
    starts = (2 * cols_four, 3 * cols_four + 2 * inner_six_ref.shape[1])
    for level, (inner_ref, outer_ref, cotan_ref, slope_ref) in enumerate(
        (
            (inner_four_ref, outer_four_ref, cotan_four_ref, slope_four_ref),
            (inner_six_ref, outer_six_ref, cotan_six_ref, slope_six_ref),
        )
    ):
        pair = moments_ref[2 * level : 2 * level + 2]
        here = slice(level, level + 1)
        edge = slice(starts[level], starts[level] + inner_ref.shape[1])
        coefs = level_coefs(pair, gain_ref[here], shift_ref[here], counts[level])
        sums += slope_level(inner_ref, outer_ref, cotan_ref, above_ref[edge], below_ref[edge], coefs, slope_ref)
    slopes_ref[...] = jnp.concatenate(sums, 0)


def backward_level(cols, inner_ref, outer_ref, slope_ref, valid, coefs, slopes, count, three):
    rows = inner_ref.shape[0] + 2
    pitch = three.shape[1]
    mean, rstd, gain, shift = coefs
    lead = gain * rstd
    offset, factor = lead * (slopes[0:1] / count), lead * rstd * (slopes[1:2] / count)

    def fill_row(row):
        if 2 <= row < rows:
            conv = inner_ref[row - 2]
        else:
            conv = outer_ref[row if row < 2 else row - rows + 2]
        centred = conv.astype(F32) - mean
        dconv = masked((0.5 * lead) * slope_ref[row] - (offset + centred * factor), cols)
        if row == 0:
            dconv = dconv * valid[0]
        elif row == rows + 1:
            dconv = dconv * valid[1]
        put_three(three, row, dconv, cols, True)

    return fill_row


def taps_beside(three, start, end, taps):
    pitch, width = three.shape[1:]
    chan = width // 3
    parts = []
    for row_tap in range(3):
        low, high = max(taps[0] - 3 * row_tap, 0), min(taps[1] - 3 * row_tap, 3)
        if low < high:
            first = start + 2 - row_tap
            rows = three[first : first + end - start, :, low * chan : high * chan]
            parts.append(rows.reshape((end - start) * pitch, (high - low) * chan))
    return jnp.concatenate(parts, 1)


def backward_bounds(rows):
    bounds = [0, min(8, rows)]
    while bounds[-1] < rows:
        bounds.append(min(bounds[-1] + 16, rows))
    return bounds


def weight_dot(turned_ref, three_four, three_six, total, taps, start, end):
    rows_four, rows_six = three_four.shape[0] - 2, three_six.shape[0] - 2
    pitch = three_four.shape[1]
    first, last = start * pitch, end * pitch
    rhs = taps_beside(three_four, start, end, taps)
    if end == rows_four:
        rhs = jnp.concatenate([rhs, taps_beside(three_six, 0, rows_six, taps)], 0)
        last = turned_ref.shape[1]
    term = jnp.dot(turned_ref[:, first:last], rhs, preferred_element_type=F32)
    total[...] = total[...] + term if start else term


def put_shares(totals, sp_count, own_ref, sent_ref):
    taps, share, chan = own_ref.shape
    places = [(total, start) for total in totals for start in range(0, total.shape[1], chan)][:taps]
    place = lax.axis_index("sp") ^ parity(lax.axis_index("rep"))
    for step in range(sp_count):
        begin = pl.multiple_of((place ^ step) * share, share)
        for tap, (total, start) in enumerate(places):
            part = total[pl.ds(begin, share), start : start + chan]
            if step == 0:
                own_ref[tap] = part
            else:
                sent_ref[step - 1, tap] = part


def backward_kernel(
    counts, sp_count, cols, turned_ref, inner_four_ref, inner_six_ref, outer_four_ref, outer_six_ref,
    slope_four_ref, slope_six_ref, moments_ref, slopes_ref, gain_ref, shift_ref, three_four, three_six, own_ref,
    sent_ref, rest_ref, grad_gain_ref, grad_shift_ref, total,
):
    valid = edges_valid(sp_count)
    grad_gain_ref[...] = jnp.concatenate([slopes_ref[1:2], slopes_ref[3:4]], 0)
    grad_shift_ref[...] = jnp.concatenate([slopes_ref[0:1], slopes_ref[2:3]], 0)
    parts = []
    for level, inner_ref, outer_ref, slope_ref, three in (
        (0, inner_four_ref, outer_four_ref, slope_four_ref, three_four),
        (1, inner_six_ref, outer_six_ref, slope_six_ref, three_six),
    ):
        here = slice(level, level + 1)
        pair = slice(2 * level, 2 * level + 2)
        coefs = level_coefs(moments_ref[pair], gain_ref[here], shift_ref[here], counts[level])
        parts.append(
            backward_level(
                cols[level], inner_ref, outer_ref, slope_ref, valid, coefs, slopes_ref[pair], counts[level], three
            )
        )
    fill_four, fill_six = parts
    rows_four, rows_six = three_four.shape[0] - 2, three_six.shape[0] - 2
    bounds = backward_bounds(rows_four)
    fills, dots, done = [], [], 0
    for start, end in zip(bounds[:-1], bounds[1:]):
        todo = [functools.partial(fill_four, row) for row in range(done, end + 2)]
        if end == rows_four:
            todo += [functools.partial(fill_six, row) for row in range(rows_six + 2)]
        fills.append(lambda todo=todo: [fill() for fill in todo])
        done = end + 2
        dots.append(
            functools.partial(weight_dot, turned_ref, three_four, three_six, total, (0, EARLY_TAPS), start, end)
        )
    staged(fills, dots)
    put_shares([total], sp_count, own_ref, sent_ref)
    rest_ref[...] = total[:, FIRST_TAPS * rest_ref.shape[0] :]


def weight_kernel(sp_count, turned_ref, three_four, three_six, rest_ref, own_ref, sent_ref, total):
    for start, end in chunks_of(three_four.shape[0] - 2, 16, 4):
        weight_dot(turned_ref, three_four, three_six, total, (EARLY_TAPS, 9), start, end)
    put_shares([rest_ref, total], sp_count, own_ref, sent_ref)


def input_chunks(three, turned, grad, chunks, offset, sent=None):
    cols, chan = grad.shape[1:]
    pitch = three.shape[1]
    for index, (start, end) in enumerate(chunks):
        size = end - start
        lhs = beside(three, (start + 2, start + 1, start), size)
        term = jnp.dot(lhs, turned[...], preferred_element_type=F32)
        grad[start - offset : end - offset] = term.reshape(size, pitch, chan)[:, :cols].astype(BF16)
        if sent is not None:
            sent(index, start, end)


def input_kernel(chunks, three_four, turned, grad_ref):
    input_chunks(three_four, turned, grad_ref, chunks, chunks[0][0])


def input_last_kernel(chunks, bounds, three_four, three_six, turned, *rest):
    count = len(bounds) - 1
    earlier, rest = rest[:count], rest[count:]
    grad_four_ref, grad_six_ref, grad_four, grad_six, sems, sems_four, sems_six = rest
    copies = [
        pltpu.make_async_copy(part, grad_four_ref.at[bounds[index] : bounds[index + 1]], sems.at[index])
        for index, part in enumerate(earlier)
    ]
    for copy in copies:
        copy.start()

    def sender(grad, grad_ref, offset, sems):
        def sent(index, start, end):
            copy = pltpu.make_async_copy(grad.at[start - offset : end - offset], grad_ref.at[start:end], sems.at[index])
            copy.start()
            copies.append(copy)

        return sent

    six_chunks = chunks_of(grad_six.shape[0], 12)
    input_chunks(three_six, turned, grad_six, six_chunks, 0, sender(grad_six, grad_six_ref, 0, sems_six))
    done = bounds[-1]
    input_chunks(three_four, turned, grad_four, chunks, done, sender(grad_four, grad_four_ref, done, sems_four))
    for copy in copies:
        copy.wait()


def swap(array, axis, stride):
    count = lax.axis_size(axis)
    return lax.ppermute(array, axis, [(i, i ^ stride) for i in range(count)])


def edge_kernel(starts, four_ref, six_ref, cotan_four_ref, cotan_six_ref, *rest):
    outs, six_rows, sems = rest[:-2], rest[-2], rest[-1]
    rows_four, cols_four = four_ref.shape[:2]
    rows_six = six_ref.shape[0]
    pitch = pitch_of(six_ref.shape[1])
    copies = []
    for number, (start, out_ref) in enumerate(zip(starts, outs)):
        last = (1 - jnp.minimum(lax.axis_index("sp"), 1)) if start is None else start
        for part, (ref, row) in enumerate(
            (
                (four_ref, last * (rows_four - 2)),
                (four_ref, last * (rows_four - 2) + 1),
                (cotan_four_ref, last * (rows_four - 1)),
                (six_ref, last * (rows_six - 2)),
                (six_ref, last * (rows_six - 2) + 1),
                (cotan_six_ref, last * (rows_six - 1)),
            )
        ):
            if part < 3:
                target = out_ref.at[part * cols_four : (part + 1) * cols_four]
            else:
                target = six_rows.at[number, part - 3]
            copies.append(pltpu.make_async_copy(ref.at[row], target, sems.at[number, part]))
    for copy in copies:
        copy.start()
    for copy in copies:
        copy.wait()
    for number, out_ref in enumerate(outs):
        for part in range(3):
            begin = 3 * cols_four + part * pitch
            out_ref[begin : begin + pitch] = widen(six_rows[number, part], pitch).astype(BF16)


def edges(four, six, cotan_four, cotan_six):
    count = lax.axis_size("sp")
    starts = (None,) if count == 2 else (0, 1)
    length = 3 * four.shape[1] + 3 * pitch_of(six.shape[1])
    vmem = pl.BlockSpec(memory_space=pltpu.VMEM)
    hbm = pl.BlockSpec(memory_space=pltpu.HBM)
    outs = pl.pallas_call(
        functools.partial(edge_kernel, starts),
        out_shape=tuple(jax.ShapeDtypeStruct((length, four.shape[2]), BF16) for _ in starts),
        in_specs=[hbm] * 4,
        out_specs=tuple(vmem for _ in starts),
        scratch_shapes=[
            pltpu.VMEM((len(starts), 3) + six.shape[1:], BF16),
            pltpu.SemaphoreType.DMA((len(starts), 6)),
        ],
        compiler_params=pltpu.CompilerParams(vmem_limit_bytes=EDGE_LIMIT),
        name="edges",
    )(four, six, cotan_four, cotan_six)
    if count == 2:
        met = swap(outs[0], "sp", 1)
        return met, met
    above = lax.ppermute(outs[1], "sp", [(i, (i + 1) % count) for i in range(count)])
    below = lax.ppermute(outs[0], "sp", [((i + 1) % count, i) for i in range(count)])
    return above, below


def swap_across(array, axis, stride):
    count, sp_count = lax.axis_size("rep"), lax.axis_size("sp")
    rep_stride, sp_stride = (stride, 1) if axis == "rep" else (0, stride ^ 1)
    pairs = [
        (rep * sp_count + sp, (rep ^ rep_stride) * sp_count + (sp ^ sp_stride))
        for rep in range(count)
        for sp in range(sp_count)
    ]
    return lax.ppermute(array, ("rep", "sp"), pairs)


def group_sum(sums):
    sums = sums + swap(sums, "sp", 1)
    stride = 2
    while stride < lax.axis_size("sp"):
        sums = sums + swap_across(sums, "sp", stride)
        stride = 2 * stride
    stride = 1
    while stride < GROUP:
        met = lax.optimization_barrier([swap_across(sums, "rep", k * stride) for k in FAR_FIRST])
        sums = (sums + met[2]) + (met[1] + met[0])
        stride = RADIX * stride
    return sums


def every_group(sums):
    stride = GROUP
    while stride < lax.axis_size("rep"):
        sums = sums + swap(sums, "rep", stride)
        stride = 2 * stride
    return sums


class Places(NamedTuple):
    digits: list
    first: list
    second: list
    odd: jax.Array


def places():
    rep = lax.axis_index("rep")
    digits = [(rep & (RADIX - 1)) ^ k for k in range(RADIX)]
    second = 9 - FIRST_TAPS
    return Places(
        digits,
        [FIRST_TAPS * digit for digit in digits],
        [RADIX * FIRST_TAPS + second * digit for digit in digits],
        parity(rep) == 1,
    )


def piece_of(pieces, index):
    sizes = (1,) + pieces.shape[1:]
    return lax.dynamic_slice(pieces, (index, 0, 0), sizes, allow_negative_indices=False)[0]


def scatter_pieces(own, met, found):
    chan = own.shape[2]
    parts = [part.reshape(RADIX, -1, chan) for part in [own] + met]

    def piece(k):
        total = piece_of(parts[0], found.digits[k])
        for part in parts[1:]:
            total = total + piece_of(part, found.digits[k])
        return total

    return piece(0), [piece(k).astype(BF16) for k in FAR_FIRST]


def added(own, met):
    return (own + met[2].astype(F32)) + (met[1].astype(F32) + met[0].astype(F32))


def fours(pieces, stride):
    return [swap(piece, "rep", k * stride) for k, piece in zip(FAR_FIRST, pieces)]


def swap_high(array, even, odd):
    count, sp_count = lax.axis_size("rep"), lax.axis_size("sp")
    pairs = []
    for rep in range(count):
        for sp in range(sp_count):
            stride = odd if (sp ^ parity(rep)) & 1 else even
            pairs.append((rep * sp_count + sp, (rep ^ stride) * sp_count + (sp ^ 1)))
    return lax.ppermute(array, ("rep", "sp"), pairs)


def bring(array, k):
    count, sp_count = lax.axis_size("rep"), lax.axis_size("sp")
    pairs = [
        (rep * sp_count + sp, (rep ^ k) * sp_count + (sp ^ parity(rep)))
        for rep in range(count)
        for sp in range(sp_count)
    ]
    return lax.ppermute(array, ("rep", "sp"), pairs)


def both(own, met):
    return (own.astype(F32) + met.astype(F32)).astype(BF16)


def every_share(total):
    stride = GROUP
    while stride < lax.axis_size("rep"):
        total = added(total.astype(F32), fours([total] * 3, stride)).astype(BF16)
        stride = RADIX * stride
    return total


def gather(total, found):
    beside = swap(total, "sp", 1)
    return [bring(total, k) for k in FAR_FIRST] + [jnp.where(found.odd, beside, total)], beside


def put_pieces(whole, pieces, starts):
    for k, piece in zip(FAR_FIRST + (0,), pieces):
        piece = piece.reshape((-1,) + whole.shape[1:]).astype(F32)
        whole = lax.dynamic_update_slice(whole, piece, (starts[k], 0, 0), allow_negative_indices=False)
    return whole


def local(level_four, level_six, conv_weight, bn_gain, bn_shift, cotan_four, cotan_six):
    sp_count = lax.axis_size("sp")
    images = level_four.shape[0]
    four, six, cot_four, cot_six = (a[0] for a in (level_four, level_six, cotan_four, cotan_six))
    rows_four, cols_four, chan = four.shape
    rows_six, cols_six = six.shape[:2]
    pitch_four, pitch_six = pitch_of(cols_four), pitch_of(cols_six)
    counts = (
        float(images * GROUP * rows_four * sp_count * cols_four),
        float(images * GROUP * rows_six * sp_count * cols_six),
    )
    found, four = lax.optimization_barrier((places(), four))
    above, below = edges(four, six, cot_four, cot_six)
    vmem = pl.BlockSpec(memory_space=pltpu.VMEM)
    hbm = pl.BlockSpec(memory_space=pltpu.HBM)
    params = pltpu.CompilerParams(vmem_limit_bytes=VMEM_LIMIT)
    framed_four = jax.ShapeDtypeStruct((rows_four + 2, pitch_four, chan), BF16)
    framed_six = jax.ShapeDtypeStruct((rows_six + 2, pitch_six, chan), BF16)
    four_sums = jax.ShapeDtypeStruct((4, chan), F32)
    flops = 2 * 9 * chan * chan * (rows_four * cols_four + rows_six * cols_six)

    def cost(share, size):
        return pl.CostEstimate(flops=int(flops * share), bytes_accessed=size, transcendentals=0)

    inner_four, inner_six, inner_moments = pl.pallas_call(
        inner_kernel,
        out_shape=(
            jax.ShapeDtypeStruct((rows_four - 2, pitch_four, chan), BF16),
            jax.ShapeDtypeStruct((rows_six - 2, pitch_six, chan), BF16),
            four_sums,
        ),
        in_specs=[vmem] * 3,
        out_specs=(vmem, vmem, vmem),
        scratch_shapes=[
            pltpu.VMEM((rows_four, pitch_four, 3 * chan), BF16),
            pltpu.VMEM((rows_six, pitch_six, 3 * chan), BF16),
        ],
        compiler_params=params,
        cost_estimate=cost(1, 4 * four.size),
        name="forward_inner",
    )(four, six, conv_weight)
    outer_four, outer_six, moments = pl.pallas_call(
        functools.partial(outer_kernel, sp_count),
        out_shape=(
            jax.ShapeDtypeStruct((4, pitch_four, chan), BF16),
            jax.ShapeDtypeStruct((4, pitch_six, chan), BF16),
            four_sums,
        ),
        in_specs=[vmem] * 6,
        out_specs=(vmem, vmem, vmem),
        scratch_shapes=[
            pltpu.VMEM((8, pitch_four, 3 * chan), BF16),
            pltpu.VMEM((8, pitch_six, 3 * chan), BF16),
        ],
        compiler_params=params,
        cost_estimate=cost(0.1, four.size),
        name="forward_outer",
    )(four, six, above, below, conv_weight, inner_moments)
    moments, four, six = lax.optimization_barrier((moments, four, six))
    turned, turned_weight = pl.pallas_call(
        turn_kernel,
        out_shape=(
            jax.ShapeDtypeStruct((chan, rows_four * cols_four + rows_six * pitch_six), BF16),
            jax.ShapeDtypeStruct((9 * chan, chan), BF16),
        ),
        in_specs=[vmem] * 3,
        out_specs=(vmem, vmem),
        compiler_params=params,
        cost_estimate=cost(0.3, 4 * four.size),
        name="turn",
    )(four, six, conv_weight)
    moments, turned, turned_weight = lax.optimization_barrier((group_sum(moments), turned, turned_weight))

    slope_four, slope_six, slopes = pl.pallas_call(
        functools.partial(slope_kernel, counts),
        out_shape=(
            jax.ShapeDtypeStruct(framed_four.shape, F32),
            jax.ShapeDtypeStruct(framed_six.shape, F32),
            four_sums,
        ),
        in_specs=[vmem] * 11,
        out_specs=(vmem,) * 3,
        compiler_params=params,
        cost_estimate=cost(0.01, 4 * four.size),
        name="slopes",
    )(
        inner_four, inner_six, outer_four, outer_six, cot_four, cot_six, above, below, moments, bn_gain, bn_shift
    )
    slopes = group_sum(slopes)

    share = chan // sp_count
    wide_four, wide_six = (
        jax.ShapeDtypeStruct(framed.shape[:2] + (3 * chan,), BF16) for framed in (framed_four, framed_six)
    )
    def shares(taps):
        return (
            jax.ShapeDtypeStruct((taps, share, chan), F32),
            jax.ShapeDtypeStruct((sp_count - 1, taps, share, chan), F32),
        )

    three_four, three_six, own_a, sent_a, rest, grad_gain, grad_shift = pl.pallas_call(
        functools.partial(backward_kernel, counts, sp_count, (cols_four, cols_six)),
        out_shape=(wide_four, wide_six)
        + shares(FIRST_TAPS)
        + (jax.ShapeDtypeStruct((chan, (EARLY_TAPS - FIRST_TAPS) * chan), F32),)
        + (jax.ShapeDtypeStruct((2, chan), F32),) * 2,
        in_specs=[vmem] * 11,
        out_specs=(vmem,) * 7,
        scratch_shapes=[pltpu.VMEM((chan, EARLY_TAPS * chan), F32)],
        compiler_params=params,
        cost_estimate=cost(0.6, 8 * four.size),
        name="backward",
    )(
        turned, inner_four, inner_six, outer_four, outer_six, slope_four, slope_six, moments, slopes,
        bn_gain, bn_shift,
    )
    sent_a, three_six = lax.optimization_barrier((sent_a, three_six))
    met_a = [swap(sent_a[step], "sp", step + 1) for step in range(sp_count - 1)]
    own_b, sent_b = pl.pallas_call(
        functools.partial(weight_kernel, sp_count),
        out_shape=shares(9 - FIRST_TAPS),
        in_specs=[vmem] * 4,
        out_specs=(vmem, vmem),
        scratch_shapes=[pltpu.VMEM((chan, (9 - EARLY_TAPS) * chan), F32)],
        compiler_params=params,
        cost_estimate=cost(0.6, 8 * four.size),
        name="weights",
    )(turned, three_four, three_six, rest)
    met_a, sent_b = lax.optimization_barrier((met_a, sent_b))
    met_b = [swap(sent_b[step], "sp", step + 1) for step in range(sp_count - 1)]

    chunks = chunks_of(rows_four, 8)
    cuts = [part * len(chunks) // 3 for part in range(4)]
    groups = [chunks[low:high] for low, high in zip(cuts[:-1], cuts[1:]) if low < high]
    bounds = [group[0][0] for group in groups]

    def inputs(group, three):
        return pl.pallas_call(
            functools.partial(input_kernel, group),
            out_shape=jax.ShapeDtypeStruct((group[-1][1] - group[0][0], cols_four, chan), BF16),
            in_specs=[vmem] * 2,
            out_specs=vmem,
            compiler_params=params,
            cost_estimate=cost(0.3, four.size),
            name="inputs",
        )(three, turned_weight)

    grad_gain, grad_shift = every_group(grad_gain), every_group(grad_shift)

    piece_a, pieces_a = scatter_pieces(own_a, met_a, found)
    met_a = fours(pieces_a, 1)
    piece_b, pieces_b = scatter_pieces(own_b, met_b, found)
    met_b = fours(pieces_b, 1)
    met_a, unused = lax.optimization_barrier((met_a, pieces_b))

    piece_a = added(piece_a, met_a).astype(BF16)
    piece_a, three_four = lax.optimization_barrier((piece_a, three_four))
    met_a = swap_high(piece_a, RADIX, 2 * RADIX)
    earlier = [inputs(groups[0], three_four)] if len(groups) > 1 else []
    met_b, earlier = lax.optimization_barrier((met_b, earlier))

    piece_b = added(piece_b, met_b).astype(BF16)
    met_b = swap_high(piece_b, RADIX, 2 * RADIX)
    met_a, unused = lax.optimization_barrier((met_a, piece_b))

    piece_a = both(piece_a, met_a)
    piece_a, three_four = lax.optimization_barrier((piece_a, three_four))
    met_a = swap_high(piece_a, 2 * RADIX, RADIX)
    if len(groups) > 2:
        earlier = earlier + [inputs(groups[1], three_four)]
    met_b, earlier = lax.optimization_barrier((met_b, earlier))

    piece_b = both(piece_b, met_b)
    met_b = swap_high(piece_b, 2 * RADIX, RADIX)
    met_a, unused = lax.optimization_barrier((met_a, piece_b))

    piece_a = every_share(both(piece_a, met_a))
    pieces_a, unused = gather(piece_a, found)
    piece_b = every_share(both(piece_b, met_b))
    pieces_b, beside = gather(piece_b, found)
    unused, three_four = lax.optimization_barrier(((beside, pieces_a[0]), three_four))
    done = bounds[-1]
    grad_four, grad_six = pl.pallas_call(
        functools.partial(input_last_kernel, groups[-1], bounds),
        out_shape=(
            jax.ShapeDtypeStruct(four.shape, BF16),
            jax.ShapeDtypeStruct(six.shape, BF16),
        ),
        in_specs=[vmem] * (3 + len(earlier)),
        out_specs=(hbm, hbm),
        scratch_shapes=[
            pltpu.VMEM((rows_four - done, cols_four, chan), BF16),
            pltpu.VMEM(six.shape, BF16),
            pltpu.SemaphoreType.DMA((len(groups),)),
            pltpu.SemaphoreType.DMA((len(chunks),)),
            pltpu.SemaphoreType.DMA((len(chunks_of(rows_six, 12)),)),
        ],
        compiler_params=params,
        cost_estimate=cost(0.4, 2 * four.size),
        name="inputs_last",
    )(three_four, three_six, turned_weight, *earlier)
    pieces_a, grad_six = lax.optimization_barrier((pieces_a, grad_six))
    whole = jnp.zeros((9 * RADIX, share // RADIX, chan), F32)
    whole = put_pieces(whole, pieces_a, found.first)
    whole = put_pieces(whole, pieces_b, found.second)
    grad_weight = whole.reshape(9, share, chan)
    return (grad_four[None], grad_six[None], grad_weight, grad_gain, grad_shift)


def solution(mesh):
    placed = (
        P("rep", "sp", None, None),
        P("rep", "sp", None, None),
        P(),
        P(),
        P(),
        P("rep", "sp", None, None),
        P("rep", "sp", None, None),
    )
    return jax.shard_map(
        local,
        mesh=mesh,
        in_specs=placed,
        out_specs=(
            P("rep", "sp", None, None),
            P("rep", "sp", None, None),
            P(None, "sp", None),
            P(),
            P(),
        ),
        check_vma=False,
    )
```

```python
import functools
from typing import NamedTuple

import jax
import jax.numpy as jnp
from jax import lax
from jax.experimental import pallas as pl
from jax.experimental.pallas import tpu as pltpu
from jax.sharding import PartitionSpec as P

GROUP = 16
RADIX = 4
FAR_FIRST = (3, 2, 1)
FIRST_TAPS = 4
EARLY_TAPS = 6
EPSILON = 1e-05
F32 = jnp.float32
BF16 = jnp.bfloat16
VMEM_LIMIT = 20 * 1024 * 1024
EDGE_LIMIT = 60 * 1024 * 1024


def chunk_of(rows, most, multiple=1):
    sizes = [size for size in range(1, most + 1) if rows % size == 0 and size % multiple == 0]
    return max(sizes) if sizes else rows


def pitch_of(cols):
    return -(-cols // 16) * 16


def parity(rep):
    return ((rep >> 2) ^ (rep >> 3)) & 1


def chunks_of(rows, most, multiple=1):
    size = chunk_of(rows, most, multiple)
    return [(start, start + size) for start in range(0, rows, size)]


def widen(cells, pitch):
    cells = cells.astype(F32)
    extra = pitch - cells.shape[0]
    if extra:
        cells = jnp.concatenate([cells, jnp.zeros((extra, cells.shape[1]), F32)], 0)
    return cells


def put_three(three, row, cells, cols, turned):
    pitch, chan = cells.shape
    left, right = pltpu.roll(cells, 1, 0), pltpu.roll(cells, pitch - 1, 0)
    if pitch == cols:
        col = lax.broadcasted_iota(jnp.int32, (8, chan), 0)
        left = jnp.concatenate([jnp.where(col == 0, 0.0, left[:8]), left[8:]], 0)
        right = jnp.concatenate([right[:-8], jnp.where(col == 7, 0.0, right[-8:])], 0)
    parts = (right, cells, left) if turned else (left, cells, right)
    for place, part in enumerate(parts):
        three[row, :, place * chan : (place + 1) * chan] = part.astype(BF16)


def beside(three, starts, size):
    pitch, width = three.shape[1:]
    return jnp.concatenate([three[start : start + size].reshape(size * pitch, width) for start in starts], 1)


def edges_valid(sp_count):
    index = lax.axis_index("sp")
    return jnp.where(index > 0, 1.0, 0.0), jnp.where(index < sp_count - 1, 1.0, 0.0)


def level_coefs(moments, gain, shift, count):
    mean = moments[0:1] / count
    spread = moments[1:2] / count - mean * mean
    return mean, lax.rsqrt(spread + EPSILON), gain, shift


def slope_of(conv, cotan, coefs):
    mean, rstd, gain, shift = coefs
    centred = conv.astype(F32) - mean
    half = centred * (0.5 * rstd * gain) + 0.5 * shift
    turn = jnp.tanh(half)
    return centred, cotan.astype(F32) * ((1.0 + turn) * (1.0 + half * (1.0 - turn)))


def masked(cells, cols):
    if cells.shape[0] == cols:
        return cells
    col = lax.broadcasted_iota(jnp.int32, cells.shape, 0)
    return jnp.where(col < cols, cells, 0.0)


def staged(fills, dots):
    fills[0]()
    for index, dot in enumerate(dots):
        if index + 1 < len(fills):
            fills[index + 1]()
        dot()


def conv_rows(lhs, w_ref):
    return jnp.dot(lhs, w_ref[...].reshape(lhs.shape[1], -1), preferred_element_type=F32).astype(BF16)


def add_moments(sums, conv, cols):
    chan = conv.shape[2]
    conv = conv.astype(F32)
    if conv.shape[1] != cols:
        conv = conv[:, :cols]
    conv = conv.reshape(-1, 8, chan)
    sums[0].append(jnp.sum(conv, 0))
    sums[1].append(jnp.sum(conv * conv, 0))


def folded(parts):
    total = parts[0]
    for part in parts[1:]:
        total = total + part
    return jnp.sum(total, 0, keepdims=True)


def inner_kernel(four_ref, six_ref, w_ref, conv_four_ref, conv_six_ref, moments_ref, three_four, three_six):
    rows_four, cols_four = four_ref.shape[:2]
    rows_six, cols_six = six_ref.shape[:2]
    pitch_four, pitch_six = three_four.shape[1], three_six.shape[1]
    sums_four, sums_six = ([], []), ([], [])
    inner = rows_four - 2
    count = max(1, inner // 9)
    bounds = [index * inner // count for index in range(count + 1)]

    def fill_four(row):
        put_three(three_four, row, four_ref[row].astype(F32), cols_four, False)

    def fill_six(row):
        put_three(three_six, row, widen(six_ref[row], pitch_six), cols_six, False)

    def dot(start, end):
        lhs = beside(three_four, (start, start + 1, start + 2), end - start)
        cells = lhs.shape[0]
        if end == inner:
            lhs = jnp.concatenate([lhs, beside(three_six, (0, 1, 2), rows_six - 2)], 0)
        conv = conv_rows(lhs, w_ref)
        four = conv[:cells].reshape(end - start, pitch_four, -1)
        conv_four_ref[start:end] = four
        add_moments(sums_four, four, cols_four)
        if end == inner:
            six = conv[cells:].reshape(rows_six - 2, pitch_six, -1)
            conv_six_ref[...] = six
            add_moments(sums_six, six, cols_six)

    fills, dots, done = [], [], 0
    for start, end in zip(bounds[:-1], bounds[1:]):
        todo = [functools.partial(fill_four, row) for row in range(done, end + 2)]
        if end == inner:
            todo += [functools.partial(fill_six, row) for row in range(rows_six)]
        fills.append(lambda todo=todo: [fill() for fill in todo])
        done = end + 2
        dots.append(functools.partial(dot, start, end))
    staged(fills, dots)
    moments_ref[...] = jnp.concatenate([folded(parts) for parts in sums_four + sums_six], 0)


def outer_level(x_ref, top, bottom, valid, three):
    rows, cols = x_ref.shape[:2]
    pitch = three.shape[1]
    for edge in range(2):
        put_three(three, edge, top(edge) * valid[0], cols, False)
        put_three(three, 2 + edge, widen(x_ref[edge], pitch), cols, False)
        put_three(three, 4 + edge, widen(x_ref[rows - 2 + edge], pitch), cols, False)
        put_three(three, 6 + edge, bottom(edge) * valid[1], cols, False)
    return [beside(three, (start, start + 1, start + 2), 2) for start in (0, 4)]


def outer_kernel(
    sp_count, four_ref, six_ref, above_ref, below_ref, w_ref, inner_ref,
    conv_four_ref, conv_six_ref, moments_ref, three_four, three_six,
):
    cols_four = four_ref.shape[1]
    valid = edges_valid(sp_count)
    base, pitch_six = 3 * cols_four, three_six.shape[1]

    def reader(ref, start, pitch):
        return lambda edge: ref[start + edge * pitch : start + (edge + 1) * pitch].astype(F32)

    lhs = outer_level(
        four_ref, reader(above_ref, 0, cols_four), reader(below_ref, 0, cols_four), valid, three_four
    ) + outer_level(
        six_ref, reader(above_ref, base, pitch_six), reader(below_ref, base, pitch_six), valid, three_six
    )
    conv = conv_rows(jnp.concatenate(lhs, 0), w_ref)
    sums, begin = [], 0
    for conv_ref, cols in ((conv_four_ref, cols_four), (conv_six_ref, six_ref.shape[1])):
        cells = conv_ref.shape[0] * conv_ref.shape[1]
        rows = conv[begin : begin + cells].reshape(conv_ref.shape)
        begin += cells
        conv_ref[...] = rows
        parts = ([], [])
        add_moments(parts, rows[1:3], cols)
        sums += [folded(part) for part in parts]
    moments_ref[...] = inner_ref[...] + jnp.concatenate(sums, 0)


def turn_kernel(four_ref, six_ref, w_ref, turned_ref, turned_w_ref):
    rows_four, cols_four, chan = four_ref.shape
    rows_six, cols_six = six_ref.shape[:2]
    pitch = pitch_of(cols_six)
    for start, end in chunks_of(rows_four, 8, 4):
        cells = four_ref[start:end].reshape((end - start) * cols_four, chan)
        turned_ref[:, start * cols_four : end * cols_four] = cells.T
    cells = six_ref[...].astype(F32)
    cells = jnp.concatenate([cells, jnp.zeros((rows_six, pitch - cols_six, chan), F32)], 1).astype(BF16)
    turned_ref[:, rows_four * cols_four :] = cells.reshape(rows_six * pitch, chan).T
    for tap in range(9):
        turned_w_ref[tap * chan : (tap + 1) * chan] = w_ref[tap].T


def slope_level(inner_ref, outer_ref, cotan_ref, above, below, coefs, slope_ref):
    rows, cols, chan = cotan_ref.shape
    pitch = inner_ref.shape[1]

    def put(row, conv, cotan):
        centred, slope = slope_of(conv, widen(cotan, pitch), coefs)
        slope_ref[row] = slope
        return centred, slope

    def add(sums, pair):
        centred, slope = pair
        first = jnp.sum(slope.reshape(-1, 8, chan), 0)
        second = jnp.sum((slope * centred).reshape(-1, 8, chan), 0)
        return sums[0] + first, sums[1] + second

    def step(row, sums):
        return add(sums, put(row + 2, inner_ref[row], cotan_ref[row + 1]))

    put(0, outer_ref[0], above)
    put(rows + 1, outer_ref[3], below)
    zero = jnp.zeros((8, chan), F32)
    sums = add((zero, zero), put(1, outer_ref[1], cotan_ref[0]))
    sums = add(sums, put(rows, outer_ref[2], cotan_ref[rows - 1]))
    for row in range(rows - 2):
        sums = step(row, sums)
    first = 0.5 * jnp.sum(sums[0], 0, keepdims=True)
    return first, 0.5 * coefs[1] * jnp.sum(sums[1], 0, keepdims=True)


def slope_kernel(
    counts, inner_four_ref, inner_six_ref, outer_four_ref, outer_six_ref, cotan_four_ref, cotan_six_ref,
    above_ref, below_ref, moments_ref, gain_ref, shift_ref, slope_four_ref, slope_six_ref, slopes_ref,
):
    sums = ()
    cols_four = cotan_four_ref.shape[1]
    starts = (2 * cols_four, 3 * cols_four + 2 * inner_six_ref.shape[1])
    for level, (inner_ref, outer_ref, cotan_ref, slope_ref) in enumerate(
        (
            (inner_four_ref, outer_four_ref, cotan_four_ref, slope_four_ref),
            (inner_six_ref, outer_six_ref, cotan_six_ref, slope_six_ref),
        )
    ):
        pair = moments_ref[2 * level : 2 * level + 2]
        here = slice(level, level + 1)
        edge = slice(starts[level], starts[level] + inner_ref.shape[1])
        coefs = level_coefs(pair, gain_ref[here], shift_ref[here], counts[level])
        sums += slope_level(inner_ref, outer_ref, cotan_ref, above_ref[edge], below_ref[edge], coefs, slope_ref)
    slopes_ref[...] = jnp.concatenate(sums, 0)


def backward_level(cols, inner_ref, outer_ref, slope_ref, valid, coefs, slopes, count, three):
    rows = inner_ref.shape[0] + 2
    pitch = three.shape[1]
    mean, rstd, gain, shift = coefs
    lead = gain * rstd
    offset, factor = lead * (slopes[0:1] / count), lead * rstd * (slopes[1:2] / count)

    def fill_row(row):
        if 2 <= row < rows:
            conv = inner_ref[row - 2]
        else:
            conv = outer_ref[row if row < 2 else row - rows + 2]
        centred = conv.astype(F32) - mean
        dconv = masked((0.5 * lead) * slope_ref[row] - (offset + centred * factor), cols)
        if row == 0:
            dconv = dconv * valid[0]
        elif row == rows + 1:
            dconv = dconv * valid[1]
        put_three(three, row, dconv, cols, True)

    return fill_row


def taps_beside(three, start, end, taps):
    pitch, width = three.shape[1:]
    chan = width // 3
    parts = []
    for row_tap in range(3):
        low, high = max(taps[0] - 3 * row_tap, 0), min(taps[1] - 3 * row_tap, 3)
        if low < high:
            first = start + 2 - row_tap
            rows = three[first : first + end - start, :, low * chan : high * chan]
            parts.append(rows.reshape((end - start) * pitch, (high - low) * chan))
    return jnp.concatenate(parts, 1)


def backward_bounds(rows):
    bounds = [0, min(8, rows)]
    while bounds[-1] < rows:
        bounds.append(min(bounds[-1] + 16, rows))
    return bounds


def weight_dot(turned_ref, three_four, three_six, total, taps, start, end):
    rows_four, rows_six = three_four.shape[0] - 2, three_six.shape[0] - 2
    pitch = three_four.shape[1]
    first, last = start * pitch, end * pitch
    rhs = taps_beside(three_four, start, end, taps)
    if end == rows_four:
        rhs = jnp.concatenate([rhs, taps_beside(three_six, 0, rows_six, taps)], 0)
        last = turned_ref.shape[1]
    term = jnp.dot(turned_ref[:, first:last], rhs, preferred_element_type=F32)
    total[...] = total[...] + term if start else term


def put_shares(totals, sp_count, own_ref, sent_ref):
    taps, share, chan = own_ref.shape
    places = [(total, start) for total in totals for start in range(0, total.shape[1], chan)][:taps]
    place = lax.axis_index("sp") ^ parity(lax.axis_index("rep"))
    for step in range(sp_count):
        begin = pl.multiple_of((place ^ step) * share, share)
        for tap, (total, start) in enumerate(places):
            part = total[pl.ds(begin, share), start : start + chan]
            if step == 0:
                own_ref[tap] = part
            else:
                sent_ref[step - 1, tap] = part


def backward_kernel(
    counts, sp_count, cols, turned_ref, inner_four_ref, inner_six_ref, outer_four_ref, outer_six_ref,
    slope_four_ref, slope_six_ref, moments_ref, slopes_ref, gain_ref, shift_ref, three_four, three_six, own_ref,
    sent_ref, rest_ref, grad_gain_ref, grad_shift_ref, total,
):
    valid = edges_valid(sp_count)
    grad_gain_ref[...] = jnp.concatenate([slopes_ref[1:2], slopes_ref[3:4]], 0)
    grad_shift_ref[...] = jnp.concatenate([slopes_ref[0:1], slopes_ref[2:3]], 0)
    parts = []
    for level, inner_ref, outer_ref, slope_ref, three in (
        (0, inner_four_ref, outer_four_ref, slope_four_ref, three_four),
        (1, inner_six_ref, outer_six_ref, slope_six_ref, three_six),
    ):
        here = slice(level, level + 1)
        pair = slice(2 * level, 2 * level + 2)
        coefs = level_coefs(moments_ref[pair], gain_ref[here], shift_ref[here], counts[level])
        parts.append(
            backward_level(
                cols[level], inner_ref, outer_ref, slope_ref, valid, coefs, slopes_ref[pair], counts[level], three
            )
        )
    fill_four, fill_six = parts
    rows_four, rows_six = three_four.shape[0] - 2, three_six.shape[0] - 2
    bounds = backward_bounds(rows_four)
    fills, dots, done = [], [], 0
    for start, end in zip(bounds[:-1], bounds[1:]):
        todo = [functools.partial(fill_four, row) for row in range(done, end + 2)]
        if end == rows_four:
            todo += [functools.partial(fill_six, row) for row in range(rows_six + 2)]
        fills.append(lambda todo=todo: [fill() for fill in todo])
        done = end + 2
        dots.append(
            functools.partial(weight_dot, turned_ref, three_four, three_six, total, (0, EARLY_TAPS), start, end)
        )
    staged(fills, dots)
    put_shares([total], sp_count, own_ref, sent_ref)
    rest_ref[...] = total[:, FIRST_TAPS * rest_ref.shape[0] :]


def weight_kernel(sp_count, turned_ref, three_four, three_six, rest_ref, own_ref, sent_ref, total):
    for start, end in chunks_of(three_four.shape[0] - 2, 16, 4):
        weight_dot(turned_ref, three_four, three_six, total, (EARLY_TAPS, 9), start, end)
    put_shares([rest_ref, total], sp_count, own_ref, sent_ref)


def input_chunks(three, turned, grad, chunks, offset, sent=None):
    cols, chan = grad.shape[1:]
    pitch = three.shape[1]
    for index, (start, end) in enumerate(chunks):
        size = end - start
        lhs = beside(three, (start + 2, start + 1, start), size)
        term = jnp.dot(lhs, turned[...], preferred_element_type=F32)
        grad[start - offset : end - offset] = term.reshape(size, pitch, chan)[:, :cols].astype(BF16)
        if sent is not None:
            sent(index, start, end)


def input_kernel(chunks, three_four, three_six, turned, grad_ref, *six_refs):
    for six_ref in six_refs:
        input_chunks(three_six, turned, six_ref, [(0, six_ref.shape[0])], 0)
    input_chunks(three_four, turned, grad_ref, chunks, chunks[0][0])


def input_last_kernel(chunks, bounds, three_four, turned, six_ref, *rest):
    count = len(bounds) - 1
    earlier, rest = rest[:count], rest[count:]
    grad_four_ref, grad_six_ref, grad_four, sems, sems_four = rest
    copies = [pltpu.make_async_copy(six_ref, grad_six_ref, sems.at[count])]
    copies += [
        pltpu.make_async_copy(part, grad_four_ref.at[bounds[index] : bounds[index + 1]], sems.at[index])
        for index, part in enumerate(earlier)
    ]
    for copy in copies:
        copy.start()
    done = bounds[-1]

    def sent(index, start, end):
        copy = pltpu.make_async_copy(
            grad_four.at[start - done : end - done], grad_four_ref.at[start:end], sems_four.at[index]
        )
        copy.start()
        copies.append(copy)

    input_chunks(three_four, turned, grad_four, chunks, done, sent)
    for copy in copies:
        copy.wait()


def swap(array, axis, stride):
    count = lax.axis_size(axis)
    return lax.ppermute(array, axis, [(i, i ^ stride) for i in range(count)])


def edge_kernel(starts, four_ref, six_ref, cotan_four_ref, cotan_six_ref, *rest):
    outs, six_rows, sems = rest[:-2], rest[-2], rest[-1]
    rows_four, cols_four = four_ref.shape[:2]
    rows_six = six_ref.shape[0]
    pitch = pitch_of(six_ref.shape[1])
    copies = []
    for number, (start, out_ref) in enumerate(zip(starts, outs)):
        last = (1 - jnp.minimum(lax.axis_index("sp"), 1)) if start is None else start
        for part, (ref, row) in enumerate(
            (
                (four_ref, last * (rows_four - 2)),
                (four_ref, last * (rows_four - 2) + 1),
                (cotan_four_ref, last * (rows_four - 1)),
                (six_ref, last * (rows_six - 2)),
                (six_ref, last * (rows_six - 2) + 1),
                (cotan_six_ref, last * (rows_six - 1)),
            )
        ):
            if part < 3:
                target = out_ref.at[part * cols_four : (part + 1) * cols_four]
            else:
                target = six_rows.at[number, part - 3]
            copies.append(pltpu.make_async_copy(ref.at[row], target, sems.at[number, part]))
    for copy in copies:
        copy.start()
    for copy in copies:
        copy.wait()
    for number, out_ref in enumerate(outs):
        for part in range(3):
            begin = 3 * cols_four + part * pitch
            out_ref[begin : begin + pitch] = widen(six_rows[number, part], pitch).astype(BF16)


def edges(four, six, cotan_four, cotan_six):
    count = lax.axis_size("sp")
    starts = (None,) if count == 2 else (0, 1)
    length = 3 * four.shape[1] + 3 * pitch_of(six.shape[1])
    vmem = pl.BlockSpec(memory_space=pltpu.VMEM)
    hbm = pl.BlockSpec(memory_space=pltpu.HBM)
    outs = pl.pallas_call(
        functools.partial(edge_kernel, starts),
        out_shape=tuple(jax.ShapeDtypeStruct((length, four.shape[2]), BF16) for _ in starts),
        in_specs=[hbm] * 4,
        out_specs=tuple(vmem for _ in starts),
        scratch_shapes=[
            pltpu.VMEM((len(starts), 3) + six.shape[1:], BF16),
            pltpu.SemaphoreType.DMA((len(starts), 6)),
        ],
        compiler_params=pltpu.CompilerParams(vmem_limit_bytes=EDGE_LIMIT),
        name="edges",
    )(four, six, cotan_four, cotan_six)
    if count == 2:
        met = swap(outs[0], "sp", 1)
        return met, met
    above = lax.ppermute(outs[1], "sp", [(i, (i + 1) % count) for i in range(count)])
    below = lax.ppermute(outs[0], "sp", [((i + 1) % count, i) for i in range(count)])
    return above, below


def swap_across(array, axis, stride):
    count, sp_count = lax.axis_size("rep"), lax.axis_size("sp")
    rep_stride, sp_stride = (stride, 1) if axis == "rep" else (0, stride ^ 1)
    pairs = [
        (rep * sp_count + sp, (rep ^ rep_stride) * sp_count + (sp ^ sp_stride))
        for rep in range(count)
        for sp in range(sp_count)
    ]
    return lax.ppermute(array, ("rep", "sp"), pairs)


def group_sum(sums):
    sums = sums + swap(sums, "sp", 1)
    stride = 2
    while stride < lax.axis_size("sp"):
        sums = sums + swap_across(sums, "sp", stride)
        stride = 2 * stride
    stride = 1
    while stride < GROUP:
        met = lax.optimization_barrier([swap_across(sums, "rep", k * stride) for k in FAR_FIRST])
        sums = (sums + met[2]) + (met[1] + met[0])
        stride = RADIX * stride
    return sums


def every_group(sums):
    stride = GROUP
    while stride < lax.axis_size("rep"):
        sums = sums + swap(sums, "rep", stride)
        stride = 2 * stride
    return sums


class Places(NamedTuple):
    digits: list
    first: list
    second: list
    odd: jax.Array


def places():
    rep = lax.axis_index("rep")
    digits = [(rep & (RADIX - 1)) ^ k for k in range(RADIX)]
    second = 9 - FIRST_TAPS
    return Places(
        digits,
        [FIRST_TAPS * digit for digit in digits],
        [RADIX * FIRST_TAPS + second * digit for digit in digits],
        parity(rep) == 1,
    )


def piece_of(pieces, index):
    sizes = (1,) + pieces.shape[1:]
    return lax.dynamic_slice(pieces, (index, 0, 0), sizes, allow_negative_indices=False)[0]


def scatter_pieces(own, met, found):
    chan = own.shape[2]
    parts = [part.reshape(RADIX, -1, chan) for part in [own] + met]

    def piece(k):
        total = piece_of(parts[0], found.digits[k])
        for part in parts[1:]:
            total = total + piece_of(part, found.digits[k])
        return total

    return piece(0), [piece(k).astype(BF16) for k in FAR_FIRST]


def added(own, met):
    return (own + met[2].astype(F32)) + (met[1].astype(F32) + met[0].astype(F32))


def fours(pieces, stride):
    return [swap(piece, "rep", k * stride) for k, piece in zip(FAR_FIRST, pieces)]


def swap_high(array, even, odd):
    count, sp_count = lax.axis_size("rep"), lax.axis_size("sp")
    pairs = []
    for rep in range(count):
        for sp in range(sp_count):
            stride = odd if (sp ^ parity(rep)) & 1 else even
            pairs.append((rep * sp_count + sp, (rep ^ stride) * sp_count + (sp ^ 1)))
    return lax.ppermute(array, ("rep", "sp"), pairs)


def bring(array, k):
    count, sp_count = lax.axis_size("rep"), lax.axis_size("sp")
    pairs = [
        (rep * sp_count + sp, (rep ^ k) * sp_count + (sp ^ parity(rep)))
        for rep in range(count)
        for sp in range(sp_count)
    ]
    return lax.ppermute(array, ("rep", "sp"), pairs)


def both(own, met):
    return (own.astype(F32) + met.astype(F32)).astype(BF16)


def every_share(total):
    stride = GROUP
    while stride < lax.axis_size("rep"):
        total = added(total.astype(F32), fours([total] * 3, stride)).astype(BF16)
        stride = RADIX * stride
    return total


def gather(total, found):
    beside = swap(total, "sp", 1)
    return [bring(total, k) for k in FAR_FIRST] + [jnp.where(found.odd, beside, total)], beside


def put_pieces(whole, pieces, starts):
    for k, piece in zip(FAR_FIRST + (0,), pieces):
        piece = piece.reshape((-1,) + whole.shape[1:]).astype(F32)
        whole = lax.dynamic_update_slice(whole, piece, (starts[k], 0, 0), allow_negative_indices=False)
    return whole


def local(level_four, level_six, conv_weight, bn_gain, bn_shift, cotan_four, cotan_six):
    sp_count = lax.axis_size("sp")
    images = level_four.shape[0]
    four, six, cot_four, cot_six = (a[0] for a in (level_four, level_six, cotan_four, cotan_six))
    rows_four, cols_four, chan = four.shape
    rows_six, cols_six = six.shape[:2]
    pitch_four, pitch_six = pitch_of(cols_four), pitch_of(cols_six)
    counts = (
        float(images * GROUP * rows_four * sp_count * cols_four),
        float(images * GROUP * rows_six * sp_count * cols_six),
    )
    found, four = lax.optimization_barrier((places(), four))
    above, below = edges(four, six, cot_four, cot_six)
    vmem = pl.BlockSpec(memory_space=pltpu.VMEM)
    hbm = pl.BlockSpec(memory_space=pltpu.HBM)
    params = pltpu.CompilerParams(vmem_limit_bytes=VMEM_LIMIT)
    framed_four = jax.ShapeDtypeStruct((rows_four + 2, pitch_four, chan), BF16)
    framed_six = jax.ShapeDtypeStruct((rows_six + 2, pitch_six, chan), BF16)
    four_sums = jax.ShapeDtypeStruct((4, chan), F32)
    flops = 2 * 9 * chan * chan * (rows_four * cols_four + rows_six * cols_six)

    def cost(share, size):
        return pl.CostEstimate(flops=int(flops * share), bytes_accessed=size, transcendentals=0)

    inner_four, inner_six, inner_moments = pl.pallas_call(
        inner_kernel,
        out_shape=(
            jax.ShapeDtypeStruct((rows_four - 2, pitch_four, chan), BF16),
            jax.ShapeDtypeStruct((rows_six - 2, pitch_six, chan), BF16),
            four_sums,
        ),
        in_specs=[vmem] * 3,
        out_specs=(vmem, vmem, vmem),
        scratch_shapes=[
            pltpu.VMEM((rows_four, pitch_four, 3 * chan), BF16),
            pltpu.VMEM((rows_six, pitch_six, 3 * chan), BF16),
        ],
        compiler_params=params,
        cost_estimate=cost(1, 4 * four.size),
        name="forward_inner",
    )(four, six, conv_weight)
    outer_four, outer_six, moments = pl.pallas_call(
        functools.partial(outer_kernel, sp_count),
        out_shape=(
            jax.ShapeDtypeStruct((4, pitch_four, chan), BF16),
            jax.ShapeDtypeStruct((4, pitch_six, chan), BF16),
            four_sums,
        ),
        in_specs=[vmem] * 6,
        out_specs=(vmem, vmem, vmem),
        scratch_shapes=[
            pltpu.VMEM((8, pitch_four, 3 * chan), BF16),
            pltpu.VMEM((8, pitch_six, 3 * chan), BF16),
        ],
        compiler_params=params,
        cost_estimate=cost(0.1, four.size),
        name="forward_outer",
    )(four, six, above, below, conv_weight, inner_moments)
    moments, four, six = lax.optimization_barrier((moments, four, six))
    turned, turned_weight = pl.pallas_call(
        turn_kernel,
        out_shape=(
            jax.ShapeDtypeStruct((chan, rows_four * cols_four + rows_six * pitch_six), BF16),
            jax.ShapeDtypeStruct((9 * chan, chan), BF16),
        ),
        in_specs=[vmem] * 3,
        out_specs=(vmem, vmem),
        compiler_params=params,
        cost_estimate=cost(0.3, 4 * four.size),
        name="turn",
    )(four, six, conv_weight)
    moments, turned, turned_weight = lax.optimization_barrier((group_sum(moments), turned, turned_weight))

    slope_four, slope_six, slopes = pl.pallas_call(
        functools.partial(slope_kernel, counts),
        out_shape=(
            jax.ShapeDtypeStruct(framed_four.shape, F32),
            jax.ShapeDtypeStruct(framed_six.shape, F32),
            four_sums,
        ),
        in_specs=[vmem] * 11,
        out_specs=(vmem,) * 3,
        compiler_params=params,
        cost_estimate=cost(0.01, 4 * four.size),
        name="slopes",
    )(
        inner_four, inner_six, outer_four, outer_six, cot_four, cot_six, above, below, moments, bn_gain, bn_shift
    )
    slopes = group_sum(slopes)

    share = chan // sp_count
    wide_four, wide_six = (
        jax.ShapeDtypeStruct(framed.shape[:2] + (3 * chan,), BF16) for framed in (framed_four, framed_six)
    )
    def shares(taps):
        return (
            jax.ShapeDtypeStruct((taps, share, chan), F32),
            jax.ShapeDtypeStruct((sp_count - 1, taps, share, chan), F32),
        )

    three_four, three_six, own_a, sent_a, rest, grad_gain, grad_shift = pl.pallas_call(
        functools.partial(backward_kernel, counts, sp_count, (cols_four, cols_six)),
        out_shape=(wide_four, wide_six)
        + shares(FIRST_TAPS)
        + (jax.ShapeDtypeStruct((chan, (EARLY_TAPS - FIRST_TAPS) * chan), F32),)
        + (jax.ShapeDtypeStruct((2, chan), F32),) * 2,
        in_specs=[vmem] * 11,
        out_specs=(vmem,) * 7,
        scratch_shapes=[pltpu.VMEM((chan, EARLY_TAPS * chan), F32)],
        compiler_params=params,
        cost_estimate=cost(0.6, 8 * four.size),
        name="backward",
    )(
        turned, inner_four, inner_six, outer_four, outer_six, slope_four, slope_six, moments, slopes,
        bn_gain, bn_shift,
    )
    sent_a, three_six = lax.optimization_barrier((sent_a, three_six))
    met_a = [swap(sent_a[step], "sp", step + 1) for step in range(sp_count - 1)]
    own_b, sent_b = pl.pallas_call(
        functools.partial(weight_kernel, sp_count),
        out_shape=shares(9 - FIRST_TAPS),
        in_specs=[vmem] * 4,
        out_specs=(vmem, vmem),
        scratch_shapes=[pltpu.VMEM((chan, (9 - EARLY_TAPS) * chan), F32)],
        compiler_params=params,
        cost_estimate=cost(0.6, 8 * four.size),
        name="weights",
    )(turned, three_four, three_six, rest)
    met_a, sent_b = lax.optimization_barrier((met_a, sent_b))
    met_b = [swap(sent_b[step], "sp", step + 1) for step in range(sp_count - 1)]

    chunks = chunks_of(rows_four, 8)
    cuts = [part * len(chunks) // 3 for part in range(4)]
    groups = [chunks[low:high] for low, high in zip(cuts[:-1], cuts[1:]) if low < high]
    bounds = [group[0][0] for group in groups]

    def inputs(number, three):
        group = groups[number]
        parts = (jax.ShapeDtypeStruct((group[-1][1] - group[0][0], cols_four, chan), BF16),)
        if number == len(groups) - 2:
            parts += (jax.ShapeDtypeStruct(six.shape, BF16),)
        return pl.pallas_call(
            functools.partial(input_kernel, group),
            out_shape=parts,
            in_specs=[vmem] * 3,
            out_specs=(vmem,) * len(parts),
            compiler_params=params,
            cost_estimate=cost(0.3, four.size),
            name="inputs",
        )(three, three_six, turned_weight)

    grad_gain, grad_shift = every_group(grad_gain), every_group(grad_shift)

    piece_a, pieces_a = scatter_pieces(own_a, met_a, found)
    met_a = fours(pieces_a, 1)
    piece_b, pieces_b = scatter_pieces(own_b, met_b, found)
    met_b = fours(pieces_b, 1)
    met_a, unused = lax.optimization_barrier((met_a, pieces_b))

    piece_a = added(piece_a, met_a).astype(BF16)
    piece_a, three_four = lax.optimization_barrier((piece_a, three_four))
    met_a = swap_high(piece_a, RADIX, 2 * RADIX)
    earlier = list(inputs(0, three_four))
    whole = jnp.zeros((9 * RADIX, share // RADIX, chan), F32)
    met_b, earlier, whole = lax.optimization_barrier((met_b, earlier, whole))

    piece_b = added(piece_b, met_b).astype(BF16)
    met_b = swap_high(piece_b, RADIX, 2 * RADIX)
    met_a, unused = lax.optimization_barrier((met_a, piece_b))

    piece_a = both(piece_a, met_a)
    piece_a, three_four = lax.optimization_barrier((piece_a, three_four))
    met_a = swap_high(piece_a, 2 * RADIX, RADIX)
    if len(groups) > 2:
        earlier = earlier + list(inputs(1, three_four))
    met_b, earlier = lax.optimization_barrier((met_b, earlier))

    piece_b = both(piece_b, met_b)
    met_b = swap_high(piece_b, 2 * RADIX, RADIX)
    met_a, unused = lax.optimization_barrier((met_a, piece_b))

    piece_a = every_share(both(piece_a, met_a))
    pieces_a, unused = gather(piece_a, found)
    piece_b = every_share(both(piece_b, met_b))
    pieces_b, beside = gather(piece_b, found)
    unused, three_four = lax.optimization_barrier(((beside, pieces_a[0]), three_four))
    done = bounds[-1]
    grad_four, grad_six = pl.pallas_call(
        functools.partial(input_last_kernel, groups[-1], bounds),
        out_shape=(
            jax.ShapeDtypeStruct(four.shape, BF16),
            jax.ShapeDtypeStruct(six.shape, BF16),
        ),
        in_specs=[vmem] * (2 + len(earlier)),
        out_specs=(hbm, hbm),
        scratch_shapes=[
            pltpu.VMEM((rows_four - done, cols_four, chan), BF16),
            pltpu.SemaphoreType.DMA((len(groups),)),
            pltpu.SemaphoreType.DMA((len(chunks),)),
        ],
        compiler_params=params,
        cost_estimate=cost(0.4, 2 * four.size),
        name="inputs_last",
    )(three_four, turned_weight, earlier[-1], *earlier[:-1])
    pieces_a, grad_six = lax.optimization_barrier((pieces_a, grad_six))
    whole = put_pieces(whole, pieces_a, found.first)
    whole = put_pieces(whole, pieces_b, found.second)
    grad_weight = whole.reshape(9, share, chan)
    return (grad_four[None], grad_six[None], grad_weight, grad_gain, grad_shift)


def solution(mesh):
    placed = (
        P("rep", "sp", None, None),
        P("rep", "sp", None, None),
        P(),
        P(),
        P(),
        P("rep", "sp", None, None),
        P("rep", "sp", None, None),
    )
    return jax.shard_map(
        local,
        mesh=mesh,
        in_specs=placed,
        out_specs=(
            P("rep", "sp", None, None),
            P("rep", "sp", None, None),
            P(None, "sp", None),
            P(),
            P(),
        ),
        check_vma=False,
    )
```

```python
import functools
from typing import NamedTuple

import jax
import jax.numpy as jnp
from jax import lax
from jax.experimental import pallas as pl
from jax.experimental.pallas import tpu as pltpu
from jax.sharding import PartitionSpec as P

GROUP = 16
RADIX = 4
FAR_FIRST = (3, 2, 1)
FIRST_TAPS = 4
EARLY_TAPS = 6
EPSILON = 1e-05
F32 = jnp.float32
BF16 = jnp.bfloat16
VMEM_LIMIT = 20 * 1024 * 1024
EDGE_LIMIT = 60 * 1024 * 1024


def chunk_of(rows, most, multiple=1):
    sizes = [size for size in range(1, most + 1) if rows % size == 0 and size % multiple == 0]
    return max(sizes) if sizes else rows


def pitch_of(cols):
    return -(-cols // 16) * 16


def parity(rep):
    return ((rep >> 2) ^ (rep >> 3)) & 1


def chunks_of(rows, most, multiple=1):
    size = chunk_of(rows, most, multiple)
    return [(start, start + size) for start in range(0, rows, size)]


def widen(cells, pitch):
    cells = cells.astype(F32)
    extra = pitch - cells.shape[0]
    if extra:
        cells = jnp.concatenate([cells, jnp.zeros((extra, cells.shape[1]), F32)], 0)
    return cells


def put_three(three, row, cells, cols, turned):
    pitch, chan = cells.shape
    left, right = pltpu.roll(cells, 1, 0), pltpu.roll(cells, pitch - 1, 0)
    if pitch == cols:
        col = lax.broadcasted_iota(jnp.int32, (8, chan), 0)
        left = jnp.concatenate([jnp.where(col == 0, 0.0, left[:8]), left[8:]], 0)
        right = jnp.concatenate([right[:-8], jnp.where(col == 7, 0.0, right[-8:])], 0)
    parts = (right, cells, left) if turned else (left, cells, right)
    for place, part in enumerate(parts):
        three[row, :, place * chan : (place + 1) * chan] = part.astype(BF16)


def beside(three, starts, size):
    pitch, width = three.shape[1:]
    return jnp.concatenate([three[start : start + size].reshape(size * pitch, width) for start in starts], 1)


def edges_valid(sp_count):
    index = lax.axis_index("sp")
    return jnp.where(index > 0, 1.0, 0.0), jnp.where(index < sp_count - 1, 1.0, 0.0)


def level_coefs(moments, gain, shift, count):
    mean = moments[0:1] / count
    spread = moments[1:2] / count - mean * mean
    return mean, lax.rsqrt(spread + EPSILON), gain, shift


def slope_of(conv, cotan, coefs):
    mean, rstd, gain, shift = coefs
    centred = conv.astype(F32) - mean
    half = centred * (0.5 * rstd * gain) + 0.5 * shift
    turn = jnp.tanh(half)
    return centred, cotan.astype(F32) * ((1.0 + turn) * (1.0 + half * (1.0 - turn)))


def masked(cells, cols):
    if cells.shape[0] == cols:
        return cells
    col = lax.broadcasted_iota(jnp.int32, cells.shape, 0)
    return jnp.where(col < cols, cells, 0.0)


def staged(fills, dots):
    fills[0]()
    for index, dot in enumerate(dots):
        if index + 1 < len(fills):
            fills[index + 1]()
        dot()


def conv_rows(lhs, w_ref):
    return jnp.dot(lhs, w_ref[...].reshape(lhs.shape[1], -1), preferred_element_type=F32).astype(BF16)


def add_moments(sums, conv, cols):
    chan = conv.shape[2]
    conv = conv.astype(F32)
    if conv.shape[1] != cols:
        conv = conv[:, :cols]
    conv = conv.reshape(-1, 8, chan)
    sums[0].append(jnp.sum(conv, 0))
    sums[1].append(jnp.sum(conv * conv, 0))


def folded(parts):
    total = parts[0]
    for part in parts[1:]:
        total = total + part
    return jnp.sum(total, 0, keepdims=True)


def inner_kernel(four_ref, six_ref, w_ref, conv_four_ref, conv_six_ref, moments_ref, three_four, three_six):
    rows_four, cols_four = four_ref.shape[:2]
    rows_six, cols_six = six_ref.shape[:2]
    pitch_four, pitch_six = three_four.shape[1], three_six.shape[1]
    sums_four, sums_six = ([], []), ([], [])
    inner = rows_four - 2
    count = max(1, inner // 9)
    bounds = [index * inner // count for index in range(count + 1)]

    def fill_four(row):
        put_three(three_four, row, four_ref[row].astype(F32), cols_four, False)

    def fill_six(row):
        put_three(three_six, row, widen(six_ref[row], pitch_six), cols_six, False)

    def dot(start, end):
        lhs = beside(three_four, (start, start + 1, start + 2), end - start)
        cells = lhs.shape[0]
        if end == inner:
            lhs = jnp.concatenate([lhs, beside(three_six, (0, 1, 2), rows_six - 2)], 0)
        conv = conv_rows(lhs, w_ref)
        four = conv[:cells].reshape(end - start, pitch_four, -1)
        conv_four_ref[start:end] = four
        add_moments(sums_four, four, cols_four)
        if end == inner:
            six = conv[cells:].reshape(rows_six - 2, pitch_six, -1)
            conv_six_ref[...] = six
            add_moments(sums_six, six, cols_six)

    fills, dots, done = [], [], 0
    for start, end in zip(bounds[:-1], bounds[1:]):
        todo = [functools.partial(fill_four, row) for row in range(done, end + 2)]
        if end == inner:
            todo += [functools.partial(fill_six, row) for row in range(rows_six)]
        fills.append(lambda todo=todo: [fill() for fill in todo])
        done = end + 2
        dots.append(functools.partial(dot, start, end))
    staged(fills, dots)
    moments_ref[...] = jnp.concatenate([folded(parts) for parts in sums_four + sums_six], 0)


def outer_level(x_ref, top, bottom, valid, three):
    rows, cols = x_ref.shape[:2]
    pitch = three.shape[1]
    for edge in range(2):
        put_three(three, edge, top(edge) * valid[0], cols, False)
        put_three(three, 2 + edge, widen(x_ref[edge], pitch), cols, False)
        put_three(three, 4 + edge, widen(x_ref[rows - 2 + edge], pitch), cols, False)
        put_three(three, 6 + edge, bottom(edge) * valid[1], cols, False)
    return [beside(three, (start, start + 1, start + 2), 2) for start in (0, 4)]


def outer_kernel(
    sp_count, four_ref, six_ref, above_ref, below_ref, w_ref, inner_ref,
    conv_four_ref, conv_six_ref, moments_ref, three_four, three_six,
):
    cols_four = four_ref.shape[1]
    valid = edges_valid(sp_count)
    base, pitch_six = 3 * cols_four, three_six.shape[1]

    def reader(ref, start, pitch):
        return lambda edge: ref[start + edge * pitch : start + (edge + 1) * pitch].astype(F32)

    lhs = outer_level(
        four_ref, reader(above_ref, 0, cols_four), reader(below_ref, 0, cols_four), valid, three_four
    ) + outer_level(
        six_ref, reader(above_ref, base, pitch_six), reader(below_ref, base, pitch_six), valid, three_six
    )
    conv = conv_rows(jnp.concatenate(lhs, 0), w_ref)
    sums, begin = [], 0
    for conv_ref, cols in ((conv_four_ref, cols_four), (conv_six_ref, six_ref.shape[1])):
        cells = conv_ref.shape[0] * conv_ref.shape[1]
        rows = conv[begin : begin + cells].reshape(conv_ref.shape)
        begin += cells
        conv_ref[...] = rows
        parts = ([], [])
        add_moments(parts, rows[1:3], cols)
        sums += [folded(part) for part in parts]
    moments_ref[...] = inner_ref[...] + jnp.concatenate(sums, 0)


def turn_kernel(four_ref, six_ref, w_ref, turned_ref, turned_w_ref):
    rows_four, cols_four, chan = four_ref.shape
    rows_six, cols_six = six_ref.shape[:2]
    pitch = pitch_of(cols_six)
    for start, end in chunks_of(rows_four, 8, 4):
        cells = four_ref[start:end].reshape((end - start) * cols_four, chan)
        turned_ref[:, start * cols_four : end * cols_four] = cells.T
    cells = six_ref[...].astype(F32)
    cells = jnp.concatenate([cells, jnp.zeros((rows_six, pitch - cols_six, chan), F32)], 1).astype(BF16)
    turned_ref[:, rows_four * cols_four :] = cells.reshape(rows_six * pitch, chan).T
    for tap in range(9):
        turned_w_ref[tap * chan : (tap + 1) * chan] = w_ref[tap].T


def slope_level(inner_ref, outer_ref, cotan_ref, above, below, coefs, slope_ref):
    rows, cols, chan = cotan_ref.shape
    pitch = inner_ref.shape[1]

    def put(row, conv, cotan):
        centred, slope = slope_of(conv, widen(cotan, pitch), coefs)
        slope_ref[row] = slope
        return centred, slope

    def add(sums, pair):
        centred, slope = pair
        first = jnp.sum(slope.reshape(-1, 8, chan), 0)
        second = jnp.sum((slope * centred).reshape(-1, 8, chan), 0)
        return sums[0] + first, sums[1] + second

    def step(row, sums):
        return add(sums, put(row + 2, inner_ref[row], cotan_ref[row + 1]))

    put(0, outer_ref[0], above)
    put(rows + 1, outer_ref[3], below)
    zero = jnp.zeros((8, chan), F32)
    sums = add((zero, zero), put(1, outer_ref[1], cotan_ref[0]))
    sums = add(sums, put(rows, outer_ref[2], cotan_ref[rows - 1]))
    for row in range(rows - 2):
        sums = step(row, sums)
    first = 0.5 * jnp.sum(sums[0], 0, keepdims=True)
    return first, 0.5 * coefs[1] * jnp.sum(sums[1], 0, keepdims=True)


def slope_kernel(
    counts, inner_four_ref, inner_six_ref, outer_four_ref, outer_six_ref, cotan_four_ref, cotan_six_ref,
    above_ref, below_ref, moments_ref, gain_ref, shift_ref, slope_four_ref, slope_six_ref, slopes_ref,
):
    sums = ()
    cols_four = cotan_four_ref.shape[1]
    starts = (2 * cols_four, 3 * cols_four + 2 * inner_six_ref.shape[1])
    for level, (inner_ref, outer_ref, cotan_ref, slope_ref) in enumerate(
        (
            (inner_four_ref, outer_four_ref, cotan_four_ref, slope_four_ref),
            (inner_six_ref, outer_six_ref, cotan_six_ref, slope_six_ref),
        )
    ):
        pair = moments_ref[2 * level : 2 * level + 2]
        here = slice(level, level + 1)
        edge = slice(starts[level], starts[level] + inner_ref.shape[1])
        coefs = level_coefs(pair, gain_ref[here], shift_ref[here], counts[level])
        sums += slope_level(inner_ref, outer_ref, cotan_ref, above_ref[edge], below_ref[edge], coefs, slope_ref)
    slopes_ref[...] = jnp.concatenate(sums, 0)


def backward_level(cols, inner_ref, outer_ref, slope_ref, valid, coefs, slopes, count, three):
    rows = inner_ref.shape[0] + 2
    pitch = three.shape[1]
    mean, rstd, gain, shift = coefs
    lead = gain * rstd
    offset, factor = lead * (slopes[0:1] / count), lead * rstd * (slopes[1:2] / count)

    def fill_row(row):
        if 2 <= row < rows:
            conv = inner_ref[row - 2]
        else:
            conv = outer_ref[row if row < 2 else row - rows + 2]
        centred = conv.astype(F32) - mean
        dconv = masked((0.5 * lead) * slope_ref[row] - (offset + centred * factor), cols)
        if row == 0:
            dconv = dconv * valid[0]
        elif row == rows + 1:
            dconv = dconv * valid[1]
        put_three(three, row, dconv, cols, True)

    return fill_row


def taps_beside(three, start, end, taps):
    pitch, width = three.shape[1:]
    chan = width // 3
    parts = []
    for row_tap in range(3):
        low, high = max(taps[0] - 3 * row_tap, 0), min(taps[1] - 3 * row_tap, 3)
        if low < high:
            first = start + 2 - row_tap
            rows = three[first : first + end - start, :, low * chan : high * chan]
            parts.append(rows.reshape((end - start) * pitch, (high - low) * chan))
    return jnp.concatenate(parts, 1)


def backward_bounds(rows):
    bounds = [0, min(8, rows)]
    while bounds[-1] < rows:
        bounds.append(min(bounds[-1] + 16, rows))
    return bounds


def weight_dot(turned_ref, three_four, three_six, total, taps, start, end):
    rows_four, rows_six = three_four.shape[0] - 2, three_six.shape[0] - 2
    pitch = three_four.shape[1]
    first, last = start * pitch, end * pitch
    rhs = taps_beside(three_four, start, end, taps)
    if end == rows_four:
        rhs = jnp.concatenate([rhs, taps_beside(three_six, 0, rows_six, taps)], 0)
        last = turned_ref.shape[1]
    term = jnp.dot(turned_ref[:, first:last], rhs, preferred_element_type=F32)
    total[...] = total[...] + term if start else term


def put_shares(totals, sp_count, own_ref, sent_ref):
    taps, share, chan = own_ref.shape
    places = [(total, start) for total in totals for start in range(0, total.shape[1], chan)][:taps]
    place = lax.axis_index("sp") ^ parity(lax.axis_index("rep"))
    for step in range(sp_count):
        begin = pl.multiple_of((place ^ step) * share, share)
        for tap, (total, start) in enumerate(places):
            part = total[pl.ds(begin, share), start : start + chan]
            if step == 0:
                own_ref[tap] = part
            else:
                sent_ref[step - 1, tap] = part


def backward_kernel(
    counts, sp_count, cols, turned_ref, inner_four_ref, inner_six_ref, outer_four_ref, outer_six_ref,
    slope_four_ref, slope_six_ref, moments_ref, slopes_ref, gain_ref, shift_ref, three_four, three_six, own_ref,
    sent_ref, rest_ref, grad_gain_ref, grad_shift_ref, total,
):
    valid = edges_valid(sp_count)
    grad_gain_ref[...] = jnp.concatenate([slopes_ref[1:2], slopes_ref[3:4]], 0)
    grad_shift_ref[...] = jnp.concatenate([slopes_ref[0:1], slopes_ref[2:3]], 0)
    parts = []
    for level, inner_ref, outer_ref, slope_ref, three in (
        (0, inner_four_ref, outer_four_ref, slope_four_ref, three_four),
        (1, inner_six_ref, outer_six_ref, slope_six_ref, three_six),
    ):
        here = slice(level, level + 1)
        pair = slice(2 * level, 2 * level + 2)
        coefs = level_coefs(moments_ref[pair], gain_ref[here], shift_ref[here], counts[level])
        parts.append(
            backward_level(
                cols[level], inner_ref, outer_ref, slope_ref, valid, coefs, slopes_ref[pair], counts[level], three
            )
        )
    fill_four, fill_six = parts
    rows_four, rows_six = three_four.shape[0] - 2, three_six.shape[0] - 2
    bounds = backward_bounds(rows_four)
    fills, dots, done = [], [], 0
    for start, end in zip(bounds[:-1], bounds[1:]):
        todo = [functools.partial(fill_four, row) for row in range(done, end + 2)]
        if end == rows_four:
            todo += [functools.partial(fill_six, row) for row in range(rows_six + 2)]
        fills.append(lambda todo=todo: [fill() for fill in todo])
        done = end + 2
        dots.append(
            functools.partial(weight_dot, turned_ref, three_four, three_six, total, (0, EARLY_TAPS), start, end)
        )
    staged(fills, dots)
    put_shares([total], sp_count, own_ref, sent_ref)
    rest_ref[...] = total[:, FIRST_TAPS * rest_ref.shape[0] :]


def weight_kernel(sp_count, turned_ref, three_four, three_six, rest_ref, own_ref, sent_ref, total):
    for start, end in chunks_of(three_four.shape[0] - 2, 16, 4):
        weight_dot(turned_ref, three_four, three_six, total, (EARLY_TAPS, 9), start, end)
    put_shares([rest_ref, total], sp_count, own_ref, sent_ref)


def input_chunks(three, turned, grad, chunks, offset, sent=None):
    cols, chan = grad.shape[1:]
    pitch = three.shape[1]
    for index, (start, end) in enumerate(chunks):
        size = end - start
        lhs = beside(three, (start + 2, start + 1, start), size)
        term = jnp.dot(lhs, turned[...], preferred_element_type=F32)
        grad[start - offset : end - offset] = term.reshape(size, pitch, chan)[:, :cols].astype(BF16)
        if sent is not None:
            sent(index, start, end)


def input_kernel(chunks, three_four, three_six, turned, grad_ref, *six_refs):
    for six_ref in six_refs:
        input_chunks(three_six, turned, six_ref, [(0, six_ref.shape[0])], 0)
    input_chunks(three_four, turned, grad_ref, chunks, chunks[0][0])


def input_last_kernel(chunks, bounds, three_four, turned, six_ref, *rest):
    count = len(bounds) - 1
    earlier, rest = rest[:count], rest[count:]
    grad_four_ref, grad_six_ref, grad_four, sems, sems_four = rest
    copies = [pltpu.make_async_copy(six_ref, grad_six_ref, sems.at[count])]
    copies += [
        pltpu.make_async_copy(part, grad_four_ref.at[bounds[index] : bounds[index + 1]], sems.at[index])
        for index, part in enumerate(earlier)
    ]
    for copy in copies:
        copy.start()
    done = bounds[-1]

    def sent(index, start, end):
        copy = pltpu.make_async_copy(
            grad_four.at[start - done : end - done], grad_four_ref.at[start:end], sems_four.at[index]
        )
        copy.start()
        copies.append(copy)

    input_chunks(three_four, turned, grad_four, chunks, done, sent)
    for copy in copies:
        copy.wait()


def swap(array, axis, stride):
    count = lax.axis_size(axis)
    return lax.ppermute(array, axis, [(i, i ^ stride) for i in range(count)])


def edge_kernel(starts, four_ref, six_ref, cotan_four_ref, cotan_six_ref, *rest):
    outs, six_rows, sems = rest[:-2], rest[-2], rest[-1]
    rows_four, cols_four = four_ref.shape[:2]
    rows_six = six_ref.shape[0]
    pitch = pitch_of(six_ref.shape[1])
    copies = []
    for number, (start, out_ref) in enumerate(zip(starts, outs)):
        last = (1 - jnp.minimum(lax.axis_index("sp"), 1)) if start is None else start
        for part, (ref, row) in enumerate(
            (
                (four_ref, last * (rows_four - 2)),
                (four_ref, last * (rows_four - 2) + 1),
                (cotan_four_ref, last * (rows_four - 1)),
                (six_ref, last * (rows_six - 2)),
                (six_ref, last * (rows_six - 2) + 1),
                (cotan_six_ref, last * (rows_six - 1)),
            )
        ):
            if part < 3:
                target = out_ref.at[part * cols_four : (part + 1) * cols_four]
            else:
                target = six_rows.at[number, part - 3]
            copies.append(pltpu.make_async_copy(ref.at[row], target, sems.at[number, part]))
    for copy in copies:
        copy.start()
    for copy in copies:
        copy.wait()
    for number, out_ref in enumerate(outs):
        for part in range(3):
            begin = 3 * cols_four + part * pitch
            out_ref[begin : begin + pitch] = widen(six_rows[number, part], pitch).astype(BF16)


def edges(four, six, cotan_four, cotan_six):
    count = lax.axis_size("sp")
    starts = (None,) if count == 2 else (0, 1)
    length = 3 * four.shape[1] + 3 * pitch_of(six.shape[1])
    vmem = pl.BlockSpec(memory_space=pltpu.VMEM)
    hbm = pl.BlockSpec(memory_space=pltpu.HBM)
    outs = pl.pallas_call(
        functools.partial(edge_kernel, starts),
        out_shape=tuple(jax.ShapeDtypeStruct((length, four.shape[2]), BF16) for _ in starts),
        in_specs=[hbm] * 4,
        out_specs=tuple(vmem for _ in starts),
        scratch_shapes=[
            pltpu.VMEM((len(starts), 3) + six.shape[1:], BF16),
            pltpu.SemaphoreType.DMA((len(starts), 6)),
        ],
        compiler_params=pltpu.CompilerParams(vmem_limit_bytes=EDGE_LIMIT),
        name="edges",
    )(four, six, cotan_four, cotan_six)
    if count == 2:
        met = swap(outs[0], "sp", 1)
        return met, met
    above = lax.ppermute(outs[1], "sp", [(i, (i + 1) % count) for i in range(count)])
    below = lax.ppermute(outs[0], "sp", [((i + 1) % count, i) for i in range(count)])
    return above, below


def swap_across(array, axis, stride):
    count, sp_count = lax.axis_size("rep"), lax.axis_size("sp")
    rep_stride, sp_stride = (stride, 1) if axis == "rep" else (0, stride ^ 1)
    pairs = [
        (rep * sp_count + sp, (rep ^ rep_stride) * sp_count + (sp ^ sp_stride))
        for rep in range(count)
        for sp in range(sp_count)
    ]
    return lax.ppermute(array, ("rep", "sp"), pairs)


def group_sum(sums):
    sums = sums + swap(sums, "sp", 1)
    stride = 2
    while stride < lax.axis_size("sp"):
        sums = sums + swap_across(sums, "sp", stride)
        stride = 2 * stride
    stride = 1
    while stride < GROUP:
        met = lax.optimization_barrier([swap_across(sums, "rep", k * stride) for k in FAR_FIRST])
        sums = (sums + met[2]) + (met[1] + met[0])
        stride = RADIX * stride
    return sums


def every_group(sums):
    stride = GROUP
    while stride < lax.axis_size("rep"):
        sums = sums + swap(sums, "rep", stride)
        stride = 2 * stride
    return sums


class Places(NamedTuple):
    digits: list
    first: list
    second: list
    odd: jax.Array


def places():
    rep = lax.axis_index("rep")
    digits = [(rep & (RADIX - 1)) ^ k for k in range(RADIX)]
    second = 9 - FIRST_TAPS
    return Places(
        digits,
        [FIRST_TAPS * digit for digit in digits],
        [RADIX * FIRST_TAPS + second * digit for digit in digits],
        parity(rep) == 1,
    )


def piece_of(pieces, index):
    sizes = (1,) + pieces.shape[1:]
    return lax.dynamic_slice(pieces, (index, 0, 0), sizes, allow_negative_indices=False)[0]


def scatter_pieces(own, met, found):
    chan = own.shape[2]
    parts = [part.reshape(RADIX, -1, chan) for part in [own] + met]

    def piece(k):
        total = piece_of(parts[0], found.digits[k])
        for part in parts[1:]:
            total = total + piece_of(part, found.digits[k])
        return total

    return piece(0), [piece(k).astype(BF16) for k in FAR_FIRST]


def added(own, met):
    return (own + met[2].astype(F32)) + (met[1].astype(F32) + met[0].astype(F32))


def fours(pieces, stride):
    return [swap(piece, "rep", k * stride) for k, piece in zip(FAR_FIRST, pieces)]


def swap_high(array, even, odd):
    count, sp_count = lax.axis_size("rep"), lax.axis_size("sp")
    pairs = []
    for rep in range(count):
        for sp in range(sp_count):
            stride = odd if (sp ^ parity(rep)) & 1 else even
            pairs.append((rep * sp_count + sp, (rep ^ stride) * sp_count + (sp ^ 1)))
    return lax.ppermute(array, ("rep", "sp"), pairs)


def bring(array, k):
    count, sp_count = lax.axis_size("rep"), lax.axis_size("sp")
    pairs = [
        (rep * sp_count + sp, (rep ^ k) * sp_count + (sp ^ parity(rep)))
        for rep in range(count)
        for sp in range(sp_count)
    ]
    return lax.ppermute(array, ("rep", "sp"), pairs)


def both(own, met):
    return (own.astype(F32) + met.astype(F32)).astype(BF16)


def every_share(total):
    stride = GROUP
    while stride < lax.axis_size("rep"):
        total = added(total.astype(F32), fours([total] * 3, stride)).astype(BF16)
        stride = RADIX * stride
    return total


def gather(total, found, tied=False):
    beside, far = swap(total, "sp", 1), bring(total, FAR_FIRST[0])
    if tied:
        beside, total = lax.optimization_barrier((beside, total))
    own = jnp.where(found.odd, beside, total)
    return [far] + [bring(total, k) for k in FAR_FIRST[1:]] + [own], beside


def put_pieces(whole, pieces, starts):
    for k, piece in zip(FAR_FIRST + (0,), pieces):
        piece = piece.reshape((-1,) + whole.shape[1:]).astype(F32)
        whole = lax.dynamic_update_slice(whole, piece, (starts[k], 0, 0), allow_negative_indices=False)
    return whole


def local(level_four, level_six, conv_weight, bn_gain, bn_shift, cotan_four, cotan_six):
    sp_count = lax.axis_size("sp")
    images = level_four.shape[0]
    four, six, cot_four, cot_six = (a[0] for a in (level_four, level_six, cotan_four, cotan_six))
    rows_four, cols_four, chan = four.shape
    rows_six, cols_six = six.shape[:2]
    pitch_four, pitch_six = pitch_of(cols_four), pitch_of(cols_six)
    counts = (
        float(images * GROUP * rows_four * sp_count * cols_four),
        float(images * GROUP * rows_six * sp_count * cols_six),
    )
    found, four = lax.optimization_barrier((places(), four))
    above, below = edges(four, six, cot_four, cot_six)
    vmem = pl.BlockSpec(memory_space=pltpu.VMEM)
    hbm = pl.BlockSpec(memory_space=pltpu.HBM)
    params = pltpu.CompilerParams(vmem_limit_bytes=VMEM_LIMIT)
    framed_four = jax.ShapeDtypeStruct((rows_four + 2, pitch_four, chan), BF16)
    framed_six = jax.ShapeDtypeStruct((rows_six + 2, pitch_six, chan), BF16)
    four_sums = jax.ShapeDtypeStruct((4, chan), F32)
    flops = 2 * 9 * chan * chan * (rows_four * cols_four + rows_six * cols_six)

    def cost(share, size):
        return pl.CostEstimate(flops=int(flops * share), bytes_accessed=size, transcendentals=0)

    inner_four, inner_six, inner_moments = pl.pallas_call(
        inner_kernel,
        out_shape=(
            jax.ShapeDtypeStruct((rows_four - 2, pitch_four, chan), BF16),
            jax.ShapeDtypeStruct((rows_six - 2, pitch_six, chan), BF16),
            four_sums,
        ),
        in_specs=[vmem] * 3,
        out_specs=(vmem, vmem, vmem),
        scratch_shapes=[
            pltpu.VMEM((rows_four, pitch_four, 3 * chan), BF16),
            pltpu.VMEM((rows_six, pitch_six, 3 * chan), BF16),
        ],
        compiler_params=params,
        cost_estimate=cost(1, 4 * four.size),
        name="forward_inner",
    )(four, six, conv_weight)
    outer_four, outer_six, moments = pl.pallas_call(
        functools.partial(outer_kernel, sp_count),
        out_shape=(
            jax.ShapeDtypeStruct((4, pitch_four, chan), BF16),
            jax.ShapeDtypeStruct((4, pitch_six, chan), BF16),
            four_sums,
        ),
        in_specs=[vmem] * 6,
        out_specs=(vmem, vmem, vmem),
        scratch_shapes=[
            pltpu.VMEM((8, pitch_four, 3 * chan), BF16),
            pltpu.VMEM((8, pitch_six, 3 * chan), BF16),
        ],
        compiler_params=params,
        cost_estimate=cost(0.1, four.size),
        name="forward_outer",
    )(four, six, above, below, conv_weight, inner_moments)
    moments, four, six = lax.optimization_barrier((moments, four, six))
    turned, turned_weight = pl.pallas_call(
        turn_kernel,
        out_shape=(
            jax.ShapeDtypeStruct((chan, rows_four * cols_four + rows_six * pitch_six), BF16),
            jax.ShapeDtypeStruct((9 * chan, chan), BF16),
        ),
        in_specs=[vmem] * 3,
        out_specs=(vmem, vmem),
        compiler_params=params,
        cost_estimate=cost(0.3, 4 * four.size),
        name="turn",
    )(four, six, conv_weight)
    moments, turned, turned_weight = lax.optimization_barrier((group_sum(moments), turned, turned_weight))

    slope_four, slope_six, slopes = pl.pallas_call(
        functools.partial(slope_kernel, counts),
        out_shape=(
            jax.ShapeDtypeStruct(framed_four.shape, F32),
            jax.ShapeDtypeStruct(framed_six.shape, F32),
            four_sums,
        ),
        in_specs=[vmem] * 11,
        out_specs=(vmem,) * 3,
        compiler_params=params,
        cost_estimate=cost(0.01, 4 * four.size),
        name="slopes",
    )(
        inner_four, inner_six, outer_four, outer_six, cot_four, cot_six, above, below, moments, bn_gain, bn_shift
    )
    slopes = group_sum(slopes)

    share = chan // sp_count
    wide_four, wide_six = (
        jax.ShapeDtypeStruct(framed.shape[:2] + (3 * chan,), BF16) for framed in (framed_four, framed_six)
    )
    def shares(taps):
        return (
            jax.ShapeDtypeStruct((taps, share, chan), F32),
            jax.ShapeDtypeStruct((sp_count - 1, taps, share, chan), F32),
        )

    three_four, three_six, own_a, sent_a, rest, grad_gain, grad_shift = pl.pallas_call(
        functools.partial(backward_kernel, counts, sp_count, (cols_four, cols_six)),
        out_shape=(wide_four, wide_six)
        + shares(FIRST_TAPS)
        + (jax.ShapeDtypeStruct((chan, (EARLY_TAPS - FIRST_TAPS) * chan), F32),)
        + (jax.ShapeDtypeStruct((2, chan), F32),) * 2,
        in_specs=[vmem] * 11,
        out_specs=(vmem,) * 7,
        scratch_shapes=[pltpu.VMEM((chan, EARLY_TAPS * chan), F32)],
        compiler_params=params,
        cost_estimate=cost(0.6, 8 * four.size),
        name="backward",
    )(
        turned, inner_four, inner_six, outer_four, outer_six, slope_four, slope_six, moments, slopes,
        bn_gain, bn_shift,
    )
    sent_a, three_six = lax.optimization_barrier((sent_a, three_six))
    met_a = [swap(sent_a[step], "sp", step + 1) for step in range(sp_count - 1)]
    own_b, sent_b = pl.pallas_call(
        functools.partial(weight_kernel, sp_count),
        out_shape=shares(9 - FIRST_TAPS),
        in_specs=[vmem] * 4,
        out_specs=(vmem, vmem),
        scratch_shapes=[pltpu.VMEM((chan, (9 - EARLY_TAPS) * chan), F32)],
        compiler_params=params,
        cost_estimate=cost(0.6, 8 * four.size),
        name="weights",
    )(turned, three_four, three_six, rest)
    met_a, sent_b = lax.optimization_barrier((met_a, sent_b))
    met_b = [swap(sent_b[step], "sp", step + 1) for step in range(sp_count - 1)]

    chunks = chunks_of(rows_four, 8)
    cuts = [part * len(chunks) // 3 for part in range(4)]
    groups = [chunks[low:high] for low, high in zip(cuts[:-1], cuts[1:]) if low < high]
    bounds = [group[0][0] for group in groups]

    def inputs(number, three):
        group = groups[number]
        parts = (jax.ShapeDtypeStruct((group[-1][1] - group[0][0], cols_four, chan), BF16),)
        if number == len(groups) - 2:
            parts += (jax.ShapeDtypeStruct(six.shape, BF16),)
        return pl.pallas_call(
            functools.partial(input_kernel, group),
            out_shape=parts,
            in_specs=[vmem] * 3,
            out_specs=(vmem,) * len(parts),
            compiler_params=params,
            cost_estimate=cost(0.3, four.size),
            name="inputs",
        )(three, three_six, turned_weight)

    grad_gain, grad_shift = every_group(grad_gain), every_group(grad_shift)

    piece_a, pieces_a = scatter_pieces(own_a, met_a, found)
    met_a = fours(pieces_a, 1)
    piece_b, pieces_b = scatter_pieces(own_b, met_b, found)
    met_b = fours(pieces_b, 1)
    met_a, unused = lax.optimization_barrier((met_a, pieces_b))

    piece_a = added(piece_a, met_a).astype(BF16)
    piece_a, three_four = lax.optimization_barrier((piece_a, three_four))
    met_a = swap_high(piece_a, RADIX, 2 * RADIX)
    earlier = list(inputs(0, three_four))
    whole = jnp.zeros((9 * RADIX, share // RADIX, chan), F32)
    met_b, earlier, whole = lax.optimization_barrier((met_b, earlier, whole))

    piece_b = added(piece_b, met_b).astype(BF16)
    met_b = swap_high(piece_b, RADIX, 2 * RADIX)
    met_a, unused = lax.optimization_barrier((met_a, piece_b))

    piece_a = both(piece_a, met_a)
    piece_a, three_four = lax.optimization_barrier((piece_a, three_four))
    met_a = swap_high(piece_a, 2 * RADIX, RADIX)
    if len(groups) > 2:
        earlier = earlier + list(inputs(1, three_four))
    met_b, earlier = lax.optimization_barrier((met_b, earlier))

    piece_b = both(piece_b, met_b)
    met_b = swap_high(piece_b, 2 * RADIX, RADIX)
    met_a, unused = lax.optimization_barrier((met_a, piece_b))

    piece_a = every_share(both(piece_a, met_a))
    pieces_a, unused = gather(piece_a, found)
    piece_b = every_share(both(piece_b, met_b))
    pieces_b, beside = gather(piece_b, found, True)
    unused, three_four = lax.optimization_barrier(((beside, pieces_a[0]), three_four))
    done = bounds[-1]
    grad_four, grad_six = pl.pallas_call(
        functools.partial(input_last_kernel, groups[-1], bounds),
        out_shape=(
            jax.ShapeDtypeStruct(four.shape, BF16),
            jax.ShapeDtypeStruct(six.shape, BF16),
        ),
        in_specs=[vmem] * (2 + len(earlier)),
        out_specs=(hbm, hbm),
        scratch_shapes=[
            pltpu.VMEM((rows_four - done, cols_four, chan), BF16),
            pltpu.SemaphoreType.DMA((len(groups),)),
            pltpu.SemaphoreType.DMA((len(chunks),)),
        ],
        compiler_params=params,
        cost_estimate=cost(0.4, 2 * four.size),
        name="inputs_last",
    )(three_four, turned_weight, earlier[-1], *earlier[:-1])
    pieces_a, grad_six = lax.optimization_barrier((pieces_a, grad_six))
    whole = put_pieces(whole, pieces_a, found.first)
    whole = put_pieces(whole, pieces_b, found.second)
    grad_weight = whole.reshape(9, share, chan)
    return (grad_four[None], grad_six[None], grad_weight, grad_gain, grad_shift)


def solution(mesh):
    placed = (
        P("rep", "sp", None, None),
        P("rep", "sp", None, None),
        P(),
        P(),
        P(),
        P("rep", "sp", None, None),
        P("rep", "sp", None, None),
    )
    return jax.shard_map(
        local,
        mesh=mesh,
        in_specs=placed,
        out_specs=(
            P("rep", "sp", None, None),
            P("rep", "sp", None, None),
            P(None, "sp", None),
            P(),
            P(),
        ),
        check_vma=False,
    )
```

```python
import functools
from typing import NamedTuple

import jax
import jax.numpy as jnp
from jax import lax
from jax.experimental import pallas as pl
from jax.experimental.pallas import tpu as pltpu
from jax.sharding import PartitionSpec as P

GROUP = 16
RADIX = 4
FAR_FIRST = (3, 2, 1)
FIRST_TAPS = 4
EARLY_TAPS = 6
EPSILON = 1e-05
F32 = jnp.float32
BF16 = jnp.bfloat16
VMEM_LIMIT = 20 * 1024 * 1024
EDGE_LIMIT = 60 * 1024 * 1024


def chunk_of(rows, most, multiple=1):
    sizes = [size for size in range(1, most + 1) if rows % size == 0 and size % multiple == 0]
    return max(sizes) if sizes else rows


def pitch_of(cols):
    return -(-cols // 16) * 16


def parity(rep):
    return ((rep >> 2) ^ (rep >> 3)) & 1


def chunks_of(rows, most, multiple=1):
    size = chunk_of(rows, most, multiple)
    return [(start, start + size) for start in range(0, rows, size)]


def widen(cells, pitch):
    cells = cells.astype(F32)
    extra = pitch - cells.shape[0]
    if extra:
        cells = jnp.concatenate([cells, jnp.zeros((extra, cells.shape[1]), F32)], 0)
    return cells


def put_three(three, row, cells, cols, turned):
    pitch, chan = cells.shape
    left, right = pltpu.roll(cells, 1, 0), pltpu.roll(cells, pitch - 1, 0)
    if pitch == cols:
        col = lax.broadcasted_iota(jnp.int32, (8, chan), 0)
        left = jnp.concatenate([jnp.where(col == 0, 0.0, left[:8]), left[8:]], 0)
        right = jnp.concatenate([right[:-8], jnp.where(col == 7, 0.0, right[-8:])], 0)
    parts = (right, cells, left) if turned else (left, cells, right)
    for place, part in enumerate(parts):
        three[row, :, place * chan : (place + 1) * chan] = part.astype(BF16)


def beside(three, starts, size):
    pitch, width = three.shape[1:]
    return jnp.concatenate([three[start : start + size].reshape(size * pitch, width) for start in starts], 1)


def edges_valid(sp_count):
    index = lax.axis_index("sp")
    return jnp.where(index > 0, 1.0, 0.0), jnp.where(index < sp_count - 1, 1.0, 0.0)


def level_coefs(moments, gain, shift, count):
    mean = moments[0:1] / count
    spread = moments[1:2] / count - mean * mean
    return mean, lax.rsqrt(spread + EPSILON), gain, shift


def slope_of(conv, cotan, coefs):
    mean, rstd, gain, shift = coefs
    centred = conv.astype(F32) - mean
    half = centred * (0.5 * rstd * gain) + 0.5 * shift
    turn = jnp.tanh(half)
    return centred, cotan.astype(F32) * ((1.0 + turn) * (1.0 + half * (1.0 - turn)))


def masked(cells, cols):
    if cells.shape[0] == cols:
        return cells
    col = lax.broadcasted_iota(jnp.int32, cells.shape, 0)
    return jnp.where(col < cols, cells, 0.0)


def staged(fills, dots):
    fills[0]()
    for index, dot in enumerate(dots):
        if index + 1 < len(fills):
            fills[index + 1]()
        dot()


def conv_rows(lhs, w_ref):
    return jnp.dot(lhs, w_ref[...].reshape(lhs.shape[1], -1), preferred_element_type=F32).astype(BF16)


def add_moments(sums, conv, cols):
    chan = conv.shape[2]
    conv = conv.astype(F32)
    if conv.shape[1] != cols:
        conv = conv[:, :cols]
    conv = conv.reshape(-1, 8, chan)
    sums[0].append(jnp.sum(conv, 0))
    sums[1].append(jnp.sum(conv * conv, 0))


def folded(parts):
    total = parts[0]
    for part in parts[1:]:
        total = total + part
    return jnp.sum(total, 0, keepdims=True)


def inner_kernel(four_ref, six_ref, w_ref, conv_four_ref, conv_six_ref, moments_ref, three_four, three_six):
    rows_four, cols_four = four_ref.shape[:2]
    rows_six, cols_six = six_ref.shape[:2]
    pitch_four, pitch_six = three_four.shape[1], three_six.shape[1]
    sums_four, sums_six = ([], []), ([], [])
    inner = rows_four - 2
    count = max(1, inner // 9)
    bounds = [index * inner // count for index in range(count + 1)]

    def fill_four(row):
        put_three(three_four, row, four_ref[row].astype(F32), cols_four, False)

    def fill_six(row):
        put_three(three_six, row, widen(six_ref[row], pitch_six), cols_six, False)

    def dot(start, end):
        lhs = beside(three_four, (start, start + 1, start + 2), end - start)
        cells = lhs.shape[0]
        if end == inner:
            lhs = jnp.concatenate([lhs, beside(three_six, (0, 1, 2), rows_six - 2)], 0)
        conv = conv_rows(lhs, w_ref)
        four = conv[:cells].reshape(end - start, pitch_four, -1)
        conv_four_ref[start:end] = four
        add_moments(sums_four, four, cols_four)
        if end == inner:
            six = conv[cells:].reshape(rows_six - 2, pitch_six, -1)
            conv_six_ref[...] = six
            add_moments(sums_six, six, cols_six)

    fills, dots, done = [], [], 0
    for start, end in zip(bounds[:-1], bounds[1:]):
        todo = [functools.partial(fill_four, row) for row in range(done, end + 2)]
        if end == inner:
            todo += [functools.partial(fill_six, row) for row in range(rows_six)]
        fills.append(lambda todo=todo: [fill() for fill in todo])
        done = end + 2
        dots.append(functools.partial(dot, start, end))
    staged(fills, dots)
    moments_ref[...] = jnp.concatenate([folded(parts) for parts in sums_four + sums_six], 0)


def outer_level(x_ref, top, bottom, valid, three):
    rows, cols = x_ref.shape[:2]
    pitch = three.shape[1]
    for edge in range(2):
        put_three(three, edge, top(edge) * valid[0], cols, False)
        put_three(three, 2 + edge, widen(x_ref[edge], pitch), cols, False)
        put_three(three, 4 + edge, widen(x_ref[rows - 2 + edge], pitch), cols, False)
        put_three(three, 6 + edge, bottom(edge) * valid[1], cols, False)
    return [beside(three, (start, start + 1, start + 2), 2) for start in (0, 4)]


def outer_kernel(
    sp_count, four_ref, six_ref, above_ref, below_ref, w_ref, inner_ref,
    conv_four_ref, conv_six_ref, moments_ref, three_four, three_six,
):
    cols_four = four_ref.shape[1]
    valid = edges_valid(sp_count)
    base, pitch_six = 3 * cols_four, three_six.shape[1]

    def reader(ref, start, pitch):
        return lambda edge: ref[start + edge * pitch : start + (edge + 1) * pitch].astype(F32)

    lhs = outer_level(
        four_ref, reader(above_ref, 0, cols_four), reader(below_ref, 0, cols_four), valid, three_four
    ) + outer_level(
        six_ref, reader(above_ref, base, pitch_six), reader(below_ref, base, pitch_six), valid, three_six
    )
    conv = conv_rows(jnp.concatenate(lhs, 0), w_ref)
    sums, begin = [], 0
    for conv_ref, cols in ((conv_four_ref, cols_four), (conv_six_ref, six_ref.shape[1])):
        cells = conv_ref.shape[0] * conv_ref.shape[1]
        rows = conv[begin : begin + cells].reshape(conv_ref.shape)
        begin += cells
        conv_ref[...] = rows
        parts = ([], [])
        add_moments(parts, rows[1:3], cols)
        sums += [folded(part) for part in parts]
    moments_ref[...] = inner_ref[...] + jnp.concatenate(sums, 0)


def turn_kernel(four_ref, six_ref, w_ref, turned_ref, turned_w_ref):
    rows_four, cols_four, chan = four_ref.shape
    rows_six, cols_six = six_ref.shape[:2]
    pitch = pitch_of(cols_six)
    for start, end in chunks_of(rows_four, 8, 4):
        cells = four_ref[start:end].reshape((end - start) * cols_four, chan)
        turned_ref[:, start * cols_four : end * cols_four] = cells.T
    cells = six_ref[...].astype(F32)
    cells = jnp.concatenate([cells, jnp.zeros((rows_six, pitch - cols_six, chan), F32)], 1).astype(BF16)
    turned_ref[:, rows_four * cols_four :] = cells.reshape(rows_six * pitch, chan).T
    for tap in range(9):
        turned_w_ref[tap * chan : (tap + 1) * chan] = w_ref[tap].T


def slope_level(inner_ref, outer_ref, cotan_ref, above, below, coefs, slope_ref):
    rows, cols, chan = cotan_ref.shape
    pitch = inner_ref.shape[1]

    def put(row, conv, cotan):
        centred, slope = slope_of(conv, widen(cotan, pitch), coefs)
        slope_ref[row] = slope
        return centred, slope

    def add(sums, pair):
        centred, slope = pair
        first = jnp.sum(slope.reshape(-1, 8, chan), 0)
        second = jnp.sum((slope * centred).reshape(-1, 8, chan), 0)
        return sums[0] + first, sums[1] + second

    def step(row, sums):
        return add(sums, put(row + 2, inner_ref[row], cotan_ref[row + 1]))

    put(0, outer_ref[0], above)
    put(rows + 1, outer_ref[3], below)
    zero = jnp.zeros((8, chan), F32)
    sums = add((zero, zero), put(1, outer_ref[1], cotan_ref[0]))
    sums = add(sums, put(rows, outer_ref[2], cotan_ref[rows - 1]))
    for row in range(rows - 2):
        sums = step(row, sums)
    first = 0.5 * jnp.sum(sums[0], 0, keepdims=True)
    return first, 0.5 * coefs[1] * jnp.sum(sums[1], 0, keepdims=True)


def slope_kernel(
    counts, inner_four_ref, inner_six_ref, outer_four_ref, outer_six_ref, cotan_four_ref, cotan_six_ref,
    above_ref, below_ref, moments_ref, gain_ref, shift_ref, slope_four_ref, slope_six_ref, slopes_ref,
):
    sums = ()
    cols_four = cotan_four_ref.shape[1]
    starts = (2 * cols_four, 3 * cols_four + 2 * inner_six_ref.shape[1])
    for level, (inner_ref, outer_ref, cotan_ref, slope_ref) in enumerate(
        (
            (inner_four_ref, outer_four_ref, cotan_four_ref, slope_four_ref),
            (inner_six_ref, outer_six_ref, cotan_six_ref, slope_six_ref),
        )
    ):
        pair = moments_ref[2 * level : 2 * level + 2]
        here = slice(level, level + 1)
        edge = slice(starts[level], starts[level] + inner_ref.shape[1])
        coefs = level_coefs(pair, gain_ref[here], shift_ref[here], counts[level])
        sums += slope_level(inner_ref, outer_ref, cotan_ref, above_ref[edge], below_ref[edge], coefs, slope_ref)
    slopes_ref[...] = jnp.concatenate(sums, 0)


def backward_level(cols, inner_ref, outer_ref, slope_ref, valid, coefs, slopes, count, three):
    rows = inner_ref.shape[0] + 2
    pitch = three.shape[1]
    mean, rstd, gain, shift = coefs
    lead = gain * rstd
    offset, factor = lead * (slopes[0:1] / count), lead * rstd * (slopes[1:2] / count)

    def fill_row(row):
        if 2 <= row < rows:
            conv = inner_ref[row - 2]
        else:
            conv = outer_ref[row if row < 2 else row - rows + 2]
        centred = conv.astype(F32) - mean
        dconv = masked((0.5 * lead) * slope_ref[row] - (offset + centred * factor), cols)
        if row == 0:
            dconv = dconv * valid[0]
        elif row == rows + 1:
            dconv = dconv * valid[1]
        put_three(three, row, dconv, cols, True)

    return fill_row


def taps_beside(three, start, end, taps):
    pitch, width = three.shape[1:]
    chan = width // 3
    parts = []
    for row_tap in range(3):
        low, high = max(taps[0] - 3 * row_tap, 0), min(taps[1] - 3 * row_tap, 3)
        if low < high:
            first = start + 2 - row_tap
            rows = three[first : first + end - start, :, low * chan : high * chan]
            parts.append(rows.reshape((end - start) * pitch, (high - low) * chan))
    return jnp.concatenate(parts, 1)


def backward_bounds(rows):
    bounds = [0, min(8, rows)]
    while bounds[-1] < rows:
        bounds.append(min(bounds[-1] + 16, rows))
    return bounds


def weight_dot(turned_ref, three_four, three_six, total, taps, start, end):
    rows_four, rows_six = three_four.shape[0] - 2, three_six.shape[0] - 2
    pitch = three_four.shape[1]
    first, last = start * pitch, end * pitch
    rhs = taps_beside(three_four, start, end, taps)
    if end == rows_four:
        rhs = jnp.concatenate([rhs, taps_beside(three_six, 0, rows_six, taps)], 0)
        last = turned_ref.shape[1]
    term = jnp.dot(turned_ref[:, first:last], rhs, preferred_element_type=F32)
    total[...] = total[...] + term if start else term


def put_shares(totals, sp_count, own_ref, sent_ref):
    taps, share, chan = own_ref.shape
    places = [(total, start) for total in totals for start in range(0, total.shape[1], chan)][:taps]
    place = lax.axis_index("sp") ^ parity(lax.axis_index("rep"))
    for step in range(sp_count):
        begin = pl.multiple_of((place ^ step) * share, share)
        for tap, (total, start) in enumerate(places):
            part = total[pl.ds(begin, share), start : start + chan]
            if step == 0:
                own_ref[tap] = part
            else:
                sent_ref[step - 1, tap] = part.astype(sent_ref.dtype)


def backward_kernel(
    counts, sp_count, cols, turned_ref, inner_four_ref, inner_six_ref, outer_four_ref, outer_six_ref,
    slope_four_ref, slope_six_ref, moments_ref, slopes_ref, gain_ref, shift_ref, three_four, three_six, own_ref,
    sent_ref, rest_ref, grad_gain_ref, grad_shift_ref, total,
):
    valid = edges_valid(sp_count)
    grad_gain_ref[...] = jnp.concatenate([slopes_ref[1:2], slopes_ref[3:4]], 0)
    grad_shift_ref[...] = jnp.concatenate([slopes_ref[0:1], slopes_ref[2:3]], 0)
    parts = []
    for level, inner_ref, outer_ref, slope_ref, three in (
        (0, inner_four_ref, outer_four_ref, slope_four_ref, three_four),
        (1, inner_six_ref, outer_six_ref, slope_six_ref, three_six),
    ):
        here = slice(level, level + 1)
        pair = slice(2 * level, 2 * level + 2)
        coefs = level_coefs(moments_ref[pair], gain_ref[here], shift_ref[here], counts[level])
        parts.append(
            backward_level(
                cols[level], inner_ref, outer_ref, slope_ref, valid, coefs, slopes_ref[pair], counts[level], three
            )
        )
    fill_four, fill_six = parts
    rows_four, rows_six = three_four.shape[0] - 2, three_six.shape[0] - 2
    bounds = backward_bounds(rows_four)
    fills, dots, done = [], [], 0
    for start, end in zip(bounds[:-1], bounds[1:]):
        todo = [functools.partial(fill_four, row) for row in range(done, end + 2)]
        if end == rows_four:
            todo += [functools.partial(fill_six, row) for row in range(rows_six + 2)]
        fills.append(lambda todo=todo: [fill() for fill in todo])
        done = end + 2
        dots.append(
            functools.partial(weight_dot, turned_ref, three_four, three_six, total, (0, EARLY_TAPS), start, end)
        )
    staged(fills, dots)
    put_shares([total], sp_count, own_ref, sent_ref)
    rest_ref[...] = total[:, FIRST_TAPS * rest_ref.shape[0] :]


def weight_kernel(sp_count, turned_ref, three_four, three_six, rest_ref, own_ref, sent_ref, total):
    for start, end in chunks_of(three_four.shape[0] - 2, 16, 4):
        weight_dot(turned_ref, three_four, three_six, total, (EARLY_TAPS, 9), start, end)
    put_shares([rest_ref, total], sp_count, own_ref, sent_ref)


def input_chunks(three, turned, grad, chunks, offset, sent=None):
    cols, chan = grad.shape[1:]
    pitch = three.shape[1]
    for index, (start, end) in enumerate(chunks):
        size = end - start
        lhs = beside(three, (start + 2, start + 1, start), size)
        term = jnp.dot(lhs, turned[...], preferred_element_type=F32)
        grad[start - offset : end - offset] = term.reshape(size, pitch, chan)[:, :cols].astype(BF16)
        if sent is not None:
            sent(index, start, end)


def input_kernel(chunks, three_four, three_six, turned, grad_ref, *six_refs):
    for six_ref in six_refs:
        input_chunks(three_six, turned, six_ref, [(0, six_ref.shape[0])], 0)
    input_chunks(three_four, turned, grad_ref, chunks, chunks[0][0])


def input_last_kernel(chunks, bounds, three_four, turned, six_ref, *rest):
    count = len(bounds) - 1
    earlier, rest = rest[:count], rest[count:]
    grad_four_ref, grad_six_ref, grad_four, sems, sems_four = rest
    copies = [pltpu.make_async_copy(six_ref, grad_six_ref, sems.at[count])]
    copies += [
        pltpu.make_async_copy(part, grad_four_ref.at[bounds[index] : bounds[index + 1]], sems.at[index])
        for index, part in enumerate(earlier)
    ]
    for copy in copies:
        copy.start()
    done = bounds[-1]

    def sent(index, start, end):
        copy = pltpu.make_async_copy(
            grad_four.at[start - done : end - done], grad_four_ref.at[start:end], sems_four.at[index]
        )
        copy.start()
        copies.append(copy)

    input_chunks(three_four, turned, grad_four, chunks, done, sent)
    for copy in copies:
        copy.wait()


def swap(array, axis, stride):
    count = lax.axis_size(axis)
    return lax.ppermute(array, axis, [(i, i ^ stride) for i in range(count)])


def edge_kernel(starts, four_ref, six_ref, cotan_four_ref, cotan_six_ref, *rest):
    outs, six_rows, sems = rest[:-2], rest[-2], rest[-1]
    rows_four, cols_four = four_ref.shape[:2]
    rows_six = six_ref.shape[0]
    pitch = pitch_of(six_ref.shape[1])
    copies = []
    for number, (start, out_ref) in enumerate(zip(starts, outs)):
        last = (1 - jnp.minimum(lax.axis_index("sp"), 1)) if start is None else start
        for part, (ref, row) in enumerate(
            (
                (four_ref, last * (rows_four - 2)),
                (four_ref, last * (rows_four - 2) + 1),
                (cotan_four_ref, last * (rows_four - 1)),
                (six_ref, last * (rows_six - 2)),
                (six_ref, last * (rows_six - 2) + 1),
                (cotan_six_ref, last * (rows_six - 1)),
            )
        ):
            if part < 3:
                target = out_ref.at[part * cols_four : (part + 1) * cols_four]
            else:
                target = six_rows.at[number, part - 3]
            copies.append(pltpu.make_async_copy(ref.at[row], target, sems.at[number, part]))
    for copy in copies:
        copy.start()
    for copy in copies:
        copy.wait()
    for number, out_ref in enumerate(outs):
        for part in range(3):
            begin = 3 * cols_four + part * pitch
            out_ref[begin : begin + pitch] = widen(six_rows[number, part], pitch).astype(BF16)


def edges(four, six, cotan_four, cotan_six):
    count = lax.axis_size("sp")
    starts = (None,) if count == 2 else (0, 1)
    length = 3 * four.shape[1] + 3 * pitch_of(six.shape[1])
    vmem = pl.BlockSpec(memory_space=pltpu.VMEM)
    hbm = pl.BlockSpec(memory_space=pltpu.HBM)
    outs = pl.pallas_call(
        functools.partial(edge_kernel, starts),
        out_shape=tuple(jax.ShapeDtypeStruct((length, four.shape[2]), BF16) for _ in starts),
        in_specs=[hbm] * 4,
        out_specs=tuple(vmem for _ in starts),
        scratch_shapes=[
            pltpu.VMEM((len(starts), 3) + six.shape[1:], BF16),
            pltpu.SemaphoreType.DMA((len(starts), 6)),
        ],
        compiler_params=pltpu.CompilerParams(vmem_limit_bytes=EDGE_LIMIT),
        name="edges",
    )(four, six, cotan_four, cotan_six)
    if count == 2:
        met = swap(outs[0], "sp", 1)
        return met, met
    above = lax.ppermute(outs[1], "sp", [(i, (i + 1) % count) for i in range(count)])
    below = lax.ppermute(outs[0], "sp", [((i + 1) % count, i) for i in range(count)])
    return above, below


def swap_across(array, axis, stride):
    count, sp_count = lax.axis_size("rep"), lax.axis_size("sp")
    rep_stride, sp_stride = (stride, 1) if axis == "rep" else (0, stride ^ 1)
    pairs = [
        (rep * sp_count + sp, (rep ^ rep_stride) * sp_count + (sp ^ sp_stride))
        for rep in range(count)
        for sp in range(sp_count)
    ]
    return lax.ppermute(array, ("rep", "sp"), pairs)


def group_sum(sums):
    sums = sums + swap(sums, "sp", 1)
    stride = 2
    while stride < lax.axis_size("sp"):
        sums = sums + swap_across(sums, "sp", stride)
        stride = 2 * stride
    stride = 1
    while stride < GROUP:
        met = lax.optimization_barrier([swap_across(sums, "rep", k * stride) for k in FAR_FIRST])
        sums = (sums + met[2]) + (met[1] + met[0])
        stride = RADIX * stride
    return sums


def every_group(sums):
    stride = GROUP
    while stride < lax.axis_size("rep"):
        sums = sums + swap(sums, "rep", stride)
        stride = 2 * stride
    return sums


class Places(NamedTuple):
    digits: list
    first: list
    second: list
    odd: jax.Array


def places():
    rep = lax.axis_index("rep")
    digits = [(rep & (RADIX - 1)) ^ k for k in range(RADIX)]
    second = 9 - FIRST_TAPS
    return Places(
        digits,
        [FIRST_TAPS * digit for digit in digits],
        [RADIX * FIRST_TAPS + second * digit for digit in digits],
        parity(rep) == 1,
    )


def piece_of(pieces, index):
    sizes = (1,) + pieces.shape[1:]
    return lax.dynamic_slice(pieces, (index, 0, 0), sizes, allow_negative_indices=False)[0]


def scatter_pieces(own, met, found):
    chan = own.shape[2]
    parts = [part.reshape(RADIX, -1, chan) for part in [own] + met]

    def piece(k):
        total = piece_of(parts[0], found.digits[k])
        for part in parts[1:]:
            total = total + piece_of(part, found.digits[k]).astype(F32)
        return total

    return piece(0), [piece(k).astype(BF16) for k in FAR_FIRST]


def added(own, met):
    return (own + met[2].astype(F32)) + (met[1].astype(F32) + met[0].astype(F32))


def fours(pieces, stride):
    return [swap(piece, "rep", k * stride) for k, piece in zip(FAR_FIRST, pieces)]


def swap_high(array, even, odd):
    count, sp_count = lax.axis_size("rep"), lax.axis_size("sp")
    pairs = []
    for rep in range(count):
        for sp in range(sp_count):
            stride = odd if (sp ^ parity(rep)) & 1 else even
            pairs.append((rep * sp_count + sp, (rep ^ stride) * sp_count + (sp ^ 1)))
    return lax.ppermute(array, ("rep", "sp"), pairs)


def bring(array, k):
    count, sp_count = lax.axis_size("rep"), lax.axis_size("sp")
    pairs = [
        (rep * sp_count + sp, (rep ^ k) * sp_count + (sp ^ parity(rep)))
        for rep in range(count)
        for sp in range(sp_count)
    ]
    return lax.ppermute(array, ("rep", "sp"), pairs)


def both(own, met):
    return (own.astype(F32) + met.astype(F32)).astype(BF16)


def every_share(total):
    stride = GROUP
    while stride < lax.axis_size("rep"):
        total = added(total.astype(F32), fours([total] * 3, stride)).astype(BF16)
        stride = RADIX * stride
    return total


def gather(total, found, tied=False):
    beside, far = swap(total, "sp", 1), bring(total, FAR_FIRST[0])
    if tied:
        beside, total = lax.optimization_barrier((beside, total))
    own = jnp.where(found.odd, beside, total)
    return [far] + [bring(total, k) for k in FAR_FIRST[1:]] + [own], beside


def put_pieces(whole, pieces, starts):
    for k, piece in zip(FAR_FIRST + (0,), pieces):
        piece = piece.reshape((-1,) + whole.shape[1:]).astype(F32)
        whole = lax.dynamic_update_slice(whole, piece, (starts[k], 0, 0), allow_negative_indices=False)
    return whole


def local(level_four, level_six, conv_weight, bn_gain, bn_shift, cotan_four, cotan_six):
    sp_count = lax.axis_size("sp")
    images = level_four.shape[0]
    four, six, cot_four, cot_six = (a[0] for a in (level_four, level_six, cotan_four, cotan_six))
    rows_four, cols_four, chan = four.shape
    rows_six, cols_six = six.shape[:2]
    pitch_four, pitch_six = pitch_of(cols_four), pitch_of(cols_six)
    counts = (
        float(images * GROUP * rows_four * sp_count * cols_four),
        float(images * GROUP * rows_six * sp_count * cols_six),
    )
    found, four = lax.optimization_barrier((places(), four))
    above, below = edges(four, six, cot_four, cot_six)
    vmem = pl.BlockSpec(memory_space=pltpu.VMEM)
    hbm = pl.BlockSpec(memory_space=pltpu.HBM)
    params = pltpu.CompilerParams(vmem_limit_bytes=VMEM_LIMIT)
    framed_four = jax.ShapeDtypeStruct((rows_four + 2, pitch_four, chan), BF16)
    framed_six = jax.ShapeDtypeStruct((rows_six + 2, pitch_six, chan), BF16)
    four_sums = jax.ShapeDtypeStruct((4, chan), F32)
    flops = 2 * 9 * chan * chan * (rows_four * cols_four + rows_six * cols_six)

    def cost(share, size):
        return pl.CostEstimate(flops=int(flops * share), bytes_accessed=size, transcendentals=0)

    inner_four, inner_six, inner_moments = pl.pallas_call(
        inner_kernel,
        out_shape=(
            jax.ShapeDtypeStruct((rows_four - 2, pitch_four, chan), BF16),
            jax.ShapeDtypeStruct((rows_six - 2, pitch_six, chan), BF16),
            four_sums,
        ),
        in_specs=[vmem] * 3,
        out_specs=(vmem, vmem, vmem),
        scratch_shapes=[
            pltpu.VMEM((rows_four, pitch_four, 3 * chan), BF16),
            pltpu.VMEM((rows_six, pitch_six, 3 * chan), BF16),
        ],
        compiler_params=params,
        cost_estimate=cost(1, 4 * four.size),
        name="forward_inner",
    )(four, six, conv_weight)
    outer_four, outer_six, moments = pl.pallas_call(
        functools.partial(outer_kernel, sp_count),
        out_shape=(
            jax.ShapeDtypeStruct((4, pitch_four, chan), BF16),
            jax.ShapeDtypeStruct((4, pitch_six, chan), BF16),
            four_sums,
        ),
        in_specs=[vmem] * 6,
        out_specs=(vmem, vmem, vmem),
        scratch_shapes=[
            pltpu.VMEM((8, pitch_four, 3 * chan), BF16),
            pltpu.VMEM((8, pitch_six, 3 * chan), BF16),
        ],
        compiler_params=params,
        cost_estimate=cost(0.1, four.size),
        name="forward_outer",
    )(four, six, above, below, conv_weight, inner_moments)
    moments, four, six = lax.optimization_barrier((moments, four, six))
    turned, turned_weight = pl.pallas_call(
        turn_kernel,
        out_shape=(
            jax.ShapeDtypeStruct((chan, rows_four * cols_four + rows_six * pitch_six), BF16),
            jax.ShapeDtypeStruct((9 * chan, chan), BF16),
        ),
        in_specs=[vmem] * 3,
        out_specs=(vmem, vmem),
        compiler_params=params,
        cost_estimate=cost(0.3, 4 * four.size),
        name="turn",
    )(four, six, conv_weight)
    moments, turned, turned_weight = lax.optimization_barrier((group_sum(moments), turned, turned_weight))

    slope_four, slope_six, slopes = pl.pallas_call(
        functools.partial(slope_kernel, counts),
        out_shape=(
            jax.ShapeDtypeStruct(framed_four.shape, F32),
            jax.ShapeDtypeStruct(framed_six.shape, F32),
            four_sums,
        ),
        in_specs=[vmem] * 11,
        out_specs=(vmem,) * 3,
        compiler_params=params,
        cost_estimate=cost(0.01, 4 * four.size),
        name="slopes",
    )(
        inner_four, inner_six, outer_four, outer_six, cot_four, cot_six, above, below, moments, bn_gain, bn_shift
    )
    slopes = group_sum(slopes)

    share = chan // sp_count
    wide_four, wide_six = (
        jax.ShapeDtypeStruct(framed.shape[:2] + (3 * chan,), BF16) for framed in (framed_four, framed_six)
    )
    def shares(taps, dtype):
        return (
            jax.ShapeDtypeStruct((taps, share, chan), F32),
            jax.ShapeDtypeStruct((sp_count - 1, taps, share, chan), dtype),
        )

    three_four, three_six, own_a, sent_a, rest, grad_gain, grad_shift = pl.pallas_call(
        functools.partial(backward_kernel, counts, sp_count, (cols_four, cols_six)),
        out_shape=(wide_four, wide_six)
        + shares(FIRST_TAPS, BF16)
        + (jax.ShapeDtypeStruct((chan, (EARLY_TAPS - FIRST_TAPS) * chan), F32),)
        + (jax.ShapeDtypeStruct((2, chan), F32),) * 2,
        in_specs=[vmem] * 11,
        out_specs=(vmem,) * 7,
        scratch_shapes=[pltpu.VMEM((chan, EARLY_TAPS * chan), F32)],
        compiler_params=params,
        cost_estimate=cost(0.6, 8 * four.size),
        name="backward",
    )(
        turned, inner_four, inner_six, outer_four, outer_six, slope_four, slope_six, moments, slopes,
        bn_gain, bn_shift,
    )
    sent_a, three_six = lax.optimization_barrier((sent_a, three_six))
    met_a = [swap(sent_a[step], "sp", step + 1) for step in range(sp_count - 1)]
    own_b, sent_b = pl.pallas_call(
        functools.partial(weight_kernel, sp_count),
        out_shape=shares(9 - FIRST_TAPS, F32),
        in_specs=[vmem] * 4,
        out_specs=(vmem, vmem),
        scratch_shapes=[pltpu.VMEM((chan, (9 - EARLY_TAPS) * chan), F32)],
        compiler_params=params,
        cost_estimate=cost(0.6, 8 * four.size),
        name="weights",
    )(turned, three_four, three_six, rest)
    met_a, sent_b = lax.optimization_barrier((met_a, sent_b))
    met_b = [swap(sent_b[step], "sp", step + 1) for step in range(sp_count - 1)]

    chunks = chunks_of(rows_four, 8)
    cuts = [part * len(chunks) // 3 for part in range(4)]
    groups = [chunks[low:high] for low, high in zip(cuts[:-1], cuts[1:]) if low < high]
    bounds = [group[0][0] for group in groups]

    def inputs(number, three):
        group = groups[number]
        parts = (jax.ShapeDtypeStruct((group[-1][1] - group[0][0], cols_four, chan), BF16),)
        if number == len(groups) - 2:
            parts += (jax.ShapeDtypeStruct(six.shape, BF16),)
        return pl.pallas_call(
            functools.partial(input_kernel, group),
            out_shape=parts,
            in_specs=[vmem] * 3,
            out_specs=(vmem,) * len(parts),
            compiler_params=params,
            cost_estimate=cost(0.3, four.size),
            name="inputs",
        )(three, three_six, turned_weight)

    grad_gain, grad_shift = every_group(grad_gain), every_group(grad_shift)

    piece_a, pieces_a = scatter_pieces(own_a, met_a, found)
    met_a = fours(pieces_a, 1)
    piece_b, pieces_b = scatter_pieces(own_b, met_b, found)
    met_b = fours(pieces_b, 1)
    met_a, unused = lax.optimization_barrier((met_a, pieces_b))

    piece_a = added(piece_a, met_a).astype(BF16)
    piece_a, three_four = lax.optimization_barrier((piece_a, three_four))
    met_a = swap_high(piece_a, RADIX, 2 * RADIX)
    earlier = list(inputs(0, three_four))
    whole = jnp.zeros((9 * RADIX, share // RADIX, chan), F32)
    met_b, earlier, whole = lax.optimization_barrier((met_b, earlier, whole))

    piece_b = added(piece_b, met_b).astype(BF16)
    met_b = swap_high(piece_b, RADIX, 2 * RADIX)
    met_a, unused = lax.optimization_barrier((met_a, piece_b))

    piece_a = both(piece_a, met_a)
    piece_a, three_four = lax.optimization_barrier((piece_a, three_four))
    met_a = swap_high(piece_a, 2 * RADIX, RADIX)
    if len(groups) > 2:
        earlier = earlier + list(inputs(1, three_four))
    met_b, earlier = lax.optimization_barrier((met_b, earlier))

    piece_b = both(piece_b, met_b)
    met_b = swap_high(piece_b, 2 * RADIX, RADIX)
    met_a, unused = lax.optimization_barrier((met_a, piece_b))

    piece_a = every_share(both(piece_a, met_a))
    pieces_a, unused = gather(piece_a, found)
    piece_b = every_share(both(piece_b, met_b))
    pieces_b, beside = gather(piece_b, found, True)
    unused, three_four = lax.optimization_barrier(((beside, pieces_a[0]), three_four))
    done = bounds[-1]
    grad_four, grad_six = pl.pallas_call(
        functools.partial(input_last_kernel, groups[-1], bounds),
        out_shape=(
            jax.ShapeDtypeStruct(four.shape, BF16),
            jax.ShapeDtypeStruct(six.shape, BF16),
        ),
        in_specs=[vmem] * (2 + len(earlier)),
        out_specs=(hbm, hbm),
        scratch_shapes=[
            pltpu.VMEM((rows_four - done, cols_four, chan), BF16),
            pltpu.SemaphoreType.DMA((len(groups),)),
            pltpu.SemaphoreType.DMA((len(chunks),)),
        ],
        compiler_params=params,
        cost_estimate=cost(0.4, 2 * four.size),
        name="inputs_last",
    )(three_four, turned_weight, earlier[-1], *earlier[:-1])
    pieces_a, grad_six = lax.optimization_barrier((pieces_a, grad_six))
    whole = put_pieces(whole, pieces_a, found.first)
    whole = put_pieces(whole, pieces_b, found.second)
    grad_weight = whole.reshape(9, share, chan)
    return (grad_four[None], grad_six[None], grad_weight, grad_gain, grad_shift)


def solution(mesh):
    placed = (
        P("rep", "sp", None, None),
        P("rep", "sp", None, None),
        P(),
        P(),
        P(),
        P("rep", "sp", None, None),
        P("rep", "sp", None, None),
    )
    return jax.shard_map(
        local,
        mesh=mesh,
        in_specs=placed,
        out_specs=(
            P("rep", "sp", None, None),
            P("rep", "sp", None, None),
            P(None, "sp", None),
            P(),
            P(),
        ),
        check_vma=False,
    )
```
